32 devices in a mesh: gx: 4 (over y, x), gy: 2 (over core), gz: 4 (over z).
Axes of the slice: x: 2, y: 2, z: 4, core: 2. Of those that a mesh axis runs over, the one named last changes fastest.
Arguments:
- positions: float32 [4, 2, 4, 3, 64], P('gx', 'gy', 'gz'), may hold values from 0 to 5
- species: int32 [4, 2, 4, 64], P('gx', 'gy', 'gz'), may hold values from 0 to 7
- counts: int32 [4, 2, 4], P('gx', 'gy', 'gz'), may hold values from 4 to 64, as said below
- embed: bfloat16 [8, 128], replicated, may hold values from -6 to 6
- radial_one: float32 [2, 4, 128], replicated, may hold values from -6 to 6
- mix_one: bfloat16 [128, 256], replicated, may hold values from -0.375 to 0.375
- read_one: float32 [128], replicated, may hold values from -0.5 to 0.5
- radial_two: float32 [4, 128], replicated, may hold values from -6 to 6
- mix_two: bfloat16 [128, 128], replicated, may hold values from -0.5 to 0.5
- read_hidden: bfloat16 [16, 128], replicated, may hold values from -0.5 to 0.5
- read_out: float32 [16], replicated, may hold values from -1.5 to 1.5
Outputs:
- forces: float32 [4, 2, 4, 3, 64], P('gx', 'gy', 'gz')
- energies: float32 [4, 2, 4, 64], P('gx', 'gy', 'gz')
- features: bfloat16 [4, 2, 4, 128, 64], P('gx', 'gy', 'gz')
The draws below stay inside these ranges and needn't reach their ends.
Inputs may be any that keep to these rules, and one draw needn't show every extreme that they name: `counts`: the first block of the grid holds exactly 64 live atoms.
All inputs are finite; a program needn't handle non-finite values.
Results may differ from the reference program's by a relative error of at most 0.018.
Values may be sent and summed in bfloat16 or wider, within the bound.
No kernel may reach another device: no remote copies, remote signals or barrier semaphores. Data moves between devices by JAX's collectives and lax.ppermute only.
A program may use at most 64 MiB of HBM per device.

```python
import functools
import math
import jax
import jax.numpy as jnp
from jax import lax

C = 128
ATOMS = 64
NB = 4
NSPEC = 8
READ = 16
NX = 4
NY = 2
NZ = 4


def draw_counts(key, part):
    values = jax.random.randint(key, (NX, NY, NZ), max(1, ATOMS // 16), ATOMS + 1)
    return values.at[0, 0, 0].set(ATOMS).astype(jnp.int32)


def with_ends(values, stream_key, low, high):
    longest = values.shape.index(max(values.shape))
    spots = []
    for shift in (0, 1):
        where = [jax.random.randint(jax.random.fold_in(stream_key, axis), (), 0, length) for axis, length in enumerate(values.shape)]
        where[longest] = (where[longest] + shift) % values.shape[longest]
        spots.append(tuple(where))
    return values.at[spots[0]].set(low).at[spots[1]].set(high)


def block_levels(stream_key, shape, shards, low, largest):
    gain = 1.0
    for position, shards_of in shards:
        heights = jax.random.uniform(jax.random.fold_in(jax.random.fold_in(stream_key, 6), position), (shards_of,), jnp.float32, low / len(shards), largest / len(shards))
        gain = gain * jnp.repeat(jnp.exp(heights), shape[position] // shards_of).reshape((-1,) + (1,) * (len(shape) - 1 - position))
    return gain


def normal_values(key, shape, deviation, limit, kind=jnp.bfloat16):
    values = jax.random.normal(key, shape, jnp.float32) * deviation
    return jnp.minimum(jnp.maximum(values, -limit), limit).astype(kind)


def setup_inputs(seed: int = 0) -> dict:
    keys = jax.random.split(jax.random.key(seed), 12)
    positions = jnp.clip(5.0 * jax.random.uniform(keys[0], (NX, NY, NZ, 3, ATOMS), jnp.float32) ** block_levels(keys[0], (NX, NY, NZ, 3, ATOMS), ((0, 4), (1, 2), (2, 4)), -0.2, 0.2), 0.0, 5.0)
    species = with_ends(jax.random.randint(keys[1], (NX, NY, NZ, ATOMS), 0, NSPEC), jax.random.fold_in(keys[1], 1), 0, NSPEC - 1).astype(jnp.int32)
    counts = draw_counts(jax.random.fold_in(keys[11], 71), 0)
    embed = normal_values(keys[3], (NSPEC, C), 1.0, 6.0)
    radial_one = normal_values(keys[4], (2, NB, C), 1.0, 6.0, jnp.float32)
    mix_one = normal_values(keys[5], (C, 2 * C), (2 * C) ** -0.5, 0.375)
    read_one = normal_values(keys[6], (C,), C ** -0.5, 0.5, jnp.float32)
    radial_two = normal_values(keys[7], (NB, C), 1.0, 6.0, jnp.float32)
    mix_two = normal_values(keys[8], (C, C), C ** -0.5, 0.5)
    read_hidden = normal_values(keys[9], (READ, C), C ** -0.5, 0.5)
    read_out = normal_values(keys[10], (READ,), READ ** -0.5, 1.5, jnp.float32)
    return dict(positions=positions, species=species, counts=counts, embed=embed, radial_one=radial_one, mix_one=mix_one, read_one=read_one, radial_two=radial_two, mix_two=mix_two, read_hidden=read_hidden, read_out=read_out)


CELL_SIDE = 5.0
CUT_SQUARE = 25.0
SOFTEN = 0.25
MSG_SCALE = 0.05
ROOT_THREE = math.sqrt(3.0)
OFFSETS = [(first, second, third) for first in (-1, 0, 1) for second in (-1, 0, 1) for third in (-1, 0, 1)]

def pair_terms(own_coords, far_coords, own_live, far_live, offset, nbasis, vectors):
    displace = jnp.array(offset, jnp.float32) * CELL_SIDE
    separation = far_coords[..., :, None, :] + displace[:, None, None] - own_coords[..., :, :, None]
    dist_sq = lax.optimization_barrier(jnp.sum(separation * separation, axis=-3)) + SOFTEN
    inverse = lax.rsqrt(dist_sq)
    radius = dist_sq * inverse
    envelope = jnp.square(jnp.maximum(1.0 - dist_sq / CUT_SQUARE, 0.0))
    pair_mask = own_live[..., :, None] & far_live[..., None, :]
    if offset == (0, 0, 0):
        slot_index = jnp.arange(own_coords.shape[-1])
        pair_mask = pair_mask & (slot_index[:, None] != slot_index[None, :])
    radial = envelope * inverse * pair_mask.astype(jnp.float32)
    waves = (jnp.arange(nbasis) + 1).astype(jnp.float32) * (math.pi / CELL_SIDE)
    basis = jnp.sin(waves[:, None, None] * radius[..., None, :, :]) * radial[..., None, :, :]
    scalar_mat = basis.astype(jnp.bfloat16)
    if not vectors:
        return scalar_mat
    unit = ROOT_THREE * separation * inverse[..., None, :, :]
    vector_mat = (unit[..., :, None, :, :] * basis[..., None, :, :, :]).astype(jnp.bfloat16)
    return (scalar_mat, vector_mat)

def first_term(own_coords, far_coords, own_live, far_live, far_weights, offset):
    nbasis = far_weights.shape[-3]
    scalar_mat, vector_mat = pair_terms(own_coords, far_coords, own_live, far_live, offset, nbasis, True)
    scalar_msg = jnp.einsum('...ncj,...nij->...ci', far_weights[..., 0, :, :, :].astype(jnp.float32), scalar_mat.astype(jnp.float32))
    vector_msg = jnp.einsum('...ncj,...knij->...kci', far_weights[..., 1, :, :, :].astype(jnp.float32), vector_mat.astype(jnp.float32))
    return (scalar_msg, vector_msg)

def second_term(own_coords, far_coords, own_live, far_live, far_weights, offset):
    nbasis = far_weights.shape[-3]
    scalar_mat = pair_terms(own_coords, far_coords, own_live, far_live, offset, nbasis, False)
    return jnp.einsum('...ncj,...nij->...ci', far_weights.astype(jnp.float32), scalar_mat.astype(jnp.float32))

def rolled(array, offset):
    return jnp.roll(array, (-offset[0], -offset[1], -offset[2]), axis=(0, 1, 2))

def reference(positions, species, counts, embed, radial_one, mix_one, read_one, radial_two, mix_two, read_hidden, read_out):
    slot_index = jnp.arange(positions.shape[-1])
    occupied = slot_index < counts[..., None]
    element = jnp.where(occupied, species, -1)
    onehot = (element[..., None, :] == jnp.arange(embed.shape[0])[:, None]).astype(jnp.float32)
    embedded = jnp.einsum('sc,xyzsa->xyzca', embed.astype(jnp.float32), onehot).astype(jnp.bfloat16)
    weighted_one = (radial_one[:, :, :, None] * embedded[..., None, None, :, :].astype(jnp.float32)).astype(jnp.bfloat16)

    def layers(coords):
        scalar_msg = jnp.zeros(embedded.shape, jnp.float32)
        vector_msg = jnp.zeros(embedded.shape[:3] + (3,) + embedded.shape[3:], jnp.float32)
        for offset in OFFSETS:
            term = jax.checkpoint(functools.partial(first_term, offset=offset))
            part_scalar, part_vector = term(coords, rolled(coords, offset), occupied, rolled(occupied, offset), rolled(weighted_one, offset))
            scalar_msg = scalar_msg + part_scalar
            vector_msg = vector_msg + part_vector
        scalar_msg = MSG_SCALE * scalar_msg
        vector_msg = MSG_SCALE * vector_msg
        invariants = jnp.concatenate([scalar_msg, lax.optimization_barrier(jnp.sum(vector_msg * vector_msg, axis=-3))], axis=-2).astype(jnp.bfloat16)
        mixing = jnp.einsum('dc,...ca->...da', mix_one.astype(jnp.float32), invariants.astype(jnp.float32))
        layer_one = (embedded.astype(jnp.float32) + jax.nn.silu(mixing)).astype(jnp.bfloat16)
        weighted_two = (radial_two[:, :, None] * layer_one[..., None, :, :].astype(jnp.float32)).astype(jnp.bfloat16)
        message_two = jnp.zeros(embedded.shape, jnp.float32)
        for offset in OFFSETS:
            term = jax.checkpoint(functools.partial(second_term, offset=offset))
            message_two = message_two + term(coords, rolled(coords, offset), occupied, rolled(occupied, offset), rolled(weighted_two, offset))
        rounded_two = (MSG_SCALE * message_two).astype(jnp.bfloat16)
        mixing_two = jnp.einsum('dc,...ca->...da', mix_two.astype(jnp.float32), rounded_two.astype(jnp.float32))
        features = (layer_one.astype(jnp.float32) + jax.nn.silu(mixing_two)).astype(jnp.bfloat16)
        hidden = jax.nn.silu(jnp.einsum('mc,...ca->...ma', read_hidden.astype(jnp.float32), features.astype(jnp.float32)))
        energy = jnp.einsum('c,...ca->...a', read_one, layer_one.astype(jnp.float32)) + jnp.einsum('m,...ma->...a', read_out, hidden)
        energy = energy * occupied.astype(jnp.float32)
        return (energy, features)
    energy, pullback, features = jax.vjp(layers, positions, has_aux=True)
    gradient, = pullback(jnp.ones_like(energy))
    return (-gradient, energy, features)
```

```python
import itertools
import math

import jax
import jax.numpy as jnp
from jax import lax
from jax.experimental import pallas as pl
from jax.experimental.pallas import tpu as pltpu
from jax.sharding import PartitionSpec as P

CELL_SIDE = 5.0
CUT_SQUARE = 25.0
SOFTEN = 0.25
MSG_SCALE = 0.05
ROOT_THREE = math.sqrt(3.0)
FAR = 1.0e4
AXES = ("gx", "gy", "gz")
F32 = jnp.float32
BF16 = jnp.bfloat16
COS_TERMS = (
    0.9999999997799041,
    -4.934802137078749,
    4.058709159554242,
    -1.335212003029471,
    0.23493731372678894,
    -0.024396324214549327,
)
SIN_TERMS = (
    3.14159265353629,
    -5.167712764624453,
    2.550163318944743,
    -0.5992521977996564,
    0.08205040170151112,
    -0.007028386239784362,
)
VMEM_LIMIT = 48 * 1024 * 1024
NT = (((1,), (1,)), ((), ()))
NN = (((1,), (0,)), ((), ()))


def dot(a, b, dims=NN):
    return lax.dot_general(a, b, dims, preferred_element_type=F32)


def dot_exact(a, b, dims=NN):
    return lax.dot_general(
        a, b, dims, precision=lax.Precision.HIGHEST, preferred_element_type=F32
    )


def split_dot(a, b):
    high = a.astype(BF16)
    low = (a - high.astype(F32)).astype(BF16)
    return dot(high, b) + dot(low, b)


def offsets_of(count):
    return (0, 1) if count == 2 else (0, 1, -1)


def poly(terms, arg):
    total = arg * terms[-1] + terms[-2]
    for term in terms[-3::-1]:
        total = total * arg + term
    return total


class Plan:
    def __init__(self, mesh, slots, nbasis, nspec):
        self.sizes = {axis: mesh.shape[axis] for axis in AXES}
        self.ndev = math.prod(self.sizes.values())
        self.tiles = list(
            itertools.product(offsets_of(self.sizes["gx"]), offsets_of(self.sizes["gz"]))
        )
        self.sides = offsets_of(self.sizes["gy"])
        self.slots = slots
        self.width = len(self.sides) * slots
        self.far = len(self.tiles) * self.width
        self.nbasis = nbasis
        self.nspec = nspec
        self.wrapped = [self.sizes[axis] == 2 for axis in AXES]

    def neighbour_ids(self):
        index = {axis: lax.axis_index(axis) for axis in AXES}

        def moved(axis, step):
            return lax.rem(index[axis] + (step + self.sizes[axis]), self.sizes[axis])

        ids = []
        for ox, oz in self.tiles:
            for oy in self.sides:
                place = (moved("gx", ox) * self.sizes["gy"] + moved("gy", oy)) * self.sizes["gz"]
                ids.append(place + moved("gz", oz))
        return jnp.stack(ids).astype(jnp.int32)

    def offset(self, tile, side):
        ox, oz = self.tiles[tile]
        return (ox, self.sides[side], oz)


def separations(plan, rows, cols):
    parts = []
    for axis in range(3):
        diff = rows[axis] - cols[axis]
        if plan.wrapped[axis]:
            diff = jnp.where(diff > CELL_SIDE, diff - 2.0 * CELL_SIDE, diff)
        parts.append(diff)
    return parts


def distance(plan, parts, tile):
    dist_sq = parts[0] * parts[0] + parts[1] * parts[1] + parts[2] * parts[2] + SOFTEN
    if tile == 0:
        row = lax.broadcasted_iota(jnp.int32, dist_sq.shape, 0)
        col = lax.broadcasted_iota(jnp.int32, dist_sq.shape, 1)
        dist_sq = jnp.where(row == col, FAR, dist_sq)
    return dist_sq, lax.rsqrt(dist_sq)


def waves(dist_sq, inverse):
    arg = jnp.minimum(dist_sq * inverse * (1.0 / CELL_SIDE) - 0.5, 0.5)
    square = arg * arg
    return poly(COS_TERMS, square), -(arg * poly(SIN_TERMS, square))


def first_kernel(plan, nrefs, ids_ref, *refs):
    far_refs, refs = refs[:nrefs], refs[nrefs:]
    (cols_ref, table_ref, embed_ref, mix_ref), refs = refs[:4], refs[4:]
    rows_ref, basis_ref, layer_ref, vector_ref, mixing_ref, pair_ref = refs
    slots, nbasis, nspec = plan.slots, plan.nbasis, plan.nspec
    cols = [cols_ref[:, axis : axis + 1] for axis in range(3)]
    species = lax.broadcasted_iota(jnp.int32, (nbasis * nspec, plan.width), 0) % nspec
    hot = []
    for tile in range(len(plan.tiles)):
        blocks = []
        for side in range(len(plan.sides)):
            block = fetch(plan, ids_ref, far_refs, tile, side)
            shift = plan.offset(tile, side)
            blocks.append([block[k : k + 1] + CELL_SIDE * shift[k] for k in range(3)] + [block[3:4]])
        rows = [jnp.concatenate(parts, axis=1) for parts in zip(*blocks)]
        for k in range(4):
            rows_ref[tile, k : k + 1] = rows[k]
        hot.append((rows[3].astype(jnp.int32) == species).astype(F32).astype(BF16))
        parts = separations(plan, rows, cols)
        dist_sq, inverse = distance(plan, parts, tile)
        sine, cosine = waves(dist_sq, inverse)
        fade = jnp.maximum(1.0 - dist_sq * (1.0 / CUT_SQUARE), 0.0)
        radial = fade * fade * inverse
        units = [part * (inverse * ROOT_THREE) for part in parts]
        before, now = None, sine * radial
        lanes = slice(tile * plan.width, (tile + 1) * plan.width)
        for n in range(nbasis):
            if n == 1:
                before, now = now, 2.0 * cosine * now
            elif n > 1:
                before, now = now, 2.0 * cosine * now - before
            packed = now.astype(BF16)
            basis_ref[n, :, lanes] = packed
            pair_ref[n, :slots, lanes] = packed
            for k in range(3):
                pair_ref[n, (k + 1) * slots : (k + 2) * slots, lanes] = (units[k] * now).astype(BF16)
    hot = jnp.concatenate(hot, axis=1)
    gathered = dot(pair_ref[...].reshape(nbasis * 4 * slots, plan.far), hot, NT)
    gathered = gathered.reshape(nbasis, 4 * slots, nbasis * nspec)
    group = lax.broadcasted_iota(jnp.int32, gathered.shape[1:], 1) // nspec
    counted = jnp.zeros(gathered.shape[1:], F32)
    for n in range(nbasis):
        counted = jnp.where(group == n, gathered[n], counted)
    scalar = MSG_SCALE * split_dot(counted[:slots], table_ref[0])
    vector = MSG_SCALE * split_dot(counted[slots:], table_ref[1])
    vector_ref[...] = vector
    squares = vector * vector
    norm = squares[:slots] + squares[slots : 2 * slots] + squares[2 * slots :]
    invariants = jnp.concatenate([scalar.astype(BF16), norm.astype(BF16)], axis=1)
    mixing = dot(invariants, mix_ref[...], NT)
    mixing_ref[...] = mixing
    layer_ref[...] = (embed_ref[...] + mixing * sigmoid(mixing)).astype(BF16)


def sigmoid(value):
    return 1.0 / (1.0 + jnp.exp(-value))


def fetch(plan, ids_ref, far_refs, tile, side):
    if len(far_refs) == 1:
        return far_refs[0][ids_ref[tile * len(plan.sides) + side]]
    return far_refs[side][tile]


def gather_far(plan, ids_ref, far_refs, all_ref):
    slots = plan.slots
    for tile in range(len(plan.tiles)):
        for side in range(len(plan.sides)):
            start = tile * plan.width + side * slots
            all_ref[start : start + slots] = fetch(plan, ids_ref, far_refs, tile, side)


def second_kernel(plan, nrefs, ids_ref, *refs):
    far_refs, refs = refs[:nrefs], refs[nrefs:]
    (layer_ref, basis_ref, cols_ref, radial_ref, mix_ref), refs = refs[:5], refs[5:]
    (hidden_ref, out_ref, one_ref), refs = refs[:3], refs[3:]
    adjoint_ref, energy_ref, features_ref, own_ref, all_ref = refs
    slots, nbasis = plan.slots, plan.nbasis
    gather_far(plan, ids_ref, far_refs, all_ref)
    summed = dot(basis_ref[...].reshape(nbasis * slots, plan.far), all_ref[...])
    message = jnp.zeros((slots, summed.shape[1]), F32)
    for n in range(nbasis):
        message = message + summed[n * slots : (n + 1) * slots] * radial_ref[n : n + 1]
    rounded = (MSG_SCALE * message).astype(BF16)
    mixing = dot(rounded, mix_ref[...], NT)
    gate = sigmoid(mixing)
    layer = layer_ref[...].astype(F32)
    features = (layer + mixing * gate).astype(BF16)
    features_ref[...] = features.astype(F32).T.astype(BF16)
    before = dot(features, hidden_ref[...], NT)
    open_hidden = sigmoid(before)
    live = cols_ref[:, 3:4]
    energy = dot_exact(one_ref[...], layer, NT) + dot_exact(out_ref[...], before * open_hidden, NT)
    live_row = dot(jnp.ones((1, 8), BF16), jnp.where(
        lax.broadcasted_iota(jnp.int32, (slots, 8), 1) == 0, live, 0.0
    ).astype(BF16), NT)
    energy_ref[...] = energy * live_row
    slope = out_ref[...] * (open_hidden * (1.0 + before * (1.0 - open_hidden))) * live
    from_hidden = dot(slope.astype(BF16), hidden_ref[...])
    own_ref[...] = from_hidden + one_ref[...] * live
    back = from_hidden * (gate * (1.0 + mixing * (1.0 - gate)))
    adjoint_ref[...] = dot(back.astype(BF16), mix_ref[...]).astype(BF16)


def slope_kernel(plan, nrefs, ids_ref, *refs):
    far_refs, refs = refs[:nrefs], refs[nrefs:]
    adjoint_ref, rows_ref, cols_ref, radial_ref, slope_ref, pair_ref, all_ref = refs
    slots, nbasis = plan.slots, plan.nbasis
    gather_far(plan, ids_ref, far_refs, all_ref)
    cols = [cols_ref[:, axis : axis + 1] for axis in range(3)]
    adjoint = adjoint_ref[...].astype(F32) * MSG_SCALE
    weighted = jnp.concatenate(
        [(adjoint * radial_ref[n : n + 1]).astype(BF16) for n in range(nbasis)], axis=0
    )
    for tile in range(len(plan.tiles)):
        lanes = slice(tile * plan.width, (tile + 1) * plan.width)
        pulled = dot(weighted, all_ref[lanes], NT)
        parts = separations(plan, [rows_ref[tile, k : k + 1] for k in range(3)], cols)
        dist_sq, inverse = distance(plan, parts, tile)
        sine, cosine = waves(dist_sq, inverse)
        fade = jnp.maximum(1.0 - dist_sq * (1.0 / CUT_SQUARE), 0.0)
        radial = fade * fade * inverse
        on_sine = -inverse * ((4.0 / CUT_SQUARE) * fade + radial * inverse)
        on_cosine = (math.pi / CELL_SIDE) * (inverse * radial)
        double = 2.0 * cosine
        before_s, now_s, before_c, now_c = None, sine, None, cosine
        total = jnp.zeros_like(dist_sq)
        for n in range(nbasis):
            if n == 1:
                before_s, now_s = now_s, double * now_s
                before_c, now_c = now_c, double * now_c - 1.0
            elif n > 1:
                before_s, now_s = now_s, double * now_s - before_s
                before_c, now_c = now_c, double * now_c - before_c
            slope = on_sine * now_s + (n + 1.0) * on_cosine * now_c
            slope_ref[n, :, lanes] = slope.astype(BF16)
            total = total + slope * pulled[n * slots : (n + 1) * slots]
        pair_ref[:, lanes] = total


def force_kernel(plan, nrefs, ids_ref, *refs):
    far_refs, refs = refs[:nrefs], refs[nrefs:]
    (own_ref, basis_ref, slope_ref, pair_ref, rows_ref, cols_ref), refs = refs[:6], refs[6:]
    (radial_ref, mixing_ref, mix_ref, vector_ref, table_ref), refs = refs[:5], refs[5:]
    out_refs, all_ref = refs[:-1], refs[-1]
    slots, nbasis, nspec, width = plan.slots, plan.nbasis, plan.nspec, plan.width
    gather_far(plan, ids_ref, far_refs, all_ref)
    summed = dot(basis_ref[...].reshape(nbasis * slots, plan.far), all_ref[...])
    adjoint = jnp.zeros((slots, summed.shape[1]), F32)
    for n in range(nbasis):
        adjoint = adjoint + summed[n * slots : (n + 1) * slots] * radial_ref[n : n + 1]
    adjoint = own_ref[...] + MSG_SCALE * adjoint
    mixing = mixing_ref[...]
    gate = sigmoid(mixing)
    back = (adjoint * (gate * (1.0 + mixing * (1.0 - gate)))).astype(BF16)
    invariants = dot(back, mix_ref[...])
    channels = invariants.shape[1] // 2
    on_scalar = (MSG_SCALE * invariants[:, :channels]).astype(BF16)
    doubled = (2.0 * MSG_SCALE) * invariants[:, channels:]
    on_vector = (vector_ref[...] * jnp.concatenate([doubled] * 3, axis=0)).astype(BF16)
    weights = jnp.concatenate(
        [dot(on_scalar, table_ref[0], NT), dot(on_vector, table_ref[1], NT)], axis=0
    ).astype(BF16)
    group = lax.broadcasted_iota(jnp.int32, weights.shape, 1) // nspec
    weights = weights.astype(F32)
    weights = jnp.concatenate(
        [jnp.where(group == n, weights, 0.0).astype(BF16) for n in range(nbasis)], axis=0
    )
    cols = [cols_ref[:, axis : axis + 1] for axis in range(3)]
    species = lax.broadcasted_iota(jnp.int32, (nbasis * nspec, width), 0) % nspec
    own = [jnp.zeros((slots, width), F32) for _ in range(3)]
    pulls = []
    for tile in range(len(plan.tiles)):
        lanes = slice(tile * width, (tile + 1) * width)
        rows = [rows_ref[tile, k : k + 1] for k in range(4)]
        hot = (rows[3].astype(jnp.int32) == species).astype(F32).astype(BF16)
        spread = dot(weights, hot)
        parts = separations(plan, rows, cols)
        dist_sq, inverse = distance(plan, parts, tile)
        scale = ROOT_THREE * inverse
        total = pair_ref[:, lanes]
        along, sides = None, [None] * 3
        for n in range(nbasis):
            start = n * 4 * slots
            piece = [spread[start + m * slots : start + (m + 1) * slots] for m in range(4)]
            slope = slope_ref[n, :, lanes].astype(F32)
            basis = basis_ref[n, :, lanes].astype(F32)
            mixed = parts[0] * piece[1] + parts[1] * piece[2] + parts[2] * piece[3]
            total = total + slope * (piece[0] + scale * mixed)
            term = basis * mixed
            along = term if along is None else along + term
            for k in range(3):
                term = basis * piece[k + 1]
                sides[k] = term if sides[k] is None else sides[k] + term
        total = total - inverse * inverse * (scale * along)
        pulls.append([])
        for k in range(3):
            pull = parts[k] * total + scale * sides[k]
            own[k] = own[k] + pull
            pulls[-1].append(jnp.sum(pull, axis=0, keepdims=True))
    ones = jnp.ones((8, width), F32)
    mine = [dot_exact(ones, own[k], NT)[:1] for k in range(3)]
    if len(out_refs) == 1:
        out_refs[0][...] = jnp.zeros_like(out_refs[0])
    for tile in range(len(plan.tiles)):
        for side in range(len(plan.sides)):
            for k in range(3):
                piece = pulls[tile][k][:, side * slots : (side + 1) * slots]
                if tile == 0 and side == 0:
                    piece = piece - mine[k]
                if len(out_refs) == 1:
                    out_refs[0][ids_ref[tile * len(plan.sides) + side], k : k + 1] = piece
                else:
                    out_refs[side][tile, k : k + 1] = piece


def call(kernel, plan, far, ids, operands, outs, scratch, flops):
    vmem = pl.BlockSpec(memory_space=pltpu.VMEM)
    smem = pl.BlockSpec(memory_space=pltpu.SMEM)

    def body(*refs):
        kernel(plan, len(far), *refs)

    return pl.pallas_call(
        body,
        out_shape=[jax.ShapeDtypeStruct(shape, dtype) for shape, dtype in outs],
        in_specs=[smem] + [vmem] * (len(far) + len(operands)),
        out_specs=[vmem] * len(outs),
        scratch_shapes=[pltpu.VMEM(shape, dtype) for shape, dtype in scratch],
        compiler_params=pltpu.CompilerParams(vmem_limit_bytes=VMEM_LIMIT),
        cost_estimate=pl.CostEstimate(flops=flops, bytes_accessed=2**20, transcendentals=0),
    )(ids, *far, *operands)


def shifted(value, axis, steps):
    count = lax.axis_size(axis)
    return lax.ppermute(value, axis, [(i, (i + steps) % count) for i in range(count)])


def neighbours_staged(plan, block):
    for axis in ("gz", "gx"):
        parts = [block] + [shifted(block, axis, -o) for o in offsets_of(plan.sizes[axis])[1:]]
        block = jnp.stack(parts)
    block = block.reshape((len(plan.tiles),) + block.shape[2:])
    return [block] + [shifted(block, "gy", -o) for o in plan.sides[1:]]


def neighbours_gathered(plan, block):
    return [lax.all_gather(block, AXES)]


def fold_staged(plan, parts):
    def folded(pieces, axis):
        total = pieces[0]
        for offset, piece in zip(offsets_of(plan.sizes[axis])[1:], pieces[1:]):
            total = total + shifted(piece, axis, offset)
        return total

    total = folded(parts, "gy")
    total = total.reshape((len(offsets_of(plan.sizes["gx"])), -1) + total.shape[1:])
    total = folded([total[m] for m in range(total.shape[0])], "gx")
    return folded([total[m] for m in range(total.shape[0])], "gz")


def fold_exchanged(plan, parts):
    return jnp.sum(lax.all_to_all(parts[0], AXES, 0, 0, tiled=True), axis=0)


def local_program(mesh):
    def local(
        positions,
        species,
        counts,
        embed,
        radial_one,
        mix_one,
        read_one,
        radial_two,
        mix_two,
        read_hidden,
        read_out,
    ):
        slots, channels = positions.shape[-1], embed.shape[1]
        nbasis, nspec = radial_two.shape[0], embed.shape[0]
        plan = Plan(mesh, slots, nbasis, nspec)
        small = plan.ndev <= 64
        near = neighbours_gathered if small else neighbours_staged
        place, kind = positions[0, 0, 0], species[0, 0, 0]
        live = jnp.arange(slots) < counts[0, 0, 0]
        sent = jnp.concatenate(
            [
                jnp.where(live, place[0], FAR)[None],
                place[1:],
                jnp.where(live, kind, -1).astype(F32)[None],
            ]
        )
        ids = plan.neighbour_ids()
        far_sent = near(plan, sent)
        cols = jnp.stack(
            [jnp.where(live, place[0], -FAR), place[1], place[2], live.astype(F32)], axis=1
        )
        table = (radial_one[:, :, None, :] * embed.astype(F32)).astype(BF16)
        table = table.reshape(2, nbasis * nspec, channels)
        own_hot = jnp.where(live, kind, -1)[:, None] == jnp.arange(nspec)
        own_embed = jnp.dot(own_hot.astype(BF16), embed, preferred_element_type=F32)
        pair_flops = 100 * slots * plan.far
        rows, basis, layer, vector, mixing = call(
            first_kernel,
            plan,
            far_sent,
            ids,
            [cols, table, own_embed, mix_one],
            [
                ((len(plan.tiles), 4, plan.width), F32),
                ((nbasis, slots, plan.far), BF16),
                ((slots, channels), BF16),
                ((3 * slots, channels), F32),
                ((slots, channels), F32),
            ],
            [((nbasis, 4 * slots, plan.far), BF16)],
            pair_flops,
        )
        far_layer = neighbours_staged(plan, layer)
        far_scratch = ((plan.far, channels), BF16)
        one_row, out_row = read_one[None], read_out[None]
        adjoint, energy, features, own_adjoint = call(
            second_kernel,
            plan,
            far_layer,
            ids,
            [layer, basis, cols, radial_two, mix_two, read_hidden, out_row, one_row],
            [
                ((slots, channels), BF16),
                ((1, slots), F32),
                ((channels, slots), BF16),
                ((slots, channels), F32),
            ],
            [far_scratch],
            pair_flops,
        )
        far_adjoint = near(plan, adjoint)
        slope, pair = call(
            slope_kernel,
            plan,
            far_layer,
            ids,
            [adjoint, rows, cols, radial_two],
            [((nbasis, slots, plan.far), BF16), ((slots, plan.far), F32)],
            [far_scratch],
            pair_flops,
        )
        if small:
            fold, pull_outs = fold_exchanged, [((plan.ndev, 3, slots), F32)]
        else:
            fold = fold_staged
            pull_outs = [((len(plan.tiles), 3, slots), F32)] * len(plan.sides)
        pulls = call(
            force_kernel,
            plan,
            far_adjoint,
            ids,
            [own_adjoint, basis, slope, pair, rows, cols, radial_two, mixing, mix_one, vector, table],
            pull_outs,
            [far_scratch],
            pair_flops,
        )
        forces = -fold(plan, pulls)
        return forces[None, None, None], energy[None, None], features[None, None, None]

    return local


def solution(mesh):
    split = [P(*AXES, None, None), P(*AXES, None), P(*AXES)]
    out_specs = (P(*AXES, None, None), P(*AXES, None), P(*AXES, None, None))
    return jax.shard_map(
        local_program(mesh),
        mesh=mesh,
        in_specs=tuple(split + [P()] * 8),
        out_specs=out_specs,
        check_vma=False,
    )
```

```python
import itertools
import math

import jax
import jax.numpy as jnp
from jax import lax
from jax.experimental import pallas as pl
from jax.experimental.pallas import tpu as pltpu
from jax.sharding import PartitionSpec as P

CELL_SIDE = 5.0
CUT_SQUARE = 25.0
SOFTEN = 0.25
MSG_SCALE = 0.05
ROOT_THREE = math.sqrt(3.0)
FAR = 1.0e4
AXES = ("gx", "gy", "gz")
F32 = jnp.float32
BF16 = jnp.bfloat16
COS_TERMS = (
    0.9999999997799041,
    -4.934802137078749,
    4.058709159554242,
    -1.335212003029471,
    0.23493731372678894,
    -0.024396324214549327,
)
SIN_TERMS = (
    3.14159265353629,
    -5.167712764624453,
    2.550163318944743,
    -0.5992521977996564,
    0.08205040170151112,
    -0.007028386239784362,
)
VMEM_LIMIT = 48 * 1024 * 1024
NT = (((1,), (1,)), ((), ()))
NN = (((1,), (0,)), ((), ()))


def dot(a, b, dims=NN):
    return lax.dot_general(a, b, dims, preferred_element_type=F32)


def dot_exact(a, b, dims=NN):
    return lax.dot_general(
        a, b, dims, precision=lax.Precision.HIGHEST, preferred_element_type=F32
    )


def split_dot(a, b):
    high = a.astype(BF16)
    low = (a - high.astype(F32)).astype(BF16)
    return dot(high, b) + dot(low, b)


def offsets_of(count):
    return (0, 1) if count == 2 else (0, 1, -1)


def poly(terms, arg):
    total = arg * terms[-1] + terms[-2]
    for term in terms[-3::-1]:
        total = total * arg + term
    return total


class Plan:
    def __init__(self, mesh, slots, nbasis, nspec):
        self.sizes = {axis: mesh.shape[axis] for axis in AXES}
        self.ndev = math.prod(self.sizes.values())
        self.tiles = list(
            itertools.product(offsets_of(self.sizes["gx"]), offsets_of(self.sizes["gz"]))
        )
        self.sides = offsets_of(self.sizes["gy"])
        self.slots = slots
        self.width = len(self.sides) * slots
        self.far = len(self.tiles) * self.width
        self.nbasis = nbasis
        self.nspec = nspec
        self.wrapped = [self.sizes[axis] == 2 for axis in AXES]

    def neighbour_ids(self):
        index = {axis: lax.axis_index(axis) for axis in AXES}

        def moved(axis, step):
            return lax.rem(index[axis] + (step + self.sizes[axis]), self.sizes[axis])

        ids, plane = [], []
        for ox, oz in self.tiles:
            for oy in self.sides:
                place = (moved("gx", ox) * self.sizes["gy"] + moved("gy", oy)) * self.sizes["gz"]
                ids.append(place + moved("gz", oz))
            plane.append(moved("gx", ox) * self.sizes["gz"] + moved("gz", oz))
        return jnp.stack(ids + plane).astype(jnp.int32)

    def offset(self, tile, side):
        ox, oz = self.tiles[tile]
        return (ox, self.sides[side], oz)


def separations(plan, rows, cols):
    parts = []
    for axis in range(3):
        diff = rows[axis] - cols[axis]
        if plan.wrapped[axis]:
            diff = jnp.where(diff > CELL_SIDE, diff - 2.0 * CELL_SIDE, diff)
        parts.append(diff)
    return parts


def distance(plan, parts, tile):
    dist_sq = parts[0] * parts[0] + parts[1] * parts[1] + parts[2] * parts[2] + SOFTEN
    if tile == 0:
        row = lax.broadcasted_iota(jnp.int32, dist_sq.shape, 0)
        col = lax.broadcasted_iota(jnp.int32, dist_sq.shape, 1)
        dist_sq = jnp.where(row == col, FAR, dist_sq)
    return dist_sq, lax.rsqrt(dist_sq)


def waves(dist_sq, inverse):
    arg = jnp.minimum(dist_sq * inverse * (1.0 / CELL_SIDE) - 0.5, 0.5)
    square = arg * arg
    return poly(COS_TERMS, square), -(arg * poly(SIN_TERMS, square))


def first_kernel(plan, nrefs, ids_ref, *refs):
    far_refs, refs = refs[:nrefs], refs[nrefs:]
    (cols_ref, table_ref, embed_ref, mix_ref), refs = refs[:4], refs[4:]
    rows_ref, basis_ref, layer_ref, vector_ref, mixing_ref, pair_ref = refs
    slots, nbasis, nspec = plan.slots, plan.nbasis, plan.nspec
    cols = [cols_ref[:, axis : axis + 1] for axis in range(3)]
    species = lax.broadcasted_iota(jnp.int32, (nbasis * nspec, plan.width), 0) % nspec
    hot = []
    for tile in range(len(plan.tiles)):
        blocks = [fetch(plan, ids_ref, far_refs, tile, side) for side in range(len(plan.sides))]
        placed = side_by_side(plan, blocks) + tile_shift(plan, tile)
        rows_ref[tile] = placed
        rows = [placed[k : k + 1] for k in range(4)]
        hot.append((rows[3].astype(jnp.int32) == species).astype(F32).astype(BF16))
        parts = separations(plan, rows, cols)
        dist_sq, inverse = distance(plan, parts, tile)
        sine, cosine = waves(dist_sq, inverse)
        fade = jnp.maximum(1.0 - dist_sq * (1.0 / CUT_SQUARE), 0.0)
        radial = fade * fade * inverse
        units = [part * (inverse * ROOT_THREE) for part in parts]
        before, now = None, sine * radial
        lanes = slice(tile * plan.width, (tile + 1) * plan.width)
        for n in range(nbasis):
            if n == 1:
                before, now = now, 2.0 * cosine * now
            elif n > 1:
                before, now = now, 2.0 * cosine * now - before
            packed = now.astype(BF16)
            basis_ref[n, :, lanes] = packed
            pair_ref[n, :slots, lanes] = packed
            for k in range(3):
                pair_ref[n, (k + 1) * slots : (k + 2) * slots, lanes] = (units[k] * now).astype(BF16)
    hot = jnp.concatenate(hot, axis=1)
    gathered = dot(pair_ref[...].reshape(nbasis * 4 * slots, plan.far), hot, NT)
    gathered = gathered.reshape(nbasis, 4 * slots, nbasis * nspec)
    group = lax.broadcasted_iota(jnp.int32, gathered.shape[1:], 1) // nspec
    counted = jnp.zeros(gathered.shape[1:], F32)
    for n in range(nbasis):
        counted = jnp.where(group == n, gathered[n], counted)
    scalar = MSG_SCALE * split_dot(counted[:slots], table_ref[0])
    vector = MSG_SCALE * split_dot(counted[slots:], table_ref[1])
    vector_ref[...] = vector
    squares = vector * vector
    norm = squares[:slots] + squares[slots : 2 * slots] + squares[2 * slots :]
    invariants = jnp.concatenate([scalar.astype(BF16), norm.astype(BF16)], axis=1)
    mixing = dot(invariants, mix_ref[...], NT)
    mixing_ref[...] = mixing
    layer = (embed_ref[...] + mixing * sigmoid(mixing)).astype(BF16)
    for copy in range(layer_ref.shape[0]):
        layer_ref[copy] = layer


def sigmoid(value):
    return 1.0 / (1.0 + jnp.exp(-value))


def fetch(plan, ids_ref, far_refs, tile, side):
    if len(far_refs) == 1:
        return far_refs[0][ids_ref[tile * len(plan.sides) + side]]
    if far_refs[side].shape[0] == len(plan.tiles):
        return far_refs[side][tile]
    return far_refs[side][ids_ref[len(plan.tiles) * len(plan.sides) + tile]]


def side_by_side(plan, blocks):
    if len(blocks) == 2:
        lane = lax.broadcasted_iota(jnp.int32, blocks[0].shape, 1)
        return jnp.where(lane < plan.slots, blocks[0], blocks[1])
    return jnp.concatenate([block[:, : plan.slots] for block in blocks], axis=1)


def tile_shift(plan, tile):
    row = lax.broadcasted_iota(jnp.int32, (4, plan.width), 0)
    side = lax.broadcasted_iota(jnp.int32, (4, plan.width), 1) // plan.slots
    shift = jnp.zeros((4, plan.width), F32)
    for s in range(len(plan.sides)):
        for k, steps in enumerate(plan.offset(tile, s)):
            if steps:
                shift = jnp.where((row == k) & (side == s), CELL_SIDE * steps, shift)
    return shift


def gather_far(plan, ids_ref, far_refs, all_ref):
    slots = plan.slots
    for tile in range(len(plan.tiles)):
        for side in range(len(plan.sides)):
            start = tile * plan.width + side * slots
            all_ref[start : start + slots] = fetch(plan, ids_ref, far_refs, tile, side)


def second_kernel(plan, nrefs, ids_ref, *refs):
    far_refs, refs = refs[:nrefs], refs[nrefs:]
    (layer_ref, basis_ref, cols_ref, radial_ref, mix_ref), refs = refs[:5], refs[5:]
    (hidden_ref, out_ref, one_ref), refs = refs[:3], refs[3:]
    adjoint_ref, energy_ref, features_ref, own_ref, all_ref = refs
    slots, nbasis = plan.slots, plan.nbasis
    gather_far(plan, ids_ref, far_refs, all_ref)
    summed = dot(basis_ref[...].reshape(nbasis * slots, plan.far), all_ref[...])
    message = jnp.zeros((slots, summed.shape[1]), F32)
    for n in range(nbasis):
        message = message + summed[n * slots : (n + 1) * slots] * radial_ref[n : n + 1]
    rounded = (MSG_SCALE * message).astype(BF16)
    mixing = dot(rounded, mix_ref[...], NT)
    gate = sigmoid(mixing)
    layer = layer_ref[0].astype(F32)
    features = (layer + mixing * gate).astype(BF16)
    features_ref[...] = features
    before = dot(features, hidden_ref[...], NT)
    open_hidden = sigmoid(before)
    live = cols_ref[:, 3:4]
    energy = dot_exact(one_ref[...], layer, NT) + dot_exact(out_ref[...], before * open_hidden, NT)
    live_row = dot(jnp.ones((1, 8), BF16), jnp.where(
        lax.broadcasted_iota(jnp.int32, (slots, 8), 1) == 0, live, 0.0
    ).astype(BF16), NT)
    energy_ref[...] = energy * live_row
    slope = out_ref[...] * (open_hidden * (1.0 + before * (1.0 - open_hidden))) * live
    from_hidden = dot(slope.astype(BF16), hidden_ref[...])
    own_ref[...] = from_hidden + one_ref[...] * live
    back = from_hidden * (gate * (1.0 + mixing * (1.0 - gate)))
    adjoint = dot(back.astype(BF16), mix_ref[...]).astype(BF16)
    for copy in range(adjoint_ref.shape[0]):
        adjoint_ref[copy] = adjoint


def slope_kernel(plan, nrefs, ids_ref, *refs):
    far_refs, refs = refs[:nrefs], refs[nrefs:]
    adjoint_ref, rows_ref, cols_ref, radial_ref, slope_ref, pair_ref, all_ref = refs
    slots, nbasis = plan.slots, plan.nbasis
    gather_far(plan, ids_ref, far_refs, all_ref)
    cols = [cols_ref[:, axis : axis + 1] for axis in range(3)]
    adjoint = adjoint_ref[0].astype(F32) * MSG_SCALE
    weighted = jnp.concatenate(
        [(adjoint * radial_ref[n : n + 1]).astype(BF16) for n in range(nbasis)], axis=0
    )
    for tile in range(len(plan.tiles)):
        lanes = slice(tile * plan.width, (tile + 1) * plan.width)
        pulled = dot(weighted, all_ref[lanes], NT)
        parts = separations(plan, [rows_ref[tile, k : k + 1] for k in range(3)], cols)
        dist_sq, inverse = distance(plan, parts, tile)
        sine, cosine = waves(dist_sq, inverse)
        fade = jnp.maximum(1.0 - dist_sq * (1.0 / CUT_SQUARE), 0.0)
        radial = fade * fade * inverse
        on_sine = -inverse * ((4.0 / CUT_SQUARE) * fade + radial * inverse)
        on_cosine = (math.pi / CELL_SIDE) * (inverse * radial)
        double = 2.0 * cosine
        before_s, now_s, before_c, now_c = None, sine, None, cosine
        total = jnp.zeros_like(dist_sq)
        for n in range(nbasis):
            if n == 1:
                before_s, now_s = now_s, double * now_s
                before_c, now_c = now_c, double * now_c - 1.0
            elif n > 1:
                before_s, now_s = now_s, double * now_s - before_s
                before_c, now_c = now_c, double * now_c - before_c
            slope = on_sine * now_s + (n + 1.0) * on_cosine * now_c
            slope_ref[n, :, lanes] = slope.astype(BF16)
            total = total + slope * pulled[n * slots : (n + 1) * slots]
        pair_ref[:, lanes] = total


def force_kernel(plan, nrefs, ids_ref, *refs):
    far_refs, refs = refs[:nrefs], refs[nrefs:]
    (own_ref, basis_ref, slope_ref, pair_ref, rows_ref, cols_ref), refs = refs[:6], refs[6:]
    (radial_ref, mixing_ref, mix_ref, vector_ref, table_ref), refs = refs[:5], refs[5:]
    out_refs, all_ref = refs[:-1], refs[-1]
    slots, nbasis, nspec, width = plan.slots, plan.nbasis, plan.nspec, plan.width
    gather_far(plan, ids_ref, far_refs, all_ref)
    summed = dot(basis_ref[...].reshape(nbasis * slots, plan.far), all_ref[...])
    adjoint = jnp.zeros((slots, summed.shape[1]), F32)
    for n in range(nbasis):
        adjoint = adjoint + summed[n * slots : (n + 1) * slots] * radial_ref[n : n + 1]
    adjoint = own_ref[...] + MSG_SCALE * adjoint
    mixing = mixing_ref[...]
    gate = sigmoid(mixing)
    back = (adjoint * (gate * (1.0 + mixing * (1.0 - gate)))).astype(BF16)
    invariants = dot(back, mix_ref[...])
    channels = invariants.shape[1] // 2
    on_scalar = (MSG_SCALE * invariants[:, :channels]).astype(BF16)
    doubled = (2.0 * MSG_SCALE) * invariants[:, channels:]
    on_vector = (vector_ref[...] * jnp.concatenate([doubled] * 3, axis=0)).astype(BF16)
    weights = jnp.concatenate(
        [dot(on_scalar, table_ref[0], NT), dot(on_vector, table_ref[1], NT)], axis=0
    ).astype(BF16)
    group = lax.broadcasted_iota(jnp.int32, weights.shape, 1) // nspec
    weights = weights.astype(F32)
    weights = jnp.concatenate(
        [jnp.where(group == n, weights, 0.0).astype(BF16) for n in range(nbasis)], axis=0
    )
    cols = [cols_ref[:, axis : axis + 1] for axis in range(3)]
    species = lax.broadcasted_iota(jnp.int32, (nbasis * nspec, width), 0) % nspec
    own = [jnp.zeros((slots, width), F32) for _ in range(3)]
    pulls = []
    for tile in range(len(plan.tiles)):
        lanes = slice(tile * width, (tile + 1) * width)
        rows = [rows_ref[tile, k : k + 1] for k in range(4)]
        hot = (rows[3].astype(jnp.int32) == species).astype(F32).astype(BF16)
        spread = dot(weights, hot)
        parts = separations(plan, rows, cols)
        dist_sq, inverse = distance(plan, parts, tile)
        scale = ROOT_THREE * inverse
        total = pair_ref[:, lanes]
        along, sides = None, [None] * 3
        for n in range(nbasis):
            start = n * 4 * slots
            piece = [spread[start + m * slots : start + (m + 1) * slots] for m in range(4)]
            slope = slope_ref[n, :, lanes].astype(F32)
            basis = basis_ref[n, :, lanes].astype(F32)
            mixed = parts[0] * piece[1] + parts[1] * piece[2] + parts[2] * piece[3]
            total = total + slope * (piece[0] + scale * mixed)
            term = basis * mixed
            along = term if along is None else along + term
            for k in range(3):
                term = basis * piece[k + 1]
                sides[k] = term if sides[k] is None else sides[k] + term
        total = total - inverse * inverse * (scale * along)
        pulls.append([])
        for k in range(3):
            pull = parts[k] * total + scale * sides[k]
            own[k] = own[k] + pull
            pulls[-1].append(jnp.sum(pull, axis=0, keepdims=True))
    ones = jnp.ones((8, width), F32)
    mine = jnp.concatenate([dot_exact(ones, own[k], NT)[:1] for k in range(3)], axis=0)
    if len(out_refs) == 1:
        out_refs[0][...] = jnp.zeros_like(out_refs[0])
    side_of = lax.broadcasted_iota(jnp.int32, (3, width), 1) // slots
    for tile in range(len(plan.tiles)):
        pulled = jnp.concatenate(pulls[tile], axis=0)
        if tile == 0:
            pulled = pulled - jnp.concatenate([mine] + [jnp.zeros_like(mine)] * (len(plan.sides) - 1), axis=1)
        for side in range(len(plan.sides)):
            if len(out_refs) == 1:
                place = ids_ref[tile * len(plan.sides) + side]
                out_refs[0][place, :3] = jnp.where(side_of == side, pulled, 0.0)
            else:
                out_refs[side][tile] = pulled[:, side * slots : (side + 1) * slots]


def prepare_kernel(plan, counts_ref, place_ref, kind_ref, sent_ref):
    live = lax.broadcasted_iota(jnp.int32, (1, plan.slots), 1) < counts_ref[0]
    rows = [
        jnp.where(live, place_ref[0], FAR),
        place_ref[1],
        place_ref[2],
        jnp.where(live, kind_ref[...], -1).astype(F32),
    ]
    rows = jnp.concatenate(rows, axis=0)
    rows = jnp.concatenate([rows, rows], axis=1)
    for copy in range(sent_ref.shape[0]):
        sent_ref[copy] = rows


def own_kernel(plan, sent_ref, embed_ref, radial_ref, cols_ref, table_ref, own_ref):
    slots, nspec = plan.slots, plan.nspec
    rows = sent_ref[0]
    cols = jnp.concatenate([rows, rows], axis=0).T[:slots]
    kind = cols[:, 3:4]
    lane = lax.broadcasted_iota(jnp.int32, cols.shape, 1)
    live = kind >= 0.0
    cols = jnp.where((lane == 0) & ~live, -FAR, cols)
    cols_ref[...] = jnp.where(lane == 3, live.astype(F32), cols)
    species = lax.broadcasted_iota(jnp.int32, (slots, nspec), 1)
    hot = (kind.astype(jnp.int32) == species).astype(F32).astype(BF16)
    embed = embed_ref[...]
    own_ref[...] = dot(hot, embed)
    embed = embed.astype(F32)
    for g in range(2):
        for n in range(plan.nbasis):
            row = radial_ref[g, n : n + 1]
            table_ref[g, n * nspec : (n + 1) * nspec] = (row * embed).astype(BF16)


def sum_kernel(plan, parts_ref, force_ref):
    total = parts_ref[0]
    for part in range(1, parts_ref.shape[0]):
        total = total + parts_ref[part]
    total = total[:, : plan.slots] + total[:, plan.slots :]
    for k in range(3):
        force_ref[k] = -total[k : k + 1]


VMEM_SPEC = pl.BlockSpec(memory_space=pltpu.VMEM)
SMEM_SPEC = pl.BlockSpec(memory_space=pltpu.SMEM)


def simple_call(kernel, plan, operands, outs, scalars=0, scratch=(), flops=2**20):
    single = not isinstance(outs, list)
    shapes = [jax.ShapeDtypeStruct(*out) for out in ([outs] if single else outs)]

    def body(*refs):
        kernel(plan, *refs)

    got = pl.pallas_call(
        body,
        out_shape=shapes,
        in_specs=[SMEM_SPEC] * scalars + [VMEM_SPEC] * (len(operands) - scalars),
        out_specs=[VMEM_SPEC] * len(shapes),
        scratch_shapes=[pltpu.VMEM(*buffer) for buffer in scratch],
        compiler_params=pltpu.CompilerParams(vmem_limit_bytes=VMEM_LIMIT),
        cost_estimate=pl.CostEstimate(flops=flops, bytes_accessed=2**20, transcendentals=0),
    )(*operands)
    return got[0] if single else got


def call(kernel, plan, far, ids, operands, outs, scratch, flops):
    def body(plan, *refs):
        kernel(plan, len(far), *refs)

    return simple_call(body, plan, [ids, *far, *operands], outs, 1, scratch, flops)


def shifted(value, axis, steps):
    count = lax.axis_size(axis)
    return lax.ppermute(value, axis, [(i, (i + steps) % count) for i in range(count)])


def neighbours_staged(plan, block):
    for axis in ("gz", "gx"):
        parts = [block] + [shifted(block, axis, -o) for o in offsets_of(plan.sizes[axis])[1:]]
        block = jnp.stack(parts)
    block = block.reshape((len(plan.tiles),) + block.shape[2:])
    return [block] + [shifted(block, "gy", -o) for o in plan.sides[1:]]


def everywhere(copies, axes):
    return lax.all_to_all(copies, axes, 0, 0, tiled=True)


def neighbours_lines(plan, copies):
    block = everywhere(copies, "gz")
    block = jnp.broadcast_to(block[None], (plan.sizes["gx"],) + block.shape)
    block = everywhere(block, "gx")
    block = block.reshape((-1,) + block.shape[2:])
    return [block, shifted(block, "gy", -1)]


def neighbours_plane(plan, copies):
    block = everywhere(copies, ("gx", "gz"))
    return [block, shifted(block, "gy", -1)]


def fold_staged(plan, parts):
    def folded(pieces, axis):
        total = pieces[0]
        for offset, piece in zip(offsets_of(plan.sizes[axis])[1:], pieces[1:]):
            total = total + shifted(piece, axis, offset)
        return total

    total = folded(parts, "gy")
    total = total.reshape((len(offsets_of(plan.sizes["gx"])), -1) + total.shape[1:])
    total = folded([total[m] for m in range(total.shape[0])], "gx")
    return folded([total[m] for m in range(total.shape[0])], "gz")


def local_program(mesh):
    def local(
        positions,
        species,
        counts,
        embed,
        radial_one,
        mix_one,
        read_one,
        radial_two,
        mix_two,
        read_hidden,
        read_out,
    ):
        slots, channels = positions.shape[-1], embed.shape[1]
        nbasis, nspec = radial_two.shape[0], embed.shape[0]
        plan = Plan(mesh, slots, nbasis, nspec)
        small = plan.ndev <= 64 and len(plan.sides) == 2
        place = positions[0, 0, 0].reshape(3, 1, slots)
        sent = simple_call(
            prepare_kernel,
            plan,
            [counts.reshape(1), place, species.reshape(1, slots)],
            ((plan.ndev if small else 1, 4, 2 * slots), F32),
            1,
        )
        ids = plan.neighbour_ids()
        far_sent = [everywhere(sent, AXES)] if small else neighbours_staged(plan, sent[0])
        cols, table, own_embed = simple_call(
            own_kernel,
            plan,
            [sent, embed, radial_one],
            [
                ((slots, 8), F32),
                ((2, nbasis * nspec, channels), BF16),
                ((slots, channels), F32),
            ],
        )
        pair_flops = 100 * slots * plan.far
        rows, basis, layer, vector, mixing = call(
            first_kernel,
            plan,
            far_sent,
            ids,
            [cols, table, own_embed, mix_one],
            [
                ((len(plan.tiles), 4, plan.width), F32),
                ((nbasis, slots, plan.far), BF16),
                ((plan.sizes["gz"] if small else 1, slots, channels), BF16),
                ((3 * slots, channels), F32),
                ((slots, channels), F32),
            ],
            [((nbasis, 4 * slots, plan.far), BF16)],
            pair_flops,
        )
        far_layer = neighbours_lines(plan, layer) if small else neighbours_staged(plan, layer[0])
        far_scratch = ((plan.far, channels), BF16)
        one_row, out_row = read_one[None], read_out[None]
        adjoint, energy, features, own_adjoint = call(
            second_kernel,
            plan,
            far_layer,
            ids,
            [layer, basis, cols, radial_two, mix_two, read_hidden, out_row, one_row],
            [
                ((plan.sizes["gx"] * plan.sizes["gz"] if small else 1, slots, channels), BF16),
                ((1, slots), F32),
                ((slots, channels), BF16),
                ((slots, channels), F32),
            ],
            [far_scratch],
            pair_flops,
        )
        if small:
            far_adjoint = neighbours_plane(plan, adjoint)
        else:
            far_adjoint = neighbours_staged(plan, adjoint[0])
        slope, pair = call(
            slope_kernel,
            plan,
            far_layer,
            ids,
            [adjoint, rows, cols, radial_two],
            [((nbasis, slots, plan.far), BF16), ((slots, plan.far), F32)],
            [far_scratch],
            pair_flops,
        )
        if small:
            pull_outs = [((plan.ndev, 4, plan.width), F32)]
        else:
            pull_outs = [((len(plan.tiles), 3, slots), F32)] * len(plan.sides)
        pulls = call(
            force_kernel,
            plan,
            far_adjoint,
            ids,
            [own_adjoint, basis, slope, pair, rows, cols, radial_two, mixing, mix_one, vector, table],
            pull_outs,
            [far_scratch],
            pair_flops,
        )
        if small:
            forces = simple_call(sum_kernel, plan, [everywhere(pulls[0], AXES)], ((3, 1, slots), F32))
        else:
            forces = -fold_staged(plan, pulls)
        return (
            forces.reshape(1, 1, 1, 3, slots),
            energy[None, None],
            features.T[None, None, None],
        )

    return local


def solution(mesh):
    split = [P(*AXES, None, None), P(*AXES, None), P(*AXES)]
    out_specs = (P(*AXES, None, None), P(*AXES, None), P(*AXES, None, None))
    return jax.shard_map(
        local_program(mesh),
        mesh=mesh,
        in_specs=tuple(split + [P()] * 8),
        out_specs=out_specs,
        check_vma=False,
    )
```

```python
import itertools
import math

import jax
import jax.numpy as jnp
from jax import lax
from jax.experimental import pallas as pl
from jax.experimental.pallas import tpu as pltpu
from jax.sharding import PartitionSpec as P

CELL_SIDE = 5.0
CUT_SQUARE = 25.0
SOFTEN = 0.25
MSG_SCALE = 0.05
ROOT_THREE = math.sqrt(3.0)
FAR = 1.0e4
AXES = ("gx", "gy", "gz")
F32 = jnp.float32
BF16 = jnp.bfloat16
COS_TERMS = (
    0.9999999997799041,
    -4.934802137078749,
    4.058709159554242,
    -1.335212003029471,
    0.23493731372678894,
    -0.024396324214549327,
)
SIN_TERMS = (
    3.14159265353629,
    -5.167712764624453,
    2.550163318944743,
    -0.5992521977996564,
    0.08205040170151112,
    -0.007028386239784362,
)
VMEM_LIMIT = 48 * 1024 * 1024
NT = (((1,), (1,)), ((), ()))
NN = (((1,), (0,)), ((), ()))


def dot(a, b, dims=NN):
    return lax.dot_general(a, b, dims, preferred_element_type=F32)


def dot_exact(a, b, dims=NN):
    return lax.dot_general(
        a, b, dims, precision=lax.Precision.HIGHEST, preferred_element_type=F32
    )


def split_dot(a, b):
    high = a.astype(BF16)
    low = (a - high.astype(F32)).astype(BF16)
    return dot(high, b) + dot(low, b)


def offsets_of(count):
    return (0, 1) if count == 2 else (0, 1, -1)


def paired(count):
    return count > 2 and count % 2 == 0


def poly(terms, arg):
    total = arg * terms[-1] + terms[-2]
    for term in terms[-3::-1]:
        total = total * arg + term
    return total


class Plan:
    def __init__(self, mesh, slots, nbasis, nspec):
        self.sizes = {axis: mesh.shape[axis] for axis in AXES}
        self.ndev = math.prod(self.sizes.values())
        self.tiles = list(
            itertools.product(offsets_of(self.sizes["gx"]), offsets_of(self.sizes["gz"]))
        )
        self.sides = offsets_of(self.sizes["gy"])
        self.slots = slots
        self.width = len(self.sides) * slots
        self.far = len(self.tiles) * self.width
        self.nbasis = nbasis
        self.nspec = nspec
        self.wrapped = [self.sizes[axis] == 2 for axis in AXES]

    def tile_places(self):
        def place(axis, offset):
            count = self.sizes[axis]
            order = offsets_of(count).index(offset)
            if order == 0 or not paired(count):
                return jnp.int32(order)
            parity = lax.rem(lax.axis_index(axis), 2)
            return 1 + parity if offset == 1 else 2 - parity

        depth = len(offsets_of(self.sizes["gz"]))
        places = [place("gx", ox) * depth + place("gz", oz) for ox, oz in self.tiles]
        return jnp.stack(places).astype(jnp.int32)

    def offset(self, tile, side):
        ox, oz = self.tiles[tile]
        return (ox, self.sides[side], oz)


def separations(plan, rows, cols):
    parts = []
    for axis in range(3):
        diff = rows[axis] - cols[axis]
        if plan.wrapped[axis]:
            diff = jnp.where(diff > CELL_SIDE, diff - 2.0 * CELL_SIDE, diff)
        parts.append(diff)
    return parts


def distance(plan, parts, tile):
    dist_sq = parts[0] * parts[0] + parts[1] * parts[1] + parts[2] * parts[2] + SOFTEN
    if tile == 0:
        row = lax.broadcasted_iota(jnp.int32, dist_sq.shape, 0)
        col = lax.broadcasted_iota(jnp.int32, dist_sq.shape, 1)
        dist_sq = jnp.where(row == col, FAR, dist_sq)
    return dist_sq, lax.rsqrt(dist_sq)


def waves(dist_sq, inverse):
    arg = jnp.minimum(dist_sq * inverse * (1.0 / CELL_SIDE) - 0.5, 0.5)
    square = arg * arg
    return poly(COS_TERMS, square), -(arg * poly(SIN_TERMS, square))


def first_kernel(plan, nrefs, places_ref, *refs):
    far_refs, refs = refs[:nrefs], refs[nrefs:]
    (cols_ref, table_ref, embed_ref, mix_ref), refs = refs[:4], refs[4:]
    rows_ref, basis_ref, layer_ref, vector_ref, mixing_ref, pair_ref = refs
    slots, nbasis, nspec = plan.slots, plan.nbasis, plan.nspec
    cols = [cols_ref[:, axis : axis + 1] for axis in range(3)]
    species = lax.broadcasted_iota(jnp.int32, (nbasis * nspec, plan.width), 0) % nspec
    hot = []
    for tile in range(len(plan.tiles)):
        blocks = [fetch(places_ref, far_refs, tile, side) for side in range(len(plan.sides))]
        placed = side_by_side(plan, blocks) + tile_shift(plan, tile)
        rows_ref[tile] = placed
        rows = [placed[k : k + 1] for k in range(4)]
        hot.append((rows[3].astype(jnp.int32) == species).astype(F32).astype(BF16))
        parts = separations(plan, rows, cols)
        dist_sq, inverse = distance(plan, parts, tile)
        sine, cosine = waves(dist_sq, inverse)
        fade = jnp.maximum(1.0 - dist_sq * (1.0 / CUT_SQUARE), 0.0)
        radial = fade * fade * inverse
        units = [part * (inverse * ROOT_THREE) for part in parts]
        before, now = None, sine * radial
        lanes = slice(tile * plan.width, (tile + 1) * plan.width)
        for n in range(nbasis):
            if n == 1:
                before, now = now, 2.0 * cosine * now
            elif n > 1:
                before, now = now, 2.0 * cosine * now - before
            packed = now.astype(BF16)
            basis_ref[n, :, lanes] = packed
            pair_ref[n, :slots, lanes] = packed
            for k in range(3):
                pair_ref[n, (k + 1) * slots : (k + 2) * slots, lanes] = (units[k] * now).astype(BF16)
    hot = jnp.concatenate(hot, axis=1)
    gathered = dot(pair_ref[...].reshape(nbasis * 4 * slots, plan.far), hot, NT)
    gathered = gathered.reshape(nbasis, 4 * slots, nbasis * nspec)
    group = lax.broadcasted_iota(jnp.int32, gathered.shape[1:], 1) // nspec
    counted = jnp.zeros(gathered.shape[1:], F32)
    for n in range(nbasis):
        counted = jnp.where(group == n, gathered[n], counted)
    scalar = MSG_SCALE * split_dot(counted[:slots], table_ref[0])
    vector = MSG_SCALE * split_dot(counted[slots:], table_ref[1])
    vector_ref[...] = vector
    squares = vector * vector
    norm = squares[:slots] + squares[slots : 2 * slots] + squares[2 * slots :]
    invariants = jnp.concatenate([scalar.astype(BF16), norm.astype(BF16)], axis=1)
    mixing = dot(invariants, mix_ref[...], NT)
    mixing_ref[...] = mixing
    layer = (embed_ref[...] + mixing * sigmoid(mixing)).astype(BF16)
    layer_ref[...] = layer


def sigmoid(value):
    return 1.0 / (1.0 + jnp.exp(-value))


def fetch(places_ref, far_refs, tile, side):
    return far_refs[side][places_ref[tile]]


def side_by_side(plan, blocks):
    if len(blocks) == 2:
        lane = lax.broadcasted_iota(jnp.int32, blocks[0].shape, 1)
        return jnp.where(lane < plan.slots, blocks[0], blocks[1])
    return jnp.concatenate([block[:, : plan.slots] for block in blocks], axis=1)


def tile_shift(plan, tile):
    row = lax.broadcasted_iota(jnp.int32, (4, plan.width), 0)
    side = lax.broadcasted_iota(jnp.int32, (4, plan.width), 1) // plan.slots
    shift = jnp.zeros((4, plan.width), F32)
    for s in range(len(plan.sides)):
        for k, steps in enumerate(plan.offset(tile, s)):
            if steps:
                shift = jnp.where((row == k) & (side == s), CELL_SIDE * steps, shift)
    return shift


def gather_far(plan, places_ref, far_refs, all_ref):
    slots = plan.slots
    for tile in range(len(plan.tiles)):
        for side in range(len(plan.sides)):
            start = tile * plan.width + side * slots
            all_ref[start : start + slots] = fetch(places_ref, far_refs, tile, side)


def second_kernel(plan, nrefs, places_ref, *refs):
    far_refs, refs = refs[:nrefs], refs[nrefs:]
    (layer_ref, basis_ref, cols_ref, radial_ref, mix_ref), refs = refs[:5], refs[5:]
    (hidden_ref, out_ref, one_ref), refs = refs[:3], refs[3:]
    adjoint_ref, energy_ref, features_ref, own_ref, all_ref = refs
    slots, nbasis = plan.slots, plan.nbasis
    gather_far(plan, places_ref, far_refs, all_ref)
    summed = dot(basis_ref[...].reshape(nbasis * slots, plan.far), all_ref[...])
    message = jnp.zeros((slots, summed.shape[1]), F32)
    for n in range(nbasis):
        message = message + summed[n * slots : (n + 1) * slots] * radial_ref[n : n + 1]
    rounded = (MSG_SCALE * message).astype(BF16)
    mixing = dot(rounded, mix_ref[...], NT)
    gate = sigmoid(mixing)
    layer = layer_ref[...].astype(F32)
    features = (layer + mixing * gate).astype(BF16)
    features_ref[...] = features
    before = dot(features, hidden_ref[...], NT)
    open_hidden = sigmoid(before)
    live = cols_ref[:, 3:4]
    energy = dot_exact(one_ref[...], layer, NT) + dot_exact(out_ref[...], before * open_hidden, NT)
    live_row = dot(jnp.ones((1, 8), BF16), jnp.where(
        lax.broadcasted_iota(jnp.int32, (slots, 8), 1) == 0, live, 0.0
    ).astype(BF16), NT)
    energy_ref[...] = energy * live_row
    slope = out_ref[...] * (open_hidden * (1.0 + before * (1.0 - open_hidden))) * live
    from_hidden = dot(slope.astype(BF16), hidden_ref[...])
    own_ref[...] = from_hidden + one_ref[...] * live
    back = from_hidden * (gate * (1.0 + mixing * (1.0 - gate)))
    adjoint_ref[...] = dot(back.astype(BF16), mix_ref[...]).astype(BF16)


def slope_kernel(plan, nrefs, places_ref, *refs):
    far_refs, refs = refs[:nrefs], refs[nrefs:]
    adjoint_ref, rows_ref, cols_ref, radial_ref, slope_ref, pair_ref, all_ref = refs
    slots, nbasis = plan.slots, plan.nbasis
    gather_far(plan, places_ref, far_refs, all_ref)
    cols = [cols_ref[:, axis : axis + 1] for axis in range(3)]
    adjoint = adjoint_ref[...].astype(F32) * MSG_SCALE
    weighted = jnp.concatenate(
        [(adjoint * radial_ref[n : n + 1]).astype(BF16) for n in range(nbasis)], axis=0
    )
    for tile in range(len(plan.tiles)):
        lanes = slice(tile * plan.width, (tile + 1) * plan.width)
        pulled = dot(weighted, all_ref[lanes], NT)
        parts = separations(plan, [rows_ref[tile, k : k + 1] for k in range(3)], cols)
        dist_sq, inverse = distance(plan, parts, tile)
        sine, cosine = waves(dist_sq, inverse)
        fade = jnp.maximum(1.0 - dist_sq * (1.0 / CUT_SQUARE), 0.0)
        radial = fade * fade * inverse
        on_sine = -inverse * ((4.0 / CUT_SQUARE) * fade + radial * inverse)
        on_cosine = (math.pi / CELL_SIDE) * (inverse * radial)
        double = 2.0 * cosine
        before_s, now_s, before_c, now_c = None, sine, None, cosine
        total = jnp.zeros_like(dist_sq)
        for n in range(nbasis):
            if n == 1:
                before_s, now_s = now_s, double * now_s
                before_c, now_c = now_c, double * now_c - 1.0
            elif n > 1:
                before_s, now_s = now_s, double * now_s - before_s
                before_c, now_c = now_c, double * now_c - before_c
            slope = on_sine * now_s + (n + 1.0) * on_cosine * now_c
            slope_ref[n, :, lanes] = slope.astype(BF16)
            total = total + slope * pulled[n * slots : (n + 1) * slots]
        pair_ref[:, lanes] = total


def force_kernel(plan, nrefs, places_ref, *refs):
    far_refs, refs = refs[:nrefs], refs[nrefs:]
    (own_ref, basis_ref, slope_ref, pair_ref, rows_ref, cols_ref), refs = refs[:6], refs[6:]
    (radial_ref, mixing_ref, mix_ref, vector_ref, table_ref), refs = refs[:5], refs[5:]
    out_ref, all_ref = refs
    slots, nbasis, nspec, width = plan.slots, plan.nbasis, plan.nspec, plan.width
    gather_far(plan, places_ref, far_refs, all_ref)
    summed = dot(basis_ref[...].reshape(nbasis * slots, plan.far), all_ref[...])
    adjoint = jnp.zeros((slots, summed.shape[1]), F32)
    for n in range(nbasis):
        adjoint = adjoint + summed[n * slots : (n + 1) * slots] * radial_ref[n : n + 1]
    adjoint = own_ref[...] + MSG_SCALE * adjoint
    mixing = mixing_ref[...]
    gate = sigmoid(mixing)
    back = (adjoint * (gate * (1.0 + mixing * (1.0 - gate)))).astype(BF16)
    invariants = dot(back, mix_ref[...])
    channels = invariants.shape[1] // 2
    on_scalar = (MSG_SCALE * invariants[:, :channels]).astype(BF16)
    doubled = (2.0 * MSG_SCALE) * invariants[:, channels:]
    on_vector = (vector_ref[...] * jnp.concatenate([doubled] * 3, axis=0)).astype(BF16)
    weights = jnp.concatenate(
        [dot(on_scalar, table_ref[0], NT), dot(on_vector, table_ref[1], NT)], axis=0
    ).astype(BF16)
    group = lax.broadcasted_iota(jnp.int32, weights.shape, 1) // nspec
    weights = weights.astype(F32)
    weights = jnp.concatenate(
        [jnp.where(group == n, weights, 0.0).astype(BF16) for n in range(nbasis)], axis=0
    )
    cols = [cols_ref[:, axis : axis + 1] for axis in range(3)]
    species = lax.broadcasted_iota(jnp.int32, (nbasis * nspec, width), 0) % nspec
    own = [jnp.zeros((slots, width), F32) for _ in range(3)]
    pulls = []
    for tile in range(len(plan.tiles)):
        lanes = slice(tile * width, (tile + 1) * width)
        rows = [rows_ref[tile, k : k + 1] for k in range(4)]
        hot = (rows[3].astype(jnp.int32) == species).astype(F32).astype(BF16)
        spread = dot(weights, hot)
        parts = separations(plan, rows, cols)
        dist_sq, inverse = distance(plan, parts, tile)
        scale = ROOT_THREE * inverse
        total = pair_ref[:, lanes]
        along, sides = None, [None] * 3
        for n in range(nbasis):
            start = n * 4 * slots
            piece = [spread[start + m * slots : start + (m + 1) * slots] for m in range(4)]
            slope = slope_ref[n, :, lanes].astype(F32)
            basis = basis_ref[n, :, lanes].astype(F32)
            mixed = parts[0] * piece[1] + parts[1] * piece[2] + parts[2] * piece[3]
            total = total + slope * (piece[0] + scale * mixed)
            term = basis * mixed
            along = term if along is None else along + term
            for k in range(3):
                term = basis * piece[k + 1]
                sides[k] = term if sides[k] is None else sides[k] + term
        total = total - inverse * inverse * (scale * along)
        pulls.append([])
        for k in range(3):
            pull = parts[k] * total + scale * sides[k]
            own[k] = own[k] + pull
            pulls[-1].append(jnp.sum(pull, axis=0, keepdims=True))
    ones = jnp.ones((8, width), F32)
    mine = jnp.concatenate([dot_exact(ones, own[k], NT)[:1] for k in range(3)], axis=0)
    for tile in range(len(plan.tiles)):
        pulled = jnp.concatenate(pulls[tile], axis=0)
        if tile == 0:
            others = [jnp.zeros_like(mine)] * (len(plan.sides) - 1)
            pulled = pulled - jnp.concatenate([mine] + others, axis=1)
        out_ref[places_ref[tile]] = pulled


def prepare_kernel(plan, counts_ref, place_ref, kind_ref, sent_ref):
    live = lax.broadcasted_iota(jnp.int32, (1, plan.slots), 1) < counts_ref[0]
    rows = [
        jnp.where(live, place_ref[0], FAR),
        place_ref[1],
        place_ref[2],
        jnp.where(live, kind_ref[...], -1).astype(F32),
    ]
    rows = jnp.concatenate(rows, axis=0)
    rows = jnp.concatenate([rows, rows], axis=1)
    sent_ref[...] = rows


def own_kernel(plan, sent_ref, embed_ref, radial_ref, cols_ref, table_ref, own_ref):
    slots, nspec = plan.slots, plan.nspec
    rows = sent_ref[...]
    cols = jnp.concatenate([rows, rows], axis=0).T[:slots]
    kind = cols[:, 3:4]
    lane = lax.broadcasted_iota(jnp.int32, cols.shape, 1)
    live = kind >= 0.0
    cols = jnp.where((lane == 0) & ~live, -FAR, cols)
    cols_ref[...] = jnp.where(lane == 3, live.astype(F32), cols)
    species = lax.broadcasted_iota(jnp.int32, (slots, nspec), 1)
    hot = (kind.astype(jnp.int32) == species).astype(F32).astype(BF16)
    embed = embed_ref[...]
    own_ref[...] = dot(hot, embed)
    embed = embed.astype(F32)
    for g in range(2):
        for n in range(plan.nbasis):
            row = radial_ref[g, n : n + 1]
            table_ref[g, n * nspec : (n + 1) * nspec] = (row * embed).astype(BF16)


VMEM_SPEC = pl.BlockSpec(memory_space=pltpu.VMEM)
SMEM_SPEC = pl.BlockSpec(memory_space=pltpu.SMEM)


def simple_call(kernel, plan, operands, outs, scalars=0, scratch=(), flops=2**20):
    single = not isinstance(outs, list)
    shapes = [jax.ShapeDtypeStruct(*out) for out in ([outs] if single else outs)]

    def body(*refs):
        kernel(plan, *refs)

    got = pl.pallas_call(
        body,
        out_shape=shapes,
        in_specs=[SMEM_SPEC] * scalars + [VMEM_SPEC] * (len(operands) - scalars),
        out_specs=[VMEM_SPEC] * len(shapes),
        scratch_shapes=[pltpu.VMEM(*buffer) for buffer in scratch],
        compiler_params=pltpu.CompilerParams(vmem_limit_bytes=VMEM_LIMIT),
        cost_estimate=pl.CostEstimate(flops=flops, bytes_accessed=2**20, transcendentals=0),
    )(*operands)
    return got[0] if single else got


def call(kernel, plan, far, places, operands, outs, scratch, flops):
    def body(plan, *refs):
        kernel(plan, len(far), *refs)

    return simple_call(body, plan, [places, *far, *operands], outs, 1, scratch, flops)


def swaps(axis):
    count = lax.axis_size(axis)
    if count == 2:
        return [[(0, 1), (1, 0)]]
    if paired(count):
        near = [(i, i ^ 1) for i in range(count)]
        far = [(i, (i - 1 + 2 * (i % 2)) % count) for i in range(count)]
        return [near, far]
    return [[((i + o) % count, i) for i in range(count)] for o in offsets_of(count)[1:]]


def brought(block, axis):
    got = [lax.ppermute(block, axis, pairs) for pairs in swaps(axis)[::-1]]
    return [block] + got[::-1]


def neighbours(plan, block):
    stacked = jnp.stack(brought(block, "gz"))
    stacked = jnp.concatenate(brought(stacked, "gx"))
    return brought(stacked, "gy")


def folded(pieces, axis):
    got = [
        lax.ppermute(piece, axis, [(to, source) for source, to in pairs])
        for piece, pairs in list(zip(pieces[1:], swaps(axis)))[::-1]
    ]
    total = pieces[0]
    for piece in got:
        total = total + piece
    return total


def fold(plan, pulls):
    for axis in ("gx", "gz"):
        parts = len(offsets_of(plan.sizes[axis]))
        pulls = pulls.reshape((parts, -1) + pulls.shape[1:])
        pulls = folded([pulls[m] for m in range(parts)], axis)
    pulls = pulls[0]
    sides = [pulls[:, m * plan.slots : (m + 1) * plan.slots] for m in range(len(plan.sides))]
    return folded(sides, "gy")


def local_program(mesh):
    def local(
        positions,
        species,
        counts,
        embed,
        radial_one,
        mix_one,
        read_one,
        radial_two,
        mix_two,
        read_hidden,
        read_out,
    ):
        slots, channels = positions.shape[-1], embed.shape[1]
        nbasis, nspec = radial_two.shape[0], embed.shape[0]
        plan = Plan(mesh, slots, nbasis, nspec)
        place = positions[0, 0, 0].reshape(3, 1, slots)
        sent = simple_call(
            prepare_kernel,
            plan,
            [counts.reshape(1), place, species.reshape(1, slots)],
            ((4, 2 * slots), F32),
            1,
        )
        places = plan.tile_places()
        far_sent = neighbours(plan, sent)
        cols, table, own_embed = simple_call(
            own_kernel,
            plan,
            [sent, embed, radial_one],
            [
                ((slots, 8), F32),
                ((2, nbasis * nspec, channels), BF16),
                ((slots, channels), F32),
            ],
        )
        pair_flops = 100 * slots * plan.far
        rows, basis, layer, vector, mixing = call(
            first_kernel,
            plan,
            far_sent,
            places,
            [cols, table, own_embed, mix_one],
            [
                ((len(plan.tiles), 4, plan.width), F32),
                ((nbasis, slots, plan.far), BF16),
                ((slots, channels), BF16),
                ((3 * slots, channels), F32),
                ((slots, channels), F32),
            ],
            [((nbasis, 4 * slots, plan.far), BF16)],
            pair_flops,
        )
        far_layer = neighbours(plan, layer)
        far_scratch = ((plan.far, channels), BF16)
        one_row, out_row = read_one[None], read_out[None]
        adjoint, energy, features, own_adjoint = call(
            second_kernel,
            plan,
            far_layer,
            places,
            [layer, basis, cols, radial_two, mix_two, read_hidden, out_row, one_row],
            [
                ((slots, channels), BF16),
                ((1, slots), F32),
                ((slots, channels), BF16),
                ((slots, channels), F32),
            ],
            [far_scratch],
            pair_flops,
        )
        far_adjoint = neighbours(plan, adjoint)
        slope, pair = call(
            slope_kernel,
            plan,
            far_layer,
            places,
            [adjoint, rows, cols, radial_two],
            [((nbasis, slots, plan.far), BF16), ((slots, plan.far), F32)],
            [far_scratch],
            pair_flops,
        )
        pulls = call(
            force_kernel,
            plan,
            far_adjoint,
            places,
            [own_adjoint, basis, slope, pair, rows, cols, radial_two, mixing, mix_one, vector, table],
            [((len(plan.tiles), 3, plan.width), F32)],
            [far_scratch],
            pair_flops,
        )
        forces = -fold(plan, pulls[0])
        return (
            forces.reshape(1, 1, 1, 3, slots),
            energy[None, None],
            features.T[None, None, None],
        )

    return local


def solution(mesh):
    split = [P(*AXES, None, None), P(*AXES, None), P(*AXES)]
    out_specs = (P(*AXES, None, None), P(*AXES, None), P(*AXES, None, None))
    return jax.shard_map(
        local_program(mesh),
        mesh=mesh,
        in_specs=tuple(split + [P()] * 8),
        out_specs=out_specs,
        check_vma=False,
    )
```

```python
import itertools
import math

import jax
import jax.numpy as jnp
from jax import lax
from jax.experimental import pallas as pl
from jax.experimental.pallas import tpu as pltpu
from jax.sharding import PartitionSpec as P

CELL_SIDE = 5.0
CUT_SQUARE = 25.0
SOFTEN = 0.25
MSG_SCALE = 0.05
ROOT_THREE = math.sqrt(3.0)
FAR = 1.0e4
AXES = ("gx", "gy", "gz")
F32 = jnp.float32
BF16 = jnp.bfloat16
COS_TERMS = (
    0.9999999997799041,
    -4.934802137078749,
    4.058709159554242,
    -1.335212003029471,
    0.23493731372678894,
    -0.024396324214549327,
)
SIN_TERMS = (
    3.14159265353629,
    -5.167712764624453,
    2.550163318944743,
    -0.5992521977996564,
    0.08205040170151112,
    -0.007028386239784362,
)
VMEM_LIMIT = 48 * 1024 * 1024
NT = (((1,), (1,)), ((), ()))
NN = (((1,), (0,)), ((), ()))


def dot(a, b, dims=NN):
    return lax.dot_general(a, b, dims, preferred_element_type=F32)


def dot_exact(a, b, dims=NN):
    return lax.dot_general(
        a, b, dims, precision=lax.Precision.HIGHEST, preferred_element_type=F32
    )


def split_dot(a, b):
    high = a.astype(BF16)
    low = (a - high.astype(F32)).astype(BF16)
    return dot(high, b) + dot(low, b)


def offsets_of(count):
    return (0, 1) if count == 2 else (0, 1, -1)


def paired(count):
    return count > 2 and count % 2 == 0


def poly(terms, arg):
    total = arg * terms[-1] + terms[-2]
    for term in terms[-3::-1]:
        total = total * arg + term
    return total


class Plan:
    def __init__(self, mesh, slots, nbasis, nspec):
        self.sizes = {axis: mesh.shape[axis] for axis in AXES}
        self.ndev = math.prod(self.sizes.values())
        self.tiles = list(
            itertools.product(offsets_of(self.sizes["gx"]), offsets_of(self.sizes["gz"]))
        )
        self.sides = offsets_of(self.sizes["gy"])
        self.slots = slots
        self.width = len(self.sides) * slots
        self.far = len(self.tiles) * self.width
        self.nbasis = nbasis
        self.nspec = nspec
        self.depth = len(offsets_of(self.sizes["gz"]))
        self.wide = len(offsets_of(self.sizes["gx"]))
        self.small = self.ndev <= 64 and len(self.sides) == 2
        self.wrapped = [self.sizes[axis] == 2 for axis in AXES]

    def places(self):
        index = {axis: lax.axis_index(axis) for axis in AXES}

        def parity(axis):
            return 1 - lax.rem(index[axis], 2) if paired(self.sizes[axis]) else jnp.int32(0)

        def moved(axis, step):
            return lax.rem(index[axis] + (step + self.sizes[axis]), self.sizes[axis])

        depth = len(offsets_of(self.sizes["gz"]))
        turn = parity("gz")
        found = [jnp.int32(0), 1 + turn, 2 - turn][:depth] + [parity("gx")]
        for ox, oz in self.tiles:
            for oy in self.sides:
                place = (moved("gx", ox) * self.sizes["gy"] + moved("gy", oy)) * self.sizes["gz"]
                found.append(place + moved("gz", oz))
        return jnp.stack(found).astype(jnp.int32)

    def global_place(self, places_ref, tile, side):
        return places_ref[self.depth + 1 + tile * len(self.sides) + side]

    def staged_place(self, places_ref, tile):
        x, z = divmod(tile, self.depth)
        flip = places_ref[self.depth]
        return (0, 1 + flip, 2 - flip)[x] * self.depth + places_ref[z]

    def offset(self, tile, side):
        ox, oz = self.tiles[tile]
        return (ox, self.sides[side], oz)


def separations(plan, rows, cols):
    parts = []
    for axis in range(3):
        diff = rows[axis] - cols[axis]
        if plan.wrapped[axis]:
            diff = jnp.where(diff > CELL_SIDE, diff - 2.0 * CELL_SIDE, diff)
        parts.append(diff)
    return parts


def distance(plan, parts, tile):
    dist_sq = parts[0] * parts[0] + parts[1] * parts[1] + parts[2] * parts[2] + SOFTEN
    if tile == 0:
        row = lax.broadcasted_iota(jnp.int32, dist_sq.shape, 0)
        col = lax.broadcasted_iota(jnp.int32, dist_sq.shape, 1)
        dist_sq = jnp.where(row == col, FAR, dist_sq)
    return dist_sq, lax.rsqrt(dist_sq)


def waves(dist_sq, inverse):
    arg = jnp.minimum(dist_sq * inverse * (1.0 / CELL_SIDE) - 0.5, 0.5)
    square = arg * arg
    return poly(COS_TERMS, square), -(arg * poly(SIN_TERMS, square))


def first_kernel(plan, nrefs, places_ref, *refs):
    far_refs, refs = refs[:nrefs], refs[nrefs:]
    (cols_ref, table_ref, embed_ref, mix_ref), refs = refs[:4], refs[4:]
    rows_ref, basis_ref, layer_ref, vector_ref, mixing_ref, pair_ref = refs
    slots, nbasis, nspec = plan.slots, plan.nbasis, plan.nspec
    cols = [cols_ref[:, axis : axis + 1] for axis in range(3)]
    species = lax.broadcasted_iota(jnp.int32, (nbasis * nspec, plan.width), 0) % nspec
    hot = []
    for tile in range(len(plan.tiles)):
        blocks = [fetch(plan, places_ref, far_refs, tile, side) for side in range(len(plan.sides))]
        placed = side_by_side(plan, blocks) + tile_shift(plan, tile)
        rows_ref[tile] = placed
        rows = [placed[k : k + 1] for k in range(4)]
        hot.append((rows[3].astype(jnp.int32) == species).astype(F32).astype(BF16))
        parts = separations(plan, rows, cols)
        dist_sq, inverse = distance(plan, parts, tile)
        sine, cosine = waves(dist_sq, inverse)
        fade = jnp.maximum(1.0 - dist_sq * (1.0 / CUT_SQUARE), 0.0)
        radial = fade * fade * inverse
        units = [part * (inverse * ROOT_THREE) for part in parts]
        before, now = None, sine * radial
        lanes = slice(tile * plan.width, (tile + 1) * plan.width)
        for n in range(nbasis):
            if n == 1:
                before, now = now, 2.0 * cosine * now
            elif n > 1:
                before, now = now, 2.0 * cosine * now - before
            packed = now.astype(BF16)
            basis_ref[n, :, lanes] = packed
            pair_ref[n, :slots, lanes] = packed
            for k in range(3):
                pair_ref[n, (k + 1) * slots : (k + 2) * slots, lanes] = (units[k] * now).astype(BF16)
    hot = jnp.concatenate(hot, axis=1)
    gathered = dot(pair_ref[...].reshape(nbasis * 4 * slots, plan.far), hot, NT)
    gathered = gathered.reshape(nbasis, 4 * slots, nbasis * nspec)
    group = lax.broadcasted_iota(jnp.int32, gathered.shape[1:], 1) // nspec
    counted = jnp.zeros(gathered.shape[1:], F32)
    for n in range(nbasis):
        counted = jnp.where(group == n, gathered[n], counted)
    scalar = MSG_SCALE * split_dot(counted[:slots], table_ref[0])
    vector = MSG_SCALE * split_dot(counted[slots:], table_ref[1])
    vector_ref[...] = vector
    squares = vector * vector
    norm = squares[:slots] + squares[slots : 2 * slots] + squares[2 * slots :]
    invariants = jnp.concatenate([scalar.astype(BF16), norm.astype(BF16)], axis=1)
    mixing = dot(invariants, mix_ref[...], NT)
    mixing_ref[...] = mixing
    layer = (embed_ref[...] + mixing * sigmoid(mixing)).astype(BF16)
    layer_ref[...] = layer


def sigmoid(value):
    return 1.0 / (1.0 + jnp.exp(-value))


def fetch(plan, places_ref, far_refs, tile, side):
    if len(far_refs) == 1:
        return far_refs[0][plan.global_place(places_ref, tile, side)]
    x, z = divmod(tile, plan.depth)
    place = places_ref[z]
    columns = far_refs[side * plan.wide : (side + 1) * plan.wide]
    if x == 0 or plan.wide == 2:
        return columns[x][place]
    kept, other = columns[x][place], columns[3 - x][place]
    return jnp.where(places_ref[plan.depth] == 0, kept, other)


def side_by_side(plan, blocks):
    if len(blocks) == 2:
        lane = lax.broadcasted_iota(jnp.int32, blocks[0].shape, 1)
        return jnp.where(lane < plan.slots, blocks[0], blocks[1])
    return jnp.concatenate([block[:, : plan.slots] for block in blocks], axis=1)


def tile_shift(plan, tile):
    row = lax.broadcasted_iota(jnp.int32, (4, plan.width), 0)
    side = lax.broadcasted_iota(jnp.int32, (4, plan.width), 1) // plan.slots
    shift = jnp.zeros((4, plan.width), F32)
    for s in range(len(plan.sides)):
        for k, steps in enumerate(plan.offset(tile, s)):
            if steps:
                shift = jnp.where((row == k) & (side == s), CELL_SIDE * steps, shift)
    return shift


def gather_far(plan, places_ref, far_refs, all_ref):
    slots = plan.slots
    for tile in range(len(plan.tiles)):
        for side in range(len(plan.sides)):
            start = tile * plan.width + side * slots
            all_ref[start : start + slots] = fetch(plan, places_ref, far_refs, tile, side)


def second_kernel(plan, nrefs, places_ref, *refs):
    far_refs, refs = refs[:nrefs], refs[nrefs:]
    (layer_ref, basis_ref, cols_ref, radial_ref, mix_ref), refs = refs[:5], refs[5:]
    (hidden_ref, out_ref, one_ref), refs = refs[:3], refs[3:]
    adjoint_ref, energy_ref, features_ref, own_ref, all_ref = refs
    slots, nbasis = plan.slots, plan.nbasis
    gather_far(plan, places_ref, far_refs, all_ref)
    summed = dot(basis_ref[...].reshape(nbasis * slots, plan.far), all_ref[...])
    message = jnp.zeros((slots, summed.shape[1]), F32)
    for n in range(nbasis):
        message = message + summed[n * slots : (n + 1) * slots] * radial_ref[n : n + 1]
    rounded = (MSG_SCALE * message).astype(BF16)
    mixing = dot(rounded, mix_ref[...], NT)
    gate = sigmoid(mixing)
    layer = layer_ref[...].astype(F32)
    features = (layer + mixing * gate).astype(BF16)
    features_ref[...] = features
    before = dot(features, hidden_ref[...], NT)
    open_hidden = sigmoid(before)
    live = cols_ref[:, 3:4]
    energy = dot_exact(one_ref[...], layer, NT) + dot_exact(out_ref[...], before * open_hidden, NT)
    live_row = dot(jnp.ones((1, 8), BF16), jnp.where(
        lax.broadcasted_iota(jnp.int32, (slots, 8), 1) == 0, live, 0.0
    ).astype(BF16), NT)
    energy_ref[...] = energy * live_row
    slope = out_ref[...] * (open_hidden * (1.0 + before * (1.0 - open_hidden))) * live
    from_hidden = dot(slope.astype(BF16), hidden_ref[...])
    own_ref[...] = from_hidden + one_ref[...] * live
    back = from_hidden * (gate * (1.0 + mixing * (1.0 - gate)))
    adjoint_ref[...] = dot(back.astype(BF16), mix_ref[...]).astype(BF16)


def slope_kernel(plan, nrefs, places_ref, *refs):
    far_refs, refs = refs[:nrefs], refs[nrefs:]
    adjoint_ref, rows_ref, cols_ref, radial_ref, slope_ref, pair_ref, all_ref = refs
    slots, nbasis = plan.slots, plan.nbasis
    gather_far(plan, places_ref, far_refs, all_ref)
    cols = [cols_ref[:, axis : axis + 1] for axis in range(3)]
    adjoint = adjoint_ref[...].astype(F32) * MSG_SCALE
    weighted = jnp.concatenate(
        [(adjoint * radial_ref[n : n + 1]).astype(BF16) for n in range(nbasis)], axis=0
    )
    for tile in range(len(plan.tiles)):
        lanes = slice(tile * plan.width, (tile + 1) * plan.width)
        pulled = dot(weighted, all_ref[lanes], NT)
        parts = separations(plan, [rows_ref[tile, k : k + 1] for k in range(3)], cols)
        dist_sq, inverse = distance(plan, parts, tile)
        sine, cosine = waves(dist_sq, inverse)
        fade = jnp.maximum(1.0 - dist_sq * (1.0 / CUT_SQUARE), 0.0)
        radial = fade * fade * inverse
        on_sine = -inverse * ((4.0 / CUT_SQUARE) * fade + radial * inverse)
        on_cosine = (math.pi / CELL_SIDE) * (inverse * radial)
        double = 2.0 * cosine
        before_s, now_s, before_c, now_c = None, sine, None, cosine
        total = jnp.zeros_like(dist_sq)
        for n in range(nbasis):
            if n == 1:
                before_s, now_s = now_s, double * now_s
                before_c, now_c = now_c, double * now_c - 1.0
            elif n > 1:
                before_s, now_s = now_s, double * now_s - before_s
                before_c, now_c = now_c, double * now_c - before_c
            slope = on_sine * now_s + (n + 1.0) * on_cosine * now_c
            slope_ref[n, :, lanes] = slope.astype(BF16)
            total = total + slope * pulled[n * slots : (n + 1) * slots]
        pair_ref[:, lanes] = total


def force_kernel(plan, nrefs, places_ref, *refs):
    far_refs, refs = refs[:nrefs], refs[nrefs:]
    (own_ref, basis_ref, slope_ref, pair_ref, rows_ref, cols_ref), refs = refs[:6], refs[6:]
    (radial_ref, mixing_ref, mix_ref, vector_ref, table_ref), refs = refs[:5], refs[5:]
    out_ref, all_ref = refs
    slots, nbasis, nspec, width = plan.slots, plan.nbasis, plan.nspec, plan.width
    gather_far(plan, places_ref, far_refs, all_ref)
    summed = dot(basis_ref[...].reshape(nbasis * slots, plan.far), all_ref[...])
    adjoint = jnp.zeros((slots, summed.shape[1]), F32)
    for n in range(nbasis):
        adjoint = adjoint + summed[n * slots : (n + 1) * slots] * radial_ref[n : n + 1]
    adjoint = own_ref[...] + MSG_SCALE * adjoint
    mixing = mixing_ref[...]
    gate = sigmoid(mixing)
    back = (adjoint * (gate * (1.0 + mixing * (1.0 - gate)))).astype(BF16)
    invariants = dot(back, mix_ref[...])
    channels = invariants.shape[1] // 2
    on_scalar = (MSG_SCALE * invariants[:, :channels]).astype(BF16)
    doubled = (2.0 * MSG_SCALE) * invariants[:, channels:]
    on_vector = (vector_ref[...] * jnp.concatenate([doubled] * 3, axis=0)).astype(BF16)
    weights = jnp.concatenate(
        [dot(on_scalar, table_ref[0], NT), dot(on_vector, table_ref[1], NT)], axis=0
    ).astype(BF16)
    group = lax.broadcasted_iota(jnp.int32, weights.shape, 1) // nspec
    weights = weights.astype(F32)
    weights = jnp.concatenate(
        [jnp.where(group == n, weights, 0.0).astype(BF16) for n in range(nbasis)], axis=0
    )
    cols = [cols_ref[:, axis : axis + 1] for axis in range(3)]
    species = lax.broadcasted_iota(jnp.int32, (nbasis * nspec, width), 0) % nspec
    own = [jnp.zeros((slots, width), F32) for _ in range(3)]
    pulls = []
    for tile in range(len(plan.tiles)):
        lanes = slice(tile * width, (tile + 1) * width)
        rows = [rows_ref[tile, k : k + 1] for k in range(4)]
        hot = (rows[3].astype(jnp.int32) == species).astype(F32).astype(BF16)
        spread = dot(weights, hot)
        parts = separations(plan, rows, cols)
        dist_sq, inverse = distance(plan, parts, tile)
        scale = ROOT_THREE * inverse
        total = pair_ref[:, lanes]
        along, sides = None, [None] * 3
        for n in range(nbasis):
            start = n * 4 * slots
            piece = [spread[start + m * slots : start + (m + 1) * slots] for m in range(4)]
            slope = slope_ref[n, :, lanes].astype(F32)
            basis = basis_ref[n, :, lanes].astype(F32)
            mixed = parts[0] * piece[1] + parts[1] * piece[2] + parts[2] * piece[3]
            total = total + slope * (piece[0] + scale * mixed)
            term = basis * mixed
            along = term if along is None else along + term
            for k in range(3):
                term = basis * piece[k + 1]
                sides[k] = term if sides[k] is None else sides[k] + term
        total = total - inverse * inverse * (scale * along)
        pulls.append([])
        for k in range(3):
            pull = parts[k] * total + scale * sides[k]
            own[k] = own[k] + pull
            pulls[-1].append(jnp.sum(pull, axis=0, keepdims=True))
    ones = jnp.ones((8, width), F32)
    mine = jnp.concatenate([dot_exact(ones, own[k], NT)[:1] for k in range(3)], axis=0)
    if plan.small:
        out_ref[...] = jnp.zeros_like(out_ref)
    side_of = lax.broadcasted_iota(jnp.int32, (3, width), 1) // slots
    for tile in range(len(plan.tiles)):
        pulled = jnp.concatenate(pulls[tile], axis=0)
        if tile == 0:
            others = [jnp.zeros_like(mine)] * (len(plan.sides) - 1)
            pulled = pulled - jnp.concatenate([mine] + others, axis=1)
        if not plan.small:
            out_ref[plan.staged_place(places_ref, tile)] = pulled
            continue
        for side in range(len(plan.sides)):
            place = plan.global_place(places_ref, tile, side)
            out_ref[place, :3] = jnp.where(side_of == side, pulled, 0.0)


def prepare_kernel(plan, counts_ref, place_ref, kind_ref, sent_ref):
    live = lax.broadcasted_iota(jnp.int32, (1, plan.slots), 1) < counts_ref[0]
    rows = [
        jnp.where(live, place_ref[0], FAR),
        place_ref[1],
        place_ref[2],
        jnp.where(live, kind_ref[...], -1).astype(F32),
    ]
    rows = jnp.concatenate(rows, axis=0)
    rows = jnp.concatenate([rows, rows], axis=1)
    for copy in range(sent_ref.shape[0]):
        sent_ref[copy] = rows


def sum_kernel(plan, parts_ref, force_ref):
    total = parts_ref[0]
    for part in range(1, parts_ref.shape[0]):
        total = total + parts_ref[part]
    total = total[:, : plan.slots] + total[:, plan.slots :]
    for k in range(3):
        force_ref[k] = -total[k : k + 1]


def own_kernel(plan, sent_ref, embed_ref, radial_ref, *refs):
    weight_refs, (cols_ref, table_ref, own_ref), kept_refs = refs[:3], refs[3:6], refs[6:]
    for weight_ref, kept_ref in zip(weight_refs, kept_refs):
        kept_ref[...] = weight_ref[...]
    slots, nspec = plan.slots, plan.nspec
    rows = sent_ref[0]
    cols = jnp.concatenate([rows, rows], axis=0).T[:slots]
    kind = cols[:, 3:4]
    lane = lax.broadcasted_iota(jnp.int32, cols.shape, 1)
    live = kind >= 0.0
    cols = jnp.where((lane == 0) & ~live, -FAR, cols)
    cols_ref[...] = jnp.where(lane == 3, live.astype(F32), cols)
    species = lax.broadcasted_iota(jnp.int32, (slots, nspec), 1)
    hot = (kind.astype(jnp.int32) == species).astype(F32).astype(BF16)
    embed = embed_ref[...]
    own_ref[...] = dot(hot, embed)
    embed = embed.astype(F32)
    for g in range(2):
        for n in range(plan.nbasis):
            row = radial_ref[g, n : n + 1]
            table_ref[g, n * nspec : (n + 1) * nspec] = (row * embed).astype(BF16)


VMEM_SPEC = pl.BlockSpec(memory_space=pltpu.VMEM)
SMEM_SPEC = pl.BlockSpec(memory_space=pltpu.SMEM)


def simple_call(kernel, plan, operands, outs, scalars=0, scratch=(), flops=2**20):
    single = not isinstance(outs, list)
    shapes = [jax.ShapeDtypeStruct(*out) for out in ([outs] if single else outs)]

    def body(*refs):
        kernel(plan, *refs)

    got = pl.pallas_call(
        body,
        out_shape=shapes,
        in_specs=[SMEM_SPEC] * scalars + [VMEM_SPEC] * (len(operands) - scalars),
        out_specs=[VMEM_SPEC] * len(shapes),
        scratch_shapes=[pltpu.VMEM(*buffer) for buffer in scratch],
        compiler_params=pltpu.CompilerParams(vmem_limit_bytes=VMEM_LIMIT),
        cost_estimate=pl.CostEstimate(flops=flops, bytes_accessed=2**20, transcendentals=0),
    )(*operands)
    return got[0] if single else got


def call(kernel, plan, far, places, operands, outs, scratch, flops):
    def body(plan, *refs):
        kernel(plan, len(far), *refs)

    return simple_call(body, plan, [places, *far, *operands], outs, 1, scratch, flops)


def swaps(axis):
    count = lax.axis_size(axis)
    if count == 2:
        return [[(0, 1), (1, 0)]]
    if paired(count):
        near = [(i, i ^ 1) for i in range(count)]
        far = [(i, (i - 1 + 2 * (i % 2)) % count) for i in range(count)]
        return [far, near]
    return [[((i + o) % count, i) for i in range(count)] for o in offsets_of(count)[1:]]


def brought(block, axis):
    return [block] + [lax.ppermute(block, axis, pairs) for pairs in swaps(axis)]


def neighbours(plan, block):
    columns = brought(jnp.stack(brought(block, "gz")), "gx")
    swapped = [brought(column, "gy") for column in columns]
    return [column[side] for side in range(len(plan.sides)) for column in swapped]


def everywhere(copies):
    return lax.all_to_all(copies, AXES, 0, 0, tiled=True)


def folded(pieces, axis):
    got = [
        lax.ppermute(piece, axis, [(to, source) for source, to in pairs])
        for piece, pairs in list(zip(pieces[1:], swaps(axis)))[::-1]
    ]
    total = pieces[0]
    for piece in got:
        total = total + piece
    return total


def fold(plan, pulls):
    for axis in ("gx", "gz"):
        parts = len(offsets_of(plan.sizes[axis]))
        pulls = pulls.reshape((parts, -1) + pulls.shape[1:])
        pulls = folded([pulls[m] for m in range(parts)], axis)
    pulls = pulls[0]
    sides = [pulls[:, m * plan.slots : (m + 1) * plan.slots] for m in range(len(plan.sides))]
    return folded(sides, "gy")


def local_program(mesh):
    def local(
        positions,
        species,
        counts,
        embed,
        radial_one,
        mix_one,
        read_one,
        radial_two,
        mix_two,
        read_hidden,
        read_out,
    ):
        slots, channels = positions.shape[-1], embed.shape[1]
        nbasis, nspec = radial_two.shape[0], embed.shape[0]
        plan = Plan(mesh, slots, nbasis, nspec)
        place = positions[0, 0, 0].reshape(3, 1, slots)
        sent = simple_call(
            prepare_kernel,
            plan,
            [counts.reshape(1), place, species.reshape(1, slots)],
            ((plan.ndev if plan.small else 1, 4, 2 * slots), F32),
            1,
        )
        places = plan.places()
        far_sent = [everywhere(sent)] if plan.small else neighbours(plan, sent[0])
        weights = [radial_two, read_out[None], read_one[None]]
        cols, table, own_embed, radial_two, out_row, one_row = simple_call(
            own_kernel,
            plan,
            [sent, embed, radial_one] + weights,
            [
                ((slots, 8), F32),
                ((2, nbasis * nspec, channels), BF16),
                ((slots, channels), F32),
            ]
            + [(weight.shape, weight.dtype) for weight in weights],
        )
        pair_flops = 100 * slots * plan.far
        rows, basis, layer, vector, mixing = call(
            first_kernel,
            plan,
            far_sent,
            places,
            [cols, table, own_embed, mix_one],
            [
                ((len(plan.tiles), 4, plan.width), F32),
                ((nbasis, slots, plan.far), BF16),
                ((slots, channels), BF16),
                ((3 * slots, channels), F32),
                ((slots, channels), F32),
            ],
            [((nbasis, 4 * slots, plan.far), BF16)],
            pair_flops,
        )
        far_layer = neighbours(plan, layer)
        far_scratch = ((plan.far, channels), BF16)
        adjoint, energy, features, own_adjoint = call(
            second_kernel,
            plan,
            far_layer,
            places,
            [layer, basis, cols, radial_two, mix_two, read_hidden, out_row, one_row],
            [
                ((slots, channels), BF16),
                ((1, slots), F32),
                ((slots, channels), BF16),
                ((slots, channels), F32),
            ],
            [far_scratch],
            pair_flops,
        )
        far_adjoint = neighbours(plan, adjoint)
        slope, pair = call(
            slope_kernel,
            plan,
            far_layer,
            places,
            [adjoint, rows, cols, radial_two],
            [((nbasis, slots, plan.far), BF16), ((slots, plan.far), F32)],
            [far_scratch],
            pair_flops,
        )
        pulls = call(
            force_kernel,
            plan,
            far_adjoint,
            places,
            [own_adjoint, basis, slope, pair, rows, cols, radial_two, mixing, mix_one, vector, table],
            [((plan.ndev, 4, plan.width) if plan.small else (len(plan.tiles), 3, plan.width), F32)],
            [far_scratch],
            pair_flops,
        )
        if plan.small:
            forces = simple_call(sum_kernel, plan, [everywhere(pulls[0])], ((3, 1, slots), F32))
        else:
            forces = -fold(plan, pulls[0])
        return (
            forces.reshape(1, 1, 1, 3, slots),
            energy[None, None],
            features.T[None, None, None],
        )

    return local


def solution(mesh):
    split = [P(*AXES, None, None), P(*AXES, None), P(*AXES)]
    out_specs = (P(*AXES, None, None), P(*AXES, None), P(*AXES, None, None))
    return jax.shard_map(
        local_program(mesh),
        mesh=mesh,
        in_specs=tuple(split + [P()] * 8),
        out_specs=out_specs,
        check_vma=False,
    )
```

```python
import itertools
import math

import jax
import jax.numpy as jnp
from jax import lax
from jax.experimental import pallas as pl
from jax.experimental.pallas import tpu as pltpu
from jax.sharding import PartitionSpec as P

CELL_SIDE = 5.0
CUT_SQUARE = 25.0
SOFTEN = 0.25
MSG_SCALE = 0.05
ROOT_THREE = math.sqrt(3.0)
FAR = 1.0e4
AXES = ("gx", "gy", "gz")
F32 = jnp.float32
BF16 = jnp.bfloat16
COS_TERMS = (
    0.9999999997799041,
    -4.934802137078749,
    4.058709159554242,
    -1.335212003029471,
    0.23493731372678894,
    -0.024396324214549327,
)
SIN_TERMS = (
    3.14159265353629,
    -5.167712764624453,
    2.550163318944743,
    -0.5992521977996564,
    0.08205040170151112,
    -0.007028386239784362,
)
VMEM_LIMIT = 24 * 1024 * 1024
FETCH_LIMIT = 60 * 1024 * 1024
NT = (((1,), (1,)), ((), ()))
NN = (((1,), (0,)), ((), ()))


def dot(a, b, dims=NN):
    return lax.dot_general(a, b, dims, preferred_element_type=F32)


def dot_exact(a, b, dims=NN):
    return lax.dot_general(
        a, b, dims, precision=lax.Precision.HIGHEST, preferred_element_type=F32
    )


def split_dot(a, b):
    high = a.astype(BF16)
    low = (a - high.astype(F32)).astype(BF16)
    return dot(high, b) + dot(low, b)


def offsets_of(count):
    return (0, 1) if count == 2 else (0, 1, -1)


def paired(count):
    return count > 2 and count % 2 == 0


def poly(terms, arg):
    total = arg * terms[-1] + terms[-2]
    for term in terms[-3::-1]:
        total = total * arg + term
    return total


class Plan:
    def __init__(self, mesh, slots, nbasis, nspec):
        self.sizes = {axis: mesh.shape[axis] for axis in AXES}
        self.ndev = math.prod(self.sizes.values())
        self.tiles = list(
            itertools.product(offsets_of(self.sizes["gx"]), offsets_of(self.sizes["gz"]))
        )
        self.sides = offsets_of(self.sizes["gy"])
        self.slots = slots
        self.width = len(self.sides) * slots
        self.far = len(self.tiles) * self.width
        self.nbasis = nbasis
        self.nspec = nspec
        self.depth = len(offsets_of(self.sizes["gz"]))
        self.wide = len(offsets_of(self.sizes["gx"]))
        self.small = self.ndev <= 64 and len(self.sides) == 2
        self.wrapped = [self.sizes[axis] == 2 for axis in AXES]

    def places(self):
        index = {axis: lax.axis_index(axis) for axis in AXES}

        def parity(axis):
            return lax.rem(index[axis], 2) if paired(self.sizes[axis]) else jnp.int32(0)

        def moved(axis, step):
            return lax.rem(index[axis] + (step + self.sizes[axis]), self.sizes[axis])

        depth = len(offsets_of(self.sizes["gz"]))
        turn = parity("gz")
        found = [jnp.int32(0), 1 + turn, 2 - turn][:depth] + [parity("gx")]
        for ox, oz in self.tiles:
            for oy in self.sides:
                place = (moved("gx", ox) * self.sizes["gy"] + moved("gy", oy)) * self.sizes["gz"]
                found.append(place + moved("gz", oz))
        return jnp.stack(found).astype(jnp.int32)

    def global_place(self, places_ref, tile, side):
        return places_ref[self.depth + 1 + tile * len(self.sides) + side]

    def staged_place(self, places_ref, tile):
        x, z = divmod(tile, self.depth)
        flip = places_ref[self.depth]
        return (0, 1 + flip, 2 - flip)[x] * self.depth + places_ref[z]

    def offset(self, tile, side):
        ox, oz = self.tiles[tile]
        return (ox, self.sides[side], oz)


def separations(plan, rows, cols):
    parts = []
    for axis in range(3):
        diff = rows[axis] - cols[axis]
        if plan.wrapped[axis]:
            diff = jnp.where(diff > CELL_SIDE, diff - 2.0 * CELL_SIDE, diff)
        parts.append(diff)
    return parts


def distance(plan, parts, tile):
    dist_sq = parts[0] * parts[0] + parts[1] * parts[1] + parts[2] * parts[2] + SOFTEN
    if tile == 0:
        row = lax.broadcasted_iota(jnp.int32, dist_sq.shape, 0)
        col = lax.broadcasted_iota(jnp.int32, dist_sq.shape, 1)
        dist_sq = jnp.where(row == col, FAR, dist_sq)
    return dist_sq, lax.rsqrt(dist_sq)


def waves(dist_sq, inverse):
    arg = jnp.minimum(dist_sq * inverse * (1.0 / CELL_SIDE) - 0.5, 0.5)
    square = arg * arg
    return poly(COS_TERMS, square), -(arg * poly(SIN_TERMS, square))


def first_kernel(plan, nrefs, places_ref, *refs):
    far_refs, refs = refs[:nrefs], refs[nrefs:]
    (cols_ref, table_ref, embed_ref, mix_ref), refs = refs[:4], refs[4:]
    rows_ref, basis_ref, layer_ref, vector_ref, mixing_ref, pair_ref = refs
    slots, nbasis, nspec = plan.slots, plan.nbasis, plan.nspec
    cols = [cols_ref[:, axis : axis + 1] for axis in range(3)]
    species = lax.broadcasted_iota(jnp.int32, (nbasis * nspec, plan.width), 0) % nspec
    hot = []
    for tile in range(len(plan.tiles)):
        blocks = [fetch(plan, places_ref, far_refs, tile, side) for side in range(len(plan.sides))]
        placed = side_by_side(plan, blocks) + tile_shift(plan, tile)
        rows_ref[tile] = placed
        rows = [placed[k : k + 1] for k in range(4)]
        hot.append((rows[3].astype(jnp.int32) == species).astype(F32).astype(BF16))
        parts = separations(plan, rows, cols)
        dist_sq, inverse = distance(plan, parts, tile)
        sine, cosine = waves(dist_sq, inverse)
        fade = jnp.maximum(1.0 - dist_sq * (1.0 / CUT_SQUARE), 0.0)
        radial = fade * fade * inverse
        units = [(part * (inverse * ROOT_THREE)).astype(BF16) for part in parts]
        before, now = None, sine * radial
        lanes = slice(tile * plan.width, (tile + 1) * plan.width)
        for n in range(nbasis):
            if n == 1:
                before, now = now, 2.0 * cosine * now
            elif n > 1:
                before, now = now, 2.0 * cosine * now - before
            packed = now.astype(BF16)
            basis_ref[n, :, lanes] = packed
            pair_ref[n, :slots, lanes] = packed
            for k in range(3):
                pair_ref[n, (k + 1) * slots : (k + 2) * slots, lanes] = units[k] * packed
    hot = jnp.concatenate(hot, axis=1)
    gathered = dot(pair_ref[...].reshape(nbasis * 4 * slots, plan.far), hot, NT)
    gathered = gathered.reshape(nbasis, 4 * slots, nbasis * nspec)
    group = lax.broadcasted_iota(jnp.int32, gathered.shape[1:], 1) // nspec
    counted = jnp.zeros(gathered.shape[1:], F32)
    for n in range(nbasis):
        counted = jnp.where(group == n, gathered[n], counted)
    scalar = MSG_SCALE * split_dot(counted[:slots], table_ref[0])
    vector = MSG_SCALE * split_dot(counted[slots:], table_ref[1])
    vector_ref[...] = vector
    squares = vector * vector
    norm = squares[:slots] + squares[slots : 2 * slots] + squares[2 * slots :]
    invariants = jnp.concatenate([scalar.astype(BF16), norm.astype(BF16)], axis=1)
    mixing = dot(invariants, mix_ref[...], NT)
    mixing_ref[...] = mixing
    layer = (embed_ref[...] + mixing * sigmoid(mixing)).astype(BF16)
    layer_ref[...] = layer


def sigmoid(value):
    return 1.0 / (1.0 + jnp.exp(-value))


def fetch(plan, places_ref, far_refs, tile, side):
    if len(far_refs) == 1:
        return far_refs[0][plan.global_place(places_ref, tile, side)]
    x, z = divmod(tile, plan.depth)
    place = places_ref[z]
    columns = far_refs[side * plan.wide : (side + 1) * plan.wide]
    if x == 0 or plan.wide == 2:
        return columns[x][place]
    kept, other = columns[x][place], columns[3 - x][place]
    return jnp.where(places_ref[plan.depth] == 0, kept, other)


def side_by_side(plan, blocks):
    if len(blocks) == 2:
        lane = lax.broadcasted_iota(jnp.int32, blocks[0].shape, 1)
        return jnp.where(lane < plan.slots, blocks[0], blocks[1])
    return jnp.concatenate([block[:, : plan.slots] for block in blocks], axis=1)


def tile_shift(plan, tile):
    row = lax.broadcasted_iota(jnp.int32, (4, plan.width), 0)
    side = lax.broadcasted_iota(jnp.int32, (4, plan.width), 1) // plan.slots
    shift = jnp.zeros((4, plan.width), F32)
    for s in range(len(plan.sides)):
        for k, steps in enumerate(plan.offset(tile, s)):
            if steps:
                shift = jnp.where((row == k) & (side == s), CELL_SIDE * steps, shift)
    return shift


def gather_far(plan, places_ref, far_refs, all_ref):
    slots = plan.slots
    for tile in range(len(plan.tiles)):
        for side in range(len(plan.sides)):
            start = tile * plan.width + side * slots
            all_ref[start : start + slots] = fetch(plan, places_ref, far_refs, tile, side)


def second_kernel(plan, nrefs, places_ref, *refs):
    far_refs, refs = refs[:nrefs], refs[nrefs:]
    (layer_ref, basis_ref, cols_ref, radial_ref, mix_ref), refs = refs[:5], refs[5:]
    (hidden_ref, out_ref, one_ref), refs = refs[:3], refs[3:]
    adjoint_ref, features_ref, before_ref, own_ref, all_ref = refs
    slots, nbasis = plan.slots, plan.nbasis
    gather_far(plan, places_ref, far_refs, all_ref)
    summed = dot(basis_ref[...].reshape(nbasis * slots, plan.far), all_ref[...])
    message = jnp.zeros((slots, summed.shape[1]), F32)
    for n in range(nbasis):
        message = message + summed[n * slots : (n + 1) * slots] * radial_ref[n : n + 1]
    rounded = (MSG_SCALE * message).astype(BF16)
    mixing = dot(rounded, mix_ref[...], NT)
    gate = sigmoid(mixing)
    layer = layer_ref[...].astype(F32)
    features = (layer + mixing * gate).astype(BF16)
    features_ref[...] = features
    before = dot(features, hidden_ref[...], NT)
    open_hidden = sigmoid(before)
    live = cols_ref[:, 3:4]
    before_ref[...] = before
    slope = out_ref[...] * (open_hidden * (1.0 + before * (1.0 - open_hidden))) * live
    from_hidden = dot(slope.astype(BF16), hidden_ref[...])
    own_ref[...] = from_hidden + one_ref[...] * live
    back = from_hidden * (gate * (1.0 + mixing * (1.0 - gate)))
    adjoint_ref[...] = dot(back.astype(BF16), mix_ref[...]).astype(BF16)


def slope_kernel(plan, rows_ref, cols_ref, layer_ref, again_ref, apart_ref, slope_ref, radial_ref, turned_ref):
    again_ref[...] = layer_ref[...]
    cols = [cols_ref[:, axis : axis + 1] for axis in range(3)]
    for tile in range(len(plan.tiles)):
        lanes = slice(tile * plan.width, (tile + 1) * plan.width)
        parts = separations(plan, [rows_ref[tile, k : k + 1] for k in range(3)], cols)
        for k in range(3):
            apart_ref[k, :, lanes] = parts[k]
        dist_sq, inverse = distance(plan, parts, tile)
        sine, cosine = waves(dist_sq, inverse)
        fade = jnp.maximum(1.0 - dist_sq * (1.0 / CUT_SQUARE), 0.0)
        radial = fade * fade * inverse
        on_sine = -inverse * ((4.0 / CUT_SQUARE) * fade + radial * inverse)
        on_cosine = (math.pi / CELL_SIDE) * (inverse * radial)
        scale = ROOT_THREE * inverse
        scaled = scale * radial
        square = inverse * inverse
        double = 2.0 * cosine
        before_s, now_s, before_c, now_c = None, sine, None, cosine
        for n in range(plan.nbasis):
            if n == 1:
                before_s, now_s = now_s, double * now_s
                before_c, now_c = now_c, double * now_c - 1.0
            elif n > 1:
                before_s, now_s = now_s, double * now_s - before_s
                before_c, now_c = now_c, double * now_c - before_c
            slope = on_sine * now_s + (n + 1.0) * on_cosine * now_c
            factor = scaled * now_s
            slope_ref[n, :, lanes] = slope
            radial_ref[n, :, lanes] = factor
            turned_ref[n, :, lanes] = scale * slope - square * factor


def energy_kernel(plan, nrefs, places_ref, *refs):
    far_refs, refs = refs[:nrefs], refs[nrefs:]
    (adjoint_ref, slope_ref, radial_ref, cols_ref, layer_ref), refs = refs[:5], refs[5:]
    (before_ref, out_ref, one_ref, kept_ref), refs = refs[:4], refs[4:]
    again_ref, pair_ref, energy_ref, features_ref, all_ref = refs
    slots, nbasis = plan.slots, plan.nbasis
    again_ref[...] = adjoint_ref[...]
    features_ref[...] = kept_ref[...]
    before = before_ref[...]
    live = jnp.where(lax.broadcasted_iota(jnp.int32, (slots, 8), 1) == 0, cols_ref[:, 3:4], 0.0)
    live_row = dot(jnp.ones((1, 8), BF16), live.astype(BF16), NT)
    energy = dot_exact(one_ref[...], layer_ref[...].astype(F32), NT)
    energy = energy + dot_exact(out_ref[...], before * sigmoid(before), NT)
    energy_ref[...] = energy * live_row
    gather_far(plan, places_ref, far_refs, all_ref)
    adjoint = adjoint_ref[...].astype(F32) * MSG_SCALE
    weighted = jnp.concatenate(
        [(adjoint * radial_ref[n : n + 1]).astype(BF16) for n in range(nbasis)], axis=0
    )
    for tile in range(len(plan.tiles)):
        lanes = slice(tile * plan.width, (tile + 1) * plan.width)
        pulled = dot(weighted, all_ref[lanes], NT)
        total = slope_ref[0, :, lanes] * pulled[:slots]
        for n in range(1, nbasis):
            total = total + slope_ref[n, :, lanes] * pulled[n * slots : (n + 1) * slots]
        pair_ref[:, lanes] = total


def force_kernel(plan, nrefs, places_ref, *refs):
    far_refs, refs = refs[:nrefs], refs[nrefs:]
    (own_ref, basis_ref, pair_ref, rows_ref), refs = refs[:4], refs[4:]
    (apart_ref, slope_ref, factor_ref, turned_ref), refs = refs[:4], refs[4:]
    (radial_ref, mixing_ref, mix_ref, vector_ref, table_ref), refs = refs[:5], refs[5:]
    out_ref, all_ref = refs
    slots, nbasis, nspec, width = plan.slots, plan.nbasis, plan.nspec, plan.width
    gather_far(plan, places_ref, far_refs, all_ref)
    summed = dot(basis_ref[...].reshape(nbasis * slots, plan.far), all_ref[...])
    adjoint = jnp.zeros((slots, summed.shape[1]), F32)
    for n in range(nbasis):
        adjoint = adjoint + summed[n * slots : (n + 1) * slots] * radial_ref[n : n + 1]
    adjoint = own_ref[...] + MSG_SCALE * adjoint
    mixing = mixing_ref[...]
    gate = sigmoid(mixing)
    back = (adjoint * (gate * (1.0 + mixing * (1.0 - gate)))).astype(BF16)
    invariants = dot(back, mix_ref[...])
    channels = invariants.shape[1] // 2
    on_scalar = (MSG_SCALE * invariants[:, :channels]).astype(BF16)
    doubled = (2.0 * MSG_SCALE) * invariants[:, channels:]
    on_vector = (vector_ref[...] * jnp.concatenate([doubled] * 3, axis=0)).astype(BF16)
    weights = jnp.concatenate(
        [dot(on_scalar, table_ref[0], NT), dot(on_vector, table_ref[1], NT)], axis=0
    ).astype(BF16)
    group = lax.broadcasted_iota(jnp.int32, weights.shape, 1) // nspec
    weights = weights.astype(F32)
    weights = jnp.concatenate(
        [jnp.where(group == n, weights, 0.0).astype(BF16) for n in range(nbasis)], axis=0
    )
    species = lax.broadcasted_iota(jnp.int32, (nbasis * nspec, width), 0) % nspec
    own = [jnp.zeros((slots, width), F32) for _ in range(3)]
    pulls = []
    for tile in range(len(plan.tiles)):
        lanes = slice(tile * width, (tile + 1) * width)
        hot = (rows_ref[tile, 3:4].astype(jnp.int32) == species).astype(F32).astype(BF16)
        spread = dot(weights, hot)
        total = pair_ref[:, lanes]
        sides, turns = [None] * 3, [None] * 3
        for n in range(nbasis):
            start = n * 4 * slots
            total = total + slope_ref[n, :, lanes] * spread[start : start + slots]
            for k in range(3):
                piece = spread[start + (k + 1) * slots : start + (k + 2) * slots]
                side = factor_ref[n, :, lanes] * piece
                turn = turned_ref[n, :, lanes] * piece
                sides[k] = side if n == 0 else sides[k] + side
                turns[k] = turn if n == 0 else turns[k] + turn
        for k in range(3):
            total = total + apart_ref[k, :, lanes] * turns[k]
        pulls.append([])
        for k in range(3):
            pull = apart_ref[k, :, lanes] * total + sides[k]
            own[k] = own[k] + pull
            pulls[-1].append(jnp.sum(pull, axis=0, keepdims=True))
    own = jnp.concatenate(own, axis=0)
    high = own.astype(BF16)
    low = (own - high.astype(F32)).astype(BF16)
    ones = jnp.ones((8, width), BF16)
    mine = (dot(ones, high, NT) + dot(ones, low, NT))[:1]
    mine = jnp.concatenate([mine[:, k * slots : (k + 1) * slots] for k in range(3)], axis=0)
    if plan.small:
        out_ref[...] = jnp.zeros_like(out_ref)
    side_of = lax.broadcasted_iota(jnp.int32, (3, width), 1) // slots
    for tile in range(len(plan.tiles)):
        pulled = jnp.concatenate(pulls[tile], axis=0)
        if tile == 0:
            others = [jnp.zeros_like(mine)] * (len(plan.sides) - 1)
            pulled = pulled - jnp.concatenate([mine] + others, axis=1)
        if not plan.small:
            out_ref[plan.staged_place(places_ref, tile)] = pulled
            continue
        for side in range(len(plan.sides)):
            place = plan.global_place(places_ref, tile, side)
            out_ref[place, :3] = jnp.where(side_of == side, pulled, 0.0)


def brought_in(pairs, sems):
    copies = [pltpu.make_async_copy(*pair, sems.at[m]) for m, pair in enumerate(pairs)]
    for copy in copies:
        copy.start()
    for copy in copies:
        copy.wait()


def live_rows(plan, counts_ref, place_ref, kind_ref):
    live = lax.broadcasted_iota(jnp.int32, (1, plan.slots), 1) < counts_ref[0]
    rows = [
        jnp.where(live, place_ref[0], FAR),
        place_ref[1],
        place_ref[2],
        jnp.where(live, kind_ref[...], -1).astype(F32),
    ]
    rows = jnp.concatenate(rows, axis=0)
    return jnp.concatenate([rows, rows], axis=1)


def prepare_kernel(plan, counts_ref, place_hbm, kind_hbm, sent_ref, place_ref, kind_ref, sems):
    brought_in([(place_hbm, place_ref), (kind_hbm, kind_ref)], sems)
    rows = live_rows(plan, counts_ref, place_ref, kind_ref)
    for copy in range(sent_ref.shape[0]):
        sent_ref[copy] = rows


def sum_kernel(plan, parts_ref, force_ref):
    total = parts_ref[0]
    for part in range(1, parts_ref.shape[0]):
        total = total + parts_ref[part]
    total = total[:, : plan.slots] + total[:, plan.slots :]
    for k in range(3):
        force_ref[k] = -total[k : k + 1]


def own_kernel(plan, counts_ref, *refs):
    fetched, weights, (cols_ref, table_ref, own_ref) = refs[:4], refs[4:10], refs[10:13]
    kept, local_refs, sems = refs[13:19], refs[19:-1], refs[-1]
    slots, nspec = plan.slots, plan.nspec
    brought_in([*zip(fetched, local_refs), *zip(weights, kept)], sems)
    place_ref, kind_ref, embed_ref, radial_ref = local_refs
    rows = live_rows(plan, counts_ref, place_ref, kind_ref)
    cols = jnp.concatenate([rows, rows], axis=0).T[:slots]
    kind = cols[:, 3:4]
    lane = lax.broadcasted_iota(jnp.int32, cols.shape, 1)
    live = kind >= 0.0
    cols = jnp.where((lane == 0) & ~live, -FAR, cols)
    cols_ref[...] = jnp.where(lane == 3, live.astype(F32), cols)
    species = lax.broadcasted_iota(jnp.int32, (slots, nspec), 1)
    hot = (kind.astype(jnp.int32) == species).astype(F32).astype(BF16)
    embed = embed_ref[...]
    own_ref[...] = dot(hot, embed)
    embed = embed.astype(F32)
    for g in range(2):
        for n in range(plan.nbasis):
            row = radial_ref[g, n : n + 1]
            table_ref[g, n * nspec : (n + 1) * nspec] = (row * embed).astype(BF16)


VMEM_SPEC = pl.BlockSpec(memory_space=pltpu.VMEM)
SMEM_SPEC = pl.BlockSpec(memory_space=pltpu.SMEM)
HBM_SPEC = pl.BlockSpec(memory_space=pltpu.HBM)


def simple_call(kernel, plan, operands, outs, scalars=0, scratch=(), flops=2**20, near=False, fetched=0):
    single = not isinstance(outs, list)
    kind = pltpu.VMEM if near else jax.ShapeDtypeStruct
    shapes = [kind(*out) for out in ([outs] if single else outs)]

    def body(*refs):
        kernel(plan, *refs)

    got = pl.pallas_call(
        body,
        out_shape=shapes,
        in_specs=[SMEM_SPEC] * scalars
        + [VMEM_SPEC] * (len(operands) - scalars - fetched)
        + [HBM_SPEC] * fetched,
        out_specs=[VMEM_SPEC] * len(shapes),
        scratch_shapes=[pltpu.VMEM(*buffer) for buffer in scratch]
        + [pltpu.SemaphoreType.DMA((fetched,))] * (fetched > 0),
        compiler_params=pltpu.CompilerParams(vmem_limit_bytes=FETCH_LIMIT if fetched else VMEM_LIMIT),
        cost_estimate=pl.CostEstimate(flops=flops, bytes_accessed=2**20, transcendentals=0),
    )(*operands)
    return got[0] if single else got


def call(kernel, plan, far, places, operands, outs, scratch, flops):
    def body(plan, *refs):
        kernel(plan, len(far), *refs)

    return simple_call(body, plan, [places, *far, *operands], outs, 1, scratch, flops)


def swaps(axis):
    count = lax.axis_size(axis)
    if count == 2:
        return [[(0, 1), (1, 0)]]
    if paired(count):
        near = [(i, i ^ 1) for i in range(count)]
        far = [(i, (i - 1 + 2 * (i % 2)) % count) for i in range(count)]
        return [near, far]
    return [[((i + o) % count, i) for i in range(count)] for o in offsets_of(count)[1:]]


def brought(block, axis):
    return [block] + [lax.ppermute(block, axis, pairs) for pairs in swaps(axis)]


def neighbours(plan, block, again=None):
    column = brought(block, "gz")
    column = jnp.stack([block if again is None else again] + column[1:])
    columns = brought(column, "gx")
    swapped = [brought(column, "gy") for column in columns]
    return [column[side] for side in range(len(plan.sides)) for column in swapped]


def everywhere(copies):
    return lax.all_to_all(copies, AXES, 0, 0, tiled=True)


def folded(pieces, axis):
    got = [
        lax.ppermute(piece, axis, [(to, source) for source, to in pairs])
        for piece, pairs in list(zip(pieces[1:], swaps(axis)))[::-1]
    ]
    total = pieces[0]
    for piece in got:
        total = total + piece
    return total


def fold(plan, pulls):
    for axis in ("gx", "gz"):
        parts = len(offsets_of(plan.sizes[axis]))
        pulls = pulls.reshape((parts, -1) + pulls.shape[1:])
        pulls = folded([pulls[m] for m in range(parts)], axis)
    pulls = pulls[0]
    sides = [pulls[:, m * plan.slots : (m + 1) * plan.slots] for m in range(len(plan.sides))]
    return folded(sides, "gy")


def local_program(mesh):
    def local(
        positions,
        species,
        counts,
        embed,
        radial_one,
        mix_one,
        read_one,
        radial_two,
        mix_two,
        read_hidden,
        read_out,
    ):
        slots, channels = positions.shape[-1], embed.shape[1]
        nbasis, nspec = radial_two.shape[0], embed.shape[0]
        plan = Plan(mesh, slots, nbasis, nspec)
        count = counts.reshape(1)
        given = [positions[0, 0, 0].reshape(3, 1, slots), species.reshape(1, slots)]
        sent = simple_call(
            prepare_kernel,
            plan,
            [count, *given],
            ((plan.ndev if plan.small else 1, 4, 2 * slots), F32),
            1,
            [(array.shape, array.dtype) for array in given],
            near=True,
            fetched=len(given),
        )
        places = plan.places()
        far_sent = [everywhere(sent)] if plan.small else neighbours(plan, sent[0])
        weights = [radial_two, read_out[None], read_one[None], mix_one, mix_two, read_hidden]
        given = given + [embed, radial_one]
        cols, table, own_embed, radial_two, out_row, one_row, mix_one, mix_two, read_hidden = simple_call(
            own_kernel,
            plan,
            [count, *given, *weights],
            [
                ((slots, 8), F32),
                ((2, nbasis * nspec, channels), BF16),
                ((slots, channels), F32),
            ]
            + [(weight.shape, weight.dtype) for weight in weights],
            1,
            [(array.shape, array.dtype) for array in given],
            near=True,
            fetched=len(given) + len(weights),
        )
        pair_flops = 100 * slots * plan.far
        rows, basis, layer, vector, mixing = call(
            first_kernel,
            plan,
            far_sent,
            places,
            [cols, table, own_embed, mix_one],
            [
                ((len(plan.tiles), 4, plan.width), F32),
                ((nbasis, slots, plan.far), BF16),
                ((slots, channels), BF16),
                ((3 * slots, channels), F32),
                ((slots, channels), F32),
            ],
            [((nbasis, 4 * slots, plan.far), BF16)],
            pair_flops,
        )
        again, apart, slope, factor, turned = simple_call(
            slope_kernel,
            plan,
            [rows, cols, layer],
            [(layer.shape, BF16)]
            + [((count, slots, plan.far), F32) for count in (3, nbasis, nbasis, nbasis)],
            flops=pair_flops,
        )
        far_layer = neighbours(plan, layer, again)
        far_scratch = ((plan.far, channels), BF16)
        adjoint, kept, before, own_adjoint = call(
            second_kernel,
            plan,
            far_layer,
            places,
            [layer, basis, cols, radial_two, mix_two, read_hidden, out_row, one_row],
            [
                ((slots, channels), BF16),
                ((slots, channels), BF16),
                ((slots, read_hidden.shape[0]), F32),
                ((slots, channels), F32),
            ],
            [far_scratch],
            pair_flops,
        )
        again, pair, energy, features = call(
            energy_kernel,
            plan,
            far_layer,
            places,
            [adjoint, slope, radial_two, cols, layer, before, out_row, one_row, kept],
            [
                ((slots, channels), BF16),
                ((slots, plan.far), F32),
                ((1, slots), F32),
                ((slots, channels), BF16),
            ],
            [far_scratch],
            pair_flops,
        )
        far_adjoint = neighbours(plan, adjoint, again)
        pulls = call(
            force_kernel,
            plan,
            far_adjoint,
            places,
            [own_adjoint, basis, pair, rows, apart, slope, factor, turned]
            + [radial_two, mixing, mix_one, vector, table],
            [((plan.ndev, 4, plan.width) if plan.small else (len(plan.tiles), 3, plan.width), F32)],
            [far_scratch],
            pair_flops,
        )
        if plan.small:
            forces = simple_call(sum_kernel, plan, [everywhere(pulls[0])], ((3, 1, slots), F32))
        else:
            forces = -fold(plan, pulls[0])
        return (
            forces.reshape(1, 1, 1, 3, slots),
            energy[None, None],
            features.T[None, None, None],
        )

    return local


def solution(mesh):
    split = [P(*AXES, None, None), P(*AXES, None), P(*AXES)]
    out_specs = (P(*AXES, None, None), P(*AXES, None), P(*AXES, None, None))
    return jax.shard_map(
        local_program(mesh),
        mesh=mesh,
        in_specs=tuple(split + [P()] * 8),
        out_specs=out_specs,
        check_vma=False,
    )
```

```python
import itertools
import math

import jax
import jax.numpy as jnp
from jax import lax
from jax.experimental import pallas as pl
from jax.experimental.pallas import tpu as pltpu
from jax.sharding import PartitionSpec as P

CELL_SIDE = 5.0
CUT_SQUARE = 25.0
SOFTEN = 0.25
MSG_SCALE = 0.05
ROOT_THREE = math.sqrt(3.0)
FAR = 1.0e4
AXES = ("gx", "gy", "gz")
F32 = jnp.float32
BF16 = jnp.bfloat16
COS_TERMS = (
    0.9999999997799041,
    -4.934802137078749,
    4.058709159554242,
    -1.335212003029471,
    0.23493731372678894,
    -0.024396324214549327,
)
SIN_TERMS = (
    3.14159265353629,
    -5.167712764624453,
    2.550163318944743,
    -0.5992521977996564,
    0.08205040170151112,
    -0.007028386239784362,
)
VMEM_LIMIT = 24 * 1024 * 1024
FETCH_LIMIT = 60 * 1024 * 1024
NT = (((1,), (1,)), ((), ()))
NN = (((1,), (0,)), ((), ()))


def dot(a, b, dims=NN):
    return lax.dot_general(a, b, dims, preferred_element_type=F32)


def dot_exact(a, b, dims=NN):
    return lax.dot_general(
        a, b, dims, precision=lax.Precision.HIGHEST, preferred_element_type=F32
    )


def split_dot(a, b):
    high = a.astype(BF16)
    low = (a - high.astype(F32)).astype(BF16)
    return dot(high, b) + dot(low, b)


def offsets_of(count):
    return (0, 1) if count == 2 else (0, 1, -1)


def paired(count):
    return count > 2 and count % 2 == 0


def matched(which, parity):
    return jnp.int32(0) if which == 0 else 1 + (parity if which == 1 else 1 - parity)


def poly(terms, arg):
    total = arg * terms[-1] + terms[-2]
    for term in terms[-3::-1]:
        total = total * arg + term
    return total


class Plan:
    def __init__(self, mesh, slots, nbasis, nspec):
        self.sizes = {axis: mesh.shape[axis] for axis in AXES}
        self.ndev = math.prod(self.sizes.values())
        self.tiles = list(
            itertools.product(offsets_of(self.sizes["gx"]), offsets_of(self.sizes["gz"]))
        )
        self.sides = offsets_of(self.sizes["gy"])
        self.slots = slots
        self.width = len(self.sides) * slots
        self.far = len(self.tiles) * self.width
        self.nbasis = nbasis
        self.nspec = nspec
        self.depth = len(offsets_of(self.sizes["gz"]))
        self.wide = len(offsets_of(self.sizes["gx"]))
        self.brought = list(itertools.product(range(self.wide), range(self.depth)))
        self.mixed = self.depth == self.wide and self.sizes["gy"] % 2 == 0
        self.small = self.ndev <= 64 and len(self.sides) == 2
        self.wrapped = [self.sizes[axis] == 2 for axis in AXES]

    def places(self):
        index = {axis: lax.axis_index(axis) for axis in AXES}

        def parity(axis):
            return lax.rem(index[axis], 2) if paired(self.sizes[axis]) else jnp.int32(0)

        def moved(axis, step):
            return lax.rem(index[axis] + (step + self.sizes[axis]), self.sizes[axis])

        turns = parity("gx"), parity("gz")
        core = lax.rem(index["gy"], 2) if self.mixed else jnp.int32(0)
        found = []
        for side in range(len(self.sides)):
            x_first = core if side == 0 or not self.mixed else 1 - core
            for second, first in self.brought:
                plain = matched(second, turns[0]) * self.depth + matched(first, turns[1])
                crossed = matched(first, turns[0]) * self.depth + matched(second, turns[1])
                tile = jnp.where(x_first == 1, crossed, plain) if self.mixed else plain
                found.append(tile * len(self.sides) + side)
        found += turns
        for ox, oz in self.tiles:
            for oy in self.sides:
                place = (moved("gx", ox) * self.sizes["gy"] + moved("gy", oy)) * self.sizes["gz"]
                found.append(place + moved("gz", oz))
        return jnp.stack(found).astype(jnp.int32)

    def brought_place(self, places_ref, side, pair):
        return places_ref[side * len(self.brought) + pair]

    def global_place(self, places_ref, tile, side):
        start = len(self.sides) * len(self.brought) + 2
        return places_ref[start + tile * len(self.sides) + side]

    def staged_place(self, places_ref, tile):
        start = len(self.sides) * len(self.brought)
        x, z = divmod(tile, self.depth)
        return matched(x, places_ref[start]) * self.depth + matched(z, places_ref[start + 1])

    def offset(self, tile, side):
        ox, oz = self.tiles[tile]
        return (ox, self.sides[side], oz)


def separations(plan, rows, cols):
    parts = []
    for axis in range(3):
        diff = rows[axis] - cols[axis]
        if plan.wrapped[axis]:
            diff = jnp.where(diff > CELL_SIDE, diff - 2.0 * CELL_SIDE, diff)
        parts.append(diff)
    return parts


def distance(plan, parts, tile):
    dist_sq = parts[0] * parts[0] + parts[1] * parts[1] + parts[2] * parts[2] + SOFTEN
    if tile == 0:
        row = lax.broadcasted_iota(jnp.int32, dist_sq.shape, 0)
        col = lax.broadcasted_iota(jnp.int32, dist_sq.shape, 1)
        dist_sq = jnp.where(row == col, FAR, dist_sq)
    return dist_sq, lax.rsqrt(dist_sq)


def waves(dist_sq, inverse):
    arg = jnp.minimum(dist_sq * inverse * (1.0 / CELL_SIDE) - 0.5, 0.5)
    square = arg * arg
    return poly(COS_TERMS, square), -(arg * poly(SIN_TERMS, square))


def first_kernel(plan, nrefs, places_ref, *refs):
    far_refs, refs = refs[:nrefs], refs[nrefs:]
    (cols_ref, table_ref, embed_ref, mix_ref), refs = refs[:4], refs[4:]
    rows_ref, basis_ref, layer_ref, vector_ref, mixing_ref, pair_ref, block_ref = refs
    slots, nbasis, nspec = plan.slots, plan.nbasis, plan.nspec
    cols = [cols_ref[:, axis : axis + 1] for axis in range(3)]
    species = lax.broadcasted_iota(jnp.int32, (nbasis * nspec, plan.width), 0) % nspec
    hot = []

    def put(place, block):
        block_ref[place] = block

    if not plan.small:
        scatter(plan, places_ref, far_refs, put)
    for tile in range(len(plan.tiles)):
        if plan.small:
            blocks = [far_refs[0][plan.global_place(places_ref, tile, s)] for s in range(len(plan.sides))]
        else:
            blocks = [block_ref[tile * len(plan.sides) + s] for s in range(len(plan.sides))]
        placed = side_by_side(plan, blocks) + tile_shift(plan, tile)
        rows_ref[tile] = placed
        rows = [placed[k : k + 1] for k in range(4)]
        hot.append((rows[3].astype(jnp.int32) == species).astype(F32).astype(BF16))
        parts = separations(plan, rows, cols)
        dist_sq, inverse = distance(plan, parts, tile)
        sine, cosine = waves(dist_sq, inverse)
        fade = jnp.maximum(1.0 - dist_sq * (1.0 / CUT_SQUARE), 0.0)
        radial = fade * fade * inverse
        units = [(part * (inverse * ROOT_THREE)).astype(BF16) for part in parts]
        before, now = None, sine * radial
        lanes = slice(tile * plan.width, (tile + 1) * plan.width)
        for n in range(nbasis):
            if n == 1:
                before, now = now, 2.0 * cosine * now
            elif n > 1:
                before, now = now, 2.0 * cosine * now - before
            packed = now.astype(BF16)
            basis_ref[n, :, lanes] = packed
            pair_ref[n, :slots, lanes] = packed
            for k in range(3):
                pair_ref[n, (k + 1) * slots : (k + 2) * slots, lanes] = units[k] * packed
    hot = jnp.concatenate(hot, axis=1)
    gathered = dot(pair_ref[...].reshape(nbasis * 4 * slots, plan.far), hot, NT)
    gathered = gathered.reshape(nbasis, 4 * slots, nbasis * nspec)
    group = lax.broadcasted_iota(jnp.int32, gathered.shape[1:], 1) // nspec
    counted = jnp.zeros(gathered.shape[1:], F32)
    for n in range(nbasis):
        counted = jnp.where(group == n, gathered[n], counted)
    scalar = MSG_SCALE * split_dot(counted[:slots], table_ref[0])
    vector = MSG_SCALE * split_dot(counted[slots:], table_ref[1])
    vector_ref[...] = vector
    squares = vector * vector
    norm = squares[:slots] + squares[slots : 2 * slots] + squares[2 * slots :]
    invariants = jnp.concatenate([scalar.astype(BF16), norm.astype(BF16)], axis=1)
    mixing = dot(invariants, mix_ref[...], NT)
    mixing_ref[...] = mixing
    layer = (embed_ref[...] + mixing * sigmoid(mixing)).astype(BF16)
    layer_ref[...] = layer


def sigmoid(value):
    return 1.0 / (1.0 + jnp.exp(-value))


def scatter(plan, places_ref, far_refs, put):
    for side in range(len(plan.sides)):
        for pair, (second, first) in enumerate(plan.brought):
            block = far_refs[side * plan.wide + second][first]
            put(plan.brought_place(places_ref, side, pair), block)


def side_by_side(plan, blocks):
    if len(blocks) == 2:
        lane = lax.broadcasted_iota(jnp.int32, blocks[0].shape, 1)
        return jnp.where(lane < plan.slots, blocks[0], blocks[1])
    return jnp.concatenate([block[:, : plan.slots] for block in blocks], axis=1)


def tile_shift(plan, tile):
    row = lax.broadcasted_iota(jnp.int32, (4, plan.width), 0)
    side = lax.broadcasted_iota(jnp.int32, (4, plan.width), 1) // plan.slots
    shift = jnp.zeros((4, plan.width), F32)
    for s in range(len(plan.sides)):
        for k, steps in enumerate(plan.offset(tile, s)):
            if steps:
                shift = jnp.where((row == k) & (side == s), CELL_SIDE * steps, shift)
    return shift


def gather_far(plan, places_ref, far_refs, all_ref):
    def put(place, block):
        start = pl.multiple_of(place * plan.slots, plan.slots)
        all_ref[pl.ds(start, plan.slots)] = block

    scatter(plan, places_ref, far_refs, put)


def second_kernel(plan, nrefs, places_ref, *refs):
    far_refs, refs = refs[:nrefs], refs[nrefs:]
    (layer_ref, basis_ref, cols_ref, radial_ref, mix_ref), refs = refs[:5], refs[5:]
    (hidden_ref, out_ref, one_ref), refs = refs[:3], refs[3:]
    adjoint_ref, features_ref, before_ref, own_ref, all_ref = refs
    slots, nbasis = plan.slots, plan.nbasis
    gather_far(plan, places_ref, far_refs, all_ref)
    summed = dot(basis_ref[...].reshape(nbasis * slots, plan.far), all_ref[...])
    message = jnp.zeros((slots, summed.shape[1]), F32)
    for n in range(nbasis):
        message = message + summed[n * slots : (n + 1) * slots] * radial_ref[n : n + 1]
    rounded = (MSG_SCALE * message).astype(BF16)
    mixing = dot(rounded, mix_ref[...], NT)
    gate = sigmoid(mixing)
    layer = layer_ref[...].astype(F32)
    features = (layer + mixing * gate).astype(BF16)
    features_ref[...] = features
    before = dot(features, hidden_ref[...], NT)
    open_hidden = sigmoid(before)
    live = cols_ref[:, 3:4]
    before_ref[...] = before
    slope = out_ref[...] * (open_hidden * (1.0 + before * (1.0 - open_hidden))) * live
    from_hidden = dot(slope.astype(BF16), hidden_ref[...])
    own_ref[...] = from_hidden + one_ref[...] * live
    back = from_hidden * (gate * (1.0 + mixing * (1.0 - gate)))
    adjoint_ref[...] = dot(back.astype(BF16), mix_ref[...]).astype(BF16)


def slope_kernel(plan, rows_ref, cols_ref, layer_ref, again_ref, apart_ref, slope_ref, radial_ref, turned_ref):
    again_ref[...] = layer_ref[...]
    cols = [cols_ref[:, axis : axis + 1] for axis in range(3)]
    for tile in range(len(plan.tiles)):
        lanes = slice(tile * plan.width, (tile + 1) * plan.width)
        parts = separations(plan, [rows_ref[tile, k : k + 1] for k in range(3)], cols)
        for k in range(3):
            apart_ref[k, :, lanes] = parts[k]
        dist_sq, inverse = distance(plan, parts, tile)
        sine, cosine = waves(dist_sq, inverse)
        fade = jnp.maximum(1.0 - dist_sq * (1.0 / CUT_SQUARE), 0.0)
        radial = fade * fade * inverse
        on_sine = -inverse * ((4.0 / CUT_SQUARE) * fade + radial * inverse)
        on_cosine = (math.pi / CELL_SIDE) * (inverse * radial)
        scale = ROOT_THREE * inverse
        scaled = scale * radial
        square = inverse * inverse
        double = 2.0 * cosine
        before_s, now_s, before_c, now_c = None, sine, None, cosine
        for n in range(plan.nbasis):
            if n == 1:
                before_s, now_s = now_s, double * now_s
                before_c, now_c = now_c, double * now_c - 1.0
            elif n > 1:
                before_s, now_s = now_s, double * now_s - before_s
                before_c, now_c = now_c, double * now_c - before_c
            slope = on_sine * now_s + (n + 1.0) * on_cosine * now_c
            factor = scaled * now_s
            slope_ref[n, :, lanes] = slope
            radial_ref[n, :, lanes] = factor
            turned_ref[n, :, lanes] = scale * slope - square * factor


def energy_kernel(plan, nrefs, places_ref, *refs):
    far_refs, refs = refs[:nrefs], refs[nrefs:]
    (adjoint_ref, slope_ref, radial_ref, cols_ref, layer_ref), refs = refs[:5], refs[5:]
    (before_ref, out_ref, one_ref, kept_ref), refs = refs[:4], refs[4:]
    again_ref, pair_ref, energy_ref, features_ref, all_ref = refs
    slots, nbasis = plan.slots, plan.nbasis
    again_ref[...] = adjoint_ref[...]
    features_ref[...] = kept_ref[...]
    before = before_ref[...]
    live = jnp.where(lax.broadcasted_iota(jnp.int32, (slots, 8), 1) == 0, cols_ref[:, 3:4], 0.0)
    live_row = dot(jnp.ones((1, 8), BF16), live.astype(BF16), NT)
    energy = dot_exact(one_ref[...], layer_ref[...].astype(F32), NT)
    energy = energy + dot_exact(out_ref[...], before * sigmoid(before), NT)
    energy_ref[...] = energy * live_row
    gather_far(plan, places_ref, far_refs, all_ref)
    adjoint = adjoint_ref[...].astype(F32) * MSG_SCALE
    weighted = jnp.concatenate(
        [(adjoint * radial_ref[n : n + 1]).astype(BF16) for n in range(nbasis)], axis=0
    )
    for tile in range(len(plan.tiles)):
        lanes = slice(tile * plan.width, (tile + 1) * plan.width)
        pulled = dot(weighted, all_ref[lanes], NT)
        total = slope_ref[0, :, lanes] * pulled[:slots]
        for n in range(1, nbasis):
            total = total + slope_ref[n, :, lanes] * pulled[n * slots : (n + 1) * slots]
        pair_ref[:, lanes] = total


def force_kernel(plan, nrefs, places_ref, *refs):
    far_refs, refs = refs[:nrefs], refs[nrefs:]
    (own_ref, basis_ref, pair_ref, rows_ref), refs = refs[:4], refs[4:]
    (apart_ref, slope_ref, factor_ref, turned_ref), refs = refs[:4], refs[4:]
    (radial_ref, mixing_ref, mix_ref, vector_ref, table_ref), refs = refs[:5], refs[5:]
    out_ref, all_ref = refs
    slots, nbasis, nspec, width = plan.slots, plan.nbasis, plan.nspec, plan.width
    gather_far(plan, places_ref, far_refs, all_ref)
    summed = dot(basis_ref[...].reshape(nbasis * slots, plan.far), all_ref[...])
    adjoint = jnp.zeros((slots, summed.shape[1]), F32)
    for n in range(nbasis):
        adjoint = adjoint + summed[n * slots : (n + 1) * slots] * radial_ref[n : n + 1]
    adjoint = own_ref[...] + MSG_SCALE * adjoint
    mixing = mixing_ref[...]
    gate = sigmoid(mixing)
    back = (adjoint * (gate * (1.0 + mixing * (1.0 - gate)))).astype(BF16)
    invariants = dot(back, mix_ref[...])
    channels = invariants.shape[1] // 2
    on_scalar = (MSG_SCALE * invariants[:, :channels]).astype(BF16)
    doubled = (2.0 * MSG_SCALE) * invariants[:, channels:]
    on_vector = (vector_ref[...] * jnp.concatenate([doubled] * 3, axis=0)).astype(BF16)
    weights = jnp.concatenate(
        [dot(on_scalar, table_ref[0], NT), dot(on_vector, table_ref[1], NT)], axis=0
    ).astype(BF16)
    group = lax.broadcasted_iota(jnp.int32, weights.shape, 1) // nspec
    weights = weights.astype(F32)
    weights = jnp.concatenate(
        [jnp.where(group == n, weights, 0.0).astype(BF16) for n in range(nbasis)], axis=0
    )
    species = lax.broadcasted_iota(jnp.int32, (nbasis * nspec, width), 0) % nspec
    own = [jnp.zeros((slots, width), F32) for _ in range(3)]
    pulls = []
    for tile in range(len(plan.tiles)):
        lanes = slice(tile * width, (tile + 1) * width)
        hot = (rows_ref[tile, 3:4].astype(jnp.int32) == species).astype(F32).astype(BF16)
        spread = dot(weights, hot)
        total = pair_ref[:, lanes]
        sides, turns = [None] * 3, [None] * 3
        for n in range(nbasis):
            start = n * 4 * slots
            total = total + slope_ref[n, :, lanes] * spread[start : start + slots]
            for k in range(3):
                piece = spread[start + (k + 1) * slots : start + (k + 2) * slots]
                side = factor_ref[n, :, lanes] * piece
                turn = turned_ref[n, :, lanes] * piece
                sides[k] = side if n == 0 else sides[k] + side
                turns[k] = turn if n == 0 else turns[k] + turn
        for k in range(3):
            total = total + apart_ref[k, :, lanes] * turns[k]
        pulls.append([])
        for k in range(3):
            pull = apart_ref[k, :, lanes] * total + sides[k]
            own[k] = own[k] + pull
            pulls[-1].append(jnp.sum(pull, axis=0, keepdims=True))
    own = jnp.concatenate(own, axis=0)
    high = own.astype(BF16)
    low = (own - high.astype(F32)).astype(BF16)
    ones = jnp.ones((8, width), BF16)
    mine = (dot(ones, high, NT) + dot(ones, low, NT))[:1]
    mine = jnp.concatenate([mine[:, k * slots : (k + 1) * slots] for k in range(3)], axis=0)
    if plan.small:
        out_ref[...] = jnp.zeros_like(out_ref)
    side_of = lax.broadcasted_iota(jnp.int32, (3, width), 1) // slots
    for tile in range(len(plan.tiles)):
        pulled = jnp.concatenate(pulls[tile], axis=0)
        if tile == 0:
            others = [jnp.zeros_like(mine)] * (len(plan.sides) - 1)
            pulled = pulled - jnp.concatenate([mine] + others, axis=1)
        if not plan.small:
            out_ref[plan.staged_place(places_ref, tile)] = pulled
            continue
        for side in range(len(plan.sides)):
            place = plan.global_place(places_ref, tile, side)
            out_ref[place, :3] = jnp.where(side_of == side, pulled, 0.0)


def brought_in(pairs, sems):
    copies = [pltpu.make_async_copy(*pair, sems.at[m]) for m, pair in enumerate(pairs)]
    for copy in copies:
        copy.start()
    for copy in copies:
        copy.wait()


def live_rows(plan, counts_ref, place_ref, kind_ref):
    live = lax.broadcasted_iota(jnp.int32, (1, plan.slots), 1) < counts_ref[0]
    rows = [
        jnp.where(live, place_ref[0], FAR),
        place_ref[1],
        place_ref[2],
        jnp.where(live, kind_ref[...], -1).astype(F32),
    ]
    rows = jnp.concatenate(rows, axis=0)
    return jnp.concatenate([rows, rows], axis=1)


def prepare_kernel(plan, counts_ref, place_hbm, kind_hbm, sent_ref, place_ref, kind_ref, sems):
    brought_in([(place_hbm, place_ref), (kind_hbm, kind_ref)], sems)
    rows = live_rows(plan, counts_ref, place_ref, kind_ref)
    for copy in range(sent_ref.shape[0]):
        sent_ref[copy] = rows


def sum_kernel(plan, parts_ref, force_ref):
    total = parts_ref[0]
    for part in range(1, parts_ref.shape[0]):
        total = total + parts_ref[part]
    total = total[:, : plan.slots] + total[:, plan.slots :]
    for k in range(3):
        force_ref[k] = -total[k : k + 1]


def own_kernel(plan, counts_ref, *refs):
    fetched, weights, (cols_ref, table_ref, own_ref) = refs[:4], refs[4:10], refs[10:13]
    kept, local_refs, sems = refs[13:19], refs[19:-1], refs[-1]
    slots, nspec = plan.slots, plan.nspec
    brought_in([*zip(fetched, local_refs), *zip(weights, kept)], sems)
    place_ref, kind_ref, embed_ref, radial_ref = local_refs
    rows = live_rows(plan, counts_ref, place_ref, kind_ref)
    cols = jnp.concatenate([rows, rows], axis=0).T[:slots]
    kind = cols[:, 3:4]
    lane = lax.broadcasted_iota(jnp.int32, cols.shape, 1)
    live = kind >= 0.0
    cols = jnp.where((lane == 0) & ~live, -FAR, cols)
    cols_ref[...] = jnp.where(lane == 3, live.astype(F32), cols)
    species = lax.broadcasted_iota(jnp.int32, (slots, nspec), 1)
    hot = (kind.astype(jnp.int32) == species).astype(F32).astype(BF16)
    embed = embed_ref[...]
    own_ref[...] = dot(hot, embed)
    embed = embed.astype(F32)
    for g in range(2):
        for n in range(plan.nbasis):
            row = radial_ref[g, n : n + 1]
            table_ref[g, n * nspec : (n + 1) * nspec] = (row * embed).astype(BF16)


VMEM_SPEC = pl.BlockSpec(memory_space=pltpu.VMEM)
SMEM_SPEC = pl.BlockSpec(memory_space=pltpu.SMEM)
HBM_SPEC = pl.BlockSpec(memory_space=pltpu.HBM)


def simple_call(kernel, plan, operands, outs, scalars=0, scratch=(), flops=2**20, near=False, fetched=0):
    single = not isinstance(outs, list)
    kind = pltpu.VMEM if near else jax.ShapeDtypeStruct
    shapes = [kind(*out) for out in ([outs] if single else outs)]

    def body(*refs):
        kernel(plan, *refs)

    got = pl.pallas_call(
        body,
        out_shape=shapes,
        in_specs=[SMEM_SPEC] * scalars
        + [VMEM_SPEC] * (len(operands) - scalars - fetched)
        + [HBM_SPEC] * fetched,
        out_specs=[VMEM_SPEC] * len(shapes),
        scratch_shapes=[pltpu.VMEM(*buffer) for buffer in scratch]
        + [pltpu.SemaphoreType.DMA((fetched,))] * (fetched > 0),
        compiler_params=pltpu.CompilerParams(vmem_limit_bytes=FETCH_LIMIT if fetched else VMEM_LIMIT),
        cost_estimate=pl.CostEstimate(flops=flops, bytes_accessed=2**20, transcendentals=0),
    )(*operands)
    return got[0] if single else got


def call(kernel, plan, far, places, operands, outs, scratch, flops):
    def body(plan, *refs):
        kernel(plan, len(far), *refs)

    return simple_call(body, plan, [places, *far, *operands], outs, 1, scratch, flops)


def swaps(count):
    if count == 2:
        return [[1, 0]]
    if paired(count):
        near = [i ^ 1 for i in range(count)]
        far = [(i - 1 + 2 * (i % 2)) % count for i in range(count)]
        return [near, far]
    return [[(i + o) % count for i in range(count)] for o in offsets_of(count)[1:]]


def brought(plan, block, second):
    sizes, sources = plan.sizes, {axis: swaps(plan.sizes[axis]) for axis in AXES}
    got = []
    for m in range(len(sources["gx" if second else "gz"])):
        pairs = []
        for x, y, z in itertools.product(*(range(sizes[axis]) for axis in AXES)):
            along_x = second != (plan.mixed and y % 2 == 1)
            source = (sources["gx"][m][x], y, z) if along_x else (x, y, sources["gz"][m][z])
            pairs.append((flat(sizes, *source), flat(sizes, x, y, z)))
        got.append(lax.ppermute(block, AXES, pairs))
    return got


def flat(sizes, x, y, z):
    return (x * sizes["gy"] + y) * sizes["gz"] + z


def along(block, axis):
    return [
        lax.ppermute(block, axis, [(source, i) for i, source in enumerate(sources)])
        for sources in swaps(lax.axis_size(axis))
    ]


def neighbours(plan, block, again=None):
    column = jnp.stack([block if again is None else again] + brought(plan, block, False))
    columns = [column] + brought(plan, column, True)
    swapped = [[column] + along(column, "gy") for column in columns]
    return [column[side] for side in range(len(plan.sides)) for column in swapped]


def everywhere(copies):
    return lax.all_to_all(copies, AXES, 0, 0, tiled=True)


def folded(pieces, axis):
    total = pieces[0]
    for piece, sources in zip(pieces[1:], swaps(lax.axis_size(axis))):
        total = total + lax.ppermute(piece, axis, list(enumerate(sources)))
    return total


def fold(plan, pulls):
    for axis in ("gx", "gz"):
        parts = len(offsets_of(plan.sizes[axis]))
        pulls = pulls.reshape((parts, -1) + pulls.shape[1:])
        pulls = folded([pulls[m] for m in range(parts)], axis)
    pulls = pulls[0]
    sides = [pulls[:, m * plan.slots : (m + 1) * plan.slots] for m in range(len(plan.sides))]
    return folded(sides, "gy")


def local_program(mesh):
    def local(
        positions,
        species,
        counts,
        embed,
        radial_one,
        mix_one,
        read_one,
        radial_two,
        mix_two,
        read_hidden,
        read_out,
    ):
        slots, channels = positions.shape[-1], embed.shape[1]
        nbasis, nspec = radial_two.shape[0], embed.shape[0]
        plan = Plan(mesh, slots, nbasis, nspec)
        count = counts.reshape(1)
        given = [positions[0, 0, 0].reshape(3, 1, slots), species.reshape(1, slots)]
        sent = simple_call(
            prepare_kernel,
            plan,
            [count, *given],
            ((plan.ndev if plan.small else 1, 4, 2 * slots), F32),
            1,
            [(array.shape, array.dtype) for array in given],
            near=True,
            fetched=len(given),
        )
        places = plan.places()
        far_sent = [everywhere(sent)] if plan.small else neighbours(plan, sent[0])
        weights = [radial_two, read_out[None], read_one[None], mix_one, mix_two, read_hidden]
        given = given + [embed, radial_one]
        cols, table, own_embed, radial_two, out_row, one_row, mix_one, mix_two, read_hidden = simple_call(
            own_kernel,
            plan,
            [count, *given, *weights],
            [
                ((slots, 8), F32),
                ((2, nbasis * nspec, channels), BF16),
                ((slots, channels), F32),
            ]
            + [(weight.shape, weight.dtype) for weight in weights],
            1,
            [(array.shape, array.dtype) for array in given],
            near=True,
            fetched=len(given) + len(weights),
        )
        pair_flops = 100 * slots * plan.far
        rows, basis, layer, vector, mixing = call(
            first_kernel,
            plan,
            far_sent,
            places,
            [cols, table, own_embed, mix_one],
            [
                ((len(plan.tiles), 4, plan.width), F32),
                ((nbasis, slots, plan.far), BF16),
                ((slots, channels), BF16),
                ((3 * slots, channels), F32),
                ((slots, channels), F32),
            ],
            [
                ((nbasis, 4 * slots, plan.far), BF16),
                ((len(plan.tiles) * len(plan.sides), 4, 2 * slots), F32),
            ],
            pair_flops,
        )
        again, apart, slope, factor, turned = simple_call(
            slope_kernel,
            plan,
            [rows, cols, layer],
            [(layer.shape, BF16)]
            + [((count, slots, plan.far), F32) for count in (3, nbasis, nbasis, nbasis)],
            flops=pair_flops,
        )
        far_layer = neighbours(plan, layer, again)
        far_scratch = ((plan.far, channels), BF16)
        adjoint, kept, before, own_adjoint = call(
            second_kernel,
            plan,
            far_layer,
            places,
            [layer, basis, cols, radial_two, mix_two, read_hidden, out_row, one_row],
            [
                ((slots, channels), BF16),
                ((slots, channels), BF16),
                ((slots, read_hidden.shape[0]), F32),
                ((slots, channels), F32),
            ],
            [far_scratch],
            pair_flops,
        )
        again, pair, energy, features = call(
            energy_kernel,
            plan,
            far_layer,
            places,
            [adjoint, slope, radial_two, cols, layer, before, out_row, one_row, kept],
            [
                ((slots, channels), BF16),
                ((slots, plan.far), F32),
                ((1, slots), F32),
                ((slots, channels), BF16),
            ],
            [far_scratch],
            pair_flops,
        )
        far_adjoint = neighbours(plan, adjoint, again)
        pulls = call(
            force_kernel,
            plan,
            far_adjoint,
            places,
            [own_adjoint, basis, pair, rows, apart, slope, factor, turned]
            + [radial_two, mixing, mix_one, vector, table],
            [((plan.ndev, 4, plan.width) if plan.small else (len(plan.tiles), 3, plan.width), F32)],
            [far_scratch],
            pair_flops,
        )
        if plan.small:
            forces = simple_call(sum_kernel, plan, [everywhere(pulls[0])], ((3, 1, slots), F32))
        else:
            forces = -fold(plan, pulls[0])
        return (
            forces.reshape(1, 1, 1, 3, slots),
            energy[None, None],
            features.T[None, None, None],
        )

    return local


def solution(mesh):
    split = [P(*AXES, None, None), P(*AXES, None), P(*AXES)]
    out_specs = (P(*AXES, None, None), P(*AXES, None), P(*AXES, None, None))
    return jax.shard_map(
        local_program(mesh),
        mesh=mesh,
        in_specs=tuple(split + [P()] * 8),
        out_specs=out_specs,
        check_vma=False,
    )
```

```python
import itertools
import math

import jax
import jax.numpy as jnp
from jax import lax
from jax.experimental import pallas as pl
from jax.experimental.pallas import tpu as pltpu
from jax.sharding import PartitionSpec as P

CELL_SIDE = 5.0
CUT_SQUARE = 25.0
SOFTEN = 0.25
MSG_SCALE = 0.05
ROOT_THREE = math.sqrt(3.0)
FAR = 1.0e4
AXES = ("gx", "gy", "gz")
F32 = jnp.float32
BF16 = jnp.bfloat16
COS_TERMS = (
    0.9999999997799041,
    -4.934802137078749,
    4.058709159554242,
    -1.335212003029471,
    0.23493731372678894,
    -0.024396324214549327,
)
SIN_TERMS = (
    3.14159265353629,
    -5.167712764624453,
    2.550163318944743,
    -0.5992521977996564,
    0.08205040170151112,
    -0.007028386239784362,
)
VMEM_LIMIT = 24 * 1024 * 1024
GROUP = 4
FETCH_LIMIT = 60 * 1024 * 1024
NT = (((1,), (1,)), ((), ()))
NN = (((1,), (0,)), ((), ()))


def dot(a, b, dims=NN):
    return lax.dot_general(a, b, dims, preferred_element_type=F32)


def dot_exact(a, b, dims=NN):
    return lax.dot_general(
        a, b, dims, precision=lax.Precision.HIGHEST, preferred_element_type=F32
    )


def split_dot(a, b):
    high = a.astype(BF16)
    low = (a - high.astype(F32)).astype(BF16)
    return dot(high, b) + dot(low, b)


def offsets_of(count):
    return (0, 1) if count == 2 else (0, 1, -1)


def paired(count):
    return count > 2 and count % 2 == 0


def matched(which, parity):
    return jnp.int32(0) if which == 0 else 1 + (parity if which == 1 else 1 - parity)


def poly(terms, arg):
    total = arg * terms[-1] + terms[-2]
    for term in terms[-3::-1]:
        total = total * arg + term
    return total


class Plan:
    def __init__(self, mesh, slots, nbasis, nspec):
        self.sizes = {axis: mesh.shape[axis] for axis in AXES}
        self.ndev = math.prod(self.sizes.values())
        self.tiles = list(
            itertools.product(offsets_of(self.sizes["gx"]), offsets_of(self.sizes["gz"]))
        )
        self.sides = offsets_of(self.sizes["gy"])
        self.slots = slots
        self.width = len(self.sides) * slots
        self.far = len(self.tiles) * self.width
        self.nbasis = nbasis
        self.nspec = nspec
        self.depth = len(offsets_of(self.sizes["gz"]))
        self.wide = len(offsets_of(self.sizes["gx"]))
        self.brought = list(itertools.product(range(self.wide), range(self.depth)))
        self.mixed = self.depth == self.wide and self.sizes["gy"] % 2 == 0
        self.small = self.ndev <= 64 and len(self.sides) == 2
        self.wrapped = [self.sizes[axis] == 2 for axis in AXES]

    def places(self):
        index = {axis: lax.axis_index(axis) for axis in AXES}

        def parity(axis):
            return lax.rem(index[axis], 2) if paired(self.sizes[axis]) else jnp.int32(0)

        def moved(axis, step):
            return lax.rem(index[axis] + (step + self.sizes[axis]), self.sizes[axis])

        turns = parity("gx"), parity("gz")
        core = lax.rem(index["gy"], 2) if self.mixed else jnp.int32(0)
        found = []
        for side in range(len(self.sides)):
            x_first = core if side == 0 or not self.mixed else 1 - core
            for second, first in self.brought:
                plain = matched(second, turns[0]) * self.depth + matched(first, turns[1])
                crossed = matched(first, turns[0]) * self.depth + matched(second, turns[1])
                tile = jnp.where(x_first == 1, crossed, plain) if self.mixed else plain
                found.append(tile * len(self.sides) + side)
        found += turns
        for ox, oz in self.tiles:
            for oy in self.sides:
                place = (moved("gx", ox) * self.sizes["gy"] + moved("gy", oy)) * self.sizes["gz"]
                found.append(place + moved("gz", oz))
        return [jnp.asarray(place, jnp.int32) for place in found]

    def brought_place(self, places, side, pair):
        return places[side * len(self.brought) + pair]

    def global_place(self, places, tile, side):
        start = len(self.sides) * len(self.brought) + 2
        return places[start + tile * len(self.sides) + side]

    def staged_place(self, places, tile):
        start = len(self.sides) * len(self.brought)
        x, z = divmod(tile, self.depth)
        return matched(x, places[start]) * self.depth + matched(z, places[start + 1])

    def offset(self, tile, side):
        ox, oz = self.tiles[tile]
        return (ox, self.sides[side], oz)


def separations(plan, rows, cols):
    parts = []
    for axis in range(3):
        diff = rows[axis] - cols[axis]
        if plan.wrapped[axis]:
            diff = jnp.where(diff > CELL_SIDE, diff - 2.0 * CELL_SIDE, diff)
        parts.append(diff)
    return parts


def distance(plan, parts, tile):
    dist_sq = parts[0] * parts[0] + parts[1] * parts[1] + parts[2] * parts[2] + SOFTEN
    if tile == 0:
        row = lax.broadcasted_iota(jnp.int32, dist_sq.shape, 0)
        col = lax.broadcasted_iota(jnp.int32, dist_sq.shape, 1)
        dist_sq = jnp.where(row == col, FAR, dist_sq)
    return dist_sq, lax.rsqrt(dist_sq)


def waves(dist_sq, inverse):
    arg = jnp.minimum(dist_sq * inverse * (1.0 / CELL_SIDE) - 0.5, 0.5)
    square = arg * arg
    return poly(COS_TERMS, square), -(arg * poly(SIN_TERMS, square))


def first_kernel(plan, nrefs, places, *refs):
    far_refs, fetched, refs = refs[:nrefs], refs[nrefs : nrefs + 8], refs[nrefs + 8 :]
    rows_ref, basis_ref, layer_ref, vector_ref, mixing_ref, cols_ref, table_ref, *refs = refs
    kept, (pair_ref, block_ref, embed_ref, radial_ref, sems) = refs[:6], refs[6:]
    mix_ref = kept[0]
    slots, nbasis, nspec = plan.slots, plan.nbasis, plan.nspec
    copies = begin(zip(fetched, (embed_ref, radial_ref, *kept)), sems)

    def put(place, block):
        block_ref[place] = block

    if not plan.small:
        scatter(plan, places, far_refs, put)

    def block_of(tile, side):
        if plan.small:
            return far_refs[0][plan.global_place(places, tile, side)]
        return block_ref[tile * len(plan.sides) + side]

    rows = block_of(0, 0)
    held = jnp.concatenate([rows, rows], axis=0).T[:slots]
    kind = held[:, 3:4]
    lane = lax.broadcasted_iota(jnp.int32, held.shape, 1)
    live = kind >= 0.0
    held = jnp.where((lane == 0) & ~live, -FAR, held)
    held = jnp.where(lane == 3, live.astype(F32), held)
    cols_ref[...] = held
    cols = [held[:, axis : axis + 1] for axis in range(3)]
    species = lax.broadcasted_iota(jnp.int32, (nbasis * nspec, plan.width), 0) % nspec
    hot, gathered = [], None
    for tile in range(len(plan.tiles)):
        blocks = [block_of(tile, side) for side in range(len(plan.sides))]
        placed = side_by_side(plan, blocks) + tile_shift(plan, tile)
        rows_ref[tile] = placed
        rows = [placed[k : k + 1] for k in range(4)]
        hot.append((rows[3].astype(jnp.int32) == species).astype(F32).astype(BF16))
        parts = separations(plan, rows, cols)
        dist_sq, inverse = distance(plan, parts, tile)
        sine, cosine = waves(dist_sq, inverse)
        fade = jnp.maximum(1.0 - dist_sq * (1.0 / CUT_SQUARE), 0.0)
        radial = fade * fade * inverse
        units = [(part * (inverse * ROOT_THREE)).astype(BF16) for part in parts]
        before, now = None, sine * radial
        lanes = slice(tile * plan.width, (tile + 1) * plan.width)
        for n in range(nbasis):
            if n == 1:
                before, now = now, 2.0 * cosine * now
            elif n > 1:
                before, now = now, 2.0 * cosine * now - before
            packed = now.astype(BF16)
            basis_ref[n, :, lanes] = packed
            pair_ref[n, :slots, lanes] = packed
            for k in range(3):
                pair_ref[n, (k + 1) * slots : (k + 2) * slots, lanes] = units[k] * packed
        if tile % GROUP == GROUP - 1 or tile == len(plan.tiles) - 1:
            lanes = slice((tile // GROUP) * GROUP * plan.width, (tile + 1) * plan.width)
            taken = pair_ref[:, :, lanes].reshape(nbasis * 4 * slots, -1)
            part = dot(taken, jnp.concatenate(hot, axis=1), NT)
            gathered = part if gathered is None else gathered + part
            hot = []
    for copy in copies:
        copy.wait()
    embed = embed_ref[...]
    for g in range(2):
        for n in range(nbasis):
            row = radial_ref[g, n : n + 1]
            weighted = row * embed.astype(F32)
            table_ref[g, n * nspec : (n + 1) * nspec] = weighted.astype(BF16)
    own_species = lax.broadcasted_iota(jnp.int32, (slots, nspec), 1)
    own_hot = (kind.astype(jnp.int32) == own_species).astype(F32).astype(BF16)
    gathered = gathered.reshape(nbasis, 4 * slots, nbasis * nspec)
    group = lax.broadcasted_iota(jnp.int32, gathered.shape[1:], 1) // nspec
    counted = jnp.zeros(gathered.shape[1:], F32)
    for n in range(nbasis):
        counted = jnp.where(group == n, gathered[n], counted)
    scalar = MSG_SCALE * split_dot(counted[:slots], table_ref[0])
    vector = MSG_SCALE * split_dot(counted[slots:], table_ref[1])
    vector_ref[...] = vector
    squares = vector * vector
    norm = squares[:slots] + squares[slots : 2 * slots] + squares[2 * slots :]
    invariants = jnp.concatenate([scalar.astype(BF16), norm.astype(BF16)], axis=1)
    mixing = dot(invariants, mix_ref[...], NT)
    mixing_ref[...] = mixing
    layer = (dot(own_hot, embed) + mixing * sigmoid(mixing)).astype(BF16)
    layer_ref[...] = layer


def sigmoid(value):
    return 1.0 / (1.0 + jnp.exp(-value))


def scatter(plan, places, far_refs, put):
    for side in range(len(plan.sides)):
        for pair, (second, first) in enumerate(plan.brought):
            block = far_refs[side * plan.wide + second][first]
            put(plan.brought_place(places, side, pair), block)


def side_by_side(plan, blocks):
    if len(blocks) == 2:
        lane = lax.broadcasted_iota(jnp.int32, blocks[0].shape, 1)
        return jnp.where(lane < plan.slots, blocks[0], blocks[1])
    return jnp.concatenate([block[:, : plan.slots] for block in blocks], axis=1)


def tile_shift(plan, tile):
    row = lax.broadcasted_iota(jnp.int32, (4, plan.width), 0)
    side = lax.broadcasted_iota(jnp.int32, (4, plan.width), 1) // plan.slots
    shift = jnp.zeros((4, plan.width), F32)
    for s in range(len(plan.sides)):
        for k, steps in enumerate(plan.offset(tile, s)):
            if steps:
                shift = jnp.where((row == k) & (side == s), CELL_SIDE * steps, shift)
    return shift


def gather_far(plan, places, far_refs, all_ref):
    def put(place, block):
        start = pl.multiple_of(place * plan.slots, plan.slots)
        all_ref[pl.ds(start, plan.slots)] = block

    scatter(plan, places, far_refs, put)


def second_kernel(plan, nrefs, places, *refs):
    far_refs, refs = refs[:nrefs], refs[nrefs:]
    (layer_ref, basis_ref, cols_ref, radial_ref, mix_ref), refs = refs[:5], refs[5:]
    (hidden_ref, out_ref, one_ref), refs = refs[:3], refs[3:]
    adjoint_ref, features_ref, before_ref, own_ref, all_ref = refs
    slots, nbasis = plan.slots, plan.nbasis
    gather_far(plan, places, far_refs, all_ref)
    summed = dot(basis_ref[...].reshape(nbasis * slots, plan.far), all_ref[...])
    message = jnp.zeros((slots, summed.shape[1]), F32)
    for n in range(nbasis):
        message = message + summed[n * slots : (n + 1) * slots] * radial_ref[n : n + 1]
    rounded = (MSG_SCALE * message).astype(BF16)
    mixing = dot(rounded, mix_ref[...], NT)
    gate = sigmoid(mixing)
    layer = layer_ref[...].astype(F32)
    features = (layer + mixing * gate).astype(BF16)
    features_ref[...] = features
    before = dot(features, hidden_ref[...], NT)
    open_hidden = sigmoid(before)
    live = cols_ref[:, 3:4]
    before_ref[...] = before
    slope = out_ref[...] * (open_hidden * (1.0 + before * (1.0 - open_hidden))) * live
    from_hidden = dot(slope.astype(BF16), hidden_ref[...])
    own_ref[...] = from_hidden + one_ref[...] * live
    back = from_hidden * (gate * (1.0 + mixing * (1.0 - gate)))
    adjoint_ref[...] = dot(back.astype(BF16), mix_ref[...]).astype(BF16)


def slope_kernel(plan, rows_ref, cols_ref, layer_ref, *refs):
    again_ref, apart_ref, slope_ref, radial_ref, turned_ref = refs
    again_ref[...] = layer_ref[...]
    cols = [cols_ref[:, axis : axis + 1] for axis in range(3)]
    for tile in range(len(plan.tiles)):
        lanes = slice(tile * plan.width, (tile + 1) * plan.width)
        parts = separations(plan, [rows_ref[tile, k : k + 1] for k in range(3)], cols)
        for k in range(3):
            apart_ref[k, :, lanes] = parts[k]
        dist_sq, inverse = distance(plan, parts, tile)
        sine, cosine = waves(dist_sq, inverse)
        fade = jnp.maximum(1.0 - dist_sq * (1.0 / CUT_SQUARE), 0.0)
        radial = fade * fade * inverse
        on_sine = -inverse * ((4.0 / CUT_SQUARE) * fade + radial * inverse)
        on_cosine = (math.pi / CELL_SIDE) * (inverse * radial)
        scale = ROOT_THREE * inverse
        scaled = scale * radial
        square = inverse * inverse
        double = 2.0 * cosine
        before_s, now_s, before_c, now_c = None, sine, None, cosine
        for n in range(plan.nbasis):
            if n == 1:
                before_s, now_s = now_s, double * now_s
                before_c, now_c = now_c, double * now_c - 1.0
            elif n > 1:
                before_s, now_s = now_s, double * now_s - before_s
                before_c, now_c = now_c, double * now_c - before_c
            slope = on_sine * now_s + (n + 1.0) * on_cosine * now_c
            factor = scaled * now_s
            slope_ref[n, :, lanes] = slope
            radial_ref[n, :, lanes] = factor
            turned_ref[n, :, lanes] = scale * slope - square * factor


def energy_kernel(plan, nrefs, places, *refs):
    far_refs, refs = refs[:nrefs], refs[nrefs:]
    (adjoint_ref, slope_ref, radial_ref, cols_ref, layer_ref), refs = refs[:5], refs[5:]
    (before_ref, out_ref, one_ref, kept_ref), refs = refs[:4], refs[4:]
    again_ref, pair_ref, energy_ref, features_ref, all_ref = refs
    slots, nbasis = plan.slots, plan.nbasis
    again_ref[...] = adjoint_ref[...]
    features_ref[...] = kept_ref[...]
    before = before_ref[...]
    live = jnp.where(lax.broadcasted_iota(jnp.int32, (slots, 8), 1) == 0, cols_ref[:, 3:4], 0.0)
    live_row = dot(jnp.ones((1, 8), BF16), live.astype(BF16), NT)
    energy = dot_exact(one_ref[...], layer_ref[...].astype(F32), NT)
    energy = energy + dot_exact(out_ref[...], before * sigmoid(before), NT)
    energy_ref[...] = energy * live_row
    gather_far(plan, places, far_refs, all_ref)
    adjoint = adjoint_ref[...].astype(F32) * MSG_SCALE
    weighted = jnp.concatenate(
        [(adjoint * radial_ref[n : n + 1]).astype(BF16) for n in range(nbasis)], axis=0
    )
    for tile in range(len(plan.tiles)):
        lanes = slice(tile * plan.width, (tile + 1) * plan.width)
        pulled = dot(weighted, all_ref[lanes], NT)
        total = slope_ref[0, :, lanes] * pulled[:slots]
        for n in range(1, nbasis):
            total = total + slope_ref[n, :, lanes] * pulled[n * slots : (n + 1) * slots]
        pair_ref[:, lanes] = total


def force_kernel(plan, nrefs, places, *refs):
    far_refs, refs = refs[:nrefs], refs[nrefs:]
    (own_ref, basis_ref, pair_ref, rows_ref), refs = refs[:4], refs[4:]
    (apart_ref, slope_ref, factor_ref, turned_ref), refs = refs[:4], refs[4:]
    (radial_ref, mixing_ref, mix_ref, vector_ref, table_ref), refs = refs[:5], refs[5:]
    out_ref, all_ref = refs
    slots, nbasis, nspec, width = plan.slots, plan.nbasis, plan.nspec, plan.width
    gather_far(plan, places, far_refs, all_ref)
    summed = dot(basis_ref[...].reshape(nbasis * slots, plan.far), all_ref[...])
    adjoint = jnp.zeros((slots, summed.shape[1]), F32)
    for n in range(nbasis):
        adjoint = adjoint + summed[n * slots : (n + 1) * slots] * radial_ref[n : n + 1]
    adjoint = own_ref[...] + MSG_SCALE * adjoint
    mixing = mixing_ref[...]
    gate = sigmoid(mixing)
    back = (adjoint * (gate * (1.0 + mixing * (1.0 - gate)))).astype(BF16)
    invariants = dot(back, mix_ref[...])
    channels = invariants.shape[1] // 2
    on_scalar = (MSG_SCALE * invariants[:, :channels]).astype(BF16)
    doubled = (2.0 * MSG_SCALE) * invariants[:, channels:]
    on_vector = (vector_ref[...] * jnp.concatenate([doubled] * 3, axis=0)).astype(BF16)
    weights = jnp.concatenate(
        [dot(on_scalar, table_ref[0], NT), dot(on_vector, table_ref[1], NT)], axis=0
    ).astype(BF16)
    group = lax.broadcasted_iota(jnp.int32, weights.shape, 1) // nspec
    weights = weights.astype(F32)
    weights = jnp.concatenate(
        [jnp.where(group == n, weights, 0.0).astype(BF16) for n in range(nbasis)], axis=0
    )
    species = lax.broadcasted_iota(jnp.int32, (nbasis * nspec, width), 0) % nspec
    own = [jnp.zeros((slots, width), F32) for _ in range(3)]
    pulls = []
    for tile in range(len(plan.tiles)):
        lanes = slice(tile * width, (tile + 1) * width)
        hot = (rows_ref[tile, 3:4].astype(jnp.int32) == species).astype(F32).astype(BF16)
        spread = dot(weights, hot)
        total = pair_ref[:, lanes]
        sides, turns = [None] * 3, [None] * 3
        for n in range(nbasis):
            start = n * 4 * slots
            total = total + slope_ref[n, :, lanes] * spread[start : start + slots]
            for k in range(3):
                piece = spread[start + (k + 1) * slots : start + (k + 2) * slots]
                side = factor_ref[n, :, lanes] * piece
                turn = turned_ref[n, :, lanes] * piece
                sides[k] = side if n == 0 else sides[k] + side
                turns[k] = turn if n == 0 else turns[k] + turn
        for k in range(3):
            total = total + apart_ref[k, :, lanes] * turns[k]
        pulls.append([])
        for k in range(3):
            pull = apart_ref[k, :, lanes] * total + sides[k]
            own[k] = own[k] + pull
            pulls[-1].append(jnp.sum(pull, axis=0, keepdims=True))
    own = jnp.concatenate(own, axis=0)
    high = own.astype(BF16)
    low = (own - high.astype(F32)).astype(BF16)
    ones = jnp.ones((8, width), BF16)
    mine = (dot(ones, high, NT) + dot(ones, low, NT))[:1]
    mine = jnp.concatenate([mine[:, k * slots : (k + 1) * slots] for k in range(3)], axis=0)
    if plan.small:
        out_ref[...] = jnp.zeros_like(out_ref)
    side_of = lax.broadcasted_iota(jnp.int32, (3, width), 1) // slots
    for tile in range(len(plan.tiles)):
        pulled = jnp.concatenate(pulls[tile], axis=0)
        if tile == 0:
            others = [jnp.zeros_like(mine)] * (len(plan.sides) - 1)
            pulled = pulled - jnp.concatenate([mine] + others, axis=1)
        if not plan.small:
            out_ref[plan.staged_place(places, tile)] = pulled
            continue
        for side in range(len(plan.sides)):
            place = plan.global_place(places, tile, side)
            out_ref[place, :3] = jnp.where(side_of == side, pulled, 0.0)


def begin(pairs, sems):
    copies = [pltpu.make_async_copy(*pair, sems.at[m]) for m, pair in enumerate(pairs)]
    for copy in copies:
        copy.start()
    return copies


def prepare_kernel(plan, counts_ref, place_hbm, kind_hbm, sent_ref, place_ref, kind_ref, sems):
    for copy in begin([(place_hbm, place_ref), (kind_hbm, kind_ref)], sems):
        copy.wait()
    live = lax.broadcasted_iota(jnp.int32, (1, plan.slots), 1) < counts_ref[0]
    rows = [
        jnp.where(live, place_ref[0], FAR),
        place_ref[1],
        place_ref[2],
        jnp.where(live, kind_ref[...], -1).astype(F32),
    ]
    rows = jnp.concatenate(rows, axis=0)
    rows = jnp.concatenate([rows, rows], axis=1)
    for copy in range(sent_ref.shape[0]):
        sent_ref[copy] = rows


def sum_kernel(plan, parts_ref, force_ref):
    total = parts_ref[0]
    for part in range(1, parts_ref.shape[0]):
        total = total + parts_ref[part]
    total = total[:, : plan.slots] + total[:, plan.slots :]
    for k in range(3):
        force_ref[k] = -total[k : k + 1]


VMEM_SPEC = pl.BlockSpec(memory_space=pltpu.VMEM)
SMEM_SPEC = pl.BlockSpec(memory_space=pltpu.SMEM)
HBM_SPEC = pl.BlockSpec(memory_space=pltpu.HBM)


def simple_call(kernel, plan, operands, outs, scalars=0, scratch=(), flops=2**20, near=False, fetched=0):
    single = not isinstance(outs, list)
    kind = pltpu.VMEM if near else jax.ShapeDtypeStruct
    shapes = [kind(*out) for out in ([outs] if single else outs)]

    def body(*refs):
        kernel(plan, *refs)

    got = pl.pallas_call(
        body,
        out_shape=shapes,
        in_specs=[SMEM_SPEC] * scalars
        + [VMEM_SPEC] * (len(operands) - scalars - fetched)
        + [HBM_SPEC] * fetched,
        out_specs=[VMEM_SPEC] * len(shapes),
        scratch_shapes=[pltpu.VMEM(*buffer) for buffer in scratch]
        + [pltpu.SemaphoreType.DMA((fetched,))] * (fetched > 0),
        compiler_params=pltpu.CompilerParams(vmem_limit_bytes=FETCH_LIMIT if fetched else VMEM_LIMIT),
        cost_estimate=pl.CostEstimate(flops=flops, bytes_accessed=2**20, transcendentals=0),
    )(*operands)
    return got[0] if single else got


def call(kernel, plan, far, operands, outs, scratch, flops, **options):
    def body(plan, *refs):
        kernel(plan, len(far), plan.places(), *refs)

    return simple_call(body, plan, [*far, *operands], outs, 0, scratch, flops, **options)


def swaps(count):
    if count == 2:
        return [[1, 0]]
    if paired(count):
        near = [i ^ 1 for i in range(count)]
        far = [(i - 1 + 2 * (i % 2)) % count for i in range(count)]
        return [near, far]
    return [[(i + o) % count for i in range(count)] for o in offsets_of(count)[1:]]


def brought(plan, block, second):
    sizes, sources = plan.sizes, {axis: swaps(plan.sizes[axis]) for axis in AXES}
    got = []
    for m in range(len(sources["gx" if second else "gz"])):
        pairs = []
        for x, y, z in itertools.product(*(range(sizes[axis]) for axis in AXES)):
            along_x = second != (plan.mixed and y % 2 == 1)
            source = (sources["gx"][m][x], y, z) if along_x else (x, y, sources["gz"][m][z])
            pairs.append((flat(sizes, *source), flat(sizes, x, y, z)))
        got.append(lax.ppermute(block, AXES, pairs))
    return got


def flat(sizes, x, y, z):
    return (x * sizes["gy"] + y) * sizes["gz"] + z


def along(block, axis):
    return [
        lax.ppermute(block, axis, [(source, i) for i, source in enumerate(sources)])
        for sources in swaps(lax.axis_size(axis))
    ]


def neighbours(plan, block, again=None):
    column = jnp.stack([block if again is None else again] + brought(plan, block, False))
    columns = [column] + brought(plan, column, True)
    swapped = [[column] + along(column, "gy") for column in columns]
    return [column[side] for side in range(len(plan.sides)) for column in swapped]


def everywhere(copies):
    return lax.all_to_all(copies, AXES, 0, 0, tiled=True)


def folded(pieces, axis):
    total = pieces[0]
    for piece, sources in zip(pieces[1:], swaps(lax.axis_size(axis))):
        total = total + lax.ppermute(piece, axis, list(enumerate(sources)))
    return total


def fold(plan, pulls):
    for axis in ("gx", "gz"):
        parts = len(offsets_of(plan.sizes[axis]))
        pulls = pulls.reshape((parts, -1) + pulls.shape[1:])
        pulls = folded([pulls[m] for m in range(parts)], axis)
    pulls = pulls[0]
    sides = [pulls[:, m * plan.slots : (m + 1) * plan.slots] for m in range(len(plan.sides))]
    return folded(sides, "gy")


def local_program(mesh):
    def local(
        positions,
        species,
        counts,
        embed,
        radial_one,
        mix_one,
        read_one,
        radial_two,
        mix_two,
        read_hidden,
        read_out,
    ):
        slots, channels = positions.shape[-1], embed.shape[1]
        nbasis, nspec = radial_two.shape[0], embed.shape[0]
        plan = Plan(mesh, slots, nbasis, nspec)
        count = counts.reshape(1)
        given = [positions[0, 0, 0].reshape(3, 1, slots), species.reshape(1, slots)]
        sent = simple_call(
            prepare_kernel,
            plan,
            [count, *given],
            ((plan.ndev if plan.small else 1, 4, 2 * slots), F32),
            1,
            [(array.shape, array.dtype) for array in given],
            near=True,
            fetched=len(given),
        )
        far_sent = [everywhere(sent)] if plan.small else neighbours(plan, sent[0])
        pair_flops = 100 * slots * plan.far
        weights = [mix_one, radial_two, read_out[None], read_one[None], mix_two, read_hidden]
        rows, basis, layer, vector, mixing, cols, table, *weights = call(
            first_kernel,
            plan,
            far_sent,
            [embed, radial_one, *weights],
            [
                ((len(plan.tiles), 4, plan.width), F32),
                ((nbasis, slots, plan.far), BF16),
                ((slots, channels), BF16),
                ((3 * slots, channels), F32),
                ((slots, channels), F32),
                ((slots, 8), F32),
                ((2, nbasis * nspec, channels), BF16),
            ]
            + [(weight.shape, weight.dtype) for weight in weights],
            [
                ((nbasis, 4 * slots, plan.far), BF16),
                ((len(plan.tiles) * len(plan.sides), 4, 2 * slots), F32),
                (embed.shape, BF16),
                (radial_one.shape, F32),
            ],
            pair_flops,
            near=True,
            fetched=2 + len(weights),
        )
        mix_one, radial_two, out_row, one_row, mix_two, read_hidden = weights
        again, apart, slope, factor, turned = simple_call(
            slope_kernel,
            plan,
            [rows, cols, layer],
            [(layer.shape, BF16)]
            + [((count, slots, plan.far), F32) for count in (3, nbasis, nbasis, nbasis)],
            flops=pair_flops,
        )
        far_layer = neighbours(plan, layer, again)
        far_scratch = ((plan.far, channels), BF16)
        adjoint, kept, before, own_adjoint = call(
            second_kernel,
            plan,
            far_layer,
            [layer, basis, cols, radial_two, mix_two, read_hidden, out_row, one_row],
            [
                ((slots, channels), BF16),
                ((slots, channels), BF16),
                ((slots, read_hidden.shape[0]), F32),
                ((slots, channels), F32),
            ],
            [far_scratch],
            pair_flops,
        )
        again, pair, energy, features = call(
            energy_kernel,
            plan,
            far_layer,
            [adjoint, slope, radial_two, cols, layer, before, out_row, one_row, kept],
            [
                ((slots, channels), BF16),
                ((slots, plan.far), F32),
                ((1, slots), F32),
                ((slots, channels), BF16),
            ],
            [far_scratch],
            pair_flops,
        )
        far_adjoint = neighbours(plan, adjoint, again)
        pulls = call(
            force_kernel,
            plan,
            far_adjoint,
            [own_adjoint, basis, pair, rows, apart, slope, factor, turned]
            + [radial_two, mixing, mix_one, vector, table],
            [((plan.ndev, 4, plan.width) if plan.small else (len(plan.tiles), 3, plan.width), F32)],
            [far_scratch],
            pair_flops,
        )
        if plan.small:
            forces = simple_call(sum_kernel, plan, [everywhere(pulls[0])], ((3, 1, slots), F32))
        else:
            forces = -fold(plan, pulls[0])
        return (
            forces.reshape(1, 1, 1, 3, slots),
            energy[None, None],
            features.T[None, None, None],
        )

    return local


def solution(mesh):
    split = [P(*AXES, None, None), P(*AXES, None), P(*AXES)]
    out_specs = (P(*AXES, None, None), P(*AXES, None), P(*AXES, None, None))
    return jax.shard_map(
        local_program(mesh),
        mesh=mesh,
        in_specs=tuple(split + [P()] * 8),
        out_specs=out_specs,
        check_vma=False,
    )
```

```python
import itertools
import math

import jax
import jax.numpy as jnp
from jax import lax
from jax.experimental import pallas as pl
from jax.experimental.pallas import tpu as pltpu
from jax.sharding import PartitionSpec as P

CELL_SIDE = 5.0
CUT_SQUARE = 25.0
SOFTEN = 0.25
MSG_SCALE = 0.05
ROOT_THREE = math.sqrt(3.0)
FAR = 1.0e4
AXES = ("gx", "gy", "gz")
F32 = jnp.float32
BF16 = jnp.bfloat16
COS_TERMS = (
    0.9999999997799041,
    -4.934802137078749,
    4.058709159554242,
    -1.335212003029471,
    0.23493731372678894,
    -0.024396324214549327,
)
SIN_TERMS = (
    3.14159265353629,
    -5.167712764624453,
    2.550163318944743,
    -0.5992521977996564,
    0.08205040170151112,
    -0.007028386239784362,
)
VMEM_LIMIT = 24 * 1024 * 1024
FETCH_LIMIT = 60 * 1024 * 1024
NT = (((1,), (1,)), ((), ()))
NN = (((1,), (0,)), ((), ()))


def dot(a, b, dims=NN):
    return lax.dot_general(a, b, dims, preferred_element_type=F32)


def dot_exact(a, b, dims=NN):
    return lax.dot_general(
        a, b, dims, precision=lax.Precision.HIGHEST, preferred_element_type=F32
    )


def split_dot(a, b):
    high = a.astype(BF16)
    low = (a - high.astype(F32)).astype(BF16)
    return dot(high, b) + dot(low, b)


def offsets_of(count):
    return (0, 1) if count == 2 else (0, 1, -1)


def paired(count):
    return count > 2 and count % 2 == 0


def matched(which, parity):
    return jnp.int32(0) if which == 0 else 1 + (parity if which == 1 else 1 - parity)


def poly(terms, arg):
    total = arg * terms[-1] + terms[-2]
    for term in terms[-3::-1]:
        total = total * arg + term
    return total


class Plan:
    def __init__(self, mesh, slots, nbasis, nspec):
        self.sizes = {axis: mesh.shape[axis] for axis in AXES}
        self.ndev = math.prod(self.sizes.values())
        self.tiles = list(
            itertools.product(offsets_of(self.sizes["gx"]), offsets_of(self.sizes["gz"]))
        )
        self.sides = offsets_of(self.sizes["gy"])
        self.slots = slots
        self.width = len(self.sides) * slots
        self.far = len(self.tiles) * self.width
        self.nbasis = nbasis
        self.nspec = nspec
        self.depth = len(offsets_of(self.sizes["gz"]))
        self.wide = len(offsets_of(self.sizes["gx"]))
        self.brought = list(itertools.product(range(self.wide), range(self.depth)))
        self.mixed = self.depth == self.wide and self.sizes["gy"] % 2 == 0
        self.small = self.ndev <= 64 and len(self.sides) == 2
        self.wrapped = [self.sizes[axis] == 2 for axis in AXES]

    def global_id(self, offset):
        place = 0
        for axis, step in zip(AXES, offset):
            count = self.sizes[axis]
            place = place * count + lax.rem(lax.axis_index(axis) + (step + count), count)
        return place

    def places(self, column_known=False):
        index = {axis: lax.axis_index(axis) for axis in AXES}

        def parity(axis):
            return lax.rem(index[axis], 2) if paired(self.sizes[axis]) else jnp.int32(0)

        turns = parity("gx"), parity("gz")
        mixed = self.mixed and not column_known
        core = lax.rem(index["gy"], 2) if mixed else jnp.int32(0)
        found = []
        for side in range(len(self.sides)):
            x_first = core if side == 0 or not mixed else 1 - core
            for second, first in self.brought:
                row = first if column_known else matched(first, turns[1])
                plain = matched(second, turns[0]) * self.depth + row
                crossed = matched(first, turns[0]) * self.depth + matched(second, turns[1])
                tile = jnp.where(x_first == 1, crossed, plain) if mixed else plain
                found.append(tile * len(self.sides) + side)
        found += turns
        return [jnp.asarray(place, jnp.int32) for place in found]

    def brought_place(self, places, side, pair):
        return places[side * len(self.brought) + pair]

    def staged_place(self, places, tile):
        start = len(self.sides) * len(self.brought)
        x, z = divmod(tile, self.depth)
        return matched(x, places[start]) * self.depth + matched(z, places[start + 1])

    def offset(self, tile, side):
        ox, oz = self.tiles[tile]
        return (ox, self.sides[side], oz)


def separations(plan, rows, cols):
    parts = []
    for axis in range(3):
        diff = rows[axis] - cols[axis]
        if plan.wrapped[axis]:
            diff = jnp.where(diff > CELL_SIDE, diff - 2.0 * CELL_SIDE, diff)
        parts.append(diff)
    return parts


def distance(plan, parts, tile):
    dist_sq = parts[0] * parts[0] + parts[1] * parts[1] + parts[2] * parts[2] + SOFTEN
    if tile == 0:
        row = lax.broadcasted_iota(jnp.int32, dist_sq.shape, 0)
        col = lax.broadcasted_iota(jnp.int32, dist_sq.shape, 1)
        dist_sq = jnp.where(row == col, FAR, dist_sq)
    return dist_sq, lax.rsqrt(dist_sq)


def waves(dist_sq, inverse):
    arg = jnp.minimum(dist_sq * inverse * (1.0 / CELL_SIDE) - 0.5, 0.5)
    square = arg * arg
    return poly(COS_TERMS, square), -(arg * poly(SIN_TERMS, square))


def first_kernel(plan, nrefs, places, *refs):
    far_refs, refs = refs[:nrefs], refs[nrefs:]
    (table_ref, embed_ref, mix_ref), refs = refs[:3], refs[3:]
    rows_ref, basis_ref, layer_ref, vector_ref, mixing_ref, cols_ref, pair_ref, block_ref = refs
    slots, nbasis, nspec = plan.slots, plan.nbasis, plan.nspec

    def put(place, block):
        block_ref[place] = block

    if not plan.small:
        scatter(plan, places, far_refs, put)

    def block_of(tile, side, up):
        if plan.small:
            x, y, z = plan.offset(tile, side)
            return far_refs[0][plan.global_id((x, y, z + up))]
        return block_ref[tile * len(plan.sides) + side]

    species = lax.broadcasted_iota(jnp.int32, (nbasis * nspec, plan.width), 0) % nspec
    shifts = [tile_shift(plan, tile) for tile in range(len(plan.tiles))]
    own, counted = [], []
    for which in range(layer_ref.shape[0]):
        up = offsets_of(plan.sizes["gz"])[which]
        held = block_of(0, 0, up)
        held = jnp.concatenate([held, held], axis=0).T[:slots]
        kind = held[:, 3:4]
        own.append(kind)
        lane = lax.broadcasted_iota(jnp.int32, held.shape, 1)
        live = kind >= 0.0
        held = jnp.where((lane == 0) & ~live, -FAR, held)
        if which == 0:
            cols_ref[...] = jnp.where(lane == 3, live.astype(F32), held)
        cols = [held[:, axis : axis + 1] for axis in range(3)]
        hot = []
        for tile in range(len(plan.tiles)):
            blocks = [block_of(tile, side, up) for side in range(len(plan.sides))]
            placed = side_by_side(plan, blocks) + shifts[tile]
            if which == 0:
                rows_ref[tile] = placed
            rows = [placed[k : k + 1] for k in range(4)]
            hot.append((rows[3].astype(jnp.int32) == species).astype(F32).astype(BF16))
            parts = separations(plan, rows, cols)
            dist_sq, inverse = distance(plan, parts, tile)
            sine, cosine = waves(dist_sq, inverse)
            fade = jnp.maximum(1.0 - dist_sq * (1.0 / CUT_SQUARE), 0.0)
            radial = fade * fade * inverse
            units = [(part * (inverse * ROOT_THREE)).astype(BF16) for part in parts]
            before, now = None, sine * radial
            double = 2.0 * cosine
            lanes = slice(tile * plan.width, (tile + 1) * plan.width)
            for n in range(nbasis):
                if n == 1:
                    before, now = now, double * now
                elif n > 1:
                    before, now = now, double * now - before
                packed = now.astype(BF16)
                if which == 0:
                    basis_ref[n, :, lanes] = packed
                pair_ref[which, n, :slots, lanes] = packed
                for k in range(3):
                    pair_ref[which, n, (k + 1) * slots : (k + 2) * slots, lanes] = units[k] * packed
        hot = jnp.concatenate(hot, axis=1)
        gathered = dot(pair_ref[which].reshape(nbasis * 4 * slots, plan.far), hot, NT)
        gathered = gathered.reshape(nbasis, 4 * slots, nbasis * nspec)
        group = lax.broadcasted_iota(jnp.int32, gathered.shape[1:], 1) // nspec
        total = gathered[0]
        for n in range(1, nbasis):
            total = jnp.where(group == n, gathered[n], total)
        counted.append(total)
    scalar = split_dot(jnp.concatenate([total[:slots] for total in counted], axis=0), table_ref[0])
    scalar = MSG_SCALE * scalar
    norm = None
    for k in range(3):
        rows = slice((k + 1) * slots, (k + 2) * slots)
        vector = split_dot(jnp.concatenate([total[rows] for total in counted], axis=0), table_ref[1])
        vector = MSG_SCALE * vector
        vector_ref[k * slots : (k + 1) * slots] = vector[:slots]
        norm = vector * vector if k == 0 else norm + vector * vector
    invariants = jnp.concatenate([scalar.astype(BF16), norm.astype(BF16)], axis=1)
    mixing = dot(invariants, mix_ref[...], NT)
    mixing_ref[...] = mixing[:slots]
    kind = jnp.concatenate(own, axis=0)
    own_species = lax.broadcasted_iota(jnp.int32, (kind.shape[0], nspec), 1)
    own_hot = (kind.astype(jnp.int32) == own_species).astype(F32).astype(BF16)
    layer = (dot(own_hot, embed_ref[...]) + mixing * sigmoid(mixing)).astype(BF16)
    for which in range(layer_ref.shape[0]):
        layer_ref[which] = layer[which * slots : (which + 1) * slots]


def sigmoid(value):
    return 1.0 / (1.0 + jnp.exp(-value))


def scatter(plan, places, far_refs, put):
    for side in range(len(plan.sides)):
        for pair, (second, first) in enumerate(plan.brought):
            block = far_refs[side * plan.wide + second][first]
            put(plan.brought_place(places, side, pair), block)


def side_by_side(plan, blocks):
    if len(blocks) == 2:
        lane = lax.broadcasted_iota(jnp.int32, blocks[0].shape, 1)
        return jnp.where(lane < plan.slots, blocks[0], blocks[1])
    return jnp.concatenate([block[:, : plan.slots] for block in blocks], axis=1)


def tile_shift(plan, tile):
    row = lax.broadcasted_iota(jnp.int32, (4, plan.width), 0)
    side = lax.broadcasted_iota(jnp.int32, (4, plan.width), 1) // plan.slots
    shift = jnp.zeros((4, plan.width), F32)
    for s in range(len(plan.sides)):
        for k, steps in enumerate(plan.offset(tile, s)):
            if steps:
                shift = jnp.where((row == k) & (side == s), CELL_SIDE * steps, shift)
    return shift


def gather_far(plan, places, far_refs, all_ref):
    def put(place, block):
        start = pl.multiple_of(place * plan.slots, plan.slots)
        all_ref[pl.ds(start, plan.slots)] = block

    scatter(plan, places, far_refs, put)


def second_kernel(plan, nrefs, places, *refs):
    far_refs, refs = refs[:nrefs], refs[nrefs:]
    (layer_ref, basis_ref, cols_ref, radial_ref, mix_ref), refs = refs[:5], refs[5:]
    (hidden_ref, out_ref, one_ref), refs = refs[:3], refs[3:]
    adjoint_ref, features_ref, before_ref, own_ref, all_ref = refs
    slots, nbasis = plan.slots, plan.nbasis
    gather_far(plan, places, far_refs, all_ref)
    summed = dot(basis_ref[...].reshape(nbasis * slots, plan.far), all_ref[...])
    message = jnp.zeros((slots, summed.shape[1]), F32)
    for n in range(nbasis):
        message = message + summed[n * slots : (n + 1) * slots] * radial_ref[n : n + 1]
    rounded = (MSG_SCALE * message).astype(BF16)
    mixing = dot(rounded, mix_ref[...], NT)
    gate = sigmoid(mixing)
    layer = layer_ref[0].astype(F32)
    features = (layer + mixing * gate).astype(BF16)
    features_ref[...] = features
    before = dot(features, hidden_ref[...], NT)
    open_hidden = sigmoid(before)
    live = cols_ref[:, 3:4]
    before_ref[...] = before
    slope = out_ref[...] * (open_hidden * (1.0 + before * (1.0 - open_hidden))) * live
    from_hidden = dot(slope.astype(BF16), hidden_ref[...])
    own_ref[...] = from_hidden + one_ref[...] * live
    back = from_hidden * (gate * (1.0 + mixing * (1.0 - gate)))
    adjoint_ref[...] = dot(back.astype(BF16), mix_ref[...]).astype(BF16)


def slope_kernel(plan, rows_ref, cols_ref, layer_ref, *refs):
    again_ref, apart_ref, slope_ref, radial_ref, turned_ref = refs
    again_ref[...] = layer_ref[...]
    cols = [cols_ref[:, axis : axis + 1] for axis in range(3)]
    for tile in range(len(plan.tiles)):
        lanes = slice(tile * plan.width, (tile + 1) * plan.width)
        parts = separations(plan, [rows_ref[tile, k : k + 1] for k in range(3)], cols)
        for k in range(3):
            apart_ref[k, :, lanes] = parts[k]
        dist_sq, inverse = distance(plan, parts, tile)
        sine, cosine = waves(dist_sq, inverse)
        fade = jnp.maximum(1.0 - dist_sq * (1.0 / CUT_SQUARE), 0.0)
        radial = fade * fade * inverse
        on_sine = -inverse * ((4.0 / CUT_SQUARE) * fade + radial * inverse)
        on_cosine = (math.pi / CELL_SIDE) * (inverse * radial)
        scale = ROOT_THREE * inverse
        scaled = scale * radial
        square = inverse * inverse
        double = 2.0 * cosine
        before_s, now_s, before_c, now_c = None, sine, None, cosine
        for n in range(plan.nbasis):
            if n == 1:
                before_s, now_s = now_s, double * now_s
                before_c, now_c = now_c, double * now_c - 1.0
            elif n > 1:
                before_s, now_s = now_s, double * now_s - before_s
                before_c, now_c = now_c, double * now_c - before_c
            slope = on_sine * now_s + (n + 1.0) * on_cosine * now_c
            factor = scaled * now_s
            slope_ref[n, :, lanes] = slope
            radial_ref[n, :, lanes] = factor
            turned_ref[n, :, lanes] = scale * slope - square * factor


def energy_kernel(plan, nrefs, places, *refs):
    far_refs, refs = refs[:nrefs], refs[nrefs:]
    (adjoint_ref, slope_ref, radial_ref, cols_ref, layer_ref), refs = refs[:5], refs[5:]
    (before_ref, out_ref, one_ref, kept_ref), refs = refs[:4], refs[4:]
    again_ref, pair_ref, energy_ref, features_ref, all_ref = refs
    slots, nbasis = plan.slots, plan.nbasis
    again_ref[...] = adjoint_ref[...]
    features_ref[...] = kept_ref[...]
    before = before_ref[...]
    live = jnp.where(lax.broadcasted_iota(jnp.int32, (slots, 8), 1) == 0, cols_ref[:, 3:4], 0.0)
    live_row = dot(jnp.ones((1, 8), BF16), live.astype(BF16), NT)
    energy = dot_exact(one_ref[...], layer_ref[0].astype(F32), NT)
    energy = energy + dot_exact(out_ref[...], before * sigmoid(before), NT)
    energy_ref[...] = energy * live_row
    gather_far(plan, places, far_refs, all_ref)
    adjoint = adjoint_ref[...].astype(F32) * MSG_SCALE
    weighted = jnp.concatenate(
        [(adjoint * radial_ref[n : n + 1]).astype(BF16) for n in range(nbasis)], axis=0
    )
    for tile in range(len(plan.tiles)):
        lanes = slice(tile * plan.width, (tile + 1) * plan.width)
        pulled = dot(weighted, all_ref[lanes], NT)
        total = slope_ref[0, :, lanes] * pulled[:slots]
        for n in range(1, nbasis):
            total = total + slope_ref[n, :, lanes] * pulled[n * slots : (n + 1) * slots]
        pair_ref[:, lanes] = total


def force_kernel(plan, nrefs, places, *refs):
    far_refs, refs = refs[:nrefs], refs[nrefs:]
    (own_ref, basis_ref, pair_ref, rows_ref), refs = refs[:4], refs[4:]
    (apart_ref, slope_ref, factor_ref, turned_ref), refs = refs[:4], refs[4:]
    (radial_ref, mixing_ref, mix_ref, vector_ref, table_ref), refs = refs[:5], refs[5:]
    out_ref, all_ref = refs
    slots, nbasis, nspec, width = plan.slots, plan.nbasis, plan.nspec, plan.width
    gather_far(plan, places, far_refs, all_ref)
    summed = dot(basis_ref[...].reshape(nbasis * slots, plan.far), all_ref[...])
    adjoint = jnp.zeros((slots, summed.shape[1]), F32)
    for n in range(nbasis):
        adjoint = adjoint + summed[n * slots : (n + 1) * slots] * radial_ref[n : n + 1]
    adjoint = own_ref[...] + MSG_SCALE * adjoint
    mixing = mixing_ref[...]
    gate = sigmoid(mixing)
    back = (adjoint * (gate * (1.0 + mixing * (1.0 - gate)))).astype(BF16)
    invariants = dot(back, mix_ref[...])
    channels = invariants.shape[1] // 2
    on_scalar = (MSG_SCALE * invariants[:, :channels]).astype(BF16)
    doubled = (2.0 * MSG_SCALE) * invariants[:, channels:]
    on_vector = (vector_ref[...] * jnp.concatenate([doubled] * 3, axis=0)).astype(BF16)
    weights = jnp.concatenate(
        [dot(on_scalar, table_ref[0], NT), dot(on_vector, table_ref[1], NT)], axis=0
    ).astype(BF16)
    group = lax.broadcasted_iota(jnp.int32, weights.shape, 1) // nspec
    weights = weights.astype(F32)
    weights = jnp.concatenate(
        [jnp.where(group == n, weights, 0.0).astype(BF16) for n in range(nbasis)], axis=0
    )
    species = lax.broadcasted_iota(jnp.int32, (nbasis * nspec, width), 0) % nspec
    own = [jnp.zeros((slots, width), F32) for _ in range(3)]
    pulls = []
    for tile in range(len(plan.tiles)):
        lanes = slice(tile * width, (tile + 1) * width)
        hot = (rows_ref[tile, 3:4].astype(jnp.int32) == species).astype(F32).astype(BF16)
        spread = dot(weights, hot)
        total = pair_ref[:, lanes]
        sides, turns = [None] * 3, [None] * 3
        for n in range(nbasis):
            start = n * 4 * slots
            total = total + slope_ref[n, :, lanes] * spread[start : start + slots]
            for k in range(3):
                piece = spread[start + (k + 1) * slots : start + (k + 2) * slots]
                side = factor_ref[n, :, lanes] * piece
                turn = turned_ref[n, :, lanes] * piece
                sides[k] = side if n == 0 else sides[k] + side
                turns[k] = turn if n == 0 else turns[k] + turn
        for k in range(3):
            total = total + apart_ref[k, :, lanes] * turns[k]
        pulls.append([])
        for k in range(3):
            pull = apart_ref[k, :, lanes] * total + sides[k]
            own[k] = own[k] + pull
            pulls[-1].append(jnp.sum(pull, axis=0, keepdims=True))
    own = jnp.concatenate(own, axis=0)
    high = own.astype(BF16)
    low = (own - high.astype(F32)).astype(BF16)
    ones = jnp.ones((8, width), BF16)
    mine = (dot(ones, high, NT) + dot(ones, low, NT))[:1]
    mine = jnp.concatenate([mine[:, k * slots : (k + 1) * slots] for k in range(3)], axis=0)
    if plan.small:
        out_ref[...] = jnp.zeros_like(out_ref)
    side_of = lax.broadcasted_iota(jnp.int32, (3, width), 1) // slots
    for tile in range(len(plan.tiles)):
        pulled = jnp.concatenate(pulls[tile], axis=0)
        if tile == 0:
            others = [jnp.zeros_like(mine)] * (len(plan.sides) - 1)
            pulled = pulled - jnp.concatenate([mine] + others, axis=1)
        if not plan.small:
            out_ref[plan.staged_place(places, tile)] = pulled
            continue
        for side in range(len(plan.sides)):
            place = plan.global_id(plan.offset(tile, side))
            out_ref[place, :3] = jnp.where(side_of == side, pulled, 0.0)


def begin(pairs, sems):
    copies = [pltpu.make_async_copy(*pair, sems.at[m]) for m, pair in enumerate(pairs)]
    for copy in copies:
        copy.start()
    return copies


def prepare_kernel(plan, counts_ref, *refs):
    fetched, sent_ref, table_ref, refs = refs[:10], refs[10], refs[11], refs[12:]
    kept, (place_ref, kind_ref, radial_ref, sems) = refs[:7], refs[7:]
    copies = begin(zip(fetched, (place_ref, kind_ref, radial_ref, *kept)), sems)
    for copy in copies[:2]:
        copy.wait()
    live = lax.broadcasted_iota(jnp.int32, (1, plan.slots), 1) < counts_ref[0]
    rows = [
        jnp.where(live, place_ref[0], FAR),
        place_ref[1],
        place_ref[2],
        jnp.where(live, kind_ref[...], -1).astype(F32),
    ]
    rows = jnp.concatenate(rows, axis=0)
    rows = jnp.concatenate([rows, rows], axis=1)
    for copy in range(sent_ref.shape[0]):
        sent_ref[copy] = rows
    for copy in copies[2:]:
        copy.wait()
    embed, nspec = kept[0][...].astype(F32), plan.nspec
    for g in range(2):
        for n in range(plan.nbasis):
            weighted = radial_ref[g, n : n + 1] * embed
            table_ref[g, n * nspec : (n + 1) * nspec] = weighted.astype(BF16)


def sum_kernel(plan, parts_ref, force_ref):
    total = parts_ref[0]
    for part in range(1, parts_ref.shape[0]):
        total = total + parts_ref[part]
    total = total[:, : plan.slots] + total[:, plan.slots :]
    for k in range(3):
        force_ref[k] = -total[k : k + 1]


VMEM_SPEC = pl.BlockSpec(memory_space=pltpu.VMEM)
SMEM_SPEC = pl.BlockSpec(memory_space=pltpu.SMEM)
HBM_SPEC = pl.BlockSpec(memory_space=pltpu.HBM)


def simple_call(kernel, plan, operands, outs, scalars=0, scratch=(), flops=2**20, near=False, fetched=0):
    single = not isinstance(outs, list)
    kind = pltpu.VMEM if near else jax.ShapeDtypeStruct
    shapes = [kind(*out) for out in ([outs] if single else outs)]

    def body(*refs):
        kernel(plan, *refs)

    got = pl.pallas_call(
        body,
        out_shape=shapes,
        in_specs=[SMEM_SPEC] * scalars
        + [VMEM_SPEC] * (len(operands) - scalars - fetched)
        + [HBM_SPEC] * fetched,
        out_specs=[VMEM_SPEC] * len(shapes),
        scratch_shapes=[pltpu.VMEM(*buffer) for buffer in scratch]
        + [pltpu.SemaphoreType.DMA((fetched,))] * (fetched > 0),
        compiler_params=pltpu.CompilerParams(vmem_limit_bytes=FETCH_LIMIT if fetched else VMEM_LIMIT),
        cost_estimate=pl.CostEstimate(flops=flops, bytes_accessed=2**20, transcendentals=0),
    )(*operands)
    return got[0] if single else got


def call(kernel, plan, far, operands, outs, scratch, flops, column_known=False, **options):
    def body(plan, *refs):
        kernel(plan, len(far), plan.places(column_known), *refs)

    return simple_call(body, plan, [*far, *operands], outs, 0, scratch, flops, **options)


def swaps(count):
    if count == 2:
        return [[1, 0]]
    if paired(count):
        near = [i ^ 1 for i in range(count)]
        far = [(i - 1 + 2 * (i % 2)) % count for i in range(count)]
        return [near, far]
    return [[(i + o) % count for i in range(count)] for o in offsets_of(count)[1:]]


def brought(plan, block, second, mixed):
    sizes, sources = plan.sizes, {axis: swaps(plan.sizes[axis]) for axis in AXES}
    got = []
    for m in range(len(sources["gx" if second else "gz"])):
        pairs = []
        for x, y, z in itertools.product(*(range(sizes[axis]) for axis in AXES)):
            along_x = second != (mixed and y % 2 == 1)
            source = (sources["gx"][m][x], y, z) if along_x else (x, y, sources["gz"][m][z])
            pairs.append((flat(sizes, *source), flat(sizes, x, y, z)))
        got.append(lax.ppermute(block, AXES, pairs))
    return got


def flat(sizes, x, y, z):
    return (x * sizes["gy"] + y) * sizes["gz"] + z


def along(block, axis):
    return [
        lax.ppermute(block, axis, [(source, i) for i, source in enumerate(sources)])
        for sources in swaps(lax.axis_size(axis))
    ]


def neighbours(plan, block, again=None):
    column = jnp.stack([block if again is None else again] + brought(plan, block, False, plan.mixed))
    return from_columns(plan, column, plan.mixed)


def from_columns(plan, column, mixed, again=None):
    columns = [column] + brought(plan, column, True, mixed)
    if again is not None:
        columns[0] = again
    swapped = [[column] + along(column, "gy") for column in columns]
    return [column[side] for side in range(len(plan.sides)) for column in swapped]


def everywhere(copies):
    return lax.all_to_all(copies, AXES, 0, 0, tiled=True)


def folded(pieces, axis):
    total = pieces[0]
    for piece, sources in zip(pieces[1:], swaps(lax.axis_size(axis))):
        total = total + lax.ppermute(piece, axis, list(enumerate(sources)))
    return total


def fold(plan, pulls):
    for axis in ("gx", "gz"):
        parts = len(offsets_of(plan.sizes[axis]))
        pulls = pulls.reshape((parts, -1) + pulls.shape[1:])
        pulls = folded([pulls[m] for m in range(parts)], axis)
    pulls = pulls[0]
    sides = [pulls[:, m * plan.slots : (m + 1) * plan.slots] for m in range(len(plan.sides))]
    return folded(sides, "gy")


def local_program(mesh):
    def local(
        positions,
        species,
        counts,
        embed,
        radial_one,
        mix_one,
        read_one,
        radial_two,
        mix_two,
        read_hidden,
        read_out,
    ):
        slots, channels = positions.shape[-1], embed.shape[1]
        nbasis, nspec = radial_two.shape[0], embed.shape[0]
        plan = Plan(mesh, slots, nbasis, nspec)
        given = [positions[0, 0, 0].reshape(3, 1, slots), species.reshape(1, slots), radial_one]
        weights = [embed, mix_one, radial_two, read_out[None], read_one[None], mix_two, read_hidden]
        sent, table, *weights = simple_call(
            prepare_kernel,
            plan,
            [counts.reshape(1), *given, *weights],
            [
                ((plan.ndev if plan.small else 1, 4, 2 * slots), F32),
                ((2, nbasis * nspec, channels), BF16),
            ]
            + [(weight.shape, weight.dtype) for weight in weights],
            1,
            [(array.shape, array.dtype) for array in given],
            near=True,
            fetched=len(given) + len(weights),
        )
        embed, mix_one, radial_two, out_row, one_row, mix_two, read_hidden = weights
        far_sent = [everywhere(sent)] if plan.small else neighbours(plan, sent[0])
        pair_flops = 100 * slots * plan.far
        known = plan.depth if plan.small else 1
        rows, basis, layer, vector, mixing, cols = call(
            first_kernel,
            plan,
            far_sent,
            [table, embed, mix_one],
            [
                ((len(plan.tiles), 4, plan.width), F32),
                ((nbasis, slots, plan.far), BF16),
                ((known, slots, channels), BF16),
                ((3 * slots, channels), F32),
                ((slots, channels), F32),
                ((slots, 8), F32),
            ],
            [
                ((known, nbasis, 4 * slots, plan.far), BF16),
                ((len(plan.tiles) * len(plan.sides), 4, 2 * slots), F32),
            ],
            pair_flops,
        )
        again, apart, slope, factor, turned = simple_call(
            slope_kernel,
            plan,
            [rows, cols, layer],
            [(layer.shape, BF16)]
            + [((count, slots, plan.far), F32) for count in (3, nbasis, nbasis, nbasis)],
            flops=pair_flops,
        )
        if plan.small:
            far_layer = from_columns(plan, layer, False, again)
        else:
            far_layer = neighbours(plan, layer[0], again[0])
        far_scratch = ((plan.far, channels), BF16)
        adjoint, kept, before, own_adjoint = call(
            second_kernel,
            plan,
            far_layer,
            [layer, basis, cols, radial_two, mix_two, read_hidden, out_row, one_row],
            [
                ((slots, channels), BF16),
                ((slots, channels), BF16),
                ((slots, read_hidden.shape[0]), F32),
                ((slots, channels), F32),
            ],
            [far_scratch],
            pair_flops,
            plan.small,
        )
        again, pair, energy, features = call(
            energy_kernel,
            plan,
            far_layer,
            [adjoint, slope, radial_two, cols, layer, before, out_row, one_row, kept],
            [
                ((slots, channels), BF16),
                ((slots, plan.far), F32),
                ((1, slots), F32),
                ((slots, channels), BF16),
            ],
            [far_scratch],
            pair_flops,
            plan.small,
        )
        far_adjoint = neighbours(plan, adjoint, again)
        pulls = call(
            force_kernel,
            plan,
            far_adjoint,
            [own_adjoint, basis, pair, rows, apart, slope, factor, turned]
            + [radial_two, mixing, mix_one, vector, table],
            [((plan.ndev, 4, plan.width) if plan.small else (len(plan.tiles), 3, plan.width), F32)],
            [far_scratch],
            pair_flops,
        )
        if plan.small:
            forces = simple_call(sum_kernel, plan, [everywhere(pulls[0])], ((3, 1, slots), F32))
        else:
            forces = -fold(plan, pulls[0])
        return (
            forces.reshape(1, 1, 1, 3, slots),
            energy[None, None],
            features.T[None, None, None],
        )

    return local


def solution(mesh):
    split = [P(*AXES, None, None), P(*AXES, None), P(*AXES)]
    out_specs = (P(*AXES, None, None), P(*AXES, None), P(*AXES, None, None))
    return jax.shard_map(
        local_program(mesh),
        mesh=mesh,
        in_specs=tuple(split + [P()] * 8),
        out_specs=out_specs,
        check_vma=False,
    )
```

```python
import itertools
import math

import jax
import jax.numpy as jnp
from jax import lax
from jax.experimental import pallas as pl
from jax.experimental.pallas import tpu as pltpu
from jax.sharding import PartitionSpec as P

CELL_SIDE = 5.0
CUT_SQUARE = 25.0
SOFTEN = 0.25
MSG_SCALE = 0.05
ROOT_THREE = math.sqrt(3.0)
FAR = 1.0e4
AXES = ("gx", "gy", "gz")
F32 = jnp.float32
BF16 = jnp.bfloat16
COS_TERMS = (
    0.9999999997799041,
    -4.934802137078749,
    4.058709159554242,
    -1.335212003029471,
    0.23493731372678894,
    -0.024396324214549327,
)
SIN_TERMS = (
    3.14159265353629,
    -5.167712764624453,
    2.550163318944743,
    -0.5992521977996564,
    0.08205040170151112,
    -0.007028386239784362,
)
VMEM_LIMIT = 24 * 1024 * 1024
FETCH_LIMIT = 60 * 1024 * 1024
NT = (((1,), (1,)), ((), ()))
NN = (((1,), (0,)), ((), ()))


def dot(a, b, dims=NN):
    return lax.dot_general(a, b, dims, preferred_element_type=F32)


def dot_exact(a, b, dims=NN):
    return lax.dot_general(
        a, b, dims, precision=lax.Precision.HIGHEST, preferred_element_type=F32
    )


def split_dot(a, b):
    high = a.astype(BF16)
    low = (a - high.astype(F32)).astype(BF16)
    return dot(high, b) + dot(low, b)


def offsets_of(count):
    return (0, 1) if count == 2 else (0, 1, -1)


def paired(count):
    return count > 2 and count % 2 == 0


def matched(which, parity):
    return jnp.int32(0) if which == 0 else 1 + (parity if which == 1 else 1 - parity)


def poly(terms, arg):
    total = arg * terms[-1] + terms[-2]
    for term in terms[-3::-1]:
        total = total * arg + term
    return total


class Plan:
    def __init__(self, mesh, slots, nbasis, nspec):
        self.sizes = {axis: mesh.shape[axis] for axis in AXES}
        self.ndev = math.prod(self.sizes.values())
        self.tiles = list(
            itertools.product(offsets_of(self.sizes["gx"]), offsets_of(self.sizes["gz"]))
        )
        self.sides = offsets_of(self.sizes["gy"])
        self.slots = slots
        self.width = len(self.sides) * slots
        self.far = len(self.tiles) * self.width
        self.nbasis = nbasis
        self.nspec = nspec
        self.depth = len(offsets_of(self.sizes["gz"]))
        self.wide = len(offsets_of(self.sizes["gx"]))
        self.brought = list(itertools.product(range(self.wide), range(self.depth)))
        self.mixed = self.depth == self.wide and self.sizes["gy"] % 2 == 0
        self.small = self.ndev <= 64 and len(self.sides) == 2
        near = offsets_of(self.sizes["gz"])
        self.column = list(near) if self.small else [0]
        for step in [a + b for a in near for b in near] if self.small else []:
            if all((step - known) % self.sizes["gz"] for known in self.column):
                self.column.append(step)
        self.known = self.depth if self.small else 1
        self.wrapped = [self.sizes[axis] == 2 for axis in AXES]

    def global_id(self, offset):
        place = 0
        for axis, step in zip(AXES, offset):
            count = self.sizes[axis]
            place = place * count + lax.rem(lax.axis_index(axis) + (step + count), count)
        return place

    def column_place(self, step):
        return [(step - known) % self.sizes["gz"] == 0 for known in self.column].index(True)

    def places(self):
        index = {axis: lax.axis_index(axis) for axis in AXES}

        def parity(axis):
            return lax.rem(index[axis], 2) if paired(self.sizes[axis]) else jnp.int32(0)

        turns = parity("gx"), parity("gz")
        core = lax.rem(index["gy"], 2) if self.mixed else jnp.int32(0)
        found = []
        for side in range(len(self.sides)):
            x_first = core if side == 0 or not self.mixed else 1 - core
            for second, first in self.brought:
                plain = matched(second, turns[0]) * self.depth + matched(first, turns[1])
                crossed = matched(first, turns[0]) * self.depth + matched(second, turns[1])
                tile = jnp.where(x_first == 1, crossed, plain) if self.mixed else plain
                found.append(tile * len(self.sides) + side)
        found += turns
        return [jnp.asarray(place, jnp.int32) for place in found]

    def brought_place(self, places, side, pair):
        return places[side * len(self.brought) + pair]

    def staged_place(self, places, tile):
        start = len(self.sides) * len(self.brought)
        x, z = divmod(tile, self.depth)
        return matched(x, places[start]) * self.depth + matched(z, places[start + 1])

    def offset(self, tile, side):
        ox, oz = self.tiles[tile]
        return (ox, self.sides[side], oz)


def separations(plan, rows, cols):
    parts = []
    for axis in range(3):
        diff = rows[axis] - cols[axis]
        if plan.wrapped[axis]:
            diff = jnp.where(diff > CELL_SIDE, diff - 2.0 * CELL_SIDE, diff)
        parts.append(diff)
    return parts


def distance(plan, parts, tile):
    dist_sq = parts[0] * parts[0] + parts[1] * parts[1] + parts[2] * parts[2] + SOFTEN
    if tile == 0:
        row = lax.broadcasted_iota(jnp.int32, dist_sq.shape, 0)
        col = lax.broadcasted_iota(jnp.int32, dist_sq.shape, 1)
        dist_sq = jnp.where(row == col, FAR, dist_sq)
    return dist_sq, lax.rsqrt(dist_sq)


def waves(dist_sq, inverse):
    arg = jnp.minimum(dist_sq * inverse * (1.0 / CELL_SIDE) - 0.5, 0.5)
    square = arg * arg
    return poly(COS_TERMS, square), -(arg * poly(SIN_TERMS, square))


def first_kernel(plan, nrefs, places, *refs):
    far_refs, refs = refs[:nrefs], refs[nrefs:]
    (table_ref, embed_ref, mix_ref), refs = refs[:3], refs[3:]
    rows_ref, basis_ref, layer_ref, vector_ref, mixing_ref, cols_ref, pair_ref, block_ref = refs
    slots, nbasis, nspec = plan.slots, plan.nbasis, plan.nspec

    def put(place, block):
        block_ref[place] = block

    if not plan.small:
        scatter(plan, places, far_refs, put)

    def block_of(tile, side, up):
        if plan.small:
            x, y, z = plan.offset(tile, side)
            return far_refs[0][plan.global_id((x, y, z + up))]
        return block_ref[tile * len(plan.sides) + side]

    species = lax.broadcasted_iota(jnp.int32, (nbasis * nspec, plan.width), 0) % nspec
    shifts = [tile_shift(plan, tile) for tile in range(len(plan.tiles))]
    own, counted = [], []
    for which, up in enumerate(plan.column):
        held = block_of(0, 0, up)
        held = jnp.concatenate([held, held], axis=0).T[:slots]
        kind = held[:, 3:4]
        own.append(kind)
        lane = lax.broadcasted_iota(jnp.int32, held.shape, 1)
        live = kind >= 0.0
        held = jnp.where((lane == 0) & ~live, -FAR, held)
        if which < plan.known:
            cols_ref[which] = jnp.where(lane == 3, live.astype(F32), held)
        cols = [held[:, axis : axis + 1] for axis in range(3)]
        hot = []
        for tile in range(len(plan.tiles)):
            blocks = [block_of(tile, side, up) for side in range(len(plan.sides))]
            placed = side_by_side(plan, blocks) + shifts[tile]
            if which == 0:
                rows_ref[tile] = placed
            rows = [placed[k : k + 1] for k in range(4)]
            hot.append((rows[3].astype(jnp.int32) == species).astype(F32).astype(BF16))
            parts = separations(plan, rows, cols)
            dist_sq, inverse = distance(plan, parts, tile)
            sine, cosine = waves(dist_sq, inverse)
            fade = jnp.maximum(1.0 - dist_sq * (1.0 / CUT_SQUARE), 0.0)
            radial = fade * fade * inverse
            units = [(part * (inverse * ROOT_THREE)).astype(BF16) for part in parts]
            before, now = None, sine * radial
            double = 2.0 * cosine
            lanes = slice(tile * plan.width, (tile + 1) * plan.width)
            for n in range(nbasis):
                if n == 1:
                    before, now = now, double * now
                elif n > 1:
                    before, now = now, double * now - before
                packed = now.astype(BF16)
                if which < plan.known:
                    basis_ref[which, n, :, lanes] = packed
                pair_ref[which, n, :slots, lanes] = packed
                for k in range(3):
                    pair_ref[which, n, (k + 1) * slots : (k + 2) * slots, lanes] = units[k] * packed
        hot = jnp.concatenate(hot, axis=1)
        gathered = dot(pair_ref[which].reshape(nbasis * 4 * slots, plan.far), hot, NT)
        gathered = gathered.reshape(nbasis, 4 * slots, nbasis * nspec)
        group = lax.broadcasted_iota(jnp.int32, gathered.shape[1:], 1) // nspec
        total = gathered[0]
        for n in range(1, nbasis):
            total = jnp.where(group == n, gathered[n], total)
        counted.append(total)
    scalar = split_dot(jnp.concatenate([total[:slots] for total in counted], axis=0), table_ref[0])
    scalar = MSG_SCALE * scalar
    norm = None
    for k in range(3):
        rows = slice((k + 1) * slots, (k + 2) * slots)
        vector = split_dot(jnp.concatenate([total[rows] for total in counted], axis=0), table_ref[1])
        vector = MSG_SCALE * vector
        vector_ref[k * slots : (k + 1) * slots] = vector[:slots]
        norm = vector * vector if k == 0 else norm + vector * vector
    invariants = jnp.concatenate([scalar.astype(BF16), norm.astype(BF16)], axis=1)
    mixing = dot(invariants, mix_ref[...], NT)
    mixing_ref[...] = mixing[:slots]
    kind = jnp.concatenate(own, axis=0)
    own_species = lax.broadcasted_iota(jnp.int32, (kind.shape[0], nspec), 1)
    own_hot = (kind.astype(jnp.int32) == own_species).astype(F32).astype(BF16)
    layer = (dot(own_hot, embed_ref[...]) + mixing * sigmoid(mixing)).astype(BF16)
    for which in range(layer_ref.shape[0]):
        layer_ref[which] = layer[which * slots : (which + 1) * slots]


def sigmoid(value):
    return 1.0 / (1.0 + jnp.exp(-value))


def scatter(plan, places, far_refs, put, up=0):
    for side in range(len(plan.sides)):
        for pair, (second, first) in enumerate(plan.brought):
            column = far_refs[side * plan.wide + second]
            if not plan.small:
                put(plan.brought_place(places, side, pair), column[first])
                continue
            turn = places[len(plan.sides) * len(plan.brought)]
            tile = matched(second, turn) * plan.depth + first
            step = offsets_of(plan.sizes["gz"])[first] + up
            put(tile * len(plan.sides) + side, column[plan.column_place(step)])


def side_by_side(plan, blocks):
    if len(blocks) == 2:
        lane = lax.broadcasted_iota(jnp.int32, blocks[0].shape, 1)
        return jnp.where(lane < plan.slots, blocks[0], blocks[1])
    return jnp.concatenate([block[:, : plan.slots] for block in blocks], axis=1)


def tile_shift(plan, tile):
    row = lax.broadcasted_iota(jnp.int32, (4, plan.width), 0)
    side = lax.broadcasted_iota(jnp.int32, (4, plan.width), 1) // plan.slots
    shift = jnp.zeros((4, plan.width), F32)
    for s in range(len(plan.sides)):
        for k, steps in enumerate(plan.offset(tile, s)):
            if steps:
                shift = jnp.where((row == k) & (side == s), CELL_SIDE * steps, shift)
    return shift


def gather_far(plan, places, far_refs, all_ref, up=0):
    def put(place, block):
        start = pl.multiple_of(place * plan.slots, plan.slots)
        all_ref[pl.ds(start, plan.slots)] = block

    scatter(plan, places, far_refs, put, up)


def second_kernel(plan, nrefs, places, *refs):
    far_refs, refs = refs[:nrefs], refs[nrefs:]
    (layer_ref, basis_ref, cols_ref, radial_ref, mix_ref), refs = refs[:5], refs[5:]
    (hidden_ref, out_ref, one_ref), refs = refs[:3], refs[3:]
    adjoint_ref, features_ref, before_ref, own_ref, own_far_ref, all_ref = refs
    slots, nbasis, known = plan.slots, plan.nbasis, plan.known
    messages = []
    for which in range(known):
        target = own_far_ref if which == 0 else all_ref.at[which - 1]
        gather_far(plan, places, far_refs, target, plan.column[which])
        summed = dot(basis_ref[which].reshape(nbasis * slots, plan.far), target[...])
        message = summed[:slots] * radial_ref[0:1]
        for n in range(1, nbasis):
            message = message + summed[n * slots : (n + 1) * slots] * radial_ref[n : n + 1]
        messages.append((MSG_SCALE * message).astype(BF16))
    mixing = dot(jnp.concatenate(messages, axis=0), mix_ref[...], NT)
    gate = sigmoid(mixing)
    layer = layer_ref[:known].reshape(known * slots, -1).astype(F32)
    features = (layer + mixing * gate).astype(BF16)
    features_ref[...] = features[:slots]
    before = dot(features, hidden_ref[...], NT)
    before_ref[...] = before[:slots]
    open_hidden = sigmoid(before)
    live = cols_ref[...].reshape(known * slots, 8)[:, 3:4]
    slope = out_ref[...] * (open_hidden * (1.0 + before * (1.0 - open_hidden))) * live
    from_hidden = dot(slope.astype(BF16), hidden_ref[...])
    own_ref[...] = from_hidden[:slots] + one_ref[...] * live[:slots]
    back = from_hidden * (gate * (1.0 + mixing * (1.0 - gate)))
    adjoint = dot(back.astype(BF16), mix_ref[...]).astype(BF16)
    for which in range(known):
        adjoint_ref[which] = adjoint[which * slots : (which + 1) * slots]


def slope_kernel(plan, rows_ref, cols_ref, layer_ref, *refs):
    again_ref, apart_ref, slope_ref, radial_ref, turned_ref = refs
    again_ref[...] = layer_ref[...]
    cols = [cols_ref[0, :, axis : axis + 1] for axis in range(3)]
    for tile in range(len(plan.tiles)):
        lanes = slice(tile * plan.width, (tile + 1) * plan.width)
        parts = separations(plan, [rows_ref[tile, k : k + 1] for k in range(3)], cols)
        for k in range(3):
            apart_ref[k, :, lanes] = parts[k]
        dist_sq, inverse = distance(plan, parts, tile)
        sine, cosine = waves(dist_sq, inverse)
        fade = jnp.maximum(1.0 - dist_sq * (1.0 / CUT_SQUARE), 0.0)
        radial = fade * fade * inverse
        on_sine = -inverse * ((4.0 / CUT_SQUARE) * fade + radial * inverse)
        on_cosine = (math.pi / CELL_SIDE) * (inverse * radial)
        scale = ROOT_THREE * inverse
        scaled = scale * radial
        square = inverse * inverse
        double = 2.0 * cosine
        before_s, now_s, before_c, now_c = None, sine, None, cosine
        for n in range(plan.nbasis):
            if n == 1:
                before_s, now_s = now_s, double * now_s
                before_c, now_c = now_c, double * now_c - 1.0
            elif n > 1:
                before_s, now_s = now_s, double * now_s - before_s
                before_c, now_c = now_c, double * now_c - before_c
            slope = on_sine * now_s + (n + 1.0) * on_cosine * now_c
            factor = scaled * now_s
            slope_ref[n, :, lanes] = slope
            radial_ref[n, :, lanes] = factor
            turned_ref[n, :, lanes] = scale * slope - square * factor


def energy_kernel(plan, *refs):
    (all_ref, adjoint_ref, slope_ref, radial_ref, cols_ref, layer_ref), refs = refs[:6], refs[6:]
    (before_ref, out_ref, one_ref, kept_ref), refs = refs[:4], refs[4:]
    again_ref, pair_ref, energy_ref, features_ref = refs
    slots, nbasis = plan.slots, plan.nbasis
    again_ref[...] = adjoint_ref[...]
    features_ref[...] = kept_ref[...]
    before = before_ref[...]
    live = jnp.where(lax.broadcasted_iota(jnp.int32, (slots, 8), 1) == 0, cols_ref[0, :, 3:4], 0.0)
    live_row = dot(jnp.ones((1, 8), BF16), live.astype(BF16), NT)
    energy = dot_exact(one_ref[...], layer_ref[0].astype(F32), NT)
    energy = energy + dot_exact(out_ref[...], before * sigmoid(before), NT)
    energy_ref[...] = energy * live_row
    adjoint = adjoint_ref[0].astype(F32) * MSG_SCALE
    weighted = jnp.concatenate(
        [(adjoint * radial_ref[n : n + 1]).astype(BF16) for n in range(nbasis)], axis=0
    )
    for tile in range(len(plan.tiles)):
        lanes = slice(tile * plan.width, (tile + 1) * plan.width)
        pulled = dot(weighted, all_ref[lanes], NT)
        total = slope_ref[0, :, lanes] * pulled[:slots]
        for n in range(1, nbasis):
            total = total + slope_ref[n, :, lanes] * pulled[n * slots : (n + 1) * slots]
        pair_ref[:, lanes] = total


def force_kernel(plan, nrefs, places, *refs):
    far_refs, refs = refs[:nrefs], refs[nrefs:]
    (own_ref, basis_ref, pair_ref, rows_ref), refs = refs[:4], refs[4:]
    (apart_ref, slope_ref, factor_ref, turned_ref), refs = refs[:4], refs[4:]
    (radial_ref, mixing_ref, mix_ref, vector_ref, table_ref), refs = refs[:5], refs[5:]
    out_ref, all_ref = refs
    slots, nbasis, nspec, width = plan.slots, plan.nbasis, plan.nspec, plan.width
    gather_far(plan, places, far_refs, all_ref)
    summed = dot(basis_ref[0].reshape(nbasis * slots, plan.far), all_ref[...])
    adjoint = jnp.zeros((slots, summed.shape[1]), F32)
    for n in range(nbasis):
        adjoint = adjoint + summed[n * slots : (n + 1) * slots] * radial_ref[n : n + 1]
    adjoint = own_ref[...] + MSG_SCALE * adjoint
    mixing = mixing_ref[...]
    gate = sigmoid(mixing)
    back = (adjoint * (gate * (1.0 + mixing * (1.0 - gate)))).astype(BF16)
    invariants = dot(back, mix_ref[...])
    channels = invariants.shape[1] // 2
    on_scalar = (MSG_SCALE * invariants[:, :channels]).astype(BF16)
    doubled = (2.0 * MSG_SCALE) * invariants[:, channels:]
    on_vector = (vector_ref[...] * jnp.concatenate([doubled] * 3, axis=0)).astype(BF16)
    weights = jnp.concatenate(
        [dot(on_scalar, table_ref[0], NT), dot(on_vector, table_ref[1], NT)], axis=0
    ).astype(BF16)
    group = lax.broadcasted_iota(jnp.int32, weights.shape, 1) // nspec
    weights = weights.astype(F32)
    weights = jnp.concatenate(
        [jnp.where(group == n, weights, 0.0).astype(BF16) for n in range(nbasis)], axis=0
    )
    species = lax.broadcasted_iota(jnp.int32, (nbasis * nspec, width), 0) % nspec
    own = [jnp.zeros((slots, width), F32) for _ in range(3)]
    pulls = []
    for tile in range(len(plan.tiles)):
        lanes = slice(tile * width, (tile + 1) * width)
        hot = (rows_ref[tile, 3:4].astype(jnp.int32) == species).astype(F32).astype(BF16)
        spread = dot(weights, hot)
        total = pair_ref[:, lanes]
        sides, turns = [None] * 3, [None] * 3
        for n in range(nbasis):
            start = n * 4 * slots
            total = total + slope_ref[n, :, lanes] * spread[start : start + slots]
            for k in range(3):
                piece = spread[start + (k + 1) * slots : start + (k + 2) * slots]
                side = factor_ref[n, :, lanes] * piece
                turn = turned_ref[n, :, lanes] * piece
                sides[k] = side if n == 0 else sides[k] + side
                turns[k] = turn if n == 0 else turns[k] + turn
        for k in range(3):
            total = total + apart_ref[k, :, lanes] * turns[k]
        pulls.append([])
        for k in range(3):
            pull = apart_ref[k, :, lanes] * total + sides[k]
            own[k] = own[k] + pull
            pulls[-1].append(jnp.sum(pull, axis=0, keepdims=True))
    own = jnp.concatenate(own, axis=0)
    high = own.astype(BF16)
    low = (own - high.astype(F32)).astype(BF16)
    ones = jnp.ones((8, width), BF16)
    mine = (dot(ones, high, NT) + dot(ones, low, NT))[:1]
    mine = jnp.concatenate([mine[:, k * slots : (k + 1) * slots] for k in range(3)], axis=0)
    if plan.small:
        out_ref[...] = jnp.zeros_like(out_ref)
    side_of = lax.broadcasted_iota(jnp.int32, (3, width), 1) // slots
    for tile in range(len(plan.tiles)):
        pulled = jnp.concatenate(pulls[tile], axis=0)
        if tile == 0:
            others = [jnp.zeros_like(mine)] * (len(plan.sides) - 1)
            pulled = pulled - jnp.concatenate([mine] + others, axis=1)
        if not plan.small:
            out_ref[plan.staged_place(places, tile)] = pulled
            continue
        for side in range(len(plan.sides)):
            place = plan.global_id(plan.offset(tile, side))
            out_ref[place, :3] = jnp.where(side_of == side, pulled, 0.0)


def begin(pairs, sems):
    copies = [pltpu.make_async_copy(*pair, sems.at[m]) for m, pair in enumerate(pairs)]
    for copy in copies:
        copy.start()
    return copies


def prepare_kernel(plan, counts_ref, *refs):
    fetched, sent_ref, table_ref, refs = refs[:10], refs[10], refs[11], refs[12:]
    kept, (place_ref, kind_ref, radial_ref, sems) = refs[:7], refs[7:]
    copies = begin(zip(fetched, (place_ref, kind_ref, radial_ref, *kept)), sems)
    for copy in copies[:2]:
        copy.wait()
    live = lax.broadcasted_iota(jnp.int32, (1, plan.slots), 1) < counts_ref[0]
    rows = [
        jnp.where(live, place_ref[0], FAR),
        place_ref[1],
        place_ref[2],
        jnp.where(live, kind_ref[...], -1).astype(F32),
    ]
    rows = jnp.concatenate(rows, axis=0)
    rows = jnp.concatenate([rows, rows], axis=1)
    for copy in range(sent_ref.shape[0]):
        sent_ref[copy] = rows
    for copy in copies[2:]:
        copy.wait()
    embed, nspec = kept[0][...].astype(F32), plan.nspec
    for g in range(2):
        for n in range(plan.nbasis):
            weighted = radial_ref[g, n : n + 1] * embed
            table_ref[g, n * nspec : (n + 1) * nspec] = weighted.astype(BF16)


def sum_kernel(plan, parts_ref, force_ref):
    total = parts_ref[0]
    for part in range(1, parts_ref.shape[0]):
        total = total + parts_ref[part]
    total = total[:, : plan.slots] + total[:, plan.slots :]
    for k in range(3):
        force_ref[k] = -total[k : k + 1]


VMEM_SPEC = pl.BlockSpec(memory_space=pltpu.VMEM)
SMEM_SPEC = pl.BlockSpec(memory_space=pltpu.SMEM)
HBM_SPEC = pl.BlockSpec(memory_space=pltpu.HBM)


def simple_call(kernel, plan, operands, outs, scalars=0, scratch=(), flops=2**20, near=False, fetched=0):
    single = not isinstance(outs, list)
    kind = pltpu.VMEM if near else jax.ShapeDtypeStruct
    shapes = [kind(*out) for out in ([outs] if single else outs)]

    def body(*refs):
        kernel(plan, *refs)

    got = pl.pallas_call(
        body,
        out_shape=shapes,
        in_specs=[SMEM_SPEC] * scalars
        + [VMEM_SPEC] * (len(operands) - scalars - fetched)
        + [HBM_SPEC] * fetched,
        out_specs=[VMEM_SPEC] * len(shapes),
        scratch_shapes=[pltpu.VMEM(*buffer) for buffer in scratch]
        + [pltpu.SemaphoreType.DMA((fetched,))] * (fetched > 0),
        compiler_params=pltpu.CompilerParams(vmem_limit_bytes=FETCH_LIMIT if fetched else VMEM_LIMIT),
        cost_estimate=pl.CostEstimate(flops=flops, bytes_accessed=2**20, transcendentals=0),
    )(*operands)
    return got[0] if single else got


def call(kernel, plan, far, operands, outs, scratch, flops, **options):
    def body(plan, *refs):
        kernel(plan, len(far), plan.places(), *refs)

    return simple_call(body, plan, [*far, *operands], outs, 0, scratch, flops, **options)


def swaps(count):
    if count == 2:
        return [[1, 0]]
    if paired(count):
        near = [i ^ 1 for i in range(count)]
        far = [(i - 1 + 2 * (i % 2)) % count for i in range(count)]
        return [near, far]
    return [[(i + o) % count for i in range(count)] for o in offsets_of(count)[1:]]


def brought(plan, block, second, mixed):
    sizes, sources = plan.sizes, {axis: swaps(plan.sizes[axis]) for axis in AXES}
    got = []
    for m in range(len(sources["gx" if second else "gz"])):
        pairs = []
        for x, y, z in itertools.product(*(range(sizes[axis]) for axis in AXES)):
            along_x = second != (mixed and y % 2 == 1)
            source = (sources["gx"][m][x], y, z) if along_x else (x, y, sources["gz"][m][z])
            pairs.append((flat(sizes, *source), flat(sizes, x, y, z)))
        got.append(lax.ppermute(block, AXES, pairs))
    return got


def flat(sizes, x, y, z):
    return (x * sizes["gy"] + y) * sizes["gz"] + z


def along(block, axis):
    return [
        lax.ppermute(block, axis, [(source, i) for i, source in enumerate(sources)])
        for sources in swaps(lax.axis_size(axis))
    ]


def neighbours(plan, block, again=None):
    column = jnp.stack([block if again is None else again] + brought(plan, block, False, plan.mixed))
    return from_columns(plan, column, plan.mixed)


def from_columns(plan, column, mixed, again=None):
    columns = [column] + brought(plan, column, True, mixed)
    if again is not None:
        columns[0] = again
    swapped = [[column] + along(column, "gy") for column in columns]
    return [column[side] for side in range(len(plan.sides)) for column in swapped]


def everywhere(copies):
    return lax.all_to_all(copies, AXES, 0, 0, tiled=True)


def folded(pieces, axis):
    total = pieces[0]
    for piece, sources in zip(pieces[1:], swaps(lax.axis_size(axis))):
        total = total + lax.ppermute(piece, axis, list(enumerate(sources)))
    return total


def fold(plan, pulls):
    for axis in ("gx", "gz"):
        parts = len(offsets_of(plan.sizes[axis]))
        pulls = pulls.reshape((parts, -1) + pulls.shape[1:])
        pulls = folded([pulls[m] for m in range(parts)], axis)
    pulls = pulls[0]
    sides = [pulls[:, m * plan.slots : (m + 1) * plan.slots] for m in range(len(plan.sides))]
    return folded(sides, "gy")


def local_program(mesh):
    def local(
        positions,
        species,
        counts,
        embed,
        radial_one,
        mix_one,
        read_one,
        radial_two,
        mix_two,
        read_hidden,
        read_out,
    ):
        slots, channels = positions.shape[-1], embed.shape[1]
        nbasis, nspec = radial_two.shape[0], embed.shape[0]
        plan = Plan(mesh, slots, nbasis, nspec)
        given = [positions[0, 0, 0].reshape(3, 1, slots), species.reshape(1, slots), radial_one]
        weights = [embed, mix_one, radial_two, read_out[None], read_one[None], mix_two, read_hidden]
        sent, table, *weights = simple_call(
            prepare_kernel,
            plan,
            [counts.reshape(1), *given, *weights],
            [
                ((plan.ndev if plan.small else 1, 4, 2 * slots), F32),
                ((2, nbasis * nspec, channels), BF16),
            ]
            + [(weight.shape, weight.dtype) for weight in weights],
            1,
            [(array.shape, array.dtype) for array in given],
            near=True,
            fetched=len(given) + len(weights),
        )
        embed, mix_one, radial_two, out_row, one_row, mix_two, read_hidden = weights
        far_sent = [everywhere(sent)] if plan.small else neighbours(plan, sent[0])
        pair_flops = 100 * slots * plan.far
        rows, basis, layer, vector, mixing, cols = call(
            first_kernel,
            plan,
            far_sent,
            [table, embed, mix_one],
            [
                ((len(plan.tiles), 4, plan.width), F32),
                ((plan.known, nbasis, slots, plan.far), BF16),
                ((len(plan.column), slots, channels), BF16),
                ((3 * slots, channels), F32),
                ((slots, channels), F32),
                ((plan.known, slots, 8), F32),
            ],
            [
                ((len(plan.column), nbasis, 4 * slots, plan.far), BF16),
                ((len(plan.tiles) * len(plan.sides), 4, 2 * slots), F32),
            ],
            pair_flops,
        )
        again, apart, slope, factor, turned = simple_call(
            slope_kernel,
            plan,
            [rows, cols, layer],
            [(layer.shape, BF16)]
            + [((count, slots, plan.far), F32) for count in (3, nbasis, nbasis, nbasis)],
            flops=pair_flops,
        )
        if plan.small:
            far_layer = from_columns(plan, layer, False, again)
        else:
            far_layer = neighbours(plan, layer[0], again[0])
        far_scratch = ((plan.far, channels), BF16)
        adjoint, kept, before, own_adjoint, own_far = call(
            second_kernel,
            plan,
            far_layer,
            [layer, basis, cols, radial_two, mix_two, read_hidden, out_row, one_row],
            [
                ((plan.known, slots, channels), BF16),
                ((slots, channels), BF16),
                ((slots, read_hidden.shape[0]), F32),
                ((slots, channels), F32),
                far_scratch,
            ],
            [((max(plan.known - 1, 1), plan.far, channels), BF16)],
            pair_flops,
        )
        again, pair, energy, features = simple_call(
            energy_kernel,
            plan,
            [own_far, adjoint, slope, radial_two, cols, layer, before, out_row, one_row, kept],
            [
                (adjoint.shape, BF16),
                ((slots, plan.far), F32),
                ((1, slots), F32),
                ((slots, channels), BF16),
            ],
            flops=pair_flops,
        )
        if plan.small:
            far_adjoint = from_columns(plan, adjoint, False, again)
        else:
            far_adjoint = neighbours(plan, adjoint[0], again[0])
        pulls = call(
            force_kernel,
            plan,
            far_adjoint,
            [own_adjoint, basis, pair, rows, apart, slope, factor, turned]
            + [radial_two, mixing, mix_one, vector, table],
            [((plan.ndev, 4, plan.width) if plan.small else (len(plan.tiles), 3, plan.width), F32)],
            [far_scratch],
            pair_flops,
        )
        if plan.small:
            forces = simple_call(sum_kernel, plan, [everywhere(pulls[0])], ((3, 1, slots), F32))
        else:
            forces = -fold(plan, pulls[0])
        return (
            forces.reshape(1, 1, 1, 3, slots),
            energy[None, None],
            features.T[None, None, None],
        )

    return local


def solution(mesh):
    split = [P(*AXES, None, None), P(*AXES, None), P(*AXES)]
    out_specs = (P(*AXES, None, None), P(*AXES, None), P(*AXES, None, None))
    return jax.shard_map(
        local_program(mesh),
        mesh=mesh,
        in_specs=tuple(split + [P()] * 8),
        out_specs=out_specs,
        check_vma=False,
    )
```

```python
import itertools
import math

import jax
import jax.numpy as jnp
from jax import lax
from jax.experimental import pallas as pl
from jax.experimental.pallas import tpu as pltpu
from jax.sharding import PartitionSpec as P

CELL_SIDE = 5.0
CUT_SQUARE = 25.0
SOFTEN = 0.25
MSG_SCALE = 0.05
ROOT_THREE = math.sqrt(3.0)
FAR = 1.0e4
AXES = ("gx", "gy", "gz")
F32 = jnp.float32
BF16 = jnp.bfloat16
COS_TERMS = (
    0.9999999532476085,
    -4.934792830619644,
    4.058411352862619,
    -1.3318765680811142,
    0.2196896110983216,
)
SIN_TERMS = (
    3.1415926401307073,
    -5.167710083507891,
    2.550077523214631,
    -0.5982912856208596,
    0.07765766030668693,
)
VMEM_LIMIT = 24 * 1024 * 1024
FETCH_LIMIT = 60 * 1024 * 1024
NT = (((1,), (1,)), ((), ()))
NN = (((1,), (0,)), ((), ()))


def dot(a, b, dims=NN):
    return lax.dot_general(a, b, dims, preferred_element_type=F32)


def dot_exact(a, b, dims=NN):
    return lax.dot_general(
        a, b, dims, precision=lax.Precision.HIGHEST, preferred_element_type=F32
    )


def split_dot(a, b):
    high = a.astype(BF16)
    low = (a - high.astype(F32)).astype(BF16)
    return dot(high, b) + dot(low, b)


def offsets_of(count):
    return (0, 1) if count == 2 else (0, 1, -1)


def paired(count):
    return count > 2 and count % 2 == 0


def matched(which, parity):
    return jnp.int32(0) if which == 0 else 1 + (parity if which == 1 else 1 - parity)


def poly(terms, arg):
    total = arg * terms[-1] + terms[-2]
    for term in terms[-3::-1]:
        total = total * arg + term
    return total


class Plan:
    def __init__(self, mesh, slots, nbasis, nspec):
        self.sizes = {axis: mesh.shape[axis] for axis in AXES}
        self.ndev = math.prod(self.sizes.values())
        self.tiles = list(
            itertools.product(offsets_of(self.sizes["gx"]), offsets_of(self.sizes["gz"]))
        )
        self.sides = offsets_of(self.sizes["gy"])
        self.slots = slots
        self.width = len(self.sides) * slots
        self.far = len(self.tiles) * self.width
        self.nbasis = nbasis
        self.nspec = nspec
        self.depth = len(offsets_of(self.sizes["gz"]))
        self.wide = len(offsets_of(self.sizes["gx"]))
        self.brought = list(itertools.product(range(self.wide), range(self.depth)))
        self.mixed = self.depth == self.wide and self.sizes["gy"] % 2 == 0
        self.small = self.ndev <= 64 and len(self.sides) == 2
        near = offsets_of(self.sizes["gz"])
        self.column = list(near) if self.small else [0]
        for step in [a + b for a in near for b in near] if self.small else []:
            if all((step - known) % self.sizes["gz"] for known in self.column):
                self.column.append(step)
        self.known = self.depth if self.small else 1
        self.wrapped = [self.sizes[axis] == 2 for axis in AXES]
        self.plain = [k for k in range(3) if not self.wrapped[k]]
        self.folded = [k for k in range(3) if self.wrapped[k]]
        self.kinds = 2 + len(self.folded)

    def global_id(self, offset):
        place = 0
        for axis, step in zip(AXES, offset):
            count = self.sizes[axis]
            place = place * count + lax.rem(lax.axis_index(axis) + (step + count), count)
        return place

    def column_place(self, step):
        return [(step - known) % self.sizes["gz"] == 0 for known in self.column].index(True)

    def places(self):
        index = {axis: lax.axis_index(axis) for axis in AXES}

        def parity(axis):
            return lax.rem(index[axis], 2) if paired(self.sizes[axis]) else jnp.int32(0)

        turns = parity("gx"), parity("gz")
        core = lax.rem(index["gy"], 2) if self.mixed else jnp.int32(0)
        found = []
        for side in range(len(self.sides)):
            x_first = core if side == 0 or not self.mixed else 1 - core
            for second, first in self.brought:
                plain = matched(second, turns[0]) * self.depth + matched(first, turns[1])
                crossed = matched(first, turns[0]) * self.depth + matched(second, turns[1])
                tile = jnp.where(x_first == 1, crossed, plain) if self.mixed else plain
                found.append(tile * len(self.sides) + side)
        found += turns
        return [jnp.asarray(place, jnp.int32) for place in found]

    def brought_place(self, places, side, pair):
        return places[side * len(self.brought) + pair]

    def staged_place(self, places, tile):
        start = len(self.sides) * len(self.brought)
        x, z = divmod(tile, self.depth)
        return matched(x, places[start]) * self.depth + matched(z, places[start + 1])

    def offset(self, tile, side):
        ox, oz = self.tiles[tile]
        return (ox, self.sides[side], oz)


def scaled(terms, factor):
    return [factor * term for term in terms]


def separations(plan, rows, cols, side=CELL_SIDE):
    parts = []
    for axis in range(3):
        diff = rows[axis] - cols[axis]
        if plan.wrapped[axis]:
            diff = jnp.where(diff > side, diff - 2.0 * side, diff)
        parts.append(diff)
    return parts


def distance(plan, parts, tile, soften=SOFTEN):
    dist_sq = parts[0] * parts[0] + parts[1] * parts[1] + parts[2] * parts[2] + soften
    if tile == 0:
        row = lax.broadcasted_iota(jnp.int32, dist_sq.shape, 0)
        col = lax.broadcasted_iota(jnp.int32, dist_sq.shape, 1)
        dist_sq = jnp.where(row == col, FAR, dist_sq)
    return dist_sq, lax.rsqrt(dist_sq)


def waves(dist_sq, inverse):
    arg = jnp.minimum(dist_sq * inverse * (1.0 / CELL_SIDE) - 0.5, 0.5)
    square = arg * arg
    return poly(COS_TERMS, square), -(arg * poly(SIN_TERMS, square))


def first_kernel(plan, nrefs, places, *refs):
    far_refs, refs = refs[:nrefs], refs[nrefs:]
    (table_ref, wide_ref, embed_ref, mix_ref), refs = refs[:4], refs[4:]
    rows_ref, basis_ref, layer_ref, vector_ref, mixing_ref, cols_ref, pair_ref, block_ref = refs
    slots, nbasis, nspec = plan.slots, plan.nbasis, plan.nspec

    def put(place, block):
        block_ref[place] = block

    if not plan.small:
        scatter(plan, places, far_refs, put)

    def block_of(tile, side, up):
        if plan.small:
            x, y, z = plan.offset(tile, side)
            return far_refs[0][plan.global_id((x, y, z + up))]
        return block_ref[tile * len(plan.sides) + side]

    species = lax.broadcasted_iota(jnp.int32, (nbasis * nspec, plan.width), 0) % nspec
    shifts = [tile_shift(plan, tile) for tile in range(len(plan.tiles))]
    own, counted, places_of = [], [], []
    for which, up in enumerate(plan.column):
        held = block_of(0, 0, up)
        held = jnp.concatenate([held, held], axis=0).T[:slots]
        kind = held[:, 3:4]
        own.append(kind)
        lane = lax.broadcasted_iota(jnp.int32, held.shape, 1)
        live = kind >= 0.0
        held = jnp.where((lane == 0) & ~live, -FAR, held)
        if which < plan.known:
            cols_ref[which] = jnp.where(lane == 3, live.astype(F32), held)
        cols = [held[:, axis : axis + 1] * (1.0 / CELL_SIDE) for axis in range(3)]
        places_of.append(cols)
        hot = []
        for tile in range(len(plan.tiles)):
            blocks = [block_of(tile, side, up) for side in range(len(plan.sides))]
            placed = side_by_side(plan, blocks) + shifts[tile]
            if which == 0:
                rows_ref[tile] = placed
            is_kind = placed[3:4].astype(jnp.int32) == species
            placed = placed * (1.0 / CELL_SIDE)
            high = placed.astype(BF16).astype(F32)
            low = placed - high
            columns = [jnp.where(is_kind, 1.0, 0.0)]
            for k in plan.plain:
                columns += [jnp.where(is_kind, part[k : k + 1], 0.0) for part in (high, low)]
            hot.append(jnp.concatenate([column.astype(BF16) for column in columns], axis=0))
            parts = separations(plan, [placed[k : k + 1] for k in range(3)], cols, 1.0)
            dist_sq, inverse = distance(plan, parts, tile, SOFTEN / CUT_SQUARE)
            turn = jnp.minimum(dist_sq * inverse - 0.5, 0.5)
            square = turn * turn
            double = turn * poly(scaled(SIN_TERMS, -2.0), square)
            fade = jnp.maximum(1.0 - dist_sq, 0.0)
            before, now = None, poly(scaled(COS_TERMS, 1.0 / CELL_SIDE), square) * (fade * fade * inverse)
            scale = inverse * ROOT_THREE
            units = [scale.astype(BF16)] + [(scale * parts[k]).astype(BF16) for k in plan.folded]
            lanes = slice(tile * plan.width, (tile + 1) * plan.width)
            for n in range(nbasis):
                if n == 1:
                    before, now = now, double * now
                elif n > 1:
                    before, now = now, double * now - before
                packed = now.astype(BF16)
                if which < plan.known:
                    basis_ref[which, n, :, lanes] = packed
                pair_ref[which, n, :slots, lanes] = packed
                for m, unit in enumerate(units):
                    pair_ref[which, n, (m + 1) * slots : (m + 2) * slots, lanes] = unit * packed
        hot = jnp.concatenate(hot, axis=1)
        gathered = dot(pair_ref[which].reshape(nbasis * plan.kinds * slots, plan.far), hot, NT)
        gathered = gathered.reshape(nbasis, plan.kinds * slots, hot.shape[0])
        group = lax.broadcasted_iota(jnp.int32, gathered.shape[1:], 1) % (nbasis * nspec) // nspec
        total = gathered[0]
        for n in range(1, nbasis):
            total = jnp.where(group == n, gathered[n], total)
        counted.append(total)
    scalar = jnp.concatenate([total[:slots, : nbasis * nspec] for total in counted], axis=0)
    scalar = MSG_SCALE * split_dot(scalar, table_ref[0])
    moved = jnp.concatenate([total[slots : 2 * slots] for total in counted], axis=0)
    moved = MSG_SCALE * split_dot(moved, wide_ref[...])
    channels = layer_ref.shape[2]
    norm = None
    for k in range(3):
        if k in plan.plain:
            start = (plan.plain.index(k) + 1) * channels
            place = jnp.concatenate([cols[k] for cols in places_of], axis=0)
            vector = moved[:, start : start + channels] - place * moved[:, :channels]
        else:
            start = (plan.folded.index(k) + 2) * slots
            vector = [total[start : start + slots, : nbasis * nspec] for total in counted]
            vector = MSG_SCALE * split_dot(jnp.concatenate(vector, axis=0), table_ref[1])
        vector_ref[k * slots : (k + 1) * slots] = vector[:slots]
        norm = vector * vector if k == 0 else norm + vector * vector
    invariants = jnp.concatenate([scalar.astype(BF16), norm.astype(BF16)], axis=1)
    mixing = dot(invariants, mix_ref[...], NT)
    mixing_ref[...] = mixing[:slots]
    kind = jnp.concatenate(own, axis=0)
    own_species = lax.broadcasted_iota(jnp.int32, (kind.shape[0], nspec), 1)
    own_hot = (kind.astype(jnp.int32) == own_species).astype(F32).astype(BF16)
    layer = (dot(own_hot, embed_ref[...]) + mixing * sigmoid(mixing)).astype(BF16)
    for which in range(layer_ref.shape[0]):
        layer_ref[which] = layer[which * slots : (which + 1) * slots]


def sigmoid(value):
    return 1.0 / (1.0 + jnp.exp(-value))


def scatter(plan, places, far_refs, put, up=0):
    for side in range(len(plan.sides)):
        for pair, (second, first) in enumerate(plan.brought):
            column = far_refs[side * plan.wide + second]
            if not plan.small:
                put(plan.brought_place(places, side, pair), column[first])
                continue
            turn = places[len(plan.sides) * len(plan.brought)]
            tile = matched(second, turn) * plan.depth + first
            step = offsets_of(plan.sizes["gz"])[first] + up
            put(tile * len(plan.sides) + side, column[plan.column_place(step)])


def side_by_side(plan, blocks):
    if len(blocks) == 2:
        lane = lax.broadcasted_iota(jnp.int32, blocks[0].shape, 1)
        return jnp.where(lane < plan.slots, blocks[0], blocks[1])
    return jnp.concatenate([block[:, : plan.slots] for block in blocks], axis=1)


def tile_shift(plan, tile):
    row = lax.broadcasted_iota(jnp.int32, (4, plan.width), 0)
    side = lax.broadcasted_iota(jnp.int32, (4, plan.width), 1) // plan.slots
    shift = jnp.zeros((4, plan.width), F32)
    for s in range(len(plan.sides)):
        for k, steps in enumerate(plan.offset(tile, s)):
            if steps:
                shift = jnp.where((row == k) & (side == s), CELL_SIDE * steps, shift)
    return shift


def gather_far(plan, places, far_refs, all_ref, up=0):
    def put(place, block):
        start = pl.multiple_of(place * plan.slots, plan.slots)
        all_ref[pl.ds(start, plan.slots)] = block

    scatter(plan, places, far_refs, put, up)


def second_kernel(plan, nrefs, places, *refs):
    far_refs, refs = refs[:nrefs], refs[nrefs:]
    (layer_ref, basis_ref, cols_ref, radial_ref, mix_ref), refs = refs[:5], refs[5:]
    (hidden_ref, out_ref, one_ref), refs = refs[:3], refs[3:]
    adjoint_ref, features_ref, before_ref, own_ref, own_far_ref, all_ref = refs
    slots, nbasis, known = plan.slots, plan.nbasis, plan.known
    messages = []
    for which in range(known):
        target = own_far_ref if which == 0 else all_ref.at[which - 1]
        gather_far(plan, places, far_refs, target, plan.column[which])
        summed = dot(basis_ref[which].reshape(nbasis * slots, plan.far), target[...])
        message = summed[:slots] * radial_ref[0:1]
        for n in range(1, nbasis):
            message = message + summed[n * slots : (n + 1) * slots] * radial_ref[n : n + 1]
        messages.append((MSG_SCALE * message).astype(BF16))
    mixing = dot(jnp.concatenate(messages, axis=0), mix_ref[...], NT)
    gate = sigmoid(mixing)
    layer = layer_ref[:known].reshape(known * slots, -1).astype(F32)
    features = (layer + mixing * gate).astype(BF16)
    features_ref[...] = features[:slots]
    before = dot(features, hidden_ref[...], NT)
    before_ref[...] = before[:slots]
    open_hidden = sigmoid(before)
    live = cols_ref[...].reshape(known * slots, 8)[:, 3:4]
    slope = out_ref[...] * (open_hidden * (1.0 + before * (1.0 - open_hidden))) * live
    from_hidden = dot(slope.astype(BF16), hidden_ref[...])
    own_ref[...] = from_hidden[:slots] + one_ref[...] * live[:slots]
    back = from_hidden * (gate * (1.0 + mixing * (1.0 - gate)))
    adjoint = dot(back.astype(BF16), mix_ref[...]).astype(BF16)
    for which in range(known):
        adjoint_ref[which] = adjoint[which * slots : (which + 1) * slots]


def slope_kernel(plan, rows_ref, cols_ref, layer_ref, *refs):
    again_ref, apart_ref, slope_ref, radial_ref, turned_ref = refs
    again_ref[...] = layer_ref[...]
    cols = [cols_ref[0, :, axis : axis + 1] for axis in range(3)]
    for tile in range(len(plan.tiles)):
        lanes = slice(tile * plan.width, (tile + 1) * plan.width)
        parts = separations(plan, [rows_ref[tile, k : k + 1] for k in range(3)], cols)
        for k in range(3):
            apart_ref[k, :, lanes] = parts[k]
        dist_sq, inverse = distance(plan, parts, tile)
        sine, cosine = waves(dist_sq, inverse)
        fade = jnp.maximum(1.0 - dist_sq * (1.0 / CUT_SQUARE), 0.0)
        radial = fade * fade * inverse
        on_sine = -inverse * ((4.0 / CUT_SQUARE) * fade + radial * inverse)
        on_cosine = (math.pi / CELL_SIDE) * (inverse * radial)
        scale = ROOT_THREE * inverse
        scaled = scale * radial
        square = inverse * inverse
        double = 2.0 * cosine
        before_s, now_s, before_c, now_c = None, sine, None, cosine
        for n in range(plan.nbasis):
            if n == 1:
                before_s, now_s = now_s, double * now_s
                before_c, now_c = now_c, double * now_c - 1.0
            elif n > 1:
                before_s, now_s = now_s, double * now_s - before_s
                before_c, now_c = now_c, double * now_c - before_c
            slope = on_sine * now_s + (n + 1.0) * on_cosine * now_c
            factor = scaled * now_s
            slope_ref[n, :, lanes] = slope
            radial_ref[n, :, lanes] = factor
            turned_ref[n, :, lanes] = scale * slope - square * factor


def energy_kernel(plan, *refs):
    (all_ref, adjoint_ref, slope_ref, radial_ref, cols_ref, layer_ref), refs = refs[:6], refs[6:]
    (before_ref, out_ref, one_ref, kept_ref), refs = refs[:4], refs[4:]
    again_ref, pair_ref, energy_ref, features_ref = refs
    slots, nbasis = plan.slots, plan.nbasis
    again_ref[...] = adjoint_ref[...]
    features_ref[...] = kept_ref[...]
    before = before_ref[...]
    live = jnp.where(lax.broadcasted_iota(jnp.int32, (slots, 8), 1) == 0, cols_ref[0, :, 3:4], 0.0)
    live_row = dot(jnp.ones((1, 8), BF16), live.astype(BF16), NT)
    energy = dot_exact(one_ref[...], layer_ref[0].astype(F32), NT)
    energy = energy + dot_exact(out_ref[...], before * sigmoid(before), NT)
    energy_ref[...] = energy * live_row
    adjoint = adjoint_ref[0].astype(F32) * MSG_SCALE
    weighted = jnp.concatenate(
        [(adjoint * radial_ref[n : n + 1]).astype(BF16) for n in range(nbasis)], axis=0
    )
    for tile in range(len(plan.tiles)):
        lanes = slice(tile * plan.width, (tile + 1) * plan.width)
        pulled = dot(weighted, all_ref[lanes], NT)
        total = slope_ref[0, :, lanes] * pulled[:slots]
        for n in range(1, nbasis):
            total = total + slope_ref[n, :, lanes] * pulled[n * slots : (n + 1) * slots]
        pair_ref[:, lanes] = total


def force_kernel(plan, nrefs, places, *refs):
    far_refs, refs = refs[:nrefs], refs[nrefs:]
    (own_ref, basis_ref, pair_ref, rows_ref), refs = refs[:4], refs[4:]
    (apart_ref, slope_ref, factor_ref, turned_ref), refs = refs[:4], refs[4:]
    (radial_ref, mixing_ref, mix_ref, vector_ref, table_ref), refs = refs[:5], refs[5:]
    out_ref, all_ref = refs
    slots, nbasis, nspec, width = plan.slots, plan.nbasis, plan.nspec, plan.width
    gather_far(plan, places, far_refs, all_ref)
    summed = dot(basis_ref[0].reshape(nbasis * slots, plan.far), all_ref[...])
    adjoint = jnp.zeros((slots, summed.shape[1]), F32)
    for n in range(nbasis):
        adjoint = adjoint + summed[n * slots : (n + 1) * slots] * radial_ref[n : n + 1]
    adjoint = own_ref[...] + MSG_SCALE * adjoint
    mixing = mixing_ref[...]
    gate = sigmoid(mixing)
    back = (adjoint * (gate * (1.0 + mixing * (1.0 - gate)))).astype(BF16)
    invariants = dot(back, mix_ref[...])
    channels = invariants.shape[1] // 2
    on_scalar = (MSG_SCALE * invariants[:, :channels]).astype(BF16)
    doubled = (2.0 * MSG_SCALE) * invariants[:, channels:]
    on_vector = (vector_ref[...] * jnp.concatenate([doubled] * 3, axis=0)).astype(BF16)
    weights = jnp.concatenate(
        [dot(on_scalar, table_ref[0], NT), dot(on_vector, table_ref[1], NT)], axis=0
    ).astype(BF16)
    group = lax.broadcasted_iota(jnp.int32, weights.shape, 1) // nspec
    weights = weights.astype(F32)
    weights = jnp.concatenate(
        [jnp.where(group == n, weights, 0.0).astype(BF16) for n in range(nbasis)], axis=0
    )
    species = lax.broadcasted_iota(jnp.int32, (nbasis * nspec, width), 0) % nspec
    own = [jnp.zeros((slots, width), F32) for _ in range(3)]
    pulls = []
    for tile in range(len(plan.tiles)):
        lanes = slice(tile * width, (tile + 1) * width)
        hot = (rows_ref[tile, 3:4].astype(jnp.int32) == species).astype(F32).astype(BF16)
        spread = dot(weights, hot)
        total = pair_ref[:, lanes]
        sides, turns = [None] * 3, [None] * 3
        for n in range(nbasis):
            start = n * 4 * slots
            total = total + slope_ref[n, :, lanes] * spread[start : start + slots]
            for k in range(3):
                piece = spread[start + (k + 1) * slots : start + (k + 2) * slots]
                side = factor_ref[n, :, lanes] * piece
                turn = turned_ref[n, :, lanes] * piece
                sides[k] = side if n == 0 else sides[k] + side
                turns[k] = turn if n == 0 else turns[k] + turn
        for k in range(3):
            total = total + apart_ref[k, :, lanes] * turns[k]
        pulls.append([])
        for k in range(3):
            pull = apart_ref[k, :, lanes] * total + sides[k]
            own[k] = own[k] + pull
            pulls[-1].append(jnp.sum(pull, axis=0, keepdims=True))
    own = jnp.concatenate(own, axis=0)
    high = own.astype(BF16)
    low = (own - high.astype(F32)).astype(BF16)
    ones = jnp.ones((8, width), BF16)
    mine = (dot(ones, high, NT) + dot(ones, low, NT))[:1]
    mine = jnp.concatenate([mine[:, k * slots : (k + 1) * slots] for k in range(3)], axis=0)
    if plan.small:
        out_ref[...] = jnp.zeros_like(out_ref)
    side_of = lax.broadcasted_iota(jnp.int32, (3, width), 1) // slots
    for tile in range(len(plan.tiles)):
        pulled = jnp.concatenate(pulls[tile], axis=0)
        if tile == 0:
            others = [jnp.zeros_like(mine)] * (len(plan.sides) - 1)
            pulled = pulled - jnp.concatenate([mine] + others, axis=1)
        if not plan.small:
            out_ref[plan.staged_place(places, tile)] = pulled
            continue
        for side in range(len(plan.sides)):
            place = plan.global_id(plan.offset(tile, side))
            out_ref[place, :3] = jnp.where(side_of == side, pulled, 0.0)


def begin(pairs, sems):
    copies = [pltpu.make_async_copy(*pair, sems.at[m]) for m, pair in enumerate(pairs)]
    for copy in copies:
        copy.start()
    return copies


def prepare_kernel(plan, counts_ref, *refs):
    fetched, (sent_ref, table_ref, wide_ref), refs = refs[:10], refs[10:13], refs[13:]
    kept, (place_ref, kind_ref, radial_ref, sems) = refs[:7], refs[7:]
    copies = begin(zip(fetched, (place_ref, kind_ref, radial_ref, *kept)), sems)
    for copy in copies[:2]:
        copy.wait()
    live = lax.broadcasted_iota(jnp.int32, (1, plan.slots), 1) < counts_ref[0]
    rows = [
        jnp.where(live, place_ref[0], FAR),
        place_ref[1],
        place_ref[2],
        jnp.where(live, kind_ref[...], -1).astype(F32),
    ]
    rows = jnp.concatenate(rows, axis=0)
    rows = jnp.concatenate([rows, rows], axis=1)
    for copy in range(sent_ref.shape[0]):
        sent_ref[copy] = rows
    for copy in copies[2:]:
        copy.wait()
    embed, nspec = kept[0][...].astype(F32), plan.nspec
    for g in range(2):
        for n in range(plan.nbasis):
            weighted = radial_ref[g, n : n + 1] * embed
            table_ref[g, n * nspec : (n + 1) * nspec] = weighted.astype(BF16)
    wide_ref[...] = jnp.zeros_like(wide_ref)
    count, channels = table_ref.shape[1:]
    for m in range(1 + 2 * len(plan.plain)):
        start = (m + 1) // 2 * channels
        wide_ref[m * count : (m + 1) * count, start : start + channels] = table_ref[1]


def sum_kernel(plan, parts_ref, force_ref):
    total = parts_ref[0]
    for part in range(1, parts_ref.shape[0]):
        total = total + parts_ref[part]
    total = total[:, : plan.slots] + total[:, plan.slots :]
    for k in range(3):
        force_ref[k] = -total[k : k + 1]


VMEM_SPEC = pl.BlockSpec(memory_space=pltpu.VMEM)
SMEM_SPEC = pl.BlockSpec(memory_space=pltpu.SMEM)
HBM_SPEC = pl.BlockSpec(memory_space=pltpu.HBM)


def simple_call(kernel, plan, operands, outs, scalars=0, scratch=(), flops=2**20, near=False, fetched=0):
    single = not isinstance(outs, list)
    kind = pltpu.VMEM if near else jax.ShapeDtypeStruct
    shapes = [kind(*out) for out in ([outs] if single else outs)]

    def body(*refs):
        kernel(plan, *refs)

    got = pl.pallas_call(
        body,
        out_shape=shapes,
        in_specs=[SMEM_SPEC] * scalars
        + [VMEM_SPEC] * (len(operands) - scalars - fetched)
        + [HBM_SPEC] * fetched,
        out_specs=[VMEM_SPEC] * len(shapes),
        scratch_shapes=[pltpu.VMEM(*buffer) for buffer in scratch]
        + [pltpu.SemaphoreType.DMA((fetched,))] * (fetched > 0),
        compiler_params=pltpu.CompilerParams(vmem_limit_bytes=FETCH_LIMIT if fetched else VMEM_LIMIT),
        cost_estimate=pl.CostEstimate(flops=flops, bytes_accessed=2**20, transcendentals=0),
    )(*operands)
    return got[0] if single else got


def call(kernel, plan, far, operands, outs, scratch, flops, **options):
    def body(plan, *refs):
        kernel(plan, len(far), plan.places(), *refs)

    return simple_call(body, plan, [*far, *operands], outs, 0, scratch, flops, **options)


def swaps(count):
    if count == 2:
        return [[1, 0]]
    if paired(count):
        near = [i ^ 1 for i in range(count)]
        far = [(i - 1 + 2 * (i % 2)) % count for i in range(count)]
        return [near, far]
    return [[(i + o) % count for i in range(count)] for o in offsets_of(count)[1:]]


def brought(plan, block, second, mixed):
    sizes, sources = plan.sizes, {axis: swaps(plan.sizes[axis]) for axis in AXES}
    got = []
    for m in range(len(sources["gx" if second else "gz"])):
        pairs = []
        for x, y, z in itertools.product(*(range(sizes[axis]) for axis in AXES)):
            along_x = second != (mixed and y % 2 == 1)
            source = (sources["gx"][m][x], y, z) if along_x else (x, y, sources["gz"][m][z])
            pairs.append((flat(sizes, *source), flat(sizes, x, y, z)))
        got.append(lax.ppermute(block, AXES, pairs))
    return got


def flat(sizes, x, y, z):
    return (x * sizes["gy"] + y) * sizes["gz"] + z


def along(block, axis):
    return [
        lax.ppermute(block, axis, [(source, i) for i, source in enumerate(sources)])
        for sources in swaps(lax.axis_size(axis))
    ]


def neighbours(plan, block, again=None):
    column = jnp.stack([block if again is None else again] + brought(plan, block, False, plan.mixed))
    return from_columns(plan, column, plan.mixed)


def from_columns(plan, column, mixed, again=None):
    columns = [column] + brought(plan, column, True, mixed)
    if again is not None:
        columns[0] = again
    swapped = [[column] + along(column, "gy") for column in columns]
    return [column[side] for side in range(len(plan.sides)) for column in swapped]


def everywhere(copies):
    return lax.all_to_all(copies, AXES, 0, 0, tiled=True)


def folded(pieces, axis):
    total = pieces[0]
    for piece, sources in zip(pieces[1:], swaps(lax.axis_size(axis))):
        total = total + lax.ppermute(piece, axis, list(enumerate(sources)))
    return total


def fold(plan, pulls):
    for axis in ("gx", "gz"):
        parts = len(offsets_of(plan.sizes[axis]))
        pulls = pulls.reshape((parts, -1) + pulls.shape[1:])
        pulls = folded([pulls[m] for m in range(parts)], axis)
    pulls = pulls[0]
    sides = [pulls[:, m * plan.slots : (m + 1) * plan.slots] for m in range(len(plan.sides))]
    return folded(sides, "gy")


def local_program(mesh):
    def local(
        positions,
        species,
        counts,
        embed,
        radial_one,
        mix_one,
        read_one,
        radial_two,
        mix_two,
        read_hidden,
        read_out,
    ):
        slots, channels = positions.shape[-1], embed.shape[1]
        nbasis, nspec = radial_two.shape[0], embed.shape[0]
        plan = Plan(mesh, slots, nbasis, nspec)
        given = [positions[0, 0, 0].reshape(3, 1, slots), species.reshape(1, slots), radial_one]
        weights = [embed, mix_one, radial_two, read_out[None], read_one[None], mix_two, read_hidden]
        sent, table, wide, *weights = simple_call(
            prepare_kernel,
            plan,
            [counts.reshape(1), *given, *weights],
            [
                ((plan.ndev if plan.small else 1, 4, 2 * slots), F32),
                ((2, nbasis * nspec, channels), BF16),
                (((1 + 2 * len(plan.plain)) * nbasis * nspec, (1 + len(plan.plain)) * channels), BF16),
            ]
            + [(weight.shape, weight.dtype) for weight in weights],
            1,
            [(array.shape, array.dtype) for array in given],
            near=True,
            fetched=len(given) + len(weights),
        )
        embed, mix_one, radial_two, out_row, one_row, mix_two, read_hidden = weights
        far_sent = [everywhere(sent)] if plan.small else neighbours(plan, sent[0])
        pair_flops = 100 * slots * plan.far
        rows, basis, layer, vector, mixing, cols = call(
            first_kernel,
            plan,
            far_sent,
            [table, wide, embed, mix_one],
            [
                ((len(plan.tiles), 4, plan.width), F32),
                ((plan.known, nbasis, slots, plan.far), BF16),
                ((len(plan.column), slots, channels), BF16),
                ((3 * slots, channels), F32),
                ((slots, channels), F32),
                ((plan.known, slots, 8), F32),
            ],
            [
                ((len(plan.column), nbasis, plan.kinds * slots, plan.far), BF16),
                ((len(plan.tiles) * len(plan.sides), 4, 2 * slots), F32),
            ],
            pair_flops,
        )
        again, apart, slope, factor, turned = simple_call(
            slope_kernel,
            plan,
            [rows, cols, layer],
            [(layer.shape, BF16)]
            + [((count, slots, plan.far), F32) for count in (3, nbasis, nbasis, nbasis)],
            flops=pair_flops,
        )
        if plan.small:
            far_layer = from_columns(plan, layer, False, again)
        else:
            far_layer = neighbours(plan, layer[0], again[0])
        far_scratch = ((plan.far, channels), BF16)
        adjoint, kept, before, own_adjoint, own_far = call(
            second_kernel,
            plan,
            far_layer,
            [layer, basis, cols, radial_two, mix_two, read_hidden, out_row, one_row],
            [
                ((plan.known, slots, channels), BF16),
                ((slots, channels), BF16),
                ((slots, read_hidden.shape[0]), F32),
                ((slots, channels), F32),
                far_scratch,
            ],
            [((max(plan.known - 1, 1), plan.far, channels), BF16)],
            pair_flops,
        )
        again, pair, energy, features = simple_call(
            energy_kernel,
            plan,
            [own_far, adjoint, slope, radial_two, cols, layer, before, out_row, one_row, kept],
            [
                (adjoint.shape, BF16),
                ((slots, plan.far), F32),
                ((1, slots), F32),
                ((slots, channels), BF16),
            ],
            flops=pair_flops,
        )
        if plan.small:
            far_adjoint = from_columns(plan, adjoint, False, again)
        else:
            far_adjoint = neighbours(plan, adjoint[0], again[0])
        pulls = call(
            force_kernel,
            plan,
            far_adjoint,
            [own_adjoint, basis, pair, rows, apart, slope, factor, turned]
            + [radial_two, mixing, mix_one, vector, table],
            [((plan.ndev, 4, plan.width) if plan.small else (len(plan.tiles), 3, plan.width), F32)],
            [far_scratch],
            pair_flops,
        )
        if plan.small:
            forces = simple_call(sum_kernel, plan, [everywhere(pulls[0])], ((3, 1, slots), F32))
        else:
            forces = -fold(plan, pulls[0])
        return (
            forces.reshape(1, 1, 1, 3, slots),
            energy[None, None],
            features.T[None, None, None],
        )

    return local


def solution(mesh):
    split = [P(*AXES, None, None), P(*AXES, None), P(*AXES)]
    out_specs = (P(*AXES, None, None), P(*AXES, None), P(*AXES, None, None))
    return jax.shard_map(
        local_program(mesh),
        mesh=mesh,
        in_specs=tuple(split + [P()] * 8),
        out_specs=out_specs,
        check_vma=False,
    )
```

```python
import itertools
import math

import jax
import jax.numpy as jnp
from jax import lax
from jax.experimental import pallas as pl
from jax.experimental.pallas import tpu as pltpu
from jax.sharding import PartitionSpec as P

CELL_SIDE = 5.0
CUT_SQUARE = 25.0
SOFTEN = 0.25
MSG_SCALE = 0.05
ROOT_THREE = math.sqrt(3.0)
FAR = 1.0e4
AXES = ("gx", "gy", "gz")
F32 = jnp.float32
BF16 = jnp.bfloat16
COS_TERMS = (
    0.9999999532476085,
    -4.934792830619644,
    4.058411352862619,
    -1.3318765680811142,
    0.2196896110983216,
)
SIN_TERMS = (
    3.1415926401307073,
    -5.167710083507891,
    2.550077523214631,
    -0.5982912856208596,
    0.07765766030668693,
)
VMEM_LIMIT = 24 * 1024 * 1024
FETCH_LIMIT = 60 * 1024 * 1024
NT = (((1,), (1,)), ((), ()))
NN = (((1,), (0,)), ((), ()))


def dot(a, b, dims=NN):
    return lax.dot_general(a, b, dims, preferred_element_type=F32)


def dot_exact(a, b, dims=NN):
    return lax.dot_general(
        a, b, dims, precision=lax.Precision.HIGHEST, preferred_element_type=F32
    )


def split_dot(a, b):
    high = a.astype(BF16)
    low = (a - high.astype(F32)).astype(BF16)
    return dot(high, b) + dot(low, b)


def offsets_of(count):
    return (0, 1) if count == 2 else (0, 1, -1)


def paired(count):
    return count > 2 and count % 2 == 0


def matched(which, parity):
    return jnp.int32(0) if which == 0 else 1 + (parity if which == 1 else 1 - parity)


def poly(terms, arg):
    total = arg * terms[-1] + terms[-2]
    for term in terms[-3::-1]:
        total = total * arg + term
    return total


class Plan:
    def __init__(self, mesh, slots, nbasis, nspec):
        self.sizes = {axis: mesh.shape[axis] for axis in AXES}
        self.ndev = math.prod(self.sizes.values())
        self.tiles = list(
            itertools.product(offsets_of(self.sizes["gx"]), offsets_of(self.sizes["gz"]))
        )
        self.sides = offsets_of(self.sizes["gy"])
        self.slots = slots
        self.width = len(self.sides) * slots
        self.far = len(self.tiles) * self.width
        self.nbasis = nbasis
        self.nspec = nspec
        self.depth = len(offsets_of(self.sizes["gz"]))
        self.wide = len(offsets_of(self.sizes["gx"]))
        self.brought = list(itertools.product(range(self.wide), range(self.depth)))
        self.mixed = self.depth == self.wide and self.sizes["gy"] % 2 == 0
        self.small = self.ndev <= 64 and len(self.sides) == 2
        self.columns, self.column = [self.reach(axis) if self.small else [0] for axis in ("gx", "gz")]
        self.known = self.depth if self.small else 1
        self.targets = self.tiles if self.small else self.tiles[:1]
        self.wrapped = [self.sizes[axis] == 2 for axis in AXES]
        self.plain = [k for k in range(3) if not self.wrapped[k]]
        self.folded = [k for k in range(3) if self.wrapped[k]]
        self.kinds = 2 + len(self.folded)

    def global_id(self, offset):
        place = 0
        for axis, step in zip(AXES, offset):
            count = self.sizes[axis]
            place = place * count + lax.rem(lax.axis_index(axis) + (step + count), count)
        return place

    def reach(self, axis):
        near, count = offsets_of(self.sizes[axis]), self.sizes[axis]
        steps = list(near)
        for step in [a + b for a in near for b in near]:
            if all((step - other) % count for other in steps):
                steps.append(step)
        return steps

    def held(self, x, z):
        found = []
        for step, steps, axis in ((x, self.columns, "gx"), (z, self.column, "gz")):
            found.append([(step - other) % self.sizes[axis] == 0 for other in steps].index(True))
        return found[0] * len(self.column) + found[1]

    def places(self):
        index = {axis: lax.axis_index(axis) for axis in AXES}

        def parity(axis):
            return lax.rem(index[axis], 2) if paired(self.sizes[axis]) else jnp.int32(0)

        turns = parity("gx"), parity("gz")
        core = lax.rem(index["gy"], 2) if self.mixed else jnp.int32(0)
        found = []
        for side in range(len(self.sides)):
            x_first = core if side == 0 or not self.mixed else 1 - core
            for second, first in self.brought:
                plain = matched(second, turns[0]) * self.depth + matched(first, turns[1])
                crossed = matched(first, turns[0]) * self.depth + matched(second, turns[1])
                tile = jnp.where(x_first == 1, crossed, plain) if self.mixed else plain
                found.append(tile * len(self.sides) + side)
        found += turns
        return [jnp.asarray(place, jnp.int32) for place in found]

    def brought_place(self, places, side, pair):
        return places[side * len(self.brought) + pair]

    def staged_place(self, places, tile):
        start = len(self.sides) * len(self.brought)
        x, z = divmod(tile, self.depth)
        return matched(x, places[start]) * self.depth + matched(z, places[start + 1])

    def offset(self, tile, side):
        ox, oz = self.tiles[tile]
        return (ox, self.sides[side], oz)


def scaled(terms, factor):
    return [factor * term for term in terms]


def separations(plan, rows, cols, side=CELL_SIDE):
    parts = []
    for axis in range(3):
        diff = rows[axis] - cols[axis]
        if plan.wrapped[axis]:
            diff = jnp.where(diff > side, diff - 2.0 * side, diff)
        parts.append(diff)
    return parts


def distance(plan, parts, tile, soften=SOFTEN):
    dist_sq = parts[0] * parts[0] + parts[1] * parts[1] + parts[2] * parts[2] + soften
    if tile == 0:
        row = lax.broadcasted_iota(jnp.int32, dist_sq.shape, 0)
        col = lax.broadcasted_iota(jnp.int32, dist_sq.shape, 1)
        dist_sq = jnp.where(row == col, FAR, dist_sq)
    return dist_sq, lax.rsqrt(dist_sq)


def waves(dist_sq, inverse):
    arg = jnp.minimum(dist_sq * inverse * (1.0 / CELL_SIDE) - 0.5, 0.5)
    square = arg * arg
    return poly(COS_TERMS, square), -(arg * poly(SIN_TERMS, square))


def global_block(plan, far_ref, tile, side, target):
    x, y, z = plan.offset(tile, side)
    return far_ref[plan.global_id((x + target[0], y, z + target[1]))]


def own_columns(plan, block):
    held = jnp.concatenate([block, block], axis=0).T[: plan.slots]
    kind = held[:, 3:4]
    lane = lax.broadcasted_iota(jnp.int32, held.shape, 1)
    live = kind >= 0.0
    held = jnp.where((lane == 0) & ~live, -FAR, held)
    return jnp.where(lane == 3, live.astype(F32), held), kind


def scaled_columns(held):
    return [held[:, axis : axis + 1] * (1.0 / CELL_SIDE) for axis in range(3)]


def basis_of(plan, placed, cols, tile):
    parts = separations(plan, [placed[k : k + 1] for k in range(3)], cols, 1.0)
    dist_sq, inverse = distance(plan, parts, tile, SOFTEN / CUT_SQUARE)
    turn = jnp.minimum(dist_sq * inverse - 0.5, 0.5)
    square = turn * turn
    double = turn * poly(scaled(SIN_TERMS, -2.0), square)
    fade = jnp.maximum(1.0 - dist_sq, 0.0)
    basis = [poly(scaled(COS_TERMS, 1.0 / CELL_SIDE), square) * (fade * fade * inverse)]
    for n in range(1, plan.nbasis):
        basis.append(double * basis[-1] if n == 1 else double * basis[-1] - basis[-2])
    return parts, inverse, basis


def first_kernel(plan, nrefs, places, *refs):
    far_refs, refs = refs[:nrefs], refs[nrefs:]
    (table_ref, wide_ref, embed_ref, mix_ref), refs = refs[:4], refs[4:]
    rows_ref, basis_ref, layer_ref, vector_ref, mixing_ref, cols_ref, pair_ref, block_ref = refs
    slots, nbasis, nspec = plan.slots, plan.nbasis, plan.nspec

    def put(place, block):
        block_ref[place] = block

    if not plan.small:
        scatter(plan, places, far_refs, put)

    def block_of(tile, side, up):
        if plan.small:
            return global_block(plan, far_refs[0], tile, side, (0, up))
        return block_ref[tile * len(plan.sides) + side]

    species = lax.broadcasted_iota(jnp.int32, (nbasis * nspec, plan.width), 0) % nspec
    shifts = [tile_shift(plan, tile) for tile in range(len(plan.tiles))]
    own, counted, places_of = [], [], []
    for which, up in enumerate(plan.column):
        held, kind = own_columns(plan, block_of(0, 0, up))
        own.append(kind)
        if which < plan.known:
            cols_ref[which] = held
        cols = scaled_columns(held)
        places_of.append(cols)
        hot = []
        for tile in range(len(plan.tiles)):
            blocks = [block_of(tile, side, up) for side in range(len(plan.sides))]
            placed = side_by_side(plan, blocks) + shifts[tile]
            if which == 0:
                rows_ref[tile] = placed
            is_kind = placed[3:4].astype(jnp.int32) == species
            placed = placed * (1.0 / CELL_SIDE)
            high = placed.astype(BF16).astype(F32)
            low = placed - high
            columns = [jnp.where(is_kind, 1.0, 0.0)]
            for k in plan.plain:
                columns += [jnp.where(is_kind, part[k : k + 1], 0.0) for part in (high, low)]
            hot.append(jnp.concatenate([column.astype(BF16) for column in columns], axis=0))
            parts, inverse, basis = basis_of(plan, placed, cols, tile)
            scale = inverse * ROOT_THREE
            units = [scale.astype(BF16)] + [(scale * parts[k]).astype(BF16) for k in plan.folded]
            lanes = slice(tile * plan.width, (tile + 1) * plan.width)
            for n in range(nbasis):
                packed = basis[n].astype(BF16)
                if which < plan.known:
                    basis_ref[which, n, :, lanes] = packed
                pair_ref[which, n, :slots, lanes] = packed
                for m, unit in enumerate(units):
                    pair_ref[which, n, (m + 1) * slots : (m + 2) * slots, lanes] = unit * packed
        hot = jnp.concatenate(hot, axis=1)
        gathered = dot(pair_ref[which].reshape(nbasis * plan.kinds * slots, plan.far), hot, NT)
        gathered = gathered.reshape(nbasis, plan.kinds * slots, hot.shape[0])
        group = lax.broadcasted_iota(jnp.int32, gathered.shape[1:], 1) % (nbasis * nspec) // nspec
        total = gathered[0]
        for n in range(1, nbasis):
            total = jnp.where(group == n, gathered[n], total)
        counted.append(total)
    scalar = jnp.concatenate([total[:slots, : nbasis * nspec] for total in counted], axis=0)
    scalar = MSG_SCALE * split_dot(scalar, table_ref[0])
    moved = jnp.concatenate([total[slots : 2 * slots] for total in counted], axis=0)
    moved = MSG_SCALE * split_dot(moved, wide_ref[...])
    channels = layer_ref.shape[2]
    norm = None
    for k in range(3):
        if k in plan.plain:
            start = (plan.plain.index(k) + 1) * channels
            place = jnp.concatenate([cols[k] for cols in places_of], axis=0)
            vector = moved[:, start : start + channels] - place * moved[:, :channels]
        else:
            start = (plan.folded.index(k) + 2) * slots
            vector = [total[start : start + slots, : nbasis * nspec] for total in counted]
            vector = MSG_SCALE * split_dot(jnp.concatenate(vector, axis=0), table_ref[1])
        vector_ref[k * slots : (k + 1) * slots] = vector[:slots]
        norm = vector * vector if k == 0 else norm + vector * vector
    invariants = jnp.concatenate([scalar.astype(BF16), norm.astype(BF16)], axis=1)
    mixing = dot(invariants, mix_ref[...], NT)
    mixing_ref[...] = mixing[:slots]
    kind = jnp.concatenate(own, axis=0)
    own_species = lax.broadcasted_iota(jnp.int32, (kind.shape[0], nspec), 1)
    own_hot = (kind.astype(jnp.int32) == own_species).astype(F32).astype(BF16)
    layer = (dot(own_hot, embed_ref[...]) + mixing * sigmoid(mixing)).astype(BF16)
    for which in range(layer_ref.shape[0]):
        layer_ref[which] = layer[which * slots : (which + 1) * slots]


def sigmoid(value):
    return 1.0 / (1.0 + jnp.exp(-value))


def scatter(plan, places, far_refs, put):
    for side in range(len(plan.sides)):
        for pair, (second, first) in enumerate(plan.brought):
            put(plan.brought_place(places, side, pair), far_refs[side * plan.wide + second][first])


def scatter_held(plan, places, far_refs, put):
    turn = places[len(plan.sides) * len(plan.brought)]
    for side in range(len(plan.sides)):
        for m in range(len(plan.columns)):
            x = matched(m, turn) if m < plan.wide else m
            for z in range(len(plan.column)):
                place = (x * len(plan.column) + z) * len(plan.sides) + side
                put(place, far_refs[side * len(plan.columns) + m][z])


def far_blocks(plan, block_ref, target):
    blocks = []
    for x, z in plan.tiles:
        place = plan.held(x + target[0], z + target[1]) * len(plan.sides)
        blocks += [block_ref[place + side] for side in range(len(plan.sides))]
    return jnp.concatenate(blocks, axis=0)


def side_by_side(plan, blocks):
    if len(blocks) == 2:
        lane = lax.broadcasted_iota(jnp.int32, blocks[0].shape, 1)
        return jnp.where(lane < plan.slots, blocks[0], blocks[1])
    return jnp.concatenate([block[:, : plan.slots] for block in blocks], axis=1)


def tile_shift(plan, tile):
    row = lax.broadcasted_iota(jnp.int32, (4, plan.width), 0)
    side = lax.broadcasted_iota(jnp.int32, (4, plan.width), 1) // plan.slots
    shift = jnp.zeros((4, plan.width), F32)
    for s in range(len(plan.sides)):
        for k, steps in enumerate(plan.offset(tile, s)):
            if steps:
                shift = jnp.where((row == k) & (side == s), CELL_SIDE * steps, shift)
    return shift


def gather_far(plan, places, far_refs, all_ref):
    def put(place, block):
        start = pl.multiple_of(place * plan.slots, plan.slots)
        all_ref[pl.ds(start, plan.slots)] = block

    scatter(plan, places, far_refs, put)


def second_kernel(plan, nrefs, places, *refs):
    far_refs, refs = refs[:nrefs], refs[nrefs:]
    (layer_ref, basis_ref, cols_ref, more_ref, more_cols_ref, radial_ref, mix_ref), refs = refs[:7], refs[7:]
    (hidden_ref, out_ref, one_ref), refs = refs[:3], refs[3:]
    adjoint_ref, features_ref, before_ref, own_ref, own_far_ref, block_ref = refs
    slots, nbasis, known = plan.slots, plan.nbasis, len(plan.targets)

    def put(place, block):
        block_ref[place] = block

    (scatter_held if plan.small else scatter)(plan, places, far_refs, put)
    messages, layers, lives = [], [], []
    for which, target in enumerate(plan.targets):
        if plan.small:
            far = far_blocks(plan, block_ref, target)
            layers.append(block_ref[plan.held(*target) * len(plan.sides)])
        else:
            far = block_ref[...].reshape(plan.far, -1)
            layers.append(layer_ref[0])
        first = which < plan.known
        held_ref, held_cols_ref = (basis_ref, cols_ref) if first else (more_ref, more_cols_ref)
        place = which if first else which - plan.known
        lives.append(held_cols_ref[place, :, 3:4])
        if which == 0:
            own_far_ref[...] = far
        summed = dot(held_ref[place].reshape(nbasis * slots, plan.far), far)
        message = summed[:slots] * radial_ref[0:1]
        for n in range(1, nbasis):
            message = message + summed[n * slots : (n + 1) * slots] * radial_ref[n : n + 1]
        messages.append((MSG_SCALE * message).astype(BF16))
    mixing = dot(jnp.concatenate(messages, axis=0), mix_ref[...], NT)
    gate = sigmoid(mixing)
    layer = jnp.concatenate(layers, axis=0).astype(F32)
    features = (layer + mixing * gate).astype(BF16)
    features_ref[...] = features[:slots]
    before = dot(features, hidden_ref[...], NT)
    before_ref[...] = before[:slots]
    open_hidden = sigmoid(before)
    live = jnp.concatenate(lives, axis=0)
    slope = out_ref[...] * (open_hidden * (1.0 + before * (1.0 - open_hidden))) * live
    from_hidden = dot(slope.astype(BF16), hidden_ref[...])
    own_ref[...] = from_hidden[:slots] + one_ref[...] * live[:slots]
    back = from_hidden * (gate * (1.0 + mixing * (1.0 - gate)))
    adjoint = dot(back.astype(BF16), mix_ref[...]).astype(BF16)
    for which in range(known):
        adjoint_ref[which] = adjoint[which * slots : (which + 1) * slots]


def slope_kernel(plan, nrefs, places, *refs):
    far_refs, (rows_ref, cols_ref, layer_ref), refs = refs[:nrefs], refs[nrefs : nrefs + 3], refs[nrefs + 3 :]
    again_ref, apart_ref, slope_ref, radial_ref, turned_ref, more_ref, more_cols_ref = refs
    again_ref[...] = layer_ref[...]
    for which, target in enumerate(plan.targets[plan.known :]):
        held, _ = own_columns(plan, global_block(plan, far_refs[0], 0, 0, target))
        more_cols_ref[which] = held
        for tile in range(len(plan.tiles)):
            lanes = slice(tile * plan.width, (tile + 1) * plan.width)
            blocks = [global_block(plan, far_refs[0], tile, s, target) for s in range(len(plan.sides))]
            placed = (side_by_side(plan, blocks) + tile_shift(plan, tile)) * (1.0 / CELL_SIDE)
            basis = basis_of(plan, placed, scaled_columns(held), tile)[2]
            for n in range(plan.nbasis):
                more_ref[which, n, :, lanes] = basis[n].astype(BF16)
    cols = [cols_ref[0, :, axis : axis + 1] for axis in range(3)]
    for tile in range(len(plan.tiles)):
        lanes = slice(tile * plan.width, (tile + 1) * plan.width)
        parts = separations(plan, [rows_ref[tile, k : k + 1] for k in range(3)], cols)
        for k in range(3):
            apart_ref[k, :, lanes] = parts[k]
        dist_sq, inverse = distance(plan, parts, tile)
        sine, cosine = waves(dist_sq, inverse)
        fade = jnp.maximum(1.0 - dist_sq * (1.0 / CUT_SQUARE), 0.0)
        radial = fade * fade * inverse
        on_sine = -inverse * ((4.0 / CUT_SQUARE) * fade + radial * inverse)
        on_cosine = (math.pi / CELL_SIDE) * (inverse * radial)
        scale = ROOT_THREE * inverse
        scaled = scale * radial
        square = inverse * inverse
        double = 2.0 * cosine
        before_s, now_s, before_c, now_c = None, sine, None, cosine
        for n in range(plan.nbasis):
            if n == 1:
                before_s, now_s = now_s, double * now_s
                before_c, now_c = now_c, double * now_c - 1.0
            elif n > 1:
                before_s, now_s = now_s, double * now_s - before_s
                before_c, now_c = now_c, double * now_c - before_c
            slope = on_sine * now_s + (n + 1.0) * on_cosine * now_c
            factor = scaled * now_s
            slope_ref[n, :, lanes] = slope
            radial_ref[n, :, lanes] = factor
            turned_ref[n, :, lanes] = scale * slope - square * factor


def energy_kernel(plan, *refs):
    (all_ref, adjoint_ref, slope_ref, radial_ref, cols_ref, layer_ref), refs = refs[:6], refs[6:]
    (before_ref, out_ref, one_ref, kept_ref), refs = refs[:4], refs[4:]
    again_ref, pair_ref, energy_ref, features_ref = refs
    slots, nbasis = plan.slots, plan.nbasis
    again_ref[...] = adjoint_ref[:1]
    features_ref[...] = kept_ref[...]
    before = before_ref[...]
    live = jnp.where(lax.broadcasted_iota(jnp.int32, (slots, 8), 1) == 0, cols_ref[0, :, 3:4], 0.0)
    live_row = dot(jnp.ones((1, 8), BF16), live.astype(BF16), NT)
    energy = dot_exact(one_ref[...], layer_ref[0].astype(F32), NT)
    energy = energy + dot_exact(out_ref[...], before * sigmoid(before), NT)
    energy_ref[...] = energy * live_row
    adjoint = adjoint_ref[0].astype(F32) * MSG_SCALE
    weighted = jnp.concatenate(
        [(adjoint * radial_ref[n : n + 1]).astype(BF16) for n in range(nbasis)], axis=0
    )
    for tile in range(len(plan.tiles)):
        lanes = slice(tile * plan.width, (tile + 1) * plan.width)
        pulled = dot(weighted, all_ref[lanes], NT)
        total = slope_ref[0, :, lanes] * pulled[:slots]
        for n in range(1, nbasis):
            total = total + slope_ref[n, :, lanes] * pulled[n * slots : (n + 1) * slots]
        pair_ref[:, lanes] = total


def force_kernel(plan, nrefs, places, *refs):
    far_refs, refs = refs[:nrefs], refs[nrefs:]
    (own_ref, basis_ref, pair_ref, rows_ref), refs = refs[:4], refs[4:]
    (apart_ref, slope_ref, factor_ref, turned_ref), refs = refs[:4], refs[4:]
    (radial_ref, mixing_ref, mix_ref, vector_ref, table_ref), refs = refs[:5], refs[5:]
    out_ref, all_ref = refs
    slots, nbasis, nspec, width = plan.slots, plan.nbasis, plan.nspec, plan.width
    if plan.small:
        far = [far_refs[side][tile] for tile in range(len(plan.tiles)) for side in range(len(plan.sides))]
        all_ref[...] = jnp.concatenate(far, axis=0)
    else:
        gather_far(plan, places, far_refs, all_ref)
    summed = dot(basis_ref[0].reshape(nbasis * slots, plan.far), all_ref[...])
    adjoint = jnp.zeros((slots, summed.shape[1]), F32)
    for n in range(nbasis):
        adjoint = adjoint + summed[n * slots : (n + 1) * slots] * radial_ref[n : n + 1]
    adjoint = own_ref[...] + MSG_SCALE * adjoint
    mixing = mixing_ref[...]
    gate = sigmoid(mixing)
    back = (adjoint * (gate * (1.0 + mixing * (1.0 - gate)))).astype(BF16)
    invariants = dot(back, mix_ref[...])
    channels = invariants.shape[1] // 2
    on_scalar = (MSG_SCALE * invariants[:, :channels]).astype(BF16)
    doubled = (2.0 * MSG_SCALE) * invariants[:, channels:]
    on_vector = (vector_ref[...] * jnp.concatenate([doubled] * 3, axis=0)).astype(BF16)
    weights = jnp.concatenate(
        [dot(on_scalar, table_ref[0], NT), dot(on_vector, table_ref[1], NT)], axis=0
    ).astype(BF16)
    group = lax.broadcasted_iota(jnp.int32, weights.shape, 1) // nspec
    weights = weights.astype(F32)
    weights = jnp.concatenate(
        [jnp.where(group == n, weights, 0.0).astype(BF16) for n in range(nbasis)], axis=0
    )
    species = lax.broadcasted_iota(jnp.int32, (nbasis * nspec, width), 0) % nspec
    own = [jnp.zeros((slots, width), F32) for _ in range(3)]
    pulls = []
    for tile in range(len(plan.tiles)):
        lanes = slice(tile * width, (tile + 1) * width)
        hot = (rows_ref[tile, 3:4].astype(jnp.int32) == species).astype(F32).astype(BF16)
        spread = dot(weights, hot)
        total = pair_ref[:, lanes]
        sides, turns = [None] * 3, [None] * 3
        for n in range(nbasis):
            start = n * 4 * slots
            total = total + slope_ref[n, :, lanes] * spread[start : start + slots]
            for k in range(3):
                piece = spread[start + (k + 1) * slots : start + (k + 2) * slots]
                side = factor_ref[n, :, lanes] * piece
                turn = turned_ref[n, :, lanes] * piece
                sides[k] = side if n == 0 else sides[k] + side
                turns[k] = turn if n == 0 else turns[k] + turn
        for k in range(3):
            total = total + apart_ref[k, :, lanes] * turns[k]
        pulls.append([])
        for k in range(3):
            pull = apart_ref[k, :, lanes] * total + sides[k]
            own[k] = own[k] + pull
            pulls[-1].append(jnp.sum(pull, axis=0, keepdims=True))
    own = jnp.concatenate(own, axis=0)
    high = own.astype(BF16)
    low = (own - high.astype(F32)).astype(BF16)
    ones = jnp.ones((8, width), BF16)
    mine = (dot(ones, high, NT) + dot(ones, low, NT))[:1]
    mine = jnp.concatenate([mine[:, k * slots : (k + 1) * slots] for k in range(3)], axis=0)
    if plan.small:
        out_ref[...] = jnp.zeros_like(out_ref)
    side_of = lax.broadcasted_iota(jnp.int32, (3, width), 1) // slots
    for tile in range(len(plan.tiles)):
        pulled = jnp.concatenate(pulls[tile], axis=0)
        if tile == 0:
            others = [jnp.zeros_like(mine)] * (len(plan.sides) - 1)
            pulled = pulled - jnp.concatenate([mine] + others, axis=1)
        if not plan.small:
            out_ref[plan.staged_place(places, tile)] = pulled
            continue
        for side in range(len(plan.sides)):
            place = plan.global_id(plan.offset(tile, side))
            out_ref[place, :3] = jnp.where(side_of == side, pulled, 0.0)


def begin(pairs, sems):
    copies = [pltpu.make_async_copy(*pair, sems.at[m]) for m, pair in enumerate(pairs)]
    for copy in copies:
        copy.start()
    return copies


def prepare_kernel(plan, counts_ref, *refs):
    fetched, (sent_ref, table_ref, wide_ref), refs = refs[:10], refs[10:13], refs[13:]
    kept, (place_ref, kind_ref, radial_ref, sems) = refs[:7], refs[7:]
    copies = begin(zip(fetched, (place_ref, kind_ref, radial_ref, *kept)), sems)
    for copy in copies[:2]:
        copy.wait()
    live = lax.broadcasted_iota(jnp.int32, (1, plan.slots), 1) < counts_ref[0]
    rows = [
        jnp.where(live, place_ref[0], FAR),
        place_ref[1],
        place_ref[2],
        jnp.where(live, kind_ref[...], -1).astype(F32),
    ]
    rows = jnp.concatenate(rows, axis=0)
    rows = jnp.concatenate([rows, rows], axis=1)
    for copy in range(sent_ref.shape[0]):
        sent_ref[copy] = rows
    for copy in copies[2:]:
        copy.wait()
    embed, nspec = kept[0][...].astype(F32), plan.nspec
    for g in range(2):
        for n in range(plan.nbasis):
            weighted = radial_ref[g, n : n + 1] * embed
            table_ref[g, n * nspec : (n + 1) * nspec] = weighted.astype(BF16)
    wide_ref[...] = jnp.zeros_like(wide_ref)
    count, channels = table_ref.shape[1:]
    for m in range(1 + 2 * len(plan.plain)):
        start = (m + 1) // 2 * channels
        wide_ref[m * count : (m + 1) * count, start : start + channels] = table_ref[1]


def sum_kernel(plan, parts_ref, force_ref):
    total = parts_ref[0]
    for part in range(1, parts_ref.shape[0]):
        total = total + parts_ref[part]
    total = total[:, : plan.slots] + total[:, plan.slots :]
    for k in range(3):
        force_ref[k] = -total[k : k + 1]


VMEM_SPEC = pl.BlockSpec(memory_space=pltpu.VMEM)
SMEM_SPEC = pl.BlockSpec(memory_space=pltpu.SMEM)
HBM_SPEC = pl.BlockSpec(memory_space=pltpu.HBM)


def simple_call(kernel, plan, operands, outs, scalars=0, scratch=(), flops=2**20, near=False, fetched=0):
    single = not isinstance(outs, list)
    kind = pltpu.VMEM if near else jax.ShapeDtypeStruct
    shapes = [kind(*out) for out in ([outs] if single else outs)]

    def body(*refs):
        kernel(plan, *refs)

    got = pl.pallas_call(
        body,
        out_shape=shapes,
        in_specs=[SMEM_SPEC] * scalars
        + [VMEM_SPEC] * (len(operands) - scalars - fetched)
        + [HBM_SPEC] * fetched,
        out_specs=[VMEM_SPEC] * len(shapes),
        scratch_shapes=[pltpu.VMEM(*buffer) for buffer in scratch]
        + [pltpu.SemaphoreType.DMA((fetched,))] * (fetched > 0),
        compiler_params=pltpu.CompilerParams(vmem_limit_bytes=FETCH_LIMIT if fetched else VMEM_LIMIT),
        cost_estimate=pl.CostEstimate(flops=flops, bytes_accessed=2**20, transcendentals=0),
    )(*operands)
    return got[0] if single else got


def call(kernel, plan, far, operands, outs, scratch, flops, **options):
    def body(plan, *refs):
        kernel(plan, len(far), plan.places(), *refs)

    return simple_call(body, plan, [*far, *operands], outs, 0, scratch, flops, **options)


def swaps(count):
    if count == 2:
        return [[1, 0]]
    if paired(count):
        near = [i ^ 1 for i in range(count)]
        far = [(i - 1 + 2 * (i % 2)) % count for i in range(count)]
        return [near, far]
    return [[(i + o) % count for i in range(count)] for o in offsets_of(count)[1:]]


def brought(plan, block, second, mixed):
    sizes, sources = plan.sizes, {axis: swaps(plan.sizes[axis]) for axis in AXES}
    got = []
    for m in range(len(sources["gx" if second else "gz"])):
        pairs = []
        for x, y, z in itertools.product(*(range(sizes[axis]) for axis in AXES)):
            along_x = second != (mixed and y % 2 == 1)
            source = (sources["gx"][m][x], y, z) if along_x else (x, y, sources["gz"][m][z])
            pairs.append((flat(sizes, *source), flat(sizes, x, y, z)))
        got.append(lax.ppermute(block, AXES, pairs))
    return got


def flat(sizes, x, y, z):
    return (x * sizes["gy"] + y) * sizes["gz"] + z


def along(block, axis):
    return [
        lax.ppermute(block, axis, [(source, i) for i, source in enumerate(sources)])
        for sources in swaps(lax.axis_size(axis))
    ]


def neighbours(plan, block, again=None):
    column = jnp.stack([block if again is None else again] + brought(plan, block, False, plan.mixed))
    return from_columns(plan, column, plan.mixed)


def from_columns(plan, column, mixed, again=None):
    columns = [column] + brought(plan, column, True, mixed)
    count = plan.sizes["gx"]
    for step in plan.columns[plan.wide :]:
        columns.append(lax.ppermute(column, "gx", [((i + step) % count, i) for i in range(count)]))
    if again is not None:
        columns[0] = again
    swapped = [[column] + along(column, "gy") for column in columns]
    return [column[side] for side in range(len(plan.sides)) for column in swapped]


def everywhere(copies):
    return lax.all_to_all(copies, AXES, 0, 0, tiled=True)


def folded(pieces, axis):
    total = pieces[0]
    for piece, sources in zip(pieces[1:], swaps(lax.axis_size(axis))):
        total = total + lax.ppermute(piece, axis, list(enumerate(sources)))
    return total


def fold(plan, pulls):
    for axis in ("gx", "gz"):
        parts = len(offsets_of(plan.sizes[axis]))
        pulls = pulls.reshape((parts, -1) + pulls.shape[1:])
        pulls = folded([pulls[m] for m in range(parts)], axis)
    pulls = pulls[0]
    sides = [pulls[:, m * plan.slots : (m + 1) * plan.slots] for m in range(len(plan.sides))]
    return folded(sides, "gy")


def local_program(mesh):
    def local(
        positions,
        species,
        counts,
        embed,
        radial_one,
        mix_one,
        read_one,
        radial_two,
        mix_two,
        read_hidden,
        read_out,
    ):
        slots, channels = positions.shape[-1], embed.shape[1]
        nbasis, nspec = radial_two.shape[0], embed.shape[0]
        plan = Plan(mesh, slots, nbasis, nspec)
        given = [positions[0, 0, 0].reshape(3, 1, slots), species.reshape(1, slots), radial_one]
        weights = [embed, mix_one, radial_two, read_out[None], read_one[None], mix_two, read_hidden]
        sent, table, wide, *weights = simple_call(
            prepare_kernel,
            plan,
            [counts.reshape(1), *given, *weights],
            [
                ((plan.ndev if plan.small else 1, 4, 2 * slots), F32),
                ((2, nbasis * nspec, channels), BF16),
                (((1 + 2 * len(plan.plain)) * nbasis * nspec, (1 + len(plan.plain)) * channels), BF16),
            ]
            + [(weight.shape, weight.dtype) for weight in weights],
            1,
            [(array.shape, array.dtype) for array in given],
            near=True,
            fetched=len(given) + len(weights),
        )
        embed, mix_one, radial_two, out_row, one_row, mix_two, read_hidden = weights
        far_sent = [everywhere(sent)] if plan.small else neighbours(plan, sent[0])
        pair_flops = 100 * slots * plan.far
        rows, basis, layer, vector, mixing, cols = call(
            first_kernel,
            plan,
            far_sent,
            [table, wide, embed, mix_one],
            [
                ((len(plan.tiles), 4, plan.width), F32),
                ((plan.known, nbasis, slots, plan.far), BF16),
                ((len(plan.column), slots, channels), BF16),
                ((3 * slots, channels), F32),
                ((slots, channels), F32),
                ((plan.known, slots, 8), F32),
            ],
            [
                ((len(plan.column), nbasis, plan.kinds * slots, plan.far), BF16),
                ((len(plan.tiles) * len(plan.sides), 4, 2 * slots), F32),
            ],
            pair_flops,
        )
        more = max(len(plan.targets) - plan.known, 1)
        again, apart, slope, factor, turned, more_basis, more_cols = call(
            slope_kernel,
            plan,
            far_sent[:1],
            [rows, cols, layer],
            [(layer.shape, BF16)]
            + [((count, slots, plan.far), F32) for count in (3, nbasis, nbasis, nbasis)]
            + [((more, nbasis, slots, plan.far), BF16), ((more, slots, 8), F32)],
            [],
            pair_flops,
        )
        if plan.small:
            far_layer = from_columns(plan, layer, False, again)
        else:
            far_layer = neighbours(plan, layer[0], again[0])
        far_scratch = ((plan.far, channels), BF16)
        held = len(plan.columns) * len(plan.column) if plan.small else len(plan.tiles)
        held = held * len(plan.sides)
        adjoint, kept, before, own_adjoint, own_far = call(
            second_kernel,
            plan,
            far_layer,
            [layer, basis, cols, more_basis, more_cols, radial_two, mix_two, read_hidden, out_row, one_row],
            [
                ((len(plan.targets), slots, channels), BF16),
                ((slots, channels), BF16),
                ((slots, read_hidden.shape[0]), F32),
                ((slots, channels), F32),
                far_scratch,
            ],
            [((held, slots, channels), BF16)],
            pair_flops,
        )
        again, pair, energy, features = simple_call(
            energy_kernel,
            plan,
            [own_far, adjoint, slope, radial_two, cols, layer, before, out_row, one_row, kept],
            [
                ((1, slots, channels), BF16),
                ((slots, plan.far), F32),
                ((1, slots), F32),
                ((slots, channels), BF16),
            ],
            flops=pair_flops,
        )
        if plan.small:
            far_adjoint = [adjoint] + along(adjoint, "gy")
        else:
            far_adjoint = neighbours(plan, adjoint[0], again[0])
        pulls = call(
            force_kernel,
            plan,
            far_adjoint,
            [own_adjoint, basis, pair, rows, apart, slope, factor, turned]
            + [radial_two, mixing, mix_one, vector, table],
            [((plan.ndev, 4, plan.width) if plan.small else (len(plan.tiles), 3, plan.width), F32)],
            [far_scratch],
            pair_flops,
        )
        if plan.small:
            forces = simple_call(sum_kernel, plan, [everywhere(pulls[0])], ((3, 1, slots), F32))
        else:
            forces = -fold(plan, pulls[0])
        return (
            forces.reshape(1, 1, 1, 3, slots),
            energy[None, None],
            features.T[None, None, None],
        )

    return local


def solution(mesh):
    split = [P(*AXES, None, None), P(*AXES, None), P(*AXES)]
    out_specs = (P(*AXES, None, None), P(*AXES, None), P(*AXES, None, None))
    return jax.shard_map(
        local_program(mesh),
        mesh=mesh,
        in_specs=tuple(split + [P()] * 8),
        out_specs=out_specs,
        check_vma=False,
    )
```

```python
import itertools
import math

import jax
import jax.numpy as jnp
from jax import lax
from jax.experimental import pallas as pl
from jax.experimental.pallas import tpu as pltpu
from jax.sharding import PartitionSpec as P

CELL_SIDE = 5.0
CUT_SQUARE = 25.0
SOFTEN = 0.25
MSG_SCALE = 0.05
ROOT_THREE = math.sqrt(3.0)
FAR = 1.0e4
AXES = ("gx", "gy", "gz")
F32 = jnp.float32
BF16 = jnp.bfloat16
COS_TERMS = (
    0.9999999532476085,
    -4.934792830619644,
    4.058411352862619,
    -1.3318765680811142,
    0.2196896110983216,
)
SIN_TERMS = (
    3.1415926401307073,
    -5.167710083507891,
    2.550077523214631,
    -0.5982912856208596,
    0.07765766030668693,
)
VMEM_LIMIT = 24 * 1024 * 1024
FETCH_LIMIT = 60 * 1024 * 1024
NT = (((1,), (1,)), ((), ()))
NN = (((1,), (0,)), ((), ()))


def dot(a, b, dims=NN):
    return lax.dot_general(a, b, dims, preferred_element_type=F32)


def dot_exact(a, b, dims=NN):
    return lax.dot_general(
        a, b, dims, precision=lax.Precision.HIGHEST, preferred_element_type=F32
    )


def split_dot(a, b):
    high = a.astype(BF16)
    low = (a - high.astype(F32)).astype(BF16)
    return dot(high, b) + dot(low, b)


def offsets_of(count):
    return (0, 1) if count == 2 else (0, 1, -1)


def paired(count):
    return count > 2 and count % 2 == 0


def matched(which, parity):
    return jnp.int32(0) if which == 0 else 1 + (parity if which == 1 else 1 - parity)


def poly(terms, arg):
    total = arg * terms[-1] + terms[-2]
    for term in terms[-3::-1]:
        total = total * arg + term
    return total


class Plan:
    def __init__(self, mesh, slots, nbasis, nspec):
        self.sizes = {axis: mesh.shape[axis] for axis in AXES}
        self.ndev = math.prod(self.sizes.values())
        self.tiles = list(
            itertools.product(offsets_of(self.sizes["gx"]), offsets_of(self.sizes["gz"]))
        )
        self.sides = offsets_of(self.sizes["gy"])
        self.slots = slots
        self.width = len(self.sides) * slots
        self.far = len(self.tiles) * self.width
        self.nbasis = nbasis
        self.nspec = nspec
        self.depth = len(offsets_of(self.sizes["gz"]))
        self.wide = len(offsets_of(self.sizes["gx"]))
        self.brought = list(itertools.product(range(self.wide), range(self.depth)))
        self.mixed = self.depth == self.wide and self.sizes["gy"] % 2 == 0
        self.small = self.ndev <= 64 and len(self.sides) == 2
        self.columns, self.column = [self.reach(axis) if self.small else [0] for axis in ("gx", "gz")]
        self.known = self.depth if self.small else 1
        self.targets = self.tiles if self.small else self.tiles[:1]
        self.wrapped = [self.sizes[axis] == 2 for axis in AXES]
        self.plain = [k for k in range(3) if not self.wrapped[k]]
        self.folded = [k for k in range(3) if self.wrapped[k]]
        self.kinds = 2 + len(self.folded)

    def global_id(self, offset):
        place = 0
        for axis, step in zip(AXES, offset):
            count = self.sizes[axis]
            place = place * count + lax.rem(lax.axis_index(axis) + (step + count), count)
        return place

    def reach(self, axis):
        near, count = offsets_of(self.sizes[axis]), self.sizes[axis]
        steps = list(near)
        for step in [a + b for a in near for b in near]:
            if all((step - other) % count for other in steps):
                steps.append(step)
        return steps

    def held(self, x, z):
        found = []
        for step, steps, axis in ((x, self.columns, "gx"), (z, self.column, "gz")):
            found.append([(step - other) % self.sizes[axis] == 0 for other in steps].index(True))
        return found[0] * len(self.column) + found[1]

    def places(self):
        index = {axis: lax.axis_index(axis) for axis in AXES}

        def parity(axis):
            return lax.rem(index[axis], 2) if paired(self.sizes[axis]) else jnp.int32(0)

        turns = parity("gx"), parity("gz")
        core = lax.rem(index["gy"], 2) if self.mixed else jnp.int32(0)
        found = []
        for side in range(len(self.sides)):
            x_first = core if side == 0 or not self.mixed else 1 - core
            for second, first in self.brought:
                plain = matched(second, turns[0]) * self.depth + matched(first, turns[1])
                crossed = matched(first, turns[0]) * self.depth + matched(second, turns[1])
                tile = jnp.where(x_first == 1, crossed, plain) if self.mixed else plain
                found.append(tile * len(self.sides) + side)
        found += turns
        return [jnp.asarray(place, jnp.int32) for place in found]

    def brought_place(self, places, side, pair):
        return places[side * len(self.brought) + pair]

    def staged_place(self, places, tile):
        start = len(self.sides) * len(self.brought)
        x, z = divmod(tile, self.depth)
        return matched(x, places[start]) * self.depth + matched(z, places[start + 1])

    def offset(self, tile, side):
        ox, oz = self.tiles[tile]
        return (ox, self.sides[side], oz)


def scaled(terms, factor):
    return [factor * term for term in terms]


def separations(plan, rows, cols, side=CELL_SIDE):
    parts = []
    for axis in range(3):
        diff = rows[axis] - cols[axis]
        if plan.wrapped[axis]:
            diff = jnp.where(diff > side, diff - 2.0 * side, diff)
        parts.append(diff)
    return parts


def distance(plan, parts, tile, soften=SOFTEN):
    dist_sq = parts[0] * parts[0] + parts[1] * parts[1] + parts[2] * parts[2] + soften
    if tile == 0:
        row = lax.broadcasted_iota(jnp.int32, dist_sq.shape, 0)
        col = lax.broadcasted_iota(jnp.int32, dist_sq.shape, 1)
        dist_sq = jnp.where(row == col, FAR, dist_sq)
    return dist_sq, lax.rsqrt(dist_sq)


def waves(dist_sq, inverse):
    arg = jnp.minimum(dist_sq * inverse * (1.0 / CELL_SIDE) - 0.5, 0.5)
    square = arg * arg
    return poly(COS_TERMS, square), -(arg * poly(SIN_TERMS, square))


def global_block(plan, far_ref, tile, side, target):
    x, y, z = plan.offset(tile, side)
    return far_ref[plan.global_id((x + target[0], y, z + target[1]))]


def own_columns(plan, block):
    held = jnp.concatenate([block, block], axis=0).T[: plan.slots]
    kind = held[:, 3:4]
    lane = lax.broadcasted_iota(jnp.int32, held.shape, 1)
    live = kind >= 0.0
    held = jnp.where((lane == 0) & ~live, -FAR, held)
    return jnp.where(lane == 3, live.astype(F32), held), kind


def scaled_columns(held):
    return [held[:, axis : axis + 1] * (1.0 / CELL_SIDE) for axis in range(3)]


def basis_of(plan, placed, cols, tile):
    parts = separations(plan, [placed[k : k + 1] for k in range(3)], cols, 1.0)
    dist_sq, inverse = distance(plan, parts, tile, SOFTEN / CUT_SQUARE)
    turn = jnp.minimum(dist_sq * inverse - 0.5, 0.5)
    square = turn * turn
    double = turn * poly(scaled(SIN_TERMS, -2.0), square)
    fade = jnp.maximum(1.0 - dist_sq, 0.0)
    basis = [poly(scaled(COS_TERMS, 1.0 / CELL_SIDE), square) * (fade * fade * inverse)]
    for n in range(1, plan.nbasis):
        basis.append(double * basis[-1] if n == 1 else double * basis[-1] - basis[-2])
    return parts, inverse, basis


def first_kernel(plan, nrefs, places, *refs):
    far_refs, refs = refs[:nrefs], refs[nrefs:]
    (table_ref, wide_ref, embed_ref, mix_ref), refs = refs[:4], refs[4:]
    rows_ref, basis_ref, layer_ref, vector_ref, mixing_ref, cols_ref, pair_ref, block_ref = refs
    slots, nbasis, nspec = plan.slots, plan.nbasis, plan.nspec

    def put(place, block):
        block_ref[place] = block

    if not plan.small:
        scatter(plan, places, far_refs, put)

    def block_of(tile, side, up):
        if plan.small:
            return global_block(plan, far_refs[0], tile, side, (0, up))
        return block_ref[tile * len(plan.sides) + side]

    species = lax.broadcasted_iota(jnp.int32, (nbasis * nspec, plan.width), 0) % nspec
    shifts = [tile_shift(plan, tile) for tile in range(len(plan.tiles))]
    own, counted, places_of = [], [], []
    for which, up in enumerate(plan.column):
        held, kind = own_columns(plan, block_of(0, 0, up))
        own.append(kind)
        if which < plan.known:
            cols_ref[which] = held
        cols = scaled_columns(held)
        places_of.append(cols)
        hot = []
        for tile in range(len(plan.tiles)):
            blocks = [block_of(tile, side, up) for side in range(len(plan.sides))]
            placed = side_by_side(plan, blocks) + shifts[tile]
            if which == 0:
                rows_ref[tile] = placed
            is_kind = placed[3:4].astype(jnp.int32) == species
            placed = placed * (1.0 / CELL_SIDE)
            high = placed.astype(BF16).astype(F32)
            low = placed - high
            columns = [jnp.where(is_kind, 1.0, 0.0)]
            for k in plan.plain:
                columns += [jnp.where(is_kind, part[k : k + 1], 0.0) for part in (high, low)]
            hot.append(jnp.concatenate([column.astype(BF16) for column in columns], axis=0))
            parts, inverse, basis = basis_of(plan, placed, cols, tile)
            scale = inverse * ROOT_THREE
            units = [scale.astype(BF16)] + [(scale * parts[k]).astype(BF16) for k in plan.folded]
            lanes = slice(tile * plan.width, (tile + 1) * plan.width)
            for n in range(nbasis):
                packed = basis[n].astype(BF16)
                if which < plan.known:
                    basis_ref[which, n, :, lanes] = packed
                pair_ref[which, n, :slots, lanes] = packed
                for m, unit in enumerate(units):
                    pair_ref[which, n, (m + 1) * slots : (m + 2) * slots, lanes] = unit * packed
        hot = jnp.concatenate(hot, axis=1)
        gathered = dot(pair_ref[which].reshape(nbasis * plan.kinds * slots, plan.far), hot, NT)
        gathered = gathered.reshape(nbasis, plan.kinds * slots, hot.shape[0])
        group = lax.broadcasted_iota(jnp.int32, gathered.shape[1:], 1) % (nbasis * nspec) // nspec
        total = gathered[0]
        for n in range(1, nbasis):
            total = jnp.where(group == n, gathered[n], total)
        counted.append(total)
    scalar = jnp.concatenate([total[:slots, : nbasis * nspec] for total in counted], axis=0)
    scalar = MSG_SCALE * split_dot(scalar, table_ref[0])
    moved = jnp.concatenate([total[slots : 2 * slots] for total in counted], axis=0)
    moved = MSG_SCALE * split_dot(moved, wide_ref[...])
    channels = layer_ref.shape[2]
    norm = None
    for k in range(3):
        if k in plan.plain:
            start = (plan.plain.index(k) + 1) * channels
            place = jnp.concatenate([cols[k] for cols in places_of], axis=0)
            vector = moved[:, start : start + channels] - place * moved[:, :channels]
        else:
            start = (plan.folded.index(k) + 2) * slots
            vector = [total[start : start + slots, : nbasis * nspec] for total in counted]
            vector = MSG_SCALE * split_dot(jnp.concatenate(vector, axis=0), table_ref[1])
        vector_ref[k * slots : (k + 1) * slots] = vector[:slots]
        norm = vector * vector if k == 0 else norm + vector * vector
    invariants = jnp.concatenate([scalar.astype(BF16), norm.astype(BF16)], axis=1)
    mixing = dot(invariants, mix_ref[...], NT)
    mixing_ref[...] = mixing[:slots]
    kind = jnp.concatenate(own, axis=0)
    own_species = lax.broadcasted_iota(jnp.int32, (kind.shape[0], nspec), 1)
    own_hot = (kind.astype(jnp.int32) == own_species).astype(F32).astype(BF16)
    layer = (dot(own_hot, embed_ref[...]) + mixing * sigmoid(mixing)).astype(BF16)
    for which in range(layer_ref.shape[0]):
        layer_ref[which] = layer[which * slots : (which + 1) * slots]


def sigmoid(value):
    return 1.0 / (1.0 + jnp.exp(-value))


def scatter(plan, places, far_refs, put):
    for side in range(len(plan.sides)):
        for pair, (second, first) in enumerate(plan.brought):
            put(plan.brought_place(places, side, pair), far_refs[side * plan.wide + second][first])


def scatter_held(plan, places, far_refs, put):
    turn = places[len(plan.sides) * len(plan.brought)]
    for side in range(len(plan.sides)):
        for m in range(len(plan.columns)):
            x = matched(m, turn) if m < plan.wide else m
            for z in range(len(plan.column)):
                place = (x * len(plan.column) + z) * len(plan.sides) + side
                put(place, far_refs[side * len(plan.columns) + m][z])


def far_blocks(plan, block_ref, target):
    blocks = []
    for x, z in plan.tiles:
        place = plan.held(x + target[0], z + target[1]) * len(plan.sides)
        blocks += [block_ref[place + side] for side in range(len(plan.sides))]
    return jnp.concatenate(blocks, axis=0)


def side_by_side(plan, blocks):
    if len(blocks) == 2:
        lane = lax.broadcasted_iota(jnp.int32, blocks[0].shape, 1)
        return jnp.where(lane < plan.slots, blocks[0], blocks[1])
    return jnp.concatenate([block[:, : plan.slots] for block in blocks], axis=1)


def tile_shift(plan, tile):
    row = lax.broadcasted_iota(jnp.int32, (4, plan.width), 0)
    side = lax.broadcasted_iota(jnp.int32, (4, plan.width), 1) // plan.slots
    shift = jnp.zeros((4, plan.width), F32)
    for s in range(len(plan.sides)):
        for k, steps in enumerate(plan.offset(tile, s)):
            if steps:
                shift = jnp.where((row == k) & (side == s), CELL_SIDE * steps, shift)
    return shift


def gather_far(plan, places, far_refs, all_ref):
    def put(place, block):
        start = pl.multiple_of(place * plan.slots, plan.slots)
        all_ref[pl.ds(start, plan.slots)] = block

    scatter(plan, places, far_refs, put)


def second_kernel(plan, nrefs, places, *refs):
    far_refs, refs = refs[:nrefs], refs[nrefs:]
    (layer_ref, basis_ref, cols_ref, more_ref, more_cols_ref, radial_ref, mix_ref), refs = refs[:7], refs[7:]
    (hidden_ref, out_ref, one_ref), refs = refs[:3], refs[3:]
    adjoint_ref, features_ref, before_ref, own_ref, own_far_ref, block_ref = refs
    slots, nbasis, known = plan.slots, plan.nbasis, len(plan.targets)

    def put(place, block):
        block_ref[place] = block

    (scatter_held if plan.small else scatter)(plan, places, far_refs, put)
    messages, layers, lives = [], [], []
    for which, target in enumerate(plan.targets):
        if plan.small:
            far = far_blocks(plan, block_ref, target)
            layers.append(block_ref[plan.held(*target) * len(plan.sides)])
        else:
            far = block_ref[...].reshape(plan.far, -1)
            layers.append(layer_ref[0])
        first = which < plan.known
        held_ref, held_cols_ref = (basis_ref, cols_ref) if first else (more_ref, more_cols_ref)
        place = which if first else which - plan.known
        lives.append(held_cols_ref[place, :, 3:4])
        if which == 0:
            own_far_ref[...] = far
        summed = dot(held_ref[place].reshape(nbasis * slots, plan.far), far)
        message = summed[:slots] * radial_ref[0:1]
        for n in range(1, nbasis):
            message = message + summed[n * slots : (n + 1) * slots] * radial_ref[n : n + 1]
        messages.append((MSG_SCALE * message).astype(BF16))
    mixing = dot(jnp.concatenate(messages, axis=0), mix_ref[...], NT)
    gate = sigmoid(mixing)
    layer = jnp.concatenate(layers, axis=0).astype(F32)
    features = (layer + mixing * gate).astype(BF16)
    features_ref[...] = features[:slots]
    before = dot(features, hidden_ref[...], NT)
    before_ref[...] = before[:slots]
    open_hidden = sigmoid(before)
    live = jnp.concatenate(lives, axis=0)
    slope = out_ref[...] * (open_hidden * (1.0 + before * (1.0 - open_hidden))) * live
    from_hidden = dot(slope.astype(BF16), hidden_ref[...])
    own_ref[...] = from_hidden[:slots] + one_ref[...] * live[:slots]
    back = from_hidden * (gate * (1.0 + mixing * (1.0 - gate)))
    adjoint = dot(back.astype(BF16), mix_ref[...]).astype(BF16)
    for which in range(known):
        adjoint_ref[which] = adjoint[which * slots : (which + 1) * slots]


def basis_kernel(plan, nrefs, places, *refs):
    far_ref, (layer_ref, again_ref, more_ref, more_cols_ref) = refs[0], refs[nrefs:]
    again_ref[...] = layer_ref[...]
    for which, target in enumerate(plan.targets[plan.known :]):
        held, _ = own_columns(plan, global_block(plan, far_ref, 0, 0, target))
        more_cols_ref[which] = held
        for tile in range(len(plan.tiles)):
            lanes = slice(tile * plan.width, (tile + 1) * plan.width)
            blocks = [global_block(plan, far_ref, tile, s, target) for s in range(len(plan.sides))]
            placed = (side_by_side(plan, blocks) + tile_shift(plan, tile)) * (1.0 / CELL_SIDE)
            basis = basis_of(plan, placed, scaled_columns(held), tile)[2]
            for n in range(plan.nbasis):
                more_ref[which, n, :, lanes] = basis[n].astype(BF16)


def slope_kernel(plan, rows_ref, cols_ref, one_ref, *refs):
    kept_ref, apart_ref, slope_ref, radial_ref, turned_ref = refs
    kept_ref[...] = one_ref[...]
    cols = [cols_ref[0, :, axis : axis + 1] for axis in range(3)]
    for tile in range(len(plan.tiles)):
        lanes = slice(tile * plan.width, (tile + 1) * plan.width)
        parts = separations(plan, [rows_ref[tile, k : k + 1] for k in range(3)], cols)
        for k in range(3):
            apart_ref[k, :, lanes] = parts[k]
        dist_sq, inverse = distance(plan, parts, tile)
        sine, cosine = waves(dist_sq, inverse)
        fade = jnp.maximum(1.0 - dist_sq * (1.0 / CUT_SQUARE), 0.0)
        radial = fade * fade * inverse
        on_sine = -inverse * ((4.0 / CUT_SQUARE) * fade + radial * inverse)
        on_cosine = (math.pi / CELL_SIDE) * (inverse * radial)
        scale = ROOT_THREE * inverse
        scaled = scale * radial
        square = inverse * inverse
        double = 2.0 * cosine
        before_s, now_s, before_c, now_c = None, sine, None, cosine
        for n in range(plan.nbasis):
            if n == 1:
                before_s, now_s = now_s, double * now_s
                before_c, now_c = now_c, double * now_c - 1.0
            elif n > 1:
                before_s, now_s = now_s, double * now_s - before_s
                before_c, now_c = now_c, double * now_c - before_c
            slope = on_sine * now_s + (n + 1.0) * on_cosine * now_c
            factor = scaled * now_s
            slope_ref[n, :, lanes] = slope
            radial_ref[n, :, lanes] = factor
            turned_ref[n, :, lanes] = scale * slope - square * factor


def energy_kernel(plan, *refs):
    (all_ref, adjoint_ref, slope_ref, radial_ref, cols_ref, layer_ref), refs = refs[:6], refs[6:]
    (before_ref, out_ref, one_ref, kept_ref), refs = refs[:4], refs[4:]
    again_ref, pair_ref, energy_ref, features_ref = refs
    slots, nbasis = plan.slots, plan.nbasis
    again_ref[...] = adjoint_ref[:1]
    features_ref[...] = kept_ref[...]
    before = before_ref[...]
    live = jnp.where(lax.broadcasted_iota(jnp.int32, (slots, 8), 1) == 0, cols_ref[0, :, 3:4], 0.0)
    live_row = dot(jnp.ones((1, 8), BF16), live.astype(BF16), NT)
    energy = dot_exact(one_ref[...], layer_ref[0].astype(F32), NT)
    energy = energy + dot_exact(out_ref[...], before * sigmoid(before), NT)
    energy_ref[...] = energy * live_row
    adjoint = adjoint_ref[0].astype(F32) * MSG_SCALE
    weighted = jnp.concatenate(
        [(adjoint * radial_ref[n : n + 1]).astype(BF16) for n in range(nbasis)], axis=0
    )
    for tile in range(len(plan.tiles)):
        lanes = slice(tile * plan.width, (tile + 1) * plan.width)
        pulled = dot(weighted, all_ref[lanes], NT)
        total = slope_ref[0, :, lanes] * pulled[:slots]
        for n in range(1, nbasis):
            total = total + slope_ref[n, :, lanes] * pulled[n * slots : (n + 1) * slots]
        pair_ref[:, lanes] = total


def force_kernel(plan, nrefs, places, *refs):
    far_refs, refs = refs[:nrefs], refs[nrefs:]
    (own_ref, basis_ref, pair_ref, rows_ref), refs = refs[:4], refs[4:]
    (apart_ref, slope_ref, factor_ref, turned_ref), refs = refs[:4], refs[4:]
    (radial_ref, mixing_ref, mix_ref, vector_ref, table_ref), refs = refs[:5], refs[5:]
    out_ref, all_ref = refs
    slots, nbasis, nspec, width = plan.slots, plan.nbasis, plan.nspec, plan.width
    if plan.small:
        far = [far_refs[side][tile] for tile in range(len(plan.tiles)) for side in range(len(plan.sides))]
        far = jnp.concatenate(far, axis=0)
    else:
        gather_far(plan, places, far_refs, all_ref)
        far = all_ref[...]
    summed = dot(basis_ref[0].reshape(nbasis * slots, plan.far), far)
    adjoint = jnp.zeros((slots, summed.shape[1]), F32)
    for n in range(nbasis):
        adjoint = adjoint + summed[n * slots : (n + 1) * slots] * radial_ref[n : n + 1]
    adjoint = own_ref[...] + MSG_SCALE * adjoint
    mixing = mixing_ref[...]
    gate = sigmoid(mixing)
    back = (adjoint * (gate * (1.0 + mixing * (1.0 - gate)))).astype(BF16)
    invariants = dot(back, mix_ref[...])
    channels = invariants.shape[1] // 2
    on_scalar = (MSG_SCALE * invariants[:, :channels]).astype(BF16)
    doubled = (2.0 * MSG_SCALE) * invariants[:, channels:]
    on_vector = (vector_ref[...] * jnp.concatenate([doubled] * 3, axis=0)).astype(BF16)
    weights = jnp.concatenate(
        [dot(on_scalar, table_ref[0], NT), dot(on_vector, table_ref[1], NT)], axis=0
    ).astype(BF16)
    group = lax.broadcasted_iota(jnp.int32, weights.shape, 1) // nspec
    weights = weights.astype(F32)
    weights = jnp.concatenate(
        [jnp.where(group == n, weights, 0.0).astype(BF16) for n in range(nbasis)], axis=0
    )
    species = lax.broadcasted_iota(jnp.int32, (nbasis * nspec, width), 0) % nspec
    own = [jnp.zeros((slots, width), F32) for _ in range(3)]
    pulls = []
    for tile in range(len(plan.tiles)):
        lanes = slice(tile * width, (tile + 1) * width)
        hot = (rows_ref[tile, 3:4].astype(jnp.int32) == species).astype(F32).astype(BF16)
        spread = dot(weights, hot)
        total = pair_ref[:, lanes]
        sides, turns = [None] * 3, [None] * 3
        for n in range(nbasis):
            start = n * 4 * slots
            total = total + slope_ref[n, :, lanes] * spread[start : start + slots]
            for k in range(3):
                piece = spread[start + (k + 1) * slots : start + (k + 2) * slots]
                side = factor_ref[n, :, lanes] * piece
                turn = turned_ref[n, :, lanes] * piece
                sides[k] = side if n == 0 else sides[k] + side
                turns[k] = turn if n == 0 else turns[k] + turn
        for k in range(3):
            total = total + apart_ref[k, :, lanes] * turns[k]
        pulls.append([])
        for k in range(3):
            pull = apart_ref[k, :, lanes] * total + sides[k]
            own[k] = own[k] + pull
            pulls[-1].append(jnp.sum(pull, axis=0, keepdims=True))
    own = jnp.concatenate(own, axis=0)
    high = own.astype(BF16)
    low = (own - high.astype(F32)).astype(BF16)
    ones = jnp.ones((8, width), BF16)
    mine = (dot(ones, high, NT) + dot(ones, low, NT))[:1]
    mine = jnp.concatenate([mine[:, k * slots : (k + 1) * slots] for k in range(3)], axis=0)
    if plan.small:
        out_ref[...] = jnp.zeros_like(out_ref)
    side_of = lax.broadcasted_iota(jnp.int32, (3, width), 1) // slots
    for tile in range(len(plan.tiles)):
        pulled = jnp.concatenate(pulls[tile], axis=0)
        if tile == 0:
            others = [jnp.zeros_like(mine)] * (len(plan.sides) - 1)
            pulled = pulled - jnp.concatenate([mine] + others, axis=1)
        if not plan.small:
            out_ref[plan.staged_place(places, tile)] = pulled
            continue
        for side in range(len(plan.sides)):
            place = plan.global_id(plan.offset(tile, side))
            out_ref[place, :3] = jnp.where(side_of == side, pulled, 0.0)


def begin(pairs, sems):
    copies = [pltpu.make_async_copy(*pair, sems.at[m]) for m, pair in enumerate(pairs)]
    for copy in copies:
        copy.start()
    return copies


def prepare_kernel(plan, counts_ref, *refs):
    fetched, (sent_ref, table_ref, wide_ref), refs = refs[:10], refs[10:13], refs[13:]
    kept, (place_ref, kind_ref, radial_ref, sems) = refs[:7], refs[7:]
    copies = begin(zip(fetched, (place_ref, kind_ref, radial_ref, *kept)), sems)
    for copy in copies[:2]:
        copy.wait()
    live = lax.broadcasted_iota(jnp.int32, (1, plan.slots), 1) < counts_ref[0]
    rows = [
        jnp.where(live, place_ref[0], FAR),
        place_ref[1],
        place_ref[2],
        jnp.where(live, kind_ref[...], -1).astype(F32),
    ]
    rows = jnp.concatenate(rows, axis=0)
    rows = jnp.concatenate([rows, rows], axis=1)
    for copy in range(sent_ref.shape[0]):
        sent_ref[copy] = rows
    for copy in copies[2:]:
        copy.wait()
    embed, nspec = kept[0][...].astype(F32), plan.nspec
    for g in range(2):
        for n in range(plan.nbasis):
            weighted = radial_ref[g, n : n + 1] * embed
            table_ref[g, n * nspec : (n + 1) * nspec] = weighted.astype(BF16)
    wide_ref[...] = jnp.zeros_like(wide_ref)
    count, channels = table_ref.shape[1:]
    for m in range(1 + 2 * len(plan.plain)):
        start = (m + 1) // 2 * channels
        wide_ref[m * count : (m + 1) * count, start : start + channels] = table_ref[1]


def sum_kernel(plan, parts_ref, force_ref):
    total = parts_ref[0]
    for part in range(1, parts_ref.shape[0]):
        total = total + parts_ref[part]
    total = total[:, : plan.slots] + total[:, plan.slots :]
    for k in range(3):
        force_ref[k] = -total[k : k + 1]


VMEM_SPEC = pl.BlockSpec(memory_space=pltpu.VMEM)
SMEM_SPEC = pl.BlockSpec(memory_space=pltpu.SMEM)
HBM_SPEC = pl.BlockSpec(memory_space=pltpu.HBM)


def simple_call(kernel, plan, operands, outs, scalars=0, scratch=(), flops=2**20, near=False, fetched=0):
    single = not isinstance(outs, list)
    kind = pltpu.VMEM if near else jax.ShapeDtypeStruct
    shapes = [kind(*out) for out in ([outs] if single else outs)]

    def body(*refs):
        kernel(plan, *refs)

    got = pl.pallas_call(
        body,
        out_shape=shapes,
        in_specs=[SMEM_SPEC] * scalars
        + [VMEM_SPEC] * (len(operands) - scalars - fetched)
        + [HBM_SPEC] * fetched,
        out_specs=[VMEM_SPEC] * len(shapes),
        scratch_shapes=[pltpu.VMEM(*buffer) for buffer in scratch]
        + [pltpu.SemaphoreType.DMA((fetched,))] * (fetched > 0),
        compiler_params=pltpu.CompilerParams(vmem_limit_bytes=FETCH_LIMIT if fetched else VMEM_LIMIT),
        cost_estimate=pl.CostEstimate(flops=flops, bytes_accessed=2**20, transcendentals=0),
    )(*operands)
    return got[0] if single else got


def call(kernel, plan, far, operands, outs, scratch, flops, **options):
    def body(plan, *refs):
        kernel(plan, len(far), plan.places(), *refs)

    return simple_call(body, plan, [*far, *operands], outs, 0, scratch, flops, **options)


def swaps(count):
    if count == 2:
        return [[1, 0]]
    if paired(count):
        near = [i ^ 1 for i in range(count)]
        far = [(i - 1 + 2 * (i % 2)) % count for i in range(count)]
        return [near, far]
    return [[(i + o) % count for i in range(count)] for o in offsets_of(count)[1:]]


def brought(plan, block, second, mixed):
    sizes, sources = plan.sizes, {axis: swaps(plan.sizes[axis]) for axis in AXES}
    got = []
    for m in range(len(sources["gx" if second else "gz"])):
        pairs = []
        for x, y, z in itertools.product(*(range(sizes[axis]) for axis in AXES)):
            along_x = second != (mixed and y % 2 == 1)
            source = (sources["gx"][m][x], y, z) if along_x else (x, y, sources["gz"][m][z])
            pairs.append((flat(sizes, *source), flat(sizes, x, y, z)))
        got.append(lax.ppermute(block, AXES, pairs))
    return got


def flat(sizes, x, y, z):
    return (x * sizes["gy"] + y) * sizes["gz"] + z


def along(block, axis):
    return [
        lax.ppermute(block, axis, [(source, i) for i, source in enumerate(sources)])
        for sources in swaps(lax.axis_size(axis))
    ]


def neighbours(plan, block, again=None):
    column = jnp.stack([block if again is None else again] + brought(plan, block, False, plan.mixed))
    return from_columns(plan, column, plan.mixed)


def from_columns(plan, column, mixed, again=None):
    columns = [column] + brought(plan, column, True, mixed)
    count = plan.sizes["gx"]
    for step in plan.columns[plan.wide :]:
        columns.append(lax.ppermute(column, "gx", [((i + step) % count, i) for i in range(count)]))
    if again is not None:
        columns[0] = again
    swapped = [[column] + along(column, "gy") for column in columns]
    return [column[side] for side in range(len(plan.sides)) for column in swapped]


def everywhere(copies):
    return lax.all_to_all(copies, AXES, 0, 0, tiled=True)


def folded(pieces, axis):
    total = pieces[0]
    for piece, sources in zip(pieces[1:], swaps(lax.axis_size(axis))):
        total = total + lax.ppermute(piece, axis, list(enumerate(sources)))
    return total


def fold(plan, pulls):
    for axis in ("gx", "gz"):
        parts = len(offsets_of(plan.sizes[axis]))
        pulls = pulls.reshape((parts, -1) + pulls.shape[1:])
        pulls = folded([pulls[m] for m in range(parts)], axis)
    pulls = pulls[0]
    sides = [pulls[:, m * plan.slots : (m + 1) * plan.slots] for m in range(len(plan.sides))]
    return folded(sides, "gy")


def local_program(mesh):
    def local(
        positions,
        species,
        counts,
        embed,
        radial_one,
        mix_one,
        read_one,
        radial_two,
        mix_two,
        read_hidden,
        read_out,
    ):
        slots, channels = positions.shape[-1], embed.shape[1]
        nbasis, nspec = radial_two.shape[0], embed.shape[0]
        plan = Plan(mesh, slots, nbasis, nspec)
        given = [positions[0, 0, 0].reshape(3, 1, slots), species.reshape(1, slots), radial_one]
        weights = [embed, mix_one, radial_two, read_out[None], read_one[None], mix_two, read_hidden]
        sent, table, wide, *weights = simple_call(
            prepare_kernel,
            plan,
            [counts.reshape(1), *given, *weights],
            [
                ((plan.ndev if plan.small else 1, 4, 2 * slots), F32),
                ((2, nbasis * nspec, channels), BF16),
                (((1 + 2 * len(plan.plain)) * nbasis * nspec, (1 + len(plan.plain)) * channels), BF16),
            ]
            + [(weight.shape, weight.dtype) for weight in weights],
            1,
            [(array.shape, array.dtype) for array in given],
            near=True,
            fetched=len(given) + len(weights),
        )
        embed, mix_one, radial_two, out_row, one_row, mix_two, read_hidden = weights
        far_sent = [everywhere(sent)] if plan.small else neighbours(plan, sent[0])
        pair_flops = 100 * slots * plan.far
        rows, basis, layer, vector, mixing, cols = call(
            first_kernel,
            plan,
            far_sent,
            [table, wide, embed, mix_one],
            [
                ((len(plan.tiles), 4, plan.width), F32),
                ((plan.known, nbasis, slots, plan.far), BF16),
                ((len(plan.column), slots, channels), BF16),
                ((3 * slots, channels), F32),
                ((slots, channels), F32),
                ((plan.known, slots, 8), F32),
            ],
            [
                ((len(plan.column), nbasis, plan.kinds * slots, plan.far), BF16),
                ((len(plan.tiles) * len(plan.sides), 4, 2 * slots), F32),
            ],
            pair_flops,
        )
        more = max(len(plan.targets) - plan.known, 1)
        again, more_basis, more_cols = call(
            basis_kernel,
            plan,
            far_sent[:1],
            [layer],
            [
                (layer.shape, BF16),
                ((more, nbasis, slots, plan.far), BF16),
                ((more, slots, 8), F32),
            ],
            [],
            pair_flops,
        )
        one_row, apart, slope, factor, turned = simple_call(
            slope_kernel,
            plan,
            [rows, cols, one_row],
            [(one_row.shape, F32)]
            + [((count, slots, plan.far), F32) for count in (3, nbasis, nbasis, nbasis)],
            flops=pair_flops,
        )
        if plan.small:
            far_layer = from_columns(plan, layer, False, again)
        else:
            far_layer = neighbours(plan, layer[0], again[0])
        far_scratch = ((plan.far, channels), BF16)
        held = len(plan.columns) * len(plan.column) if plan.small else len(plan.tiles)
        held = held * len(plan.sides)
        adjoint, kept, before, own_adjoint, own_far = call(
            second_kernel,
            plan,
            far_layer,
            [layer, basis, cols, more_basis, more_cols, radial_two, mix_two, read_hidden, out_row, one_row],
            [
                ((len(plan.targets), slots, channels), BF16),
                ((slots, channels), BF16),
                ((slots, read_hidden.shape[0]), F32),
                ((slots, channels), F32),
                far_scratch,
            ],
            [((held, slots, channels), BF16)],
            pair_flops,
        )
        again, pair, energy, features = simple_call(
            energy_kernel,
            plan,
            [own_far, adjoint, slope, radial_two, cols, layer, before, out_row, one_row, kept],
            [
                ((1, slots, channels), BF16),
                ((slots, plan.far), F32),
                ((1, slots), F32),
                ((slots, channels), BF16),
            ],
            flops=pair_flops,
        )
        if plan.small:
            far_adjoint = [adjoint] + along(adjoint, "gy")
        else:
            far_adjoint = neighbours(plan, adjoint[0], again[0])
        pulls = call(
            force_kernel,
            plan,
            far_adjoint,
            [own_adjoint, basis, pair, rows, apart, slope, factor, turned]
            + [radial_two, mixing, mix_one, vector, table],
            [((plan.ndev, 4, plan.width) if plan.small else (len(plan.tiles), 3, plan.width), F32)],
            [far_scratch],
            pair_flops,
        )
        if plan.small:
            forces = simple_call(sum_kernel, plan, [everywhere(pulls[0])], ((3, 1, slots), F32))
        else:
            forces = -fold(plan, pulls[0])
        return (
            forces.reshape(1, 1, 1, 3, slots),
            energy[None, None],
            features.T[None, None, None],
        )

    return local


def solution(mesh):
    split = [P(*AXES, None, None), P(*AXES, None), P(*AXES)]
    out_specs = (P(*AXES, None, None), P(*AXES, None), P(*AXES, None, None))
    return jax.shard_map(
        local_program(mesh),
        mesh=mesh,
        in_specs=tuple(split + [P()] * 8),
        out_specs=out_specs,
        check_vma=False,
    )
```

```python
import itertools
import math

import jax
import jax.numpy as jnp
from jax import lax
from jax.experimental import pallas as pl
from jax.experimental.pallas import tpu as pltpu
from jax.sharding import PartitionSpec as P

CELL_SIDE = 5.0
CUT_SQUARE = 25.0
SOFTEN = 0.25
MSG_SCALE = 0.05
ROOT_THREE = math.sqrt(3.0)
FAR = 1.0e4
AXES = ("gx", "gy", "gz")
F32 = jnp.float32
BF16 = jnp.bfloat16
COS_TERMS = (
    0.9999999532476085,
    -4.934792830619644,
    4.058411352862619,
    -1.3318765680811142,
    0.2196896110983216,
)
SIN_TERMS = (
    3.1415926401307073,
    -5.167710083507891,
    2.550077523214631,
    -0.5982912856208596,
    0.07765766030668693,
)
VMEM_LIMIT = 24 * 1024 * 1024
FETCH_LIMIT = 60 * 1024 * 1024
NT = (((1,), (1,)), ((), ()))
NN = (((1,), (0,)), ((), ()))


def dot(a, b, dims=NN):
    return lax.dot_general(a, b, dims, preferred_element_type=F32)


def dot_exact(a, b, dims=NN):
    return lax.dot_general(
        a, b, dims, precision=lax.Precision.HIGHEST, preferred_element_type=F32
    )


def split_dot(a, b):
    high = a.astype(BF16)
    low = (a - high.astype(F32)).astype(BF16)
    return dot(high, b) + dot(low, b)


def offsets_of(count):
    return (0, 1) if count == 2 else (0, 1, -1)


def paired(count):
    return count > 2 and count % 2 == 0


def matched(which, parity):
    return jnp.int32(0) if which == 0 else 1 + (parity if which == 1 else 1 - parity)


def poly(terms, arg):
    total = arg * terms[-1] + terms[-2]
    for term in terms[-3::-1]:
        total = total * arg + term
    return total


class Plan:
    def __init__(self, mesh, slots, nbasis, nspec):
        self.sizes = {axis: mesh.shape[axis] for axis in AXES}
        self.ndev = math.prod(self.sizes.values())
        self.tiles = list(
            itertools.product(offsets_of(self.sizes["gx"]), offsets_of(self.sizes["gz"]))
        )
        self.sides = offsets_of(self.sizes["gy"])
        self.slots = slots
        self.width = len(self.sides) * slots
        self.far = len(self.tiles) * self.width
        self.nbasis = nbasis
        self.nspec = nspec
        self.depth = len(offsets_of(self.sizes["gz"]))
        self.wide = len(offsets_of(self.sizes["gx"]))
        self.brought = list(itertools.product(range(self.wide), range(self.depth)))
        self.mixed = self.depth == self.wide and self.sizes["gy"] % 2 == 0
        self.small = self.ndev <= 64 and len(self.sides) == 2
        self.columns, self.column = [self.reach(axis) if self.small else [0] for axis in ("gx", "gz")]
        self.known = self.depth if self.small else 1
        self.targets = self.tiles if self.small else self.tiles[:1]
        self.wrapped = [self.sizes[axis] == 2 for axis in AXES]
        self.plain = [k for k in range(3) if not self.wrapped[k]]
        self.folded = [k for k in range(3) if self.wrapped[k]]
        self.kinds = 2 + len(self.folded)

    def global_id(self, offset):
        place = 0
        for axis, step in zip(AXES, offset):
            count = self.sizes[axis]
            place = place * count + lax.rem(lax.axis_index(axis) + (step + count), count)
        return place

    def reach(self, axis):
        near, count = offsets_of(self.sizes[axis]), self.sizes[axis]
        steps = list(near)
        for step in [a + b for a in near for b in near]:
            if all((step - other) % count for other in steps):
                steps.append(step)
        return steps

    def held(self, x, z):
        found = []
        for step, steps, axis in ((x, self.columns, "gx"), (z, self.column, "gz")):
            found.append([(step - other) % self.sizes[axis] == 0 for other in steps].index(True))
        return found[0] * len(self.column) + found[1]

    def places(self):
        index = {axis: lax.axis_index(axis) for axis in AXES}

        def parity(axis):
            return lax.rem(index[axis], 2) if paired(self.sizes[axis]) else jnp.int32(0)

        turns = parity("gx"), parity("gz")
        core = lax.rem(index["gy"], 2) if self.mixed else jnp.int32(0)
        found = []
        for side in range(len(self.sides)):
            x_first = core if side == 0 or not self.mixed else 1 - core
            for second, first in self.brought:
                plain = matched(second, turns[0]) * self.depth + matched(first, turns[1])
                crossed = matched(first, turns[0]) * self.depth + matched(second, turns[1])
                tile = jnp.where(x_first == 1, crossed, plain) if self.mixed else plain
                found.append(tile * len(self.sides) + side)
        found += turns
        return [jnp.asarray(place, jnp.int32) for place in found]

    def brought_place(self, places, side, pair):
        return places[side * len(self.brought) + pair]

    def staged_place(self, places, tile):
        start = len(self.sides) * len(self.brought)
        x, z = divmod(tile, self.depth)
        return matched(x, places[start]) * self.depth + matched(z, places[start + 1])

    def offset(self, tile, side):
        ox, oz = self.tiles[tile]
        return (ox, self.sides[side], oz)


def scaled(terms, factor):
    return [factor * term for term in terms]


def separations(plan, rows, cols, side=CELL_SIDE):
    parts = []
    for axis in range(3):
        diff = rows[axis] - cols[axis]
        if plan.wrapped[axis]:
            diff = jnp.where(diff > side, diff - 2.0 * side, diff)
        parts.append(diff)
    return parts


def distance(plan, parts, tile, soften=SOFTEN):
    dist_sq = parts[0] * parts[0] + parts[1] * parts[1] + parts[2] * parts[2] + soften
    if tile == 0:
        row = lax.broadcasted_iota(jnp.int32, dist_sq.shape, 0)
        col = lax.broadcasted_iota(jnp.int32, dist_sq.shape, 1)
        dist_sq = jnp.where(row == col, FAR, dist_sq)
    return dist_sq, lax.rsqrt(dist_sq)


def waves(dist_sq, inverse):
    arg = jnp.minimum(dist_sq * inverse * (1.0 / CELL_SIDE) - 0.5, 0.5)
    square = arg * arg
    return poly(COS_TERMS, square), -(arg * poly(SIN_TERMS, square))


def global_block(plan, far_ref, tile, side, target):
    x, y, z = plan.offset(tile, side)
    return far_ref[plan.global_id((x + target[0], y, z + target[1]))]


def own_columns(plan, block):
    held = jnp.concatenate([block, block], axis=0).T[: plan.slots]
    kind = held[:, 3:4]
    lane = lax.broadcasted_iota(jnp.int32, held.shape, 1)
    live = kind >= 0.0
    held = jnp.where((lane == 0) & ~live, -FAR, held)
    return jnp.where(lane == 3, live.astype(F32), held), kind


def scaled_columns(held):
    return [held[:, axis : axis + 1] * (1.0 / CELL_SIDE) for axis in range(3)]


def basis_of(plan, placed, cols, tile):
    parts = separations(plan, [placed[k : k + 1] for k in range(3)], cols, 1.0)
    dist_sq, inverse = distance(plan, parts, tile, SOFTEN / CUT_SQUARE)
    turn = jnp.minimum(dist_sq * inverse - 0.5, 0.5)
    square = turn * turn
    double = turn * poly(scaled(SIN_TERMS, -2.0), square)
    fade = jnp.maximum(1.0 - dist_sq, 0.0)
    basis = [poly(scaled(COS_TERMS, 1.0 / CELL_SIDE), square) * (fade * fade * inverse)]
    for n in range(1, plan.nbasis):
        basis.append(double * basis[-1] if n == 1 else double * basis[-1] - basis[-2])
    return parts, inverse, basis


def first_kernel(plan, nrefs, places, *refs):
    far_refs, refs = refs[:nrefs], refs[nrefs:]
    (table_ref, wide_ref, embed_ref, mix_ref), refs = refs[:4], refs[4:]
    rows_ref, basis_ref, layer_ref, vector_ref, mixing_ref, cols_ref, pair_ref, block_ref = refs
    slots, nbasis, nspec = plan.slots, plan.nbasis, plan.nspec

    def put(place, block):
        block_ref[place] = block

    if not plan.small:
        scatter(plan, places, far_refs, put)

    def block_of(tile, side, up):
        if plan.small:
            return global_block(plan, far_refs[0], tile, side, (0, up))
        return block_ref[tile * len(plan.sides) + side]

    species = lax.broadcasted_iota(jnp.int32, (nbasis * nspec, plan.width), 0) % nspec
    shifts = [tile_shift(plan, tile) for tile in range(len(plan.tiles))]
    own, counted, places_of = [], [], []
    for which, up in enumerate(plan.column):
        held, kind = own_columns(plan, block_of(0, 0, up))
        own.append(kind)
        if which < plan.known:
            cols_ref[which] = held
        cols = scaled_columns(held)
        places_of.append(cols)
        hot = []
        for tile in range(len(plan.tiles)):
            blocks = [block_of(tile, side, up) for side in range(len(plan.sides))]
            placed = side_by_side(plan, blocks) + shifts[tile]
            if which == 0:
                rows_ref[tile] = placed
            is_kind = placed[3:4].astype(jnp.int32) == species
            placed = placed * (1.0 / CELL_SIDE)
            high = placed.astype(BF16).astype(F32)
            low = placed - high
            columns = [jnp.where(is_kind, 1.0, 0.0)]
            for k in plan.plain:
                columns += [jnp.where(is_kind, part[k : k + 1], 0.0) for part in (high, low)]
            hot.append(jnp.concatenate([column.astype(BF16) for column in columns], axis=0))
            parts, inverse, basis = basis_of(plan, placed, cols, tile)
            scale = inverse * ROOT_THREE
            units = [scale.astype(BF16)] + [(scale * parts[k]).astype(BF16) for k in plan.folded]
            lanes = slice(tile * plan.width, (tile + 1) * plan.width)
            for n in range(nbasis):
                packed = basis[n].astype(BF16)
                if which < plan.known:
                    basis_ref[which, n, :, lanes] = packed
                pair_ref[which, n, :slots, lanes] = packed
                for m, unit in enumerate(units):
                    pair_ref[which, n, (m + 1) * slots : (m + 2) * slots, lanes] = unit * packed
        hot = jnp.concatenate(hot, axis=1)
        gathered = dot(pair_ref[which].reshape(nbasis * plan.kinds * slots, plan.far), hot, NT)
        gathered = gathered.reshape(nbasis, plan.kinds * slots, hot.shape[0])
        group = lax.broadcasted_iota(jnp.int32, gathered.shape[1:], 1) % (nbasis * nspec) // nspec
        total = gathered[0]
        for n in range(1, nbasis):
            total = jnp.where(group == n, gathered[n], total)
        counted.append(total)
    scalar = jnp.concatenate([total[:slots, : nbasis * nspec] for total in counted], axis=0)
    scalar = MSG_SCALE * split_dot(scalar, table_ref[0])
    moved = jnp.concatenate([total[slots : 2 * slots] for total in counted], axis=0)
    moved = MSG_SCALE * split_dot(moved, wide_ref[...])
    channels = layer_ref.shape[2]
    norm = None
    for k in range(3):
        if k in plan.plain:
            start = (plan.plain.index(k) + 1) * channels
            place = jnp.concatenate([cols[k] for cols in places_of], axis=0)
            vector = moved[:, start : start + channels] - place * moved[:, :channels]
        else:
            start = (plan.folded.index(k) + 2) * slots
            vector = [total[start : start + slots, : nbasis * nspec] for total in counted]
            vector = MSG_SCALE * split_dot(jnp.concatenate(vector, axis=0), table_ref[1])
        vector_ref[k * slots : (k + 1) * slots] = vector[:slots]
        norm = vector * vector if k == 0 else norm + vector * vector
    invariants = jnp.concatenate([scalar.astype(BF16), norm.astype(BF16)], axis=1)
    mixing = dot(invariants, mix_ref[...], NT)
    mixing_ref[...] = mixing[:slots]
    kind = jnp.concatenate(own, axis=0)
    own_species = lax.broadcasted_iota(jnp.int32, (kind.shape[0], nspec), 1)
    own_hot = (kind.astype(jnp.int32) == own_species).astype(F32).astype(BF16)
    layer = (dot(own_hot, embed_ref[...]) + mixing * sigmoid(mixing)).astype(BF16)
    for which in range(layer_ref.shape[0]):
        layer_ref[which] = layer[which * slots : (which + 1) * slots]


def sigmoid(value):
    return 1.0 / (1.0 + jnp.exp(-value))


def scatter(plan, places, far_refs, put):
    for side in range(len(plan.sides)):
        for pair, (second, first) in enumerate(plan.brought):
            put(plan.brought_place(places, side, pair), far_refs[side * plan.wide + second][first])


def scatter_held(plan, places, far_refs, put):
    turn = places[len(plan.sides) * len(plan.brought)]
    for side in range(len(plan.sides)):
        for m in range(len(plan.columns)):
            x = matched(m, turn) if m < plan.wide else m
            for z in range(len(plan.column)):
                place = (x * len(plan.column) + z) * len(plan.sides) + side
                put(place, far_refs[m][z] if side == 0 else far_refs[len(plan.columns)][m, z])


def far_blocks(plan, block_ref, target):
    blocks = []
    for x, z in plan.tiles:
        place = plan.held(x + target[0], z + target[1]) * len(plan.sides)
        blocks += [block_ref[place + side] for side in range(len(plan.sides))]
    return jnp.concatenate(blocks, axis=0)


def side_by_side(plan, blocks):
    if len(blocks) == 2:
        lane = lax.broadcasted_iota(jnp.int32, blocks[0].shape, 1)
        return jnp.where(lane < plan.slots, blocks[0], blocks[1])
    return jnp.concatenate([block[:, : plan.slots] for block in blocks], axis=1)


def tile_shift(plan, tile):
    row = lax.broadcasted_iota(jnp.int32, (4, plan.width), 0)
    side = lax.broadcasted_iota(jnp.int32, (4, plan.width), 1) // plan.slots
    shift = jnp.zeros((4, plan.width), F32)
    for s in range(len(plan.sides)):
        for k, steps in enumerate(plan.offset(tile, s)):
            if steps:
                shift = jnp.where((row == k) & (side == s), CELL_SIDE * steps, shift)
    return shift


def gather_far(plan, places, far_refs, all_ref):
    def put(place, block):
        start = pl.multiple_of(place * plan.slots, plan.slots)
        all_ref[pl.ds(start, plan.slots)] = block

    scatter(plan, places, far_refs, put)


def second_kernel(plan, nrefs, places, *refs):
    far_refs, refs = refs[:nrefs], refs[nrefs:]
    (layer_ref, basis_ref, cols_ref, more_ref, more_cols_ref, radial_ref, mix_ref), refs = refs[:7], refs[7:]
    (hidden_ref, out_ref, one_ref), refs = refs[:3], refs[3:]
    adjoint_ref, features_ref, before_ref, own_ref, own_far_ref, block_ref = refs
    slots, nbasis, known = plan.slots, plan.nbasis, len(plan.targets)

    def put(place, block):
        block_ref[place] = block

    (scatter_held if plan.small else scatter)(plan, places, far_refs, put)
    messages, layers, lives = [], [], []
    for which, target in enumerate(plan.targets):
        if plan.small:
            far = far_blocks(plan, block_ref, target)
            layers.append(block_ref[plan.held(*target) * len(plan.sides)])
        else:
            far = block_ref[...].reshape(plan.far, -1)
            layers.append(layer_ref[0])
        first = which < plan.known
        held_ref, held_cols_ref = (basis_ref, cols_ref) if first else (more_ref, more_cols_ref)
        place = which if first else which - plan.known
        lives.append(held_cols_ref[place, :, 3:4])
        if which == 0:
            own_far_ref[...] = far
        summed = dot(held_ref[place].reshape(nbasis * slots, plan.far), far)
        message = summed[:slots] * radial_ref[0:1]
        for n in range(1, nbasis):
            message = message + summed[n * slots : (n + 1) * slots] * radial_ref[n : n + 1]
        messages.append((MSG_SCALE * message).astype(BF16))
    mixing = dot(jnp.concatenate(messages, axis=0), mix_ref[...], NT)
    gate = sigmoid(mixing)
    layer = jnp.concatenate(layers, axis=0).astype(F32)
    features = (layer + mixing * gate).astype(BF16)
    features_ref[...] = features[:slots]
    before = dot(features, hidden_ref[...], NT)
    before_ref[...] = before[:slots]
    open_hidden = sigmoid(before)
    live = jnp.concatenate(lives, axis=0)
    slope = out_ref[...] * (open_hidden * (1.0 + before * (1.0 - open_hidden))) * live
    from_hidden = dot(slope.astype(BF16), hidden_ref[...])
    own_ref[...] = from_hidden[:slots] + one_ref[...] * live[:slots]
    back = from_hidden * (gate * (1.0 + mixing * (1.0 - gate)))
    adjoint = dot(back.astype(BF16), mix_ref[...]).astype(BF16)
    for which in range(known):
        adjoint_ref[which] = adjoint[which * slots : (which + 1) * slots]


def basis_kernel(plan, nrefs, places, *refs):
    far_ref, (layer_ref, again_ref, more_ref, more_cols_ref) = refs[0], refs[nrefs:]
    again_ref[...] = layer_ref[...]
    for which, target in enumerate(plan.targets[plan.known :]):
        held, _ = own_columns(plan, global_block(plan, far_ref, 0, 0, target))
        more_cols_ref[which] = held
        for tile in range(len(plan.tiles)):
            lanes = slice(tile * plan.width, (tile + 1) * plan.width)
            blocks = [global_block(plan, far_ref, tile, s, target) for s in range(len(plan.sides))]
            placed = (side_by_side(plan, blocks) + tile_shift(plan, tile)) * (1.0 / CELL_SIDE)
            basis = basis_of(plan, placed, scaled_columns(held), tile)[2]
            for n in range(plan.nbasis):
                more_ref[which, n, :, lanes] = basis[n].astype(BF16)


def slope_kernel(plan, rows_ref, cols_ref, one_ref, *refs):
    kept_ref, apart_ref, slope_ref, radial_ref, turned_ref = refs
    kept_ref[...] = one_ref[...]
    cols = [cols_ref[0, :, axis : axis + 1] for axis in range(3)]
    for tile in range(len(plan.tiles)):
        lanes = slice(tile * plan.width, (tile + 1) * plan.width)
        parts = separations(plan, [rows_ref[tile, k : k + 1] for k in range(3)], cols)
        for k in range(3):
            apart_ref[k, :, lanes] = parts[k]
        dist_sq, inverse = distance(plan, parts, tile)
        sine, cosine = waves(dist_sq, inverse)
        fade = jnp.maximum(1.0 - dist_sq * (1.0 / CUT_SQUARE), 0.0)
        radial = fade * fade * inverse
        on_sine = -inverse * ((4.0 / CUT_SQUARE) * fade + radial * inverse)
        on_cosine = (math.pi / CELL_SIDE) * (inverse * radial)
        scale = ROOT_THREE * inverse
        scaled = scale * radial
        square = inverse * inverse
        double = 2.0 * cosine
        before_s, now_s, before_c, now_c = None, sine, None, cosine
        for n in range(plan.nbasis):
            if n == 1:
                before_s, now_s = now_s, double * now_s
                before_c, now_c = now_c, double * now_c - 1.0
            elif n > 1:
                before_s, now_s = now_s, double * now_s - before_s
                before_c, now_c = now_c, double * now_c - before_c
            slope = on_sine * now_s + (n + 1.0) * on_cosine * now_c
            factor = scaled * now_s
            slope_ref[n, :, lanes] = slope
            radial_ref[n, :, lanes] = factor
            turned_ref[n, :, lanes] = scale * slope - square * factor


def energy_kernel(plan, *refs):
    (all_ref, adjoint_ref, slope_ref, radial_ref, cols_ref, layer_ref), refs = refs[:6], refs[6:]
    (before_ref, out_ref, one_ref, kept_ref), refs = refs[:4], refs[4:]
    again_ref, pair_ref, energy_ref, features_ref = refs
    slots, nbasis = plan.slots, plan.nbasis
    again_ref[...] = adjoint_ref[:1]
    features_ref[...] = kept_ref[...]
    before = before_ref[...]
    live = jnp.where(lax.broadcasted_iota(jnp.int32, (slots, 8), 1) == 0, cols_ref[0, :, 3:4], 0.0)
    live_row = dot(jnp.ones((1, 8), BF16), live.astype(BF16), NT)
    energy = dot_exact(one_ref[...], layer_ref[0].astype(F32), NT)
    energy = energy + dot_exact(out_ref[...], before * sigmoid(before), NT)
    energy_ref[...] = energy * live_row
    adjoint = adjoint_ref[0].astype(F32) * MSG_SCALE
    weighted = jnp.concatenate(
        [(adjoint * radial_ref[n : n + 1]).astype(BF16) for n in range(nbasis)], axis=0
    )
    for tile in range(len(plan.tiles)):
        lanes = slice(tile * plan.width, (tile + 1) * plan.width)
        pulled = dot(weighted, all_ref[lanes], NT)
        total = slope_ref[0, :, lanes] * pulled[:slots]
        for n in range(1, nbasis):
            total = total + slope_ref[n, :, lanes] * pulled[n * slots : (n + 1) * slots]
        pair_ref[:, lanes] = total


def force_kernel(plan, nrefs, places, *refs):
    far_refs, refs = refs[:nrefs], refs[nrefs:]
    (own_ref, basis_ref, pair_ref, rows_ref), refs = refs[:4], refs[4:]
    (apart_ref, slope_ref, factor_ref, turned_ref), refs = refs[:4], refs[4:]
    (radial_ref, mixing_ref, mix_ref, vector_ref, table_ref), refs = refs[:5], refs[5:]
    out_ref, all_ref = refs
    slots, nbasis, nspec, width = plan.slots, plan.nbasis, plan.nspec, plan.width
    if plan.small:
        far = [far_refs[side][tile] for tile in range(len(plan.tiles)) for side in range(len(plan.sides))]
        far = jnp.concatenate(far, axis=0)
    else:
        gather_far(plan, places, far_refs, all_ref)
        far = all_ref[...]
    summed = dot(basis_ref[0].reshape(nbasis * slots, plan.far), far)
    adjoint = jnp.zeros((slots, summed.shape[1]), F32)
    for n in range(nbasis):
        adjoint = adjoint + summed[n * slots : (n + 1) * slots] * radial_ref[n : n + 1]
    adjoint = own_ref[...] + MSG_SCALE * adjoint
    mixing = mixing_ref[...]
    gate = sigmoid(mixing)
    back = (adjoint * (gate * (1.0 + mixing * (1.0 - gate)))).astype(BF16)
    invariants = dot(back, mix_ref[...])
    channels = invariants.shape[1] // 2
    on_scalar = (MSG_SCALE * invariants[:, :channels]).astype(BF16)
    doubled = (2.0 * MSG_SCALE) * invariants[:, channels:]
    on_vector = (vector_ref[...] * jnp.concatenate([doubled] * 3, axis=0)).astype(BF16)
    weights = jnp.concatenate(
        [dot(on_scalar, table_ref[0], NT), dot(on_vector, table_ref[1], NT)], axis=0
    ).astype(BF16)
    group = lax.broadcasted_iota(jnp.int32, weights.shape, 1) // nspec
    weights = weights.astype(F32)
    weights = jnp.concatenate(
        [jnp.where(group == n, weights, 0.0).astype(BF16) for n in range(nbasis)], axis=0
    )
    species = lax.broadcasted_iota(jnp.int32, (nbasis * nspec, width), 0) % nspec
    own = [jnp.zeros((slots, width), F32) for _ in range(3)]
    pulls = []
    for tile in range(len(plan.tiles)):
        lanes = slice(tile * width, (tile + 1) * width)
        hot = (rows_ref[tile, 3:4].astype(jnp.int32) == species).astype(F32).astype(BF16)
        spread = dot(weights, hot)
        total = pair_ref[:, lanes]
        sides, turns = [None] * 3, [None] * 3
        for n in range(nbasis):
            start = n * 4 * slots
            total = total + slope_ref[n, :, lanes] * spread[start : start + slots]
            for k in range(3):
                piece = spread[start + (k + 1) * slots : start + (k + 2) * slots]
                side = factor_ref[n, :, lanes] * piece
                turn = turned_ref[n, :, lanes] * piece
                sides[k] = side if n == 0 else sides[k] + side
                turns[k] = turn if n == 0 else turns[k] + turn
        for k in range(3):
            total = total + apart_ref[k, :, lanes] * turns[k]
        pulls.append([])
        for k in range(3):
            pull = apart_ref[k, :, lanes] * total + sides[k]
            own[k] = own[k] + pull
            pulls[-1].append(jnp.sum(pull, axis=0, keepdims=True))
    own = jnp.concatenate(own, axis=0)
    high = own.astype(BF16)
    low = (own - high.astype(F32)).astype(BF16)
    ones = jnp.ones((8, width), BF16)
    mine = (dot(ones, high, NT) + dot(ones, low, NT))[:1]
    mine = jnp.concatenate([mine[:, k * slots : (k + 1) * slots] for k in range(3)], axis=0)
    if plan.small:
        out_ref[...] = jnp.zeros_like(out_ref)
    side_of = lax.broadcasted_iota(jnp.int32, (3, width), 1) // slots
    for tile in range(len(plan.tiles)):
        pulled = jnp.concatenate(pulls[tile], axis=0)
        if tile == 0:
            others = [jnp.zeros_like(mine)] * (len(plan.sides) - 1)
            pulled = pulled - jnp.concatenate([mine] + others, axis=1)
        if not plan.small:
            out_ref[plan.staged_place(places, tile)] = pulled
            continue
        for side in range(len(plan.sides)):
            place = plan.global_id(plan.offset(tile, side))
            out_ref[place, :3] = jnp.where(side_of == side, pulled, 0.0)


def begin(pairs, sems):
    copies = [pltpu.make_async_copy(*pair, sems.at[m]) for m, pair in enumerate(pairs)]
    for copy in copies:
        copy.start()
    return copies


def prepare_kernel(plan, counts_ref, *refs):
    fetched, (sent_ref, table_ref, wide_ref), refs = refs[:10], refs[10:13], refs[13:]
    kept, (place_ref, kind_ref, radial_ref, sems) = refs[:7], refs[7:]
    copies = begin(zip(fetched, (place_ref, kind_ref, radial_ref, *kept)), sems)
    for copy in copies[:2]:
        copy.wait()
    live = lax.broadcasted_iota(jnp.int32, (1, plan.slots), 1) < counts_ref[0]
    rows = [
        jnp.where(live, place_ref[0], FAR),
        place_ref[1],
        place_ref[2],
        jnp.where(live, kind_ref[...], -1).astype(F32),
    ]
    rows = jnp.concatenate(rows, axis=0)
    rows = jnp.concatenate([rows, rows], axis=1)
    for copy in range(sent_ref.shape[0]):
        sent_ref[copy] = rows
    for copy in copies[2:]:
        copy.wait()
    embed, nspec = kept[0][...].astype(F32), plan.nspec
    for g in range(2):
        for n in range(plan.nbasis):
            weighted = radial_ref[g, n : n + 1] * embed
            table_ref[g, n * nspec : (n + 1) * nspec] = weighted.astype(BF16)
    wide_ref[...] = jnp.zeros_like(wide_ref)
    count, channels = table_ref.shape[1:]
    for m in range(1 + 2 * len(plan.plain)):
        start = (m + 1) // 2 * channels
        wide_ref[m * count : (m + 1) * count, start : start + channels] = table_ref[1]


def sum_kernel(plan, parts_ref, force_ref):
    total = parts_ref[0]
    for part in range(1, parts_ref.shape[0]):
        total = total + parts_ref[part]
    total = total[:, : plan.slots] + total[:, plan.slots :]
    for k in range(3):
        force_ref[k] = -total[k : k + 1]


VMEM_SPEC = pl.BlockSpec(memory_space=pltpu.VMEM)
SMEM_SPEC = pl.BlockSpec(memory_space=pltpu.SMEM)
HBM_SPEC = pl.BlockSpec(memory_space=pltpu.HBM)


def simple_call(kernel, plan, operands, outs, scalars=0, scratch=(), flops=2**20, near=False, fetched=0):
    single = not isinstance(outs, list)
    kind = pltpu.VMEM if near else jax.ShapeDtypeStruct
    shapes = [kind(*out) for out in ([outs] if single else outs)]

    def body(*refs):
        kernel(plan, *refs)

    got = pl.pallas_call(
        body,
        out_shape=shapes,
        in_specs=[SMEM_SPEC] * scalars
        + [VMEM_SPEC] * (len(operands) - scalars - fetched)
        + [HBM_SPEC] * fetched,
        out_specs=[VMEM_SPEC] * len(shapes),
        scratch_shapes=[pltpu.VMEM(*buffer) for buffer in scratch]
        + [pltpu.SemaphoreType.DMA((fetched,))] * (fetched > 0),
        compiler_params=pltpu.CompilerParams(vmem_limit_bytes=FETCH_LIMIT if fetched else VMEM_LIMIT),
        cost_estimate=pl.CostEstimate(flops=flops, bytes_accessed=2**20, transcendentals=0),
    )(*operands)
    return got[0] if single else got


def call(kernel, plan, far, operands, outs, scratch, flops, **options):
    def body(plan, *refs):
        kernel(plan, len(far), plan.places(), *refs)

    return simple_call(body, plan, [*far, *operands], outs, 0, scratch, flops, **options)


def swaps(count):
    if count == 2:
        return [[1, 0]]
    if paired(count):
        near = [i ^ 1 for i in range(count)]
        far = [(i - 1 + 2 * (i % 2)) % count for i in range(count)]
        return [near, far]
    return [[(i + o) % count for i in range(count)] for o in offsets_of(count)[1:]]


def brought(plan, block, second, mixed):
    sizes, sources = plan.sizes, {axis: swaps(plan.sizes[axis]) for axis in AXES}
    got = []
    for m in range(len(sources["gx" if second else "gz"])):
        pairs = []
        for x, y, z in itertools.product(*(range(sizes[axis]) for axis in AXES)):
            along_x = second != (mixed and y % 2 == 1)
            source = (sources["gx"][m][x], y, z) if along_x else (x, y, sources["gz"][m][z])
            pairs.append((flat(sizes, *source), flat(sizes, x, y, z)))
        got.append(lax.ppermute(block, AXES, pairs))
    return got


def flat(sizes, x, y, z):
    return (x * sizes["gy"] + y) * sizes["gz"] + z


def along(block, axis):
    return [
        lax.ppermute(block, axis, [(source, i) for i, source in enumerate(sources)])
        for sources in swaps(lax.axis_size(axis))
    ]


def neighbours(plan, block, again=None):
    column = jnp.stack([block if again is None else again] + brought(plan, block, False, plan.mixed))
    return from_columns(plan, column, plan.mixed)


def from_columns(plan, column, mixed):
    columns = [column] + brought(plan, column, True, mixed)
    swapped = [[column] + along(column, "gy") for column in columns]
    return [column[side] for side in range(len(plan.sides)) for column in swapped]


def held_columns(plan, column, again):
    count = plan.sizes["gx"]
    columns = brought(plan, column, True, False)
    for step in plan.columns[plan.wide :]:
        columns.append(lax.ppermute(column, "gx", [((i + step) % count, i) for i in range(count)]))
    return [column, *columns] + along(jnp.stack([again, *columns]), "gy")


def everywhere(copies):
    return lax.all_to_all(copies, AXES, 0, 0, tiled=True)


def folded(pieces, axis):
    total = pieces[0]
    for piece, sources in zip(pieces[1:], swaps(lax.axis_size(axis))):
        total = total + lax.ppermute(piece, axis, list(enumerate(sources)))
    return total


def fold(plan, pulls):
    for axis in ("gx", "gz"):
        parts = len(offsets_of(plan.sizes[axis]))
        pulls = pulls.reshape((parts, -1) + pulls.shape[1:])
        pulls = folded([pulls[m] for m in range(parts)], axis)
    pulls = pulls[0]
    sides = [pulls[:, m * plan.slots : (m + 1) * plan.slots] for m in range(len(plan.sides))]
    return folded(sides, "gy")


def local_program(mesh):
    def local(
        positions,
        species,
        counts,
        embed,
        radial_one,
        mix_one,
        read_one,
        radial_two,
        mix_two,
        read_hidden,
        read_out,
    ):
        slots, channels = positions.shape[-1], embed.shape[1]
        nbasis, nspec = radial_two.shape[0], embed.shape[0]
        plan = Plan(mesh, slots, nbasis, nspec)
        given = [positions[0, 0, 0].reshape(3, 1, slots), species.reshape(1, slots), radial_one]
        weights = [embed, mix_one, radial_two, read_out[None], read_one[None], mix_two, read_hidden]
        sent, table, wide, *weights = simple_call(
            prepare_kernel,
            plan,
            [counts.reshape(1), *given, *weights],
            [
                ((plan.ndev if plan.small else 1, 4, 2 * slots), F32),
                ((2, nbasis * nspec, channels), BF16),
                (((1 + 2 * len(plan.plain)) * nbasis * nspec, (1 + len(plan.plain)) * channels), BF16),
            ]
            + [(weight.shape, weight.dtype) for weight in weights],
            1,
            [(array.shape, array.dtype) for array in given],
            near=True,
            fetched=len(given) + len(weights),
        )
        embed, mix_one, radial_two, out_row, one_row, mix_two, read_hidden = weights
        far_sent = [everywhere(sent)] if plan.small else neighbours(plan, sent[0])
        pair_flops = 100 * slots * plan.far
        rows, basis, layer, vector, mixing, cols = call(
            first_kernel,
            plan,
            far_sent,
            [table, wide, embed, mix_one],
            [
                ((len(plan.tiles), 4, plan.width), F32),
                ((plan.known, nbasis, slots, plan.far), BF16),
                ((len(plan.column), slots, channels), BF16),
                ((3 * slots, channels), F32),
                ((slots, channels), F32),
                ((plan.known, slots, 8), F32),
            ],
            [
                ((len(plan.column), nbasis, plan.kinds * slots, plan.far), BF16),
                ((len(plan.tiles) * len(plan.sides), 4, 2 * slots), F32),
            ],
            pair_flops,
        )
        more = max(len(plan.targets) - plan.known, 1)
        again, more_basis, more_cols = call(
            basis_kernel,
            plan,
            far_sent[:1],
            [layer],
            [
                (layer.shape, BF16),
                ((more, nbasis, slots, plan.far), BF16),
                ((more, slots, 8), F32),
            ],
            [],
            pair_flops,
        )
        one_row, apart, slope, factor, turned = simple_call(
            slope_kernel,
            plan,
            [rows, cols, one_row],
            [(one_row.shape, F32)]
            + [((count, slots, plan.far), F32) for count in (3, nbasis, nbasis, nbasis)],
            flops=pair_flops,
        )
        if plan.small:
            far_layer = held_columns(plan, layer, again)
        else:
            far_layer = neighbours(plan, layer[0], again[0])
        far_scratch = ((plan.far, channels), BF16)
        held = len(plan.columns) * len(plan.column) if plan.small else len(plan.tiles)
        held = held * len(plan.sides)
        adjoint, kept, before, own_adjoint, own_far = call(
            second_kernel,
            plan,
            far_layer,
            [layer, basis, cols, more_basis, more_cols, radial_two, mix_two, read_hidden, out_row, one_row],
            [
                ((len(plan.targets), slots, channels), BF16),
                ((slots, channels), BF16),
                ((slots, read_hidden.shape[0]), F32),
                ((slots, channels), F32),
                far_scratch,
            ],
            [((held, slots, channels), BF16)],
            pair_flops,
        )
        again, pair, energy, features = simple_call(
            energy_kernel,
            plan,
            [own_far, adjoint, slope, radial_two, cols, layer, before, out_row, one_row, kept],
            [
                ((1, slots, channels), BF16),
                ((slots, plan.far), F32),
                ((1, slots), F32),
                ((slots, channels), BF16),
            ],
            flops=pair_flops,
        )
        if plan.small:
            far_adjoint = [adjoint] + along(adjoint, "gy")
        else:
            far_adjoint = neighbours(plan, adjoint[0], again[0])
        pulls = call(
            force_kernel,
            plan,
            far_adjoint,
            [own_adjoint, basis, pair, rows, apart, slope, factor, turned]
            + [radial_two, mixing, mix_one, vector, table],
            [((plan.ndev, 4, plan.width) if plan.small else (len(plan.tiles), 3, plan.width), F32)],
            [far_scratch],
            pair_flops,
        )
        if plan.small:
            forces = simple_call(sum_kernel, plan, [everywhere(pulls[0])], ((3, 1, slots), F32))
        else:
            forces = -fold(plan, pulls[0])
        return (
            forces.reshape(1, 1, 1, 3, slots),
            energy[None, None],
            features.T[None, None, None],
        )

    return local


def solution(mesh):
    split = [P(*AXES, None, None), P(*AXES, None), P(*AXES)]
    out_specs = (P(*AXES, None, None), P(*AXES, None), P(*AXES, None, None))
    return jax.shard_map(
        local_program(mesh),
        mesh=mesh,
        in_specs=tuple(split + [P()] * 8),
        out_specs=out_specs,
        check_vma=False,
    )
```

```python
import itertools
import math

import jax
import jax.numpy as jnp
from jax import lax
from jax.experimental import pallas as pl
from jax.experimental.pallas import tpu as pltpu
from jax.sharding import PartitionSpec as P

CELL_SIDE = 5.0
CUT_SQUARE = 25.0
SOFTEN = 0.25
MSG_SCALE = 0.05
ROOT_THREE = math.sqrt(3.0)
FAR = 1.0e4
AXES = ("gx", "gy", "gz")
F32 = jnp.float32
BF16 = jnp.bfloat16
COS_TERMS = (
    0.9999999532476085,
    -4.934792830619644,
    4.058411352862619,
    -1.3318765680811142,
    0.2196896110983216,
)
SIN_TERMS = (
    3.1415926401307073,
    -5.167710083507891,
    2.550077523214631,
    -0.5982912856208596,
    0.07765766030668693,
)
VMEM_LIMIT = 24 * 1024 * 1024
FETCH_LIMIT = 60 * 1024 * 1024
NT = (((1,), (1,)), ((), ()))
NN = (((1,), (0,)), ((), ()))


def dot(a, b, dims=NN):
    return lax.dot_general(a, b, dims, preferred_element_type=F32)


def dot_exact(a, b, dims=NN):
    return lax.dot_general(
        a, b, dims, precision=lax.Precision.HIGHEST, preferred_element_type=F32
    )


def split_dot(a, b):
    high = a.astype(BF16)
    low = (a - high.astype(F32)).astype(BF16)
    return dot(high, b) + dot(low, b)


def offsets_of(count):
    return (0, 1) if count == 2 else (0, 1, -1)


def paired(count):
    return count > 2 and count % 2 == 0


def matched(which, parity):
    return jnp.int32(0) if which == 0 else 1 + (parity if which == 1 else 1 - parity)


def poly(terms, arg):
    total = arg * terms[-1] + terms[-2]
    for term in terms[-3::-1]:
        total = total * arg + term
    return total


class Plan:
    def __init__(self, mesh, slots, nbasis, nspec):
        self.sizes = {axis: mesh.shape[axis] for axis in AXES}
        self.ndev = math.prod(self.sizes.values())
        self.tiles = list(
            itertools.product(offsets_of(self.sizes["gx"]), offsets_of(self.sizes["gz"]))
        )
        self.sides = offsets_of(self.sizes["gy"])
        self.slots = slots
        self.width = len(self.sides) * slots
        self.far = len(self.tiles) * self.width
        self.nbasis = nbasis
        self.nspec = nspec
        self.depth = len(offsets_of(self.sizes["gz"]))
        self.wide = len(offsets_of(self.sizes["gx"]))
        self.brought = list(itertools.product(range(self.wide), range(self.depth)))
        self.mixed = self.depth == self.wide and self.sizes["gy"] % 2 == 0
        self.small = self.ndev <= 64 and len(self.sides) == 2
        self.columns, self.column = [self.reach(axis) if self.small else [0] for axis in ("gx", "gz")]
        self.known = self.depth if self.small else 1
        self.targets = self.tiles if self.small else self.tiles[:1]
        self.wrapped = [self.sizes[axis] == 2 for axis in AXES]
        self.plain = [k for k in range(3) if not self.wrapped[k]]
        self.folded = [k for k in range(3) if self.wrapped[k]]
        self.kinds = 2 + len(self.folded)

    def global_id(self, offset):
        place = 0
        for axis, step in zip(AXES, offset):
            count = self.sizes[axis]
            place = place * count + lax.rem(lax.axis_index(axis) + (step + count), count)
        return place

    def reach(self, axis):
        near, count = offsets_of(self.sizes[axis]), self.sizes[axis]
        steps = list(near)
        for step in [a + b for a in near for b in near]:
            if all((step - other) % count for other in steps):
                steps.append(step)
        return steps

    def held(self, x, z):
        found = []
        for step, steps, axis in ((x, self.columns, "gx"), (z, self.column, "gz")):
            found.append([(step - other) % self.sizes[axis] == 0 for other in steps].index(True))
        return found[0] * len(self.column) + found[1]

    def places(self):
        index = {axis: lax.axis_index(axis) for axis in AXES}

        def parity(axis):
            return lax.rem(index[axis], 2) if paired(self.sizes[axis]) else jnp.int32(0)

        turns = parity("gx"), parity("gz")
        core = lax.rem(index["gy"], 2) if self.mixed else jnp.int32(0)
        found = []
        for side in range(len(self.sides)):
            x_first = core if side == 0 or not self.mixed else 1 - core
            for second, first in self.brought:
                plain = matched(second, turns[0]) * self.depth + matched(first, turns[1])
                crossed = matched(first, turns[0]) * self.depth + matched(second, turns[1])
                tile = jnp.where(x_first == 1, crossed, plain) if self.mixed else plain
                found.append(tile * len(self.sides) + side)
        found += turns
        return [jnp.asarray(place, jnp.int32) for place in found]

    def brought_place(self, places, side, pair):
        return places[side * len(self.brought) + pair]

    def staged_place(self, places, tile):
        start = len(self.sides) * len(self.brought)
        x, z = divmod(tile, self.depth)
        return matched(x, places[start]) * self.depth + matched(z, places[start + 1])

    def offset(self, tile, side):
        ox, oz = self.tiles[tile]
        return (ox, self.sides[side], oz)


def scaled(terms, factor):
    return [factor * term for term in terms]


def separations(plan, rows, cols, side=CELL_SIDE):
    parts = []
    for axis in range(3):
        diff = rows[axis] - cols[axis]
        if plan.wrapped[axis]:
            diff = jnp.where(diff > side, diff - 2.0 * side, diff)
        parts.append(diff)
    return parts


def distance(plan, parts, tile, soften=SOFTEN):
    dist_sq = parts[0] * parts[0] + parts[1] * parts[1] + parts[2] * parts[2] + soften
    if tile == 0:
        row = lax.broadcasted_iota(jnp.int32, dist_sq.shape, 0)
        col = lax.broadcasted_iota(jnp.int32, dist_sq.shape, 1)
        dist_sq = jnp.where(row == col, FAR, dist_sq)
    return dist_sq, lax.rsqrt(dist_sq)


def waves(dist_sq, inverse):
    arg = jnp.minimum(dist_sq * inverse * (1.0 / CELL_SIDE) - 0.5, 0.5)
    square = arg * arg
    return poly(COS_TERMS, square), -(arg * poly(SIN_TERMS, square))


def global_block(plan, far_ref, tile, side, target):
    x, y, z = plan.offset(tile, side)
    return far_ref[plan.global_id((x + target[0], y, z + target[1]))]


def own_columns(plan, block):
    held = jnp.concatenate([block, block], axis=0).T[: plan.slots]
    kind = held[:, 3:4]
    lane = lax.broadcasted_iota(jnp.int32, held.shape, 1)
    live = kind >= 0.0
    held = jnp.where((lane == 0) & ~live, -FAR, held)
    return jnp.where(lane == 3, live.astype(F32), held), kind


def scaled_columns(held):
    return [held[:, axis : axis + 1] * (1.0 / CELL_SIDE) for axis in range(3)]


def basis_of(plan, placed, cols, tile):
    parts = separations(plan, [placed[k : k + 1] for k in range(3)], cols, 1.0)
    dist_sq, inverse = distance(plan, parts, tile, SOFTEN / CUT_SQUARE)
    turn = jnp.minimum(dist_sq * inverse - 0.5, 0.5)
    square = turn * turn
    double = turn * poly(scaled(SIN_TERMS, -2.0), square)
    fade = jnp.maximum(1.0 - dist_sq, 0.0)
    basis = [poly(scaled(COS_TERMS, 1.0 / CELL_SIDE), square) * (fade * fade * inverse)]
    for n in range(1, plan.nbasis):
        basis.append(double * basis[-1] if n == 1 else double * basis[-1] - basis[-2])
    return parts, inverse, basis


def first_kernel(plan, nrefs, places, *refs):
    far_refs, refs = refs[:nrefs], refs[nrefs:]
    (table_ref, wide_ref, embed_ref, mix_ref), refs = refs[:4], refs[4:]
    rows_ref, basis_ref, layer_ref, vector_ref, mixing_ref, cols_ref, pair_ref, block_ref = refs
    slots, nbasis, nspec = plan.slots, plan.nbasis, plan.nspec

    def put(place, block):
        block_ref[place] = block

    if not plan.small:
        scatter(plan, places, far_refs, put)

    def block_of(tile, side, up):
        if plan.small:
            return global_block(plan, far_refs[0], tile, side, (0, up))
        return block_ref[tile * len(plan.sides) + side]

    species = lax.broadcasted_iota(jnp.int32, (nbasis * nspec, plan.width), 0) % nspec
    shifts = [tile_shift(plan, tile) for tile in range(len(plan.tiles))]
    own, counted, places_of = [], [], []
    for which, up in enumerate(plan.column):
        held, kind = own_columns(plan, block_of(0, 0, up))
        own.append(kind)
        if which < plan.known:
            cols_ref[which] = held
        cols = scaled_columns(held)
        places_of.append(cols)
        hot = []
        for tile in range(len(plan.tiles)):
            blocks = [block_of(tile, side, up) for side in range(len(plan.sides))]
            placed = side_by_side(plan, blocks) + shifts[tile]
            if which == 0:
                rows_ref[tile] = placed
            is_kind = placed[3:4].astype(jnp.int32) == species
            placed = placed * (1.0 / CELL_SIDE)
            high = placed.astype(BF16).astype(F32)
            low = placed - high
            columns = [jnp.where(is_kind, 1.0, 0.0)]
            for k in plan.plain:
                columns += [jnp.where(is_kind, part[k : k + 1], 0.0) for part in (high, low)]
            hot.append(jnp.concatenate([column.astype(BF16) for column in columns], axis=0))
            parts, inverse, basis = basis_of(plan, placed, cols, tile)
            scale = inverse * ROOT_THREE
            units = [scale.astype(BF16)] + [(scale * parts[k]).astype(BF16) for k in plan.folded]
            lanes = slice(tile * plan.width, (tile + 1) * plan.width)
            for n in range(nbasis):
                packed = basis[n].astype(BF16)
                if which < plan.known:
                    basis_ref[which, n, :, lanes] = packed
                pair_ref[which, n, :slots, lanes] = packed
                for m, unit in enumerate(units):
                    pair_ref[which, n, (m + 1) * slots : (m + 2) * slots, lanes] = unit * packed
        hot = jnp.concatenate(hot, axis=1)
        gathered = dot(pair_ref[which].reshape(nbasis * plan.kinds * slots, plan.far), hot, NT)
        gathered = gathered.reshape(nbasis, plan.kinds * slots, hot.shape[0])
        group = lax.broadcasted_iota(jnp.int32, gathered.shape[1:], 1) % (nbasis * nspec) // nspec
        total = gathered[0]
        for n in range(1, nbasis):
            total = jnp.where(group == n, gathered[n], total)
        counted.append(total)
    scalar = jnp.concatenate([total[:slots, : nbasis * nspec] for total in counted], axis=0)
    scalar = MSG_SCALE * split_dot(scalar, table_ref[0])
    moved = jnp.concatenate([total[slots : 2 * slots] for total in counted], axis=0)
    moved = MSG_SCALE * split_dot(moved, wide_ref[...])
    channels = layer_ref.shape[2]
    norm = None
    for k in range(3):
        if k in plan.plain:
            start = (plan.plain.index(k) + 1) * channels
            place = jnp.concatenate([cols[k] for cols in places_of], axis=0)
            vector = moved[:, start : start + channels] - place * moved[:, :channels]
        else:
            start = (plan.folded.index(k) + 2) * slots
            vector = [total[start : start + slots, : nbasis * nspec] for total in counted]
            vector = MSG_SCALE * split_dot(jnp.concatenate(vector, axis=0), table_ref[1])
        vector_ref[k * slots : (k + 1) * slots] = vector[:slots]
        norm = vector * vector if k == 0 else norm + vector * vector
    invariants = jnp.concatenate([scalar.astype(BF16), norm.astype(BF16)], axis=1)
    mixing = dot(invariants, mix_ref[...], NT)
    mixing_ref[...] = mixing[:slots]
    kind = jnp.concatenate(own, axis=0)
    own_species = lax.broadcasted_iota(jnp.int32, (kind.shape[0], nspec), 1)
    own_hot = (kind.astype(jnp.int32) == own_species).astype(F32).astype(BF16)
    layer = (dot(own_hot, embed_ref[...]) + mixing * sigmoid(mixing)).astype(BF16)
    for which in range(layer_ref.shape[0]):
        layer_ref[which] = layer[which * slots : (which + 1) * slots]


def sigmoid(value):
    return 1.0 / (1.0 + jnp.exp(-value))


def scatter(plan, places, far_refs, put):
    for side in range(len(plan.sides)):
        for pair, (second, first) in enumerate(plan.brought):
            put(plan.brought_place(places, side, pair), far_refs[side * plan.wide + second][first])


def scatter_held(plan, places, far_refs, put):
    turn = places[len(plan.sides) * len(plan.brought)]
    for side in range(len(plan.sides)):
        for m in range(len(plan.columns)):
            x = matched(m, turn) if m < plan.wide else m
            for z in range(len(plan.column)):
                place = (x * len(plan.column) + z) * len(plan.sides) + side
                put(place, far_refs[m][z] if side == 0 else far_refs[len(plan.columns)][m, z])


def far_blocks(plan, block_ref, target):
    blocks = []
    for x, z in plan.tiles:
        place = plan.held(x + target[0], z + target[1]) * len(plan.sides)
        blocks += [block_ref[place + side] for side in range(len(plan.sides))]
    return jnp.concatenate(blocks, axis=0)


def side_by_side(plan, blocks):
    if len(blocks) == 2:
        lane = lax.broadcasted_iota(jnp.int32, blocks[0].shape, 1)
        return jnp.where(lane < plan.slots, blocks[0], blocks[1])
    return jnp.concatenate([block[:, : plan.slots] for block in blocks], axis=1)


def tile_shift(plan, tile):
    row = lax.broadcasted_iota(jnp.int32, (4, plan.width), 0)
    side = lax.broadcasted_iota(jnp.int32, (4, plan.width), 1) // plan.slots
    shift = jnp.zeros((4, plan.width), F32)
    for s in range(len(plan.sides)):
        for k, steps in enumerate(plan.offset(tile, s)):
            if steps:
                shift = jnp.where((row == k) & (side == s), CELL_SIDE * steps, shift)
    return shift


def gather_far(plan, places, far_refs, all_ref):
    def put(place, block):
        start = pl.multiple_of(place * plan.slots, plan.slots)
        all_ref[pl.ds(start, plan.slots)] = block

    scatter(plan, places, far_refs, put)


def second_kernel(plan, nrefs, places, *refs):
    far_refs, refs = refs[:nrefs], refs[nrefs:]
    (layer_ref, basis_ref, cols_ref, more_ref, more_cols_ref, radial_ref, mix_ref), refs = refs[:7], refs[7:]
    (hidden_ref, out_ref, one_ref), refs = refs[:3], refs[3:]
    adjoint_ref, features_ref, before_ref, own_ref, own_far_ref, block_ref = refs
    slots, nbasis, known = plan.slots, plan.nbasis, len(plan.targets)

    def put(place, block):
        block_ref[place] = block

    (scatter_held if plan.small else scatter)(plan, places, far_refs, put)
    messages, layers, lives = [], [], []
    for which, target in enumerate(plan.targets):
        if plan.small:
            far = far_blocks(plan, block_ref, target)
            layers.append(block_ref[plan.held(*target) * len(plan.sides)])
        else:
            far = block_ref[...].reshape(plan.far, -1)
            layers.append(layer_ref[0])
        first = which < plan.known
        held_ref, held_cols_ref = (basis_ref, cols_ref) if first else (more_ref, more_cols_ref)
        place = which if first else which - plan.known
        lives.append(held_cols_ref[place, :, 3:4])
        if which == 0:
            own_far_ref[...] = far
        summed = dot(held_ref[place].reshape(nbasis * slots, plan.far), far)
        message = summed[:slots] * radial_ref[0:1]
        for n in range(1, nbasis):
            message = message + summed[n * slots : (n + 1) * slots] * radial_ref[n : n + 1]
        messages.append((MSG_SCALE * message).astype(BF16))
    mixing = dot(jnp.concatenate(messages, axis=0), mix_ref[...], NT)
    gate = sigmoid(mixing)
    layer = jnp.concatenate(layers, axis=0).astype(F32)
    features = (layer + mixing * gate).astype(BF16)
    features_ref[...] = features[:slots]
    before = dot(features, hidden_ref[...], NT)
    before_ref[...] = before[:slots]
    open_hidden = sigmoid(before)
    live = jnp.concatenate(lives, axis=0)
    slope = out_ref[...] * (open_hidden * (1.0 + before * (1.0 - open_hidden))) * live
    from_hidden = dot(slope.astype(BF16), hidden_ref[...])
    own_ref[...] = from_hidden[:slots] + one_ref[...] * live[:slots]
    back = from_hidden * (gate * (1.0 + mixing * (1.0 - gate)))
    adjoint = dot(back.astype(BF16), mix_ref[...]).astype(BF16)
    for which in range(known):
        adjoint_ref[which] = adjoint[which * slots : (which + 1) * slots]


def basis_kernel(plan, nrefs, places, *refs):
    far_ref, (layer_ref, again_ref, more_ref, more_cols_ref) = refs[0], refs[nrefs:]
    again_ref[...] = layer_ref[...]
    for which, target in enumerate(plan.targets[plan.known :]):
        held, _ = own_columns(plan, global_block(plan, far_ref, 0, 0, target))
        more_cols_ref[which] = held
        for tile in range(len(plan.tiles)):
            lanes = slice(tile * plan.width, (tile + 1) * plan.width)
            blocks = [global_block(plan, far_ref, tile, s, target) for s in range(len(plan.sides))]
            placed = (side_by_side(plan, blocks) + tile_shift(plan, tile)) * (1.0 / CELL_SIDE)
            basis = basis_of(plan, placed, scaled_columns(held), tile)[2]
            for n in range(plan.nbasis):
                more_ref[which, n, :, lanes] = basis[n].astype(BF16)


def slope_kernel(plan, rows_ref, cols_ref, one_ref, *refs):
    kept_ref, apart_ref, slope_ref, radial_ref, turned_ref = refs
    kept_ref[...] = one_ref[...]
    cols = [cols_ref[0, :, axis : axis + 1] for axis in range(3)]
    for tile in range(len(plan.tiles)):
        lanes = slice(tile * plan.width, (tile + 1) * plan.width)
        parts = separations(plan, [rows_ref[tile, k : k + 1] for k in range(3)], cols)
        for k in range(3):
            apart_ref[k, :, lanes] = parts[k]
        dist_sq, inverse = distance(plan, parts, tile)
        sine, cosine = waves(dist_sq, inverse)
        fade = jnp.maximum(1.0 - dist_sq * (1.0 / CUT_SQUARE), 0.0)
        radial = fade * fade * inverse
        on_sine = -inverse * ((4.0 / CUT_SQUARE) * fade + radial * inverse)
        on_cosine = (math.pi / CELL_SIDE) * (inverse * radial)
        scale = ROOT_THREE * inverse
        scaled = scale * radial
        square = inverse * inverse
        double = 2.0 * cosine
        before_s, now_s, before_c, now_c = None, sine, None, cosine
        for n in range(plan.nbasis):
            if n == 1:
                before_s, now_s = now_s, double * now_s
                before_c, now_c = now_c, double * now_c - 1.0
            elif n > 1:
                before_s, now_s = now_s, double * now_s - before_s
                before_c, now_c = now_c, double * now_c - before_c
            slope = on_sine * now_s + (n + 1.0) * on_cosine * now_c
            factor = scaled * now_s
            slope_ref[n, :, lanes] = slope
            radial_ref[n, :, lanes] = factor
            turned_ref[n, :, lanes] = scale * slope - square * factor


def energy_kernel(plan, *refs):
    (all_ref, adjoint_ref, slope_ref, radial_ref, cols_ref, layer_ref), refs = refs[:6], refs[6:]
    (before_ref, out_ref, one_ref, kept_ref), refs = refs[:4], refs[4:]
    again_ref, pair_ref, energy_ref, features_ref = refs
    slots, nbasis = plan.slots, plan.nbasis
    again_ref[...] = adjoint_ref[:1]
    features_ref[...] = kept_ref[...]
    before = before_ref[...]
    live = jnp.where(lax.broadcasted_iota(jnp.int32, (slots, 8), 1) == 0, cols_ref[0, :, 3:4], 0.0)
    live_row = dot(jnp.ones((1, 8), BF16), live.astype(BF16), NT)
    energy = dot_exact(one_ref[...], layer_ref[0].astype(F32), NT)
    energy = energy + dot_exact(out_ref[...], before * sigmoid(before), NT)
    energy_ref[...] = energy * live_row
    adjoint = adjoint_ref[0].astype(F32) * MSG_SCALE
    weighted = jnp.concatenate(
        [(adjoint * radial_ref[n : n + 1]).astype(BF16) for n in range(nbasis)], axis=0
    )
    for tile in range(len(plan.tiles)):
        lanes = slice(tile * plan.width, (tile + 1) * plan.width)
        pulled = dot(weighted, all_ref[lanes], NT)
        total = slope_ref[0, :, lanes] * pulled[:slots]
        for n in range(1, nbasis):
            total = total + slope_ref[n, :, lanes] * pulled[n * slots : (n + 1) * slots]
        pair_ref[:, lanes] = total


def force_kernel(plan, nrefs, places, *refs):
    far_refs, refs = refs[:nrefs], refs[nrefs:]
    (own_ref, basis_ref, pair_ref, rows_ref), refs = refs[:4], refs[4:]
    (apart_ref, slope_ref, factor_ref, turned_ref), refs = refs[:4], refs[4:]
    (radial_ref, mixing_ref, mix_ref, vector_ref, table_ref), refs = refs[:5], refs[5:]
    out_ref, all_ref = refs
    slots, nbasis, nspec, width = plan.slots, plan.nbasis, plan.nspec, plan.width
    if plan.small:
        far = [far_refs[side][tile] for tile in range(len(plan.tiles)) for side in range(len(plan.sides))]
        far = jnp.concatenate(far, axis=0)
    else:
        gather_far(plan, places, far_refs, all_ref)
        far = all_ref[...]
    summed = dot(basis_ref[0].reshape(nbasis * slots, plan.far), far)
    adjoint = jnp.zeros((slots, summed.shape[1]), F32)
    for n in range(nbasis):
        adjoint = adjoint + summed[n * slots : (n + 1) * slots] * radial_ref[n : n + 1]
    adjoint = own_ref[...] + MSG_SCALE * adjoint
    mixing = mixing_ref[...]
    gate = sigmoid(mixing)
    back = (adjoint * (gate * (1.0 + mixing * (1.0 - gate)))).astype(BF16)
    invariants = dot(back, mix_ref[...])
    channels = invariants.shape[1] // 2
    on_scalar = (MSG_SCALE * invariants[:, :channels]).astype(BF16)
    doubled = (2.0 * MSG_SCALE) * invariants[:, channels:]
    on_vector = (vector_ref[...] * jnp.concatenate([doubled] * 3, axis=0)).astype(BF16)
    weights = jnp.concatenate(
        [dot(on_scalar, table_ref[0], NT), dot(on_vector, table_ref[1], NT)], axis=0
    ).astype(BF16)
    group = lax.broadcasted_iota(jnp.int32, weights.shape, 1) // nspec
    weights = weights.astype(F32)
    weights = jnp.concatenate(
        [jnp.where(group == n, weights, 0.0).astype(BF16) for n in range(nbasis)], axis=0
    )
    species = lax.broadcasted_iota(jnp.int32, (nbasis * nspec, width), 0) % nspec
    own = [jnp.zeros((slots, width), F32) for _ in range(3)]
    pulls = []
    for tile in range(len(plan.tiles)):
        lanes = slice(tile * width, (tile + 1) * width)
        hot = (rows_ref[tile, 3:4].astype(jnp.int32) == species).astype(F32).astype(BF16)
        spread = dot(weights, hot)
        total = pair_ref[:, lanes]
        sides, turns = [None] * 3, [None] * 3
        for n in range(nbasis):
            start = n * 4 * slots
            total = total + slope_ref[n, :, lanes] * spread[start : start + slots]
            for k in range(3):
                piece = spread[start + (k + 1) * slots : start + (k + 2) * slots]
                side = factor_ref[n, :, lanes] * piece
                turn = turned_ref[n, :, lanes] * piece
                sides[k] = side if n == 0 else sides[k] + side
                turns[k] = turn if n == 0 else turns[k] + turn
        for k in range(3):
            total = total + apart_ref[k, :, lanes] * turns[k]
        pulls.append([])
        for k in range(3):
            pull = apart_ref[k, :, lanes] * total + sides[k]
            own[k] = own[k] + pull
            pulls[-1].append(jnp.sum(pull, axis=0, keepdims=True))
    own = jnp.concatenate(own, axis=0)
    high = own.astype(BF16)
    low = (own - high.astype(F32)).astype(BF16)
    ones = jnp.ones((8, width), BF16)
    mine = (dot(ones, high, NT) + dot(ones, low, NT))[:1]
    mine = jnp.concatenate([mine[:, k * slots : (k + 1) * slots] for k in range(3)], axis=0)
    if plan.small:
        out_ref[...] = jnp.zeros_like(out_ref)
    side_of = lax.broadcasted_iota(jnp.int32, (3, width), 1) // slots
    for tile in range(len(plan.tiles)):
        pulled = jnp.concatenate(pulls[tile], axis=0)
        if tile == 0:
            others = [jnp.zeros_like(mine)] * (len(plan.sides) - 1)
            pulled = pulled - jnp.concatenate([mine] + others, axis=1)
        if not plan.small:
            out_ref[plan.staged_place(places, tile)] = pulled
            continue
        for side in range(len(plan.sides)):
            place = plan.global_id(plan.offset(tile, side))
            out_ref[place, :3] = jnp.where(side_of == side, pulled, 0.0)


def begin(pairs, sems):
    copies = [pltpu.make_async_copy(*pair, sems.at[m]) for m, pair in enumerate(pairs)]
    for copy in copies:
        copy.start()
    return copies


def prepare_kernel(plan, counts_ref, *refs):
    embed_ref, fetched, (sent_ref, table_ref, wide_ref, again_ref) = refs[0], refs[1:10], refs[10:14]
    kept, (place_ref, kind_ref, radial_ref, sems) = refs[14:20], refs[20:]
    copies = begin(zip(fetched, (place_ref, kind_ref, radial_ref, *kept)), sems)
    for copy in copies[:2]:
        copy.wait()
    live = lax.broadcasted_iota(jnp.int32, (1, plan.slots), 1) < counts_ref[0]
    rows = [
        jnp.where(live, place_ref[0], FAR),
        place_ref[1],
        place_ref[2],
        jnp.where(live, kind_ref[...], -1).astype(F32),
    ]
    rows = jnp.concatenate(rows, axis=0)
    rows = jnp.concatenate([rows, rows], axis=1)
    for copy in range(sent_ref.shape[0]):
        sent_ref[copy] = rows
    for copy in copies[2:]:
        copy.wait()
    again_ref[...] = embed_ref[...]
    embed = embed_ref[...].astype(F32)
    for g in range(2):
        weighted = [radial_ref[g, n : n + 1] * embed for n in range(plan.nbasis)]
        table_ref[g] = jnp.concatenate(weighted, axis=0).astype(BF16)
    wide_ref[...] = jnp.zeros_like(wide_ref)
    count, channels = table_ref.shape[1:]
    for m in range(1 + 2 * len(plan.plain)):
        start = (m + 1) // 2 * channels
        wide_ref[m * count : (m + 1) * count, start : start + channels] = table_ref[1]


def sum_kernel(plan, parts_ref, force_ref):
    total = parts_ref[0]
    for part in range(1, parts_ref.shape[0]):
        total = total + parts_ref[part]
    total = total[:, : plan.slots] + total[:, plan.slots :]
    for k in range(3):
        force_ref[k] = -total[k : k + 1]


VMEM_SPEC = pl.BlockSpec(memory_space=pltpu.VMEM)
SMEM_SPEC = pl.BlockSpec(memory_space=pltpu.SMEM)
HBM_SPEC = pl.BlockSpec(memory_space=pltpu.HBM)


def simple_call(kernel, plan, operands, outs, scalars=0, scratch=(), flops=2**20, near=False, fetched=0):
    single = not isinstance(outs, list)
    kind = pltpu.VMEM if near else jax.ShapeDtypeStruct
    shapes = [kind(*out) for out in ([outs] if single else outs)]

    def body(*refs):
        kernel(plan, *refs)

    got = pl.pallas_call(
        body,
        out_shape=shapes,
        in_specs=[SMEM_SPEC] * scalars
        + [VMEM_SPEC] * (len(operands) - scalars - fetched)
        + [HBM_SPEC] * fetched,
        out_specs=[VMEM_SPEC] * len(shapes),
        scratch_shapes=[pltpu.VMEM(*buffer) for buffer in scratch]
        + [pltpu.SemaphoreType.DMA((fetched,))] * (fetched > 0),
        compiler_params=pltpu.CompilerParams(vmem_limit_bytes=FETCH_LIMIT if fetched else VMEM_LIMIT),
        cost_estimate=pl.CostEstimate(flops=flops, bytes_accessed=2**20, transcendentals=0),
    )(*operands)
    return got[0] if single else got


def call(kernel, plan, far, operands, outs, scratch, flops, **options):
    def body(plan, *refs):
        kernel(plan, len(far), plan.places(), *refs)

    return simple_call(body, plan, [*far, *operands], outs, 0, scratch, flops, **options)


def swaps(count):
    if count == 2:
        return [[1, 0]]
    if paired(count):
        near = [i ^ 1 for i in range(count)]
        far = [(i - 1 + 2 * (i % 2)) % count for i in range(count)]
        return [near, far]
    return [[(i + o) % count for i in range(count)] for o in offsets_of(count)[1:]]


def brought(plan, block, second, mixed):
    sizes, sources = plan.sizes, {axis: swaps(plan.sizes[axis]) for axis in AXES}
    got = []
    for m in range(len(sources["gx" if second else "gz"])):
        pairs = []
        for x, y, z in itertools.product(*(range(sizes[axis]) for axis in AXES)):
            along_x = second != (mixed and y % 2 == 1)
            source = (sources["gx"][m][x], y, z) if along_x else (x, y, sources["gz"][m][z])
            pairs.append((flat(sizes, *source), flat(sizes, x, y, z)))
        got.append(lax.ppermute(block, AXES, pairs))
    return got


def flat(sizes, x, y, z):
    return (x * sizes["gy"] + y) * sizes["gz"] + z


def along(block, axis):
    return [
        lax.ppermute(block, axis, [(source, i) for i, source in enumerate(sources)])
        for sources in swaps(lax.axis_size(axis))
    ]


def neighbours(plan, block, again=None):
    column = jnp.stack([block if again is None else again] + brought(plan, block, False, plan.mixed))
    return from_columns(plan, column, plan.mixed)


def from_columns(plan, column, mixed):
    columns = [column] + brought(plan, column, True, mixed)
    swapped = [[column] + along(column, "gy") for column in columns]
    return [column[side] for side in range(len(plan.sides)) for column in swapped]


def held_columns(plan, column, again):
    count = plan.sizes["gx"]
    columns = brought(plan, column, True, False)
    for step in plan.columns[plan.wide :]:
        columns.append(lax.ppermute(column, "gx", [((i + step) % count, i) for i in range(count)]))
    return [column, *columns] + along(jnp.stack([again, *columns]), "gy")


def everywhere(copies):
    return lax.all_to_all(copies, AXES, 0, 0, tiled=True)


def folded(pieces, axis):
    total = pieces[0]
    for piece, sources in zip(pieces[1:], swaps(lax.axis_size(axis))):
        total = total + lax.ppermute(piece, axis, list(enumerate(sources)))
    return total


def fold(plan, pulls):
    for axis in ("gx", "gz"):
        parts = len(offsets_of(plan.sizes[axis]))
        pulls = pulls.reshape((parts, -1) + pulls.shape[1:])
        pulls = folded([pulls[m] for m in range(parts)], axis)
    pulls = pulls[0]
    sides = [pulls[:, m * plan.slots : (m + 1) * plan.slots] for m in range(len(plan.sides))]
    return folded(sides, "gy")


def local_program(mesh):
    def local(
        positions,
        species,
        counts,
        embed,
        radial_one,
        mix_one,
        read_one,
        radial_two,
        mix_two,
        read_hidden,
        read_out,
    ):
        slots, channels = positions.shape[-1], embed.shape[1]
        nbasis, nspec = radial_two.shape[0], embed.shape[0]
        plan = Plan(mesh, slots, nbasis, nspec)
        given = [positions[0, 0, 0].reshape(3, 1, slots), species.reshape(1, slots), radial_one]
        weights = [mix_one, radial_two, read_out[None], read_one[None], mix_two, read_hidden]
        sent, table, wide, embed, *weights = simple_call(
            prepare_kernel,
            plan,
            [counts.reshape(1), embed, *given, *weights],
            [
                ((plan.ndev if plan.small else 1, 4, 2 * slots), F32),
                ((2, nbasis * nspec, channels), BF16),
                (((1 + 2 * len(plan.plain)) * nbasis * nspec, (1 + len(plan.plain)) * channels), BF16),
                (embed.shape, BF16),
            ]
            + [(weight.shape, weight.dtype) for weight in weights],
            1,
            [(array.shape, array.dtype) for array in given],
            near=True,
            fetched=len(given) + len(weights),
        )
        mix_one, radial_two, out_row, one_row, mix_two, read_hidden = weights
        far_sent = [everywhere(sent)] if plan.small else neighbours(plan, sent[0])
        pair_flops = 100 * slots * plan.far
        rows, basis, layer, vector, mixing, cols = call(
            first_kernel,
            plan,
            far_sent,
            [table, wide, embed, mix_one],
            [
                ((len(plan.tiles), 4, plan.width), F32),
                ((plan.known, nbasis, slots, plan.far), BF16),
                ((len(plan.column), slots, channels), BF16),
                ((3 * slots, channels), F32),
                ((slots, channels), F32),
                ((plan.known, slots, 8), F32),
            ],
            [
                ((len(plan.column), nbasis, plan.kinds * slots, plan.far), BF16),
                ((len(plan.tiles) * len(plan.sides), 4, 2 * slots), F32),
            ],
            pair_flops,
        )
        more = max(len(plan.targets) - plan.known, 1)
        again, more_basis, more_cols = call(
            basis_kernel,
            plan,
            far_sent[:1],
            [layer],
            [
                (layer.shape, BF16),
                ((more, nbasis, slots, plan.far), BF16),
                ((more, slots, 8), F32),
            ],
            [],
            pair_flops,
        )
        one_row, apart, slope, factor, turned = simple_call(
            slope_kernel,
            plan,
            [rows, cols, one_row],
            [(one_row.shape, F32)]
            + [((count, slots, plan.far), F32) for count in (3, nbasis, nbasis, nbasis)],
            flops=pair_flops,
        )
        if plan.small:
            far_layer = held_columns(plan, layer, again)
        else:
            far_layer = neighbours(plan, layer[0], again[0])
        far_scratch = ((plan.far, channels), BF16)
        held = len(plan.columns) * len(plan.column) if plan.small else len(plan.tiles)
        held = held * len(plan.sides)
        adjoint, kept, before, own_adjoint, own_far = call(
            second_kernel,
            plan,
            far_layer,
            [layer, basis, cols, more_basis, more_cols, radial_two, mix_two, read_hidden, out_row, one_row],
            [
                ((len(plan.targets), slots, channels), BF16),
                ((slots, channels), BF16),
                ((slots, read_hidden.shape[0]), F32),
                ((slots, channels), F32),
                far_scratch,
            ],
            [((held, slots, channels), BF16)],
            pair_flops,
        )
        again, pair, energy, features = simple_call(
            energy_kernel,
            plan,
            [own_far, adjoint, slope, radial_two, cols, layer, before, out_row, one_row, kept],
            [
                ((1, slots, channels), BF16),
                ((slots, plan.far), F32),
                ((1, slots), F32),
                ((slots, channels), BF16),
            ],
            flops=pair_flops,
        )
        if plan.small:
            far_adjoint = [adjoint] + along(adjoint, "gy")
        else:
            far_adjoint = neighbours(plan, adjoint[0], again[0])
        pulls = call(
            force_kernel,
            plan,
            far_adjoint,
            [own_adjoint, basis, pair, rows, apart, slope, factor, turned]
            + [radial_two, mixing, mix_one, vector, table],
            [((plan.ndev, 4, plan.width) if plan.small else (len(plan.tiles), 3, plan.width), F32)],
            [far_scratch],
            pair_flops,
        )
        if plan.small:
            forces = simple_call(sum_kernel, plan, [everywhere(pulls[0])], ((3, 1, slots), F32))
        else:
            forces = -fold(plan, pulls[0])
        return (
            forces.reshape(1, 1, 1, 3, slots),
            energy[None, None],
            features.T[None, None, None],
        )

    return local


def solution(mesh):
    split = [P(*AXES, None, None), P(*AXES, None), P(*AXES)]
    out_specs = (P(*AXES, None, None), P(*AXES, None), P(*AXES, None, None))
    return jax.shard_map(
        local_program(mesh),
        mesh=mesh,
        in_specs=tuple(split + [P()] * 8),
        out_specs=out_specs,
        check_vma=False,
    )
```

```python
import itertools
import math

import jax
import jax.numpy as jnp
from jax import lax
from jax.experimental import pallas as pl
from jax.experimental.pallas import tpu as pltpu
from jax.sharding import PartitionSpec as P

CELL_SIDE = 5.0
CUT_SQUARE = 25.0
SOFTEN = 0.25
MSG_SCALE = 0.05
ROOT_THREE = math.sqrt(3.0)
FAR = 1.0e4
AXES = ("gx", "gy", "gz")
F32 = jnp.float32
BF16 = jnp.bfloat16
COS_TERMS = (
    0.9999999532476085,
    -4.934792830619644,
    4.058411352862619,
    -1.3318765680811142,
    0.2196896110983216,
)
SIN_TERMS = (
    3.1415926401307073,
    -5.167710083507891,
    2.550077523214631,
    -0.5982912856208596,
    0.07765766030668693,
)
VMEM_LIMIT = 24 * 1024 * 1024
FETCH_LIMIT = 60 * 1024 * 1024
NT = (((1,), (1,)), ((), ()))
NN = (((1,), (0,)), ((), ()))


def dot(a, b, dims=NN):
    return lax.dot_general(a, b, dims, preferred_element_type=F32)


def dot_exact(a, b, dims=NN):
    return lax.dot_general(
        a, b, dims, precision=lax.Precision.HIGHEST, preferred_element_type=F32
    )


def split_dot(a, b):
    high = a.astype(BF16)
    low = (a - high.astype(F32)).astype(BF16)
    return dot(high, b) + dot(low, b)


def offsets_of(count):
    return (0, 1) if count == 2 else (0, 1, -1)


def paired(count):
    return count > 2 and count % 2 == 0


def matched(which, parity):
    return jnp.int32(0) if which == 0 else 1 + (parity if which == 1 else 1 - parity)


def poly(terms, arg):
    total = arg * terms[-1] + terms[-2]
    for term in terms[-3::-1]:
        total = total * arg + term
    return total


class Plan:
    def __init__(self, mesh, slots, nbasis, nspec):
        self.sizes = {axis: mesh.shape[axis] for axis in AXES}
        self.ndev = math.prod(self.sizes.values())
        self.tiles = list(
            itertools.product(offsets_of(self.sizes["gx"]), offsets_of(self.sizes["gz"]))
        )
        self.sides = offsets_of(self.sizes["gy"])
        self.slots = slots
        self.width = len(self.sides) * slots
        self.far = len(self.tiles) * self.width
        self.nbasis = nbasis
        self.nspec = nspec
        self.depth = len(offsets_of(self.sizes["gz"]))
        self.wide = len(offsets_of(self.sizes["gx"]))
        self.brought = list(itertools.product(range(self.wide), range(self.depth)))
        self.mixed = self.depth == self.wide and self.sizes["gy"] % 2 == 0
        self.small = self.ndev <= 64 and len(self.sides) == 2
        self.columns, self.column = [self.reach(axis) if self.small else [0] for axis in ("gx", "gz")]
        self.known = self.depth if self.small else 1
        self.targets = self.tiles if self.small else self.tiles[:1]
        self.wrapped = [self.sizes[axis] == 2 for axis in AXES]
        self.plain = [k for k in range(3) if not self.wrapped[k]]
        self.folded = [k for k in range(3) if self.wrapped[k]]
        self.kinds = 2 + len(self.folded)

    def global_id(self, offset):
        place = 0
        for axis, step in zip(AXES, offset):
            count = self.sizes[axis]
            place = place * count + lax.rem(lax.axis_index(axis) + (step + count), count)
        return place

    def reach(self, axis):
        near, count = offsets_of(self.sizes[axis]), self.sizes[axis]
        steps = list(near)
        for step in [a + b for a in near for b in near]:
            if all((step - other) % count for other in steps):
                steps.append(step)
        return steps

    def held(self, x, z):
        found = []
        for step, steps, axis in ((x, self.columns, "gx"), (z, self.column, "gz")):
            found.append([(step - other) % self.sizes[axis] == 0 for other in steps].index(True))
        return found[0] * len(self.column) + found[1]

    def places(self):
        index = {axis: lax.axis_index(axis) for axis in AXES}

        def parity(axis):
            return lax.rem(index[axis], 2) if paired(self.sizes[axis]) else jnp.int32(0)

        turns = parity("gx"), parity("gz")
        core = lax.rem(index["gy"], 2) if self.mixed else jnp.int32(0)
        found = []
        for side in range(len(self.sides)):
            x_first = core if side == 0 or not self.mixed else 1 - core
            for second, first in self.brought:
                plain = matched(second, turns[0]) * self.depth + matched(first, turns[1])
                crossed = matched(first, turns[0]) * self.depth + matched(second, turns[1])
                tile = jnp.where(x_first == 1, crossed, plain) if self.mixed else plain
                found.append(tile * len(self.sides) + side)
        found += turns
        return [jnp.asarray(place, jnp.int32) for place in found]

    def brought_place(self, places, side, pair):
        return places[side * len(self.brought) + pair]

    def staged_place(self, places, tile):
        start = len(self.sides) * len(self.brought)
        x, z = divmod(tile, self.depth)
        return matched(x, places[start]) * self.depth + matched(z, places[start + 1])

    def offset(self, tile, side):
        ox, oz = self.tiles[tile]
        return (ox, self.sides[side], oz)


def scaled(terms, factor):
    return [factor * term for term in terms]


def separations(plan, rows, cols, side=CELL_SIDE):
    parts = []
    for axis in range(3):
        diff = rows[axis] - cols[axis]
        if plan.wrapped[axis]:
            diff = jnp.where(diff > side, diff - 2.0 * side, diff)
        parts.append(diff)
    return parts


def distance(plan, parts, tile, soften=SOFTEN):
    dist_sq = parts[0] * parts[0] + parts[1] * parts[1] + parts[2] * parts[2] + soften
    if tile == 0:
        row = lax.broadcasted_iota(jnp.int32, dist_sq.shape, 0)
        col = lax.broadcasted_iota(jnp.int32, dist_sq.shape, 1)
        dist_sq = jnp.where(row == col, FAR, dist_sq)
    return dist_sq, lax.rsqrt(dist_sq)


def waves(dist_sq, inverse):
    arg = jnp.minimum(dist_sq * inverse * (1.0 / CELL_SIDE) - 0.5, 0.5)
    square = arg * arg
    return poly(COS_TERMS, square), -(arg * poly(SIN_TERMS, square))


def global_block(plan, far_ref, tile, side, target):
    x, y, z = plan.offset(tile, side)
    return far_ref[plan.global_id((x + target[0], y, z + target[1]))]


def own_columns(plan, block):
    held = jnp.concatenate([block, block], axis=0).T[: plan.slots]
    kind = held[:, 3:4]
    lane = lax.broadcasted_iota(jnp.int32, held.shape, 1)
    live = kind >= 0.0
    held = jnp.where((lane == 0) & ~live, -FAR, held)
    return jnp.where(lane == 3, live.astype(F32), held), kind


def scaled_columns(held):
    return [held[:, axis : axis + 1] * (1.0 / CELL_SIDE) for axis in range(3)]


def basis_of(plan, placed, cols, tile):
    parts = separations(plan, [placed[k : k + 1] for k in range(3)], cols, 1.0)
    dist_sq, inverse = distance(plan, parts, tile, SOFTEN / CUT_SQUARE)
    turn = jnp.minimum(dist_sq * inverse - 0.5, 0.5)
    square = turn * turn
    double = turn * poly(scaled(SIN_TERMS, -2.0), square)
    fade = jnp.maximum(1.0 - dist_sq, 0.0)
    basis = [poly(scaled(COS_TERMS, 1.0 / CELL_SIDE), square) * (fade * fade * inverse)]
    for n in range(1, plan.nbasis):
        basis.append(double * basis[-1] if n == 1 else double * basis[-1] - basis[-2])
    return parts, inverse, basis


def first_kernel(plan, nrefs, places, *refs):
    far_refs, refs = refs[:nrefs], refs[nrefs:]
    (table_ref, wide_ref, embed_ref, mix_ref), refs = refs[:4], refs[4:]
    rows_ref, basis_ref, layer_ref, vector_ref, mixing_ref, cols_ref, pair_ref, block_ref = refs
    slots, nbasis, nspec = plan.slots, plan.nbasis, plan.nspec

    def put(place, block):
        block_ref[place] = block

    if not plan.small:
        scatter(plan, places, far_refs, put)

    def block_of(tile, side, up):
        if plan.small:
            return global_block(plan, far_refs[0], tile, side, (0, up))
        return block_ref[tile * len(plan.sides) + side]

    species = lax.broadcasted_iota(jnp.int32, (nbasis * nspec, plan.width), 0) % nspec
    shifts = [tile_shift(plan, tile) for tile in range(len(plan.tiles))]
    own, counted, places_of = [], [], []
    for which, up in enumerate(plan.column):
        held, kind = own_columns(plan, block_of(0, 0, up))
        own.append(kind)
        if which < plan.known:
            cols_ref[which] = held
        cols = scaled_columns(held)
        places_of.append(cols)
        hot = []
        for tile in range(len(plan.tiles)):
            blocks = [block_of(tile, side, up) for side in range(len(plan.sides))]
            placed = side_by_side(plan, blocks) + shifts[tile]
            if which == 0:
                rows_ref[tile] = placed
            is_kind = placed[3:4].astype(jnp.int32) == species
            placed = placed * (1.0 / CELL_SIDE)
            high = placed.astype(BF16).astype(F32)
            low = placed - high
            columns = [jnp.where(is_kind, 1.0, 0.0)]
            for k in plan.plain:
                columns += [jnp.where(is_kind, part[k : k + 1], 0.0) for part in (high, low)]
            hot.append(jnp.concatenate([column.astype(BF16) for column in columns], axis=0))
            parts, inverse, basis = basis_of(plan, placed, cols, tile)
            scale = inverse * ROOT_THREE
            units = [scale.astype(BF16)] + [(scale * parts[k]).astype(BF16) for k in plan.folded]
            lanes = slice(tile * plan.width, (tile + 1) * plan.width)
            for n in range(nbasis):
                packed = basis[n].astype(BF16)
                if which < plan.known:
                    basis_ref[which, n, :, lanes] = packed
                pair_ref[which, n, :slots, lanes] = packed
                for m, unit in enumerate(units):
                    pair_ref[which, n, (m + 1) * slots : (m + 2) * slots, lanes] = unit * packed
        hot = jnp.concatenate(hot, axis=1)
        gathered = dot(pair_ref[which].reshape(nbasis * plan.kinds * slots, plan.far), hot, NT)
        gathered = gathered.reshape(nbasis, plan.kinds * slots, hot.shape[0])
        group = lax.broadcasted_iota(jnp.int32, gathered.shape[1:], 1) % (nbasis * nspec) // nspec
        total = gathered[0]
        for n in range(1, nbasis):
            total = jnp.where(group == n, gathered[n], total)
        counted.append(total)
    scalar = jnp.concatenate([total[:slots, : nbasis * nspec] for total in counted], axis=0)
    scalar = MSG_SCALE * split_dot(scalar, table_ref[0])
    moved = jnp.concatenate([total[slots : 2 * slots] for total in counted], axis=0)
    moved = MSG_SCALE * split_dot(moved, wide_ref[...])
    channels = layer_ref.shape[2]
    norm = None
    for k in range(3):
        if k in plan.plain:
            start = (plan.plain.index(k) + 1) * channels
            place = jnp.concatenate([cols[k] for cols in places_of], axis=0)
            vector = moved[:, start : start + channels] - place * moved[:, :channels]
        else:
            start = (plan.folded.index(k) + 2) * slots
            vector = [total[start : start + slots, : nbasis * nspec] for total in counted]
            vector = MSG_SCALE * split_dot(jnp.concatenate(vector, axis=0), table_ref[1])
        vector_ref[k * slots : (k + 1) * slots] = vector[:slots]
        norm = vector * vector if k == 0 else norm + vector * vector
    invariants = jnp.concatenate([scalar.astype(BF16), norm.astype(BF16)], axis=1)
    mixing = dot(invariants, mix_ref[...], NT)
    mixing_ref[...] = mixing[:slots]
    kind = jnp.concatenate(own, axis=0)
    own_species = lax.broadcasted_iota(jnp.int32, (kind.shape[0], nspec), 1)
    own_hot = (kind.astype(jnp.int32) == own_species).astype(F32).astype(BF16)
    layer = (dot(own_hot, embed_ref[...]) + mixing * sigmoid(mixing)).astype(BF16)
    for which in range(layer_ref.shape[0]):
        layer_ref[which] = layer[which * slots : (which + 1) * slots]


def sigmoid(value):
    return 1.0 / (1.0 + jnp.exp(-value))


def scatter(plan, places, far_refs, put):
    for side in range(len(plan.sides)):
        for pair, (second, first) in enumerate(plan.brought):
            put(plan.brought_place(places, side, pair), far_refs[side * plan.wide + second][first])


def scatter_held(plan, places, far_refs, put):
    turn = places[len(plan.sides) * len(plan.brought)]
    for side in range(len(plan.sides)):
        for m in range(len(plan.columns)):
            x = matched(m, turn) if m < plan.wide else m
            for z in range(len(plan.column)):
                place = (x * len(plan.column) + z) * len(plan.sides) + side
                put(place, far_refs[m][z] if side == 0 else far_refs[len(plan.columns)][m, z])


def far_blocks(plan, block_ref, target):
    blocks = []
    for x, z in plan.tiles:
        place = plan.held(x + target[0], z + target[1]) * len(plan.sides)
        blocks += [block_ref[place + side] for side in range(len(plan.sides))]
    return jnp.concatenate(blocks, axis=0)


def side_by_side(plan, blocks):
    if len(blocks) == 2:
        lane = lax.broadcasted_iota(jnp.int32, blocks[0].shape, 1)
        return jnp.where(lane < plan.slots, blocks[0], blocks[1])
    return jnp.concatenate([block[:, : plan.slots] for block in blocks], axis=1)


def tile_shift(plan, tile):
    row = lax.broadcasted_iota(jnp.int32, (4, plan.width), 0)
    side = lax.broadcasted_iota(jnp.int32, (4, plan.width), 1) // plan.slots
    shift = jnp.zeros((4, plan.width), F32)
    for s in range(len(plan.sides)):
        for k, steps in enumerate(plan.offset(tile, s)):
            if steps:
                shift = jnp.where((row == k) & (side == s), CELL_SIDE * steps, shift)
    return shift


def gather_far(plan, places, far_refs, all_ref):
    def put(place, block):
        start = pl.multiple_of(place * plan.slots, plan.slots)
        all_ref[pl.ds(start, plan.slots)] = block

    scatter(plan, places, far_refs, put)


def second_kernel(plan, nrefs, places, *refs):
    far_refs, refs = refs[:nrefs], refs[nrefs:]
    (layer_ref, basis_ref, cols_ref, more_ref, more_cols_ref, radial_ref, mix_ref), refs = refs[:7], refs[7:]
    (hidden_ref, out_ref, one_ref), refs = refs[:3], refs[3:]
    adjoint_ref, features_ref, before_ref, own_ref, own_far_ref, block_ref = refs
    slots, nbasis, known = plan.slots, plan.nbasis, len(plan.targets)

    def put(place, block):
        block_ref[place] = block

    (scatter_held if plan.small else scatter)(plan, places, far_refs, put)
    messages, layers, lives = [], [], []
    for which, target in enumerate(plan.targets):
        if plan.small:
            far = far_blocks(plan, block_ref, target)
            layers.append(block_ref[plan.held(*target) * len(plan.sides)])
        else:
            far = block_ref[...].reshape(plan.far, -1)
            layers.append(layer_ref[0])
        first = which < plan.known
        held_ref, held_cols_ref = (basis_ref, cols_ref) if first else (more_ref, more_cols_ref)
        place = which if first else which - plan.known
        lives.append(held_cols_ref[place, :, 3:4])
        if which == 0:
            own_far_ref[...] = far
        summed = dot(held_ref[place].reshape(nbasis * slots, plan.far), far)
        message = summed[:slots] * radial_ref[0:1]
        for n in range(1, nbasis):
            message = message + summed[n * slots : (n + 1) * slots] * radial_ref[n : n + 1]
        messages.append((MSG_SCALE * message).astype(BF16))
    mixing = dot(jnp.concatenate(messages, axis=0), mix_ref[...], NT)
    gate = sigmoid(mixing)
    layer = jnp.concatenate(layers, axis=0).astype(F32)
    features = (layer + mixing * gate).astype(BF16)
    features_ref[...] = features[:slots]
    before = dot(features, hidden_ref[...], NT)
    before_ref[...] = before[:slots]
    open_hidden = sigmoid(before)
    live = jnp.concatenate(lives, axis=0)
    slope = out_ref[...] * (open_hidden * (1.0 + before * (1.0 - open_hidden))) * live
    from_hidden = dot(slope.astype(BF16), hidden_ref[...])
    own_ref[...] = from_hidden[:slots] + one_ref[...] * live[:slots]
    back = from_hidden * (gate * (1.0 + mixing * (1.0 - gate)))
    adjoint = dot(back.astype(BF16), mix_ref[...]).astype(BF16)
    for which in range(known):
        adjoint_ref[which] = adjoint[which * slots : (which + 1) * slots]


def basis_kernel(plan, nrefs, places, *refs):
    far_ref, (layer_ref, again_ref, more_ref, more_cols_ref) = refs[0], refs[nrefs:]
    again_ref[...] = layer_ref[...]
    for which, target in enumerate(plan.targets[plan.known :]):
        held, _ = own_columns(plan, global_block(plan, far_ref, 0, 0, target))
        more_cols_ref[which] = held
        for tile in range(len(plan.tiles)):
            lanes = slice(tile * plan.width, (tile + 1) * plan.width)
            blocks = [global_block(plan, far_ref, tile, s, target) for s in range(len(plan.sides))]
            placed = (side_by_side(plan, blocks) + tile_shift(plan, tile)) * (1.0 / CELL_SIDE)
            basis = basis_of(plan, placed, scaled_columns(held), tile)[2]
            for n in range(plan.nbasis):
                more_ref[which, n, :, lanes] = basis[n].astype(BF16)


def slope_kernel(plan, rows_ref, cols_ref, one_ref, *refs):
    kept_ref, apart_ref, slope_ref, radial_ref, turned_ref = refs
    kept_ref[...] = one_ref[...]
    cols = [cols_ref[0, :, axis : axis + 1] for axis in range(3)]
    for tile in range(len(plan.tiles)):
        lanes = slice(tile * plan.width, (tile + 1) * plan.width)
        parts = separations(plan, [rows_ref[tile, k : k + 1] for k in range(3)], cols)
        for k in range(3):
            apart_ref[k, :, lanes] = parts[k]
        dist_sq, inverse = distance(plan, parts, tile)
        sine, cosine = waves(dist_sq, inverse)
        fade = jnp.maximum(1.0 - dist_sq * (1.0 / CUT_SQUARE), 0.0)
        radial = fade * fade * inverse
        on_sine = -inverse * ((4.0 / CUT_SQUARE) * fade + radial * inverse)
        on_cosine = (math.pi / CELL_SIDE) * (inverse * radial)
        scale = ROOT_THREE * inverse
        scaled = scale * radial
        square = inverse * inverse
        double = 2.0 * cosine
        before_s, now_s, before_c, now_c = None, sine, None, cosine
        for n in range(plan.nbasis):
            if n == 1:
                before_s, now_s = now_s, double * now_s
                before_c, now_c = now_c, double * now_c - 1.0
            elif n > 1:
                before_s, now_s = now_s, double * now_s - before_s
                before_c, now_c = now_c, double * now_c - before_c
            slope = on_sine * now_s + (n + 1.0) * on_cosine * now_c
            factor = scaled * now_s
            slope_ref[n, :, lanes] = slope
            radial_ref[n, :, lanes] = factor
            turned_ref[n, :, lanes] = scale * slope - square * factor


def energy_kernel(plan, *refs):
    (all_ref, adjoint_ref, slope_ref, radial_ref, cols_ref, layer_ref), refs = refs[:6], refs[6:]
    (before_ref, out_ref, one_ref, kept_ref), refs = refs[:4], refs[4:]
    again_ref, pair_ref, energy_ref, features_ref = refs
    slots, nbasis = plan.slots, plan.nbasis
    again_ref[...] = adjoint_ref[:1]
    features_ref[...] = kept_ref[...]
    before = before_ref[...]
    live = jnp.where(lax.broadcasted_iota(jnp.int32, (slots, 8), 1) == 0, cols_ref[0, :, 3:4], 0.0)
    live_row = dot(jnp.ones((1, 8), BF16), live.astype(BF16), NT)
    energy = dot_exact(one_ref[...], layer_ref[0].astype(F32), NT)
    energy = energy + dot_exact(out_ref[...], before * sigmoid(before), NT)
    energy_ref[...] = energy * live_row
    adjoint = adjoint_ref[0].astype(F32) * MSG_SCALE
    weighted = jnp.concatenate(
        [(adjoint * radial_ref[n : n + 1]).astype(BF16) for n in range(nbasis)], axis=0
    )
    for tile in range(len(plan.tiles)):
        lanes = slice(tile * plan.width, (tile + 1) * plan.width)
        pulled = dot(weighted, all_ref[lanes], NT)
        total = slope_ref[0, :, lanes] * pulled[:slots]
        for n in range(1, nbasis):
            total = total + slope_ref[n, :, lanes] * pulled[n * slots : (n + 1) * slots]
        pair_ref[:, lanes] = total


def force_kernel(plan, nrefs, places, *refs):
    far_refs, refs = refs[:nrefs], refs[nrefs:]
    (own_ref, basis_ref, pair_ref, rows_ref), refs = refs[:4], refs[4:]
    (apart_ref, slope_ref, factor_ref, turned_ref), refs = refs[:4], refs[4:]
    (radial_ref, mixing_ref, mix_ref, vector_ref, table_ref), refs = refs[:5], refs[5:]
    out_ref, all_ref = refs
    slots, nbasis, nspec, width = plan.slots, plan.nbasis, plan.nspec, plan.width
    if plan.small:
        far = [far_refs[side][tile] for tile in range(len(plan.tiles)) for side in range(len(plan.sides))]
        far = jnp.concatenate(far, axis=0)
    else:
        gather_far(plan, places, far_refs, all_ref)
        far = all_ref[...]
    summed = dot(basis_ref[0].reshape(nbasis * slots, plan.far), far)
    adjoint = jnp.zeros((slots, summed.shape[1]), F32)
    for n in range(nbasis):
        adjoint = adjoint + summed[n * slots : (n + 1) * slots] * radial_ref[n : n + 1]
    adjoint = own_ref[...] + MSG_SCALE * adjoint
    mixing = mixing_ref[...]
    gate = sigmoid(mixing)
    back = (adjoint * (gate * (1.0 + mixing * (1.0 - gate)))).astype(BF16)
    invariants = dot(back, mix_ref[...])
    channels = invariants.shape[1] // 2
    on_scalar = (MSG_SCALE * invariants[:, :channels]).astype(BF16)
    doubled = (2.0 * MSG_SCALE) * invariants[:, channels:]
    on_vector = (vector_ref[...] * jnp.concatenate([doubled] * 3, axis=0)).astype(BF16)
    weights = jnp.concatenate(
        [dot(on_scalar, table_ref[0], NT), dot(on_vector, table_ref[1], NT)], axis=0
    ).astype(BF16)
    group = lax.broadcasted_iota(jnp.int32, weights.shape, 1) // nspec
    weights = weights.astype(F32)
    weights = jnp.concatenate(
        [jnp.where(group == n, weights, 0.0).astype(BF16) for n in range(nbasis)], axis=0
    )
    species = lax.broadcasted_iota(jnp.int32, (nbasis * nspec, width), 0) % nspec
    own = [jnp.zeros((slots, width), F32) for _ in range(3)]
    pulls = []
    for tile in range(len(plan.tiles)):
        lanes = slice(tile * width, (tile + 1) * width)
        hot = (rows_ref[tile, 3:4].astype(jnp.int32) == species).astype(F32).astype(BF16)
        spread = dot(weights, hot)
        total = pair_ref[:, lanes]
        sides, turns = [None] * 3, [None] * 3
        for n in range(nbasis):
            start = n * 4 * slots
            total = total + slope_ref[n, :, lanes] * spread[start : start + slots]
            for k in range(3):
                piece = spread[start + (k + 1) * slots : start + (k + 2) * slots]
                side = factor_ref[n, :, lanes] * piece
                turn = turned_ref[n, :, lanes] * piece
                sides[k] = side if n == 0 else sides[k] + side
                turns[k] = turn if n == 0 else turns[k] + turn
        for k in range(3):
            total = total + apart_ref[k, :, lanes] * turns[k]
        pulls.append([])
        for k in range(3):
            pull = apart_ref[k, :, lanes] * total + sides[k]
            own[k] = own[k] + pull
            pulls[-1].append(jnp.sum(pull, axis=0, keepdims=True))
    own = jnp.concatenate(own, axis=0)
    high = own.astype(BF16)
    low = (own - high.astype(F32)).astype(BF16)
    ones = jnp.ones((8, width), BF16)
    mine = (dot(ones, high, NT) + dot(ones, low, NT))[:1]
    mine = jnp.concatenate([mine[:, k * slots : (k + 1) * slots] for k in range(3)], axis=0)
    if plan.small:
        out_ref[...] = jnp.zeros_like(out_ref)
    side_of = lax.broadcasted_iota(jnp.int32, (3, width), 1) // slots
    for tile in range(len(plan.tiles)):
        pulled = jnp.concatenate(pulls[tile], axis=0)
        if tile == 0:
            others = [jnp.zeros_like(mine)] * (len(plan.sides) - 1)
            pulled = pulled - jnp.concatenate([mine] + others, axis=1)
        if not plan.small:
            out_ref[plan.staged_place(places, tile)] = pulled
            continue
        for side in range(len(plan.sides)):
            place = plan.global_id(plan.offset(tile, side))
            out_ref[place, :3] = jnp.where(side_of == side, pulled, 0.0)


def begin(pairs, sems):
    copies = [pltpu.make_async_copy(*pair, sems.at[m]) for m, pair in enumerate(pairs)]
    for copy in copies:
        copy.start()
    return copies


def prepare_kernel(plan, counts_ref, *refs):
    fetched, (sent_ref, table_ref, wide_ref), refs = refs[:10], refs[10:13], refs[13:]
    kept, (place_ref, kind_ref, radial_ref, sems) = refs[:7], refs[7:]
    copies = begin(zip(fetched, (place_ref, kind_ref, radial_ref, *kept)), sems)
    wide_ref[...] = jnp.zeros_like(wide_ref)
    for copy in copies[:2]:
        copy.wait()
    live = lax.broadcasted_iota(jnp.int32, (1, plan.slots), 1) < counts_ref[0]
    rows = [
        jnp.where(live, place_ref[0], FAR),
        place_ref[1],
        place_ref[2],
        jnp.where(live, kind_ref[...], -1).astype(F32),
    ]
    rows = jnp.concatenate(rows, axis=0)
    rows = jnp.concatenate([rows, rows], axis=1)
    for copy in range(sent_ref.shape[0]):
        sent_ref[copy] = rows
    for copy in copies[2:4]:
        copy.wait()
    embed, nspec = kept[0][...].astype(F32), plan.nspec
    for g in range(2):
        for n in range(plan.nbasis):
            weighted = radial_ref[g, n : n + 1] * embed
            table_ref[g, n * nspec : (n + 1) * nspec] = weighted.astype(BF16)
    count, channels = table_ref.shape[1:]
    for m in range(1 + 2 * len(plan.plain)):
        start = (m + 1) // 2 * channels
        wide_ref[m * count : (m + 1) * count, start : start + channels] = table_ref[1]
    for copy in copies[4:]:
        copy.wait()


def sum_kernel(plan, parts_ref, force_ref):
    total = parts_ref[0]
    for part in range(1, parts_ref.shape[0]):
        total = total + parts_ref[part]
    total = total[:, : plan.slots] + total[:, plan.slots :]
    for k in range(3):
        force_ref[k] = -total[k : k + 1]


VMEM_SPEC = pl.BlockSpec(memory_space=pltpu.VMEM)
SMEM_SPEC = pl.BlockSpec(memory_space=pltpu.SMEM)
HBM_SPEC = pl.BlockSpec(memory_space=pltpu.HBM)


def simple_call(kernel, plan, operands, outs, scalars=0, scratch=(), flops=2**20, near=False, fetched=0):
    single = not isinstance(outs, list)
    kind = pltpu.VMEM if near else jax.ShapeDtypeStruct
    shapes = [kind(*out) for out in ([outs] if single else outs)]

    def body(*refs):
        kernel(plan, *refs)

    got = pl.pallas_call(
        body,
        out_shape=shapes,
        in_specs=[SMEM_SPEC] * scalars
        + [VMEM_SPEC] * (len(operands) - scalars - fetched)
        + [HBM_SPEC] * fetched,
        out_specs=[VMEM_SPEC] * len(shapes),
        scratch_shapes=[pltpu.VMEM(*buffer) for buffer in scratch]
        + [pltpu.SemaphoreType.DMA((fetched,))] * (fetched > 0),
        compiler_params=pltpu.CompilerParams(vmem_limit_bytes=FETCH_LIMIT if fetched else VMEM_LIMIT),
        cost_estimate=pl.CostEstimate(flops=flops, bytes_accessed=2**20, transcendentals=0),
    )(*operands)
    return got[0] if single else got


def call(kernel, plan, far, operands, outs, scratch, flops, **options):
    def body(plan, *refs):
        kernel(plan, len(far), plan.places(), *refs)

    return simple_call(body, plan, [*far, *operands], outs, 0, scratch, flops, **options)


def swaps(count):
    if count == 2:
        return [[1, 0]]
    if paired(count):
        near = [i ^ 1 for i in range(count)]
        far = [(i - 1 + 2 * (i % 2)) % count for i in range(count)]
        return [near, far]
    return [[(i + o) % count for i in range(count)] for o in offsets_of(count)[1:]]


def brought(plan, block, second, mixed):
    sizes, sources = plan.sizes, {axis: swaps(plan.sizes[axis]) for axis in AXES}
    got = []
    for m in range(len(sources["gx" if second else "gz"])):
        pairs = []
        for x, y, z in itertools.product(*(range(sizes[axis]) for axis in AXES)):
            along_x = second != (mixed and y % 2 == 1)
            source = (sources["gx"][m][x], y, z) if along_x else (x, y, sources["gz"][m][z])
            pairs.append((flat(sizes, *source), flat(sizes, x, y, z)))
        got.append(lax.ppermute(block, AXES, pairs))
    return got


def flat(sizes, x, y, z):
    return (x * sizes["gy"] + y) * sizes["gz"] + z


def along(block, axis):
    return [
        lax.ppermute(block, axis, [(source, i) for i, source in enumerate(sources)])
        for sources in swaps(lax.axis_size(axis))
    ]


def neighbours(plan, block, again=None):
    column = jnp.stack([block if again is None else again] + brought(plan, block, False, plan.mixed))
    return from_columns(plan, column, plan.mixed)


def from_columns(plan, column, mixed):
    columns = [column] + brought(plan, column, True, mixed)
    swapped = [[column] + along(column, "gy") for column in columns]
    return [column[side] for side in range(len(plan.sides)) for column in swapped]


def held_columns(plan, column, again):
    count = plan.sizes["gx"]
    columns = brought(plan, column, True, False)
    for step in plan.columns[plan.wide :]:
        columns.append(lax.ppermute(column, "gx", [((i + step) % count, i) for i in range(count)]))
    return [column, *columns] + along(jnp.stack([again, *columns]), "gy")


def everywhere(copies):
    return lax.all_to_all(copies, AXES, 0, 0, tiled=True)


def folded(pieces, axis):
    total = pieces[0]
    for piece, sources in zip(pieces[1:], swaps(lax.axis_size(axis))):
        total = total + lax.ppermute(piece, axis, list(enumerate(sources)))
    return total


def fold(plan, pulls):
    for axis in ("gx", "gz"):
        parts = len(offsets_of(plan.sizes[axis]))
        pulls = pulls.reshape((parts, -1) + pulls.shape[1:])
        pulls = folded([pulls[m] for m in range(parts)], axis)
    pulls = pulls[0]
    sides = [pulls[:, m * plan.slots : (m + 1) * plan.slots] for m in range(len(plan.sides))]
    return folded(sides, "gy")


def local_program(mesh):
    def local(
        positions,
        species,
        counts,
        embed,
        radial_one,
        mix_one,
        read_one,
        radial_two,
        mix_two,
        read_hidden,
        read_out,
    ):
        slots, channels = positions.shape[-1], embed.shape[1]
        nbasis, nspec = radial_two.shape[0], embed.shape[0]
        plan = Plan(mesh, slots, nbasis, nspec)
        given = [positions[0, 0, 0].reshape(3, 1, slots), species.reshape(1, slots), radial_one]
        weights = [embed, mix_one, radial_two, read_out[None], read_one[None], mix_two, read_hidden]
        sent, table, wide, *weights = simple_call(
            prepare_kernel,
            plan,
            [counts.reshape(1), *given, *weights],
            [
                ((plan.ndev if plan.small else 1, 4, 2 * slots), F32),
                ((2, nbasis * nspec, channels), BF16),
                (((1 + 2 * len(plan.plain)) * nbasis * nspec, (1 + len(plan.plain)) * channels), BF16),
            ]
            + [(weight.shape, weight.dtype) for weight in weights],
            1,
            [(array.shape, array.dtype) for array in given],
            near=True,
            fetched=len(given) + len(weights),
        )
        embed, mix_one, radial_two, out_row, one_row, mix_two, read_hidden = weights
        far_sent = [everywhere(sent)] if plan.small else neighbours(plan, sent[0])
        pair_flops = 100 * slots * plan.far
        rows, basis, layer, vector, mixing, cols = call(
            first_kernel,
            plan,
            far_sent,
            [table, wide, embed, mix_one],
            [
                ((len(plan.tiles), 4, plan.width), F32),
                ((plan.known, nbasis, slots, plan.far), BF16),
                ((len(plan.column), slots, channels), BF16),
                ((3 * slots, channels), F32),
                ((slots, channels), F32),
                ((plan.known, slots, 8), F32),
            ],
            [
                ((len(plan.column), nbasis, plan.kinds * slots, plan.far), BF16),
                ((len(plan.tiles) * len(plan.sides), 4, 2 * slots), F32),
            ],
            pair_flops,
        )
        more = max(len(plan.targets) - plan.known, 1)
        again, more_basis, more_cols = call(
            basis_kernel,
            plan,
            far_sent[:1],
            [layer],
            [
                (layer.shape, BF16),
                ((more, nbasis, slots, plan.far), BF16),
                ((more, slots, 8), F32),
            ],
            [],
            pair_flops,
        )
        one_row, apart, slope, factor, turned = simple_call(
            slope_kernel,
            plan,
            [rows, cols, one_row],
            [(one_row.shape, F32)]
            + [((count, slots, plan.far), F32) for count in (3, nbasis, nbasis, nbasis)],
            flops=pair_flops,
        )
        if plan.small:
            far_layer = held_columns(plan, layer, again)
        else:
            far_layer = neighbours(plan, layer[0], again[0])
        far_scratch = ((plan.far, channels), BF16)
        held = len(plan.columns) * len(plan.column) if plan.small else len(plan.tiles)
        held = held * len(plan.sides)
        adjoint, kept, before, own_adjoint, own_far = call(
            second_kernel,
            plan,
            far_layer,
            [layer, basis, cols, more_basis, more_cols, radial_two, mix_two, read_hidden, out_row, one_row],
            [
                ((len(plan.targets), slots, channels), BF16),
                ((slots, channels), BF16),
                ((slots, read_hidden.shape[0]), F32),
                ((slots, channels), F32),
                far_scratch,
            ],
            [((held, slots, channels), BF16)],
            pair_flops,
        )
        again, pair, energy, features = simple_call(
            energy_kernel,
            plan,
            [own_far, adjoint, slope, radial_two, cols, layer, before, out_row, one_row, kept],
            [
                ((1, slots, channels), BF16),
                ((slots, plan.far), F32),
                ((1, slots), F32),
                ((slots, channels), BF16),
            ],
            flops=pair_flops,
        )
        if plan.small:
            far_adjoint = [adjoint] + along(adjoint, "gy")
        else:
            far_adjoint = neighbours(plan, adjoint[0], again[0])
        pulls = call(
            force_kernel,
            plan,
            far_adjoint,
            [own_adjoint, basis, pair, rows, apart, slope, factor, turned]
            + [radial_two, mixing, mix_one, vector, table],
            [((plan.ndev, 4, plan.width) if plan.small else (len(plan.tiles), 3, plan.width), F32)],
            [far_scratch],
            pair_flops,
        )
        if plan.small:
            forces = simple_call(sum_kernel, plan, [everywhere(pulls[0])], ((3, 1, slots), F32))
        else:
            forces = -fold(plan, pulls[0])
        return (
            forces.reshape(1, 1, 1, 3, slots),
            energy[None, None],
            features.T[None, None, None],
        )

    return local


def solution(mesh):
    split = [P(*AXES, None, None), P(*AXES, None), P(*AXES)]
    out_specs = (P(*AXES, None, None), P(*AXES, None), P(*AXES, None, None))
    return jax.shard_map(
        local_program(mesh),
        mesh=mesh,
        in_specs=tuple(split + [P()] * 8),
        out_specs=out_specs,
        check_vma=False,
    )
```
